32 devices in a mesh: dp: 4 (over x, core), fsdp: 8 (over z, y).
Axes of the slice: x: 2, y: 2, z: 4, core: 2. Of those that a mesh axis runs over, the one named last changes fastest.
Arguments:
- tokens: bfloat16 [2, 16384, 768], P(None, ('dp', 'fsdp')), may hold values from -6 to 6
- lengths: int32 [2, 32], P(None, ('dp', 'fsdp')), may hold values from 256 to 512, as said below
- cotangent: bfloat16 [2, 16384, 768], P(None, ('dp', 'fsdp')), may hold values from -6 to 6
- mixer_in: bfloat16 [768, 3072], P(('dp', 'fsdp')), may hold values from -0.21875 to 0.21875
- w_eta: bfloat16 [768, 12], P(('dp', 'fsdp')), may hold values from -0.21875 to 0.21875
- eta_bias: bfloat16 [12], replicated, may hold values from -1 to 1
- w_out: bfloat16 [768, 768], P(('dp', 'fsdp')), may hold values from -0.4375 to 0.4375
- inner_w: bfloat16 [768, 64], P(('dp', 'fsdp')), may hold values from -0.75 to 0.75
- inner_b: bfloat16 [768], P(('dp', 'fsdp')), may hold values from -3 to 3
- ttt_gain: bfloat16 [768], P(('dp', 'fsdp')), may hold values from 0.5 to 1.5
- ttt_shift: bfloat16 [768], P(('dp', 'fsdp')), may hold values from -2 to 2
- norm_one: bfloat16 [768], P(('dp', 'fsdp')), may hold values from 0.5 to 1.5
- post_gain: bfloat16 [768], P(('dp', 'fsdp')), may hold values from 0.5 to 1.5
- post_shift: bfloat16 [768], P(('dp', 'fsdp')), may hold values from -2 to 2
- w_gate_up: bfloat16 [768, 4096], P(('dp', 'fsdp')), may hold values from -0.21875 to 0.21875
- w_down: bfloat16 [2048, 768], P(('dp', 'fsdp')), may hold values from -0.25 to 0.25
- norm_two: bfloat16 [768], P(('dp', 'fsdp')), may hold values from 0.5 to 1.5
Outputs:
- block_out: bfloat16 [2, 16384, 768], P(None, ('dp', 'fsdp'))
- grad_tokens: bfloat16 [2, 16384, 768], P(None, ('dp', 'fsdp'))
- grad_mixer_in: float32 [768, 3072], P(('dp', 'fsdp'))
- grad_w_eta: float32 [768, 12], P(('dp', 'fsdp'))
- grad_eta_bias: float32 [12], replicated
- grad_w_out: float32 [768, 768], P(('dp', 'fsdp'))
- grad_inner_w: float32 [768, 64], P(('dp', 'fsdp'))
- grad_inner_b: float32 [768], P(('dp', 'fsdp'))
- grad_ttt_gain: float32 [768], P(('dp', 'fsdp'))
- grad_ttt_shift: float32 [768], P(('dp', 'fsdp'))
- grad_norm_one: float32 [768], P(('dp', 'fsdp'))
- grad_post_gain: float32 [768], P(('dp', 'fsdp'))
- grad_post_shift: float32 [768], P(('dp', 'fsdp'))
- grad_w_gate_up: float32 [768, 4096], P(('dp', 'fsdp'))
- grad_w_down: float32 [2048, 768], P(('dp', 'fsdp'))
- grad_norm_two: float32 [768], P(('dp', 'fsdp'))
The draws below stay inside these ranges and needn't reach their ends.
Inputs may be any that keep to these rules, and one draw needn't show every extreme that they name: `lengths`: every entry is a multiple of 16; some entry equals 512.
All inputs are finite; a program needn't handle non-finite values.
Results may differ from the reference program's by a relative error of at most 0.0085.
The reference program's roundings to bfloat16 on the way count: a program that leaves them out, or rounds other values in their place, can miss the bound.
Values may be sent and summed in bfloat16 or wider, within the bound.
No kernel may reach another device: no remote copies, remote signals or barrier semaphores. Data moves between devices by JAX's collectives and lax.ppermute only.
A program may use at most 256 MiB of HBM per device.

```python
import math
import jax
import jax.numpy as jnp
from jax import lax

D = 768
HEADS = 12
HEAD_DIM = 64
FF = 2048
MINI = 16
SLOT = 512
MICRO = 2
SEQS = 32
TOKENS = 16384


def draw_lengths(key, part):
    key = jax.random.fold_in(key, 7)
    first_key, second_key = jax.random.split(key)
    blocks = jax.random.randint(first_key, (MICRO * SEQS,), SLOT // (2 * MINI), SLOT // MINI + 1)
    chosen = jax.random.randint(second_key, (), 0, MICRO * SEQS)
    places = jnp.arange(MICRO * SEQS, dtype=jnp.int32)
    blocks = jnp.where(places == chosen, SLOT // MINI, blocks)
    return (blocks * MINI).reshape(MICRO, SEQS).astype(jnp.int32)


def level_of(own_key, shape, cuts, smallest, high):
    def one(axis_at, blocks):
        draws = jax.random.uniform(jax.random.fold_in(jax.random.fold_in(own_key, 6), axis_at), (blocks,), jnp.float32, smallest / len(cuts), high / len(cuts))
        return jnp.repeat(jnp.exp(draws), shape[axis_at] // blocks).reshape((-1,) + (1,) * (len(shape) - axis_at - 1))

    gain = one(*cuts[0])
    for cut in cuts[1:]:
        gain = gain * one(*cut)
    return gain


def bell_draw(rng, dims, scale, limit, cuts=(), kind=jnp.bfloat16):
    entries = jax.random.normal(rng, dims, jnp.float32) * scale
    if len(cuts) > 0:
        entries = level_of(rng, dims, cuts, -0.22, 0.18) * entries
    return jnp.clip(entries, min=-limit, max=limit).astype(kind)


def setup_inputs(seed: int = 0) -> dict:
    streams_of = jax.random.split(jax.random.key(seed), 18)
    return {
        "tokens": bell_draw(streams_of[0], (MICRO, TOKENS, D), 1.0, 6.0, ((1, 32),)),
        "lengths": draw_lengths(jax.random.fold_in(streams_of[17], 71), 0),
        "cotangent": bell_draw(streams_of[2], (MICRO, TOKENS, D), 1.0, 6.0, ((1, 32),)),
        "mixer_in": bell_draw(streams_of[3], (D, 4 * D), D ** -0.5, 0.21875, ((0, 32),)),
        "w_eta": bell_draw(streams_of[4], (D, HEADS), D ** -0.5, 0.21875, ((0, 32),)),
        "eta_bias": jnp.clip(jax.random.uniform(streams_of[5], (HEADS,), jnp.float32, -1.0, 1.0), -1.0, 1.0).astype(jnp.bfloat16),
        "w_out": bell_draw(streams_of[6], (D, D), (D // 4) ** -0.5, 0.4375, ((0, 32),)),
        "inner_w": bell_draw(streams_of[7], (D, HEAD_DIM), HEAD_DIM ** -0.5, 0.75, ((0, 32),)),
        "inner_b": bell_draw(streams_of[8], (D,), 0.5, 3.0, ((0, 32),)),
        "ttt_gain": jnp.clip(1.0 + 0.1 * jax.random.normal(streams_of[9], (D,), jnp.float32), 0.5, 1.5).astype(jnp.bfloat16),
        "ttt_shift": bell_draw(streams_of[10], (D,), 0.3, 2.0, ((0, 32),)),
        "norm_one": jnp.clip(1.0 + 0.1 * jax.random.normal(streams_of[11], (D,), jnp.float32), 0.5, 1.5).astype(jnp.bfloat16),
        "post_gain": jnp.clip(1.0 + 0.1 * jax.random.normal(streams_of[12], (D,), jnp.float32), 0.5, 1.5).astype(jnp.bfloat16),
        "post_shift": bell_draw(streams_of[13], (D,), 0.3, 2.0, ((0, 32),)),
        "w_gate_up": bell_draw(streams_of[14], (D, 2 * FF), D ** -0.5, 0.21875, ((0, 32),)),
        "w_down": bell_draw(streams_of[15], (FF, D), (FF // 4) ** -0.5, 0.25, ((0, 32),)),
        "norm_two": jnp.clip(1.0 + 0.1 * jax.random.normal(streams_of[16], (D,), jnp.float32), 0.5, 1.5).astype(jnp.bfloat16),
    }


@jax.custom_vjp
def low(v):
    return lax.optimization_barrier(v.astype(jnp.bfloat16)).astype(jnp.float32)

@jax.custom_vjp
def low_back(v):
    return v

def low_keep(v):
    return (low(v), None)

def low_pass(kept, grad):
    return (grad,)

def back_keep(v):
    return (v, None)

def back_low(kept, grad):
    return (low(grad),)
low.defvjp(low_keep, low_pass)
low_back.defvjp(back_keep, back_low)
epsilon = 1e-06
highest = lax.Precision.HIGHEST

def matmul_high(former, latter):
    return jnp.matmul(former, latter, precision=highest)

def rms_norm(values, gains):
    return values * lax.rsqrt(lax.optimization_barrier(jnp.mean(values * values, axis=-1, keepdims=True)) + epsilon) * gains

def layer_norm(values, gains, shifts):
    centred = values - lax.optimization_barrier(jnp.mean(values, axis=-1, keepdims=True))
    return centred * lax.rsqrt(lax.optimization_barrier(jnp.mean(centred * centred, axis=-1, keepdims=True)) + epsilon) * gains + shifts

def inner_step(gains, shifts, running, pieces):
    weight, offset = running
    queries, key_rows, value_rows, rates = pieces
    block_size = queries.shape[-2]
    row_ids = lax.broadcasted_iota(jnp.int32, (block_size, block_size), 0)
    col_ids = lax.broadcasted_iota(jnp.int32, (block_size, block_size), 1)
    lower_mask = (row_ids >= col_ids).astype(queries.dtype)
    token_scale = 1.0 / (row_ids[:, 0] + 1).astype(queries.dtype)
    hidden = jnp.einsum('ghme,ghef->ghmf', key_rows, weight, precision=highest) + offset[:, :, None, :]
    centred = hidden - lax.optimization_barrier(jnp.mean(hidden, axis=-1, keepdims=True))
    inverse = lax.rsqrt(lax.optimization_barrier(jnp.mean(centred * centred, axis=-1, keepdims=True)) + epsilon)
    normed = centred * inverse
    residual_grad = (gains * normed + shifts - (value_rows - key_rows)) * gains
    inner_grad = (residual_grad - lax.optimization_barrier(jnp.mean(residual_grad, axis=-1, keepdims=True)) - normed * lax.optimization_barrier(jnp.mean(residual_grad * normed, axis=-1, keepdims=True))) * inverse
    eta_matrix = token_scale[:, None] * rates[:, :, None, :] * lower_mask
    scores = jnp.einsum('ghme,ghne->ghmn', queries, key_rows, precision=highest)
    updated = jnp.einsum('ghme,ghef->ghmf', queries, weight, precision=highest) + offset[:, :, None, :] - jnp.einsum('ghmn,ghnf->ghmf', eta_matrix * scores + eta_matrix, inner_grad, precision=highest)
    last_row = eta_matrix[:, :, -1, :]
    weight_next = weight - jnp.einsum('ghme,ghmf->ghef', key_rows * last_row[..., None], inner_grad, precision=highest)
    offset_next = offset - jnp.einsum('ghm,ghmf->ghf', last_row, inner_grad, precision=highest)
    result = queries + layer_norm(updated, gains, shifts)
    return ((weight_next, offset_next), result)

def inner_layer(queries, key_rows, value_rows, rates, inner_w, inner_b, ttt_gain, ttt_shift):
    groups, length, width = queries.shape
    heads = rates.shape[-1]
    head_size = width // heads
    blocks = length // MINI

    def split_heads(values):
        return values.reshape(groups, blocks, MINI, heads, head_size).transpose(1, 0, 3, 2, 4)
    rate_blocks = rates.reshape(groups, blocks, MINI, heads).transpose(1, 0, 3, 2)
    start = (jnp.broadcast_to(inner_w.reshape(heads, head_size, head_size), (groups, heads, head_size, head_size)), jnp.broadcast_to(inner_b.reshape(heads, head_size), (groups, heads, head_size)))
    gains = ttt_gain.reshape(heads, 1, head_size)
    shifts = ttt_shift.reshape(heads, 1, head_size)
    stepper = jax.checkpoint(lambda running, pieces: inner_step(gains, shifts, running, pieces))
    final_state, outputs = lax.scan(stepper, start, (split_heads(queries), split_heads(key_rows), split_heads(value_rows), rate_blocks))
    return outputs.transpose(1, 0, 3, 2, 4).reshape(groups, length, width)

def forward(tokens, live_mask, mixer_in, w_eta, eta_bias, w_out, inner_w, inner_b, ttt_gain, ttt_shift, norm_one, post_gain, post_shift, w_gate_up, w_down, norm_two):
    width = tokens.shape[-1]
    heads = eta_bias.shape[0]
    normed = low(rms_norm(tokens, norm_one))
    projected = low_back(matmul_high(normed, mixer_in))
    logits = low_back(matmul_high(normed, w_eta)) + eta_bias
    rates = jax.nn.sigmoid(logits) / (width // heads) * live_mask[..., None]
    inner_out = inner_layer(projected[..., :width], projected[..., width:2 * width], projected[..., 2 * width:3 * width], rates, inner_w, inner_b, ttt_gain, ttt_shift)
    mixed = low(layer_norm(inner_out, post_gain, post_shift) * jax.nn.gelu(projected[..., 3 * width:], approximate=True))
    first = tokens + low_back(matmul_high(mixed, w_out))
    second = low(rms_norm(first, norm_two))
    both = low_back(matmul_high(second, w_gate_up))
    half_width = both.shape[-1] // 2
    activated = low(jax.nn.silu(both[..., :half_width]) * both[..., half_width:])
    return first + low_back(matmul_high(activated, w_down))

def reference(tokens, lengths, cotangent, mixer_in, w_eta, eta_bias, w_out, inner_w, inner_b, ttt_gain, ttt_shift, norm_one, post_gain, post_shift, w_gate_up, w_down, norm_two):
    params = tuple((weight.astype(jnp.float32) for weight in (mixer_in, w_eta, eta_bias, w_out, inner_w, inner_b, ttt_gain, ttt_shift, norm_one, post_gain, post_shift, w_gate_up, w_down, norm_two)))
    per_step = math.gcd(SEQS, max(1, 4096 // SLOT))
    step_count = MICRO * SEQS // per_step
    places = jnp.arange(SLOT, dtype=jnp.int32)
    live_mask = (places[None, None, :] < lengths[:, :, None]).astype(jnp.float32)
    inputs = tokens.astype(jnp.float32).reshape(step_count, per_step, SLOT, D)
    cotangents = cotangent.astype(jnp.float32).reshape(step_count, per_step, SLOT, D)
    masks = live_mask.reshape(step_count, per_step, SLOT)

    def one_group(totals, pieces):
        group_rows, group_cot, group_mask = pieces
        result, pulled = jax.vjp(lambda rows_in, *weights: forward(rows_in, group_mask, *weights), group_rows, *params)
        gradients = pulled(group_cot * group_mask[..., None])
        totals = tuple((former + latter for former, latter in zip(totals, gradients[1:])))
        return (totals, (result, gradients[0]))
    zeroed = tuple((jnp.zeros_like(weight) for weight in params))
    totals, (results, backs) = lax.scan(one_group, zeroed, (inputs, cotangents, masks))
    block_out = results.reshape(MICRO, SEQS * SLOT, D).astype(jnp.bfloat16)
    grad_tokens = backs.reshape(MICRO, SEQS * SLOT, D).astype(jnp.bfloat16)
    return (block_out, grad_tokens, totals[0], totals[1], totals[2], totals[3], totals[4], totals[5], totals[6], totals[7], totals[8], totals[9], totals[10], totals[11], totals[12], totals[13])
```

```python
import jax
import jax.numpy as jnp
from jax import lax
from jax.experimental import pallas as pl
from jax.experimental.pallas import tpu as pltpu
from jax.sharding import PartitionSpec as P
import numpy as np

MINI = 16
HEAD = 64
PAIR = 2 * HEAD
epsilon = 1e-06
low = jnp.bfloat16
full = jnp.float32


def dot_nn(former, latter):
    return lax.dot_general(former, latter, (((1,), (0,)), ((), ())), preferred_element_type=full)


def dot_nt(former, latter):
    return lax.dot_general(former, latter, (((1,), (1,)), ((), ())), preferred_element_type=full)


def tile_of(rows, at):
    return rows[:, PAIR * at : PAIR * (at + 1)]


def expand(rows, sides):
    count = rows.shape[1] // PAIR
    zero = jnp.zeros((MINI, PAIR), rows.dtype)
    blocks = []
    for side in range(2):
        for at in range(count):
            kept = tile_of(rows, at) * sides[side]
            blocks.append(jnp.concatenate([kept if other == at else zero for other in range(count)], axis=1))
    return jnp.concatenate(blocks, axis=0)


def to_feature(rows, left):
    count = rows.shape[1] // PAIR
    stacked = jnp.concatenate([tile_of(rows, at) for at in range(count)] * 2, axis=0).T
    return jnp.where(left[:HEAD], stacked[:HEAD], stacked[HEAD:])


def to_rows(columns, left):
    turned = jnp.concatenate([columns, columns], axis=0).T
    count = 4
    return jnp.concatenate(
        [
            jnp.where(left[:MINI], turned[MINI * at : MINI * (at + 1)], turned[HEAD + MINI * at : HEAD + MINI * (at + 1)])
            for at in range(count)
        ],
        axis=1,
    )


def mean_rows(values):
    return jnp.sum(values, axis=0, keepdims=True) * (1.0 / values.shape[0])


def both_sequences(ref, rows, base, width):
    return jnp.concatenate([ref[0, rows, base : base + width], ref[1, rows, base : base + width]], axis=1)


def store_sequences(ref, rows, base, width, pieces, kind):
    whole = jnp.concatenate(pieces, axis=1)
    ref[0, rows, base : base + width] = whole[:, :width].astype(kind)
    ref[1, rows, base : base + width] = whole[:, width:].astype(kind)


def ttt_forward_kernel(steps, q_ref, k_ref, v_ref, rate_ref, w0_ref, b0_ref, gain_ref, shift_ref, sides_ref, tri_ref, ones_ref,
                       *outs):
    out_ref, w_ref, xh_ref, h_ref, grs_ref, xb_ref, stat_ref, score_ref, w_run, b_run = outs[-10:]
    width = 768

    @pl.when(pl.program_id(0) == 0)
    def _():
        w_run[...] = w0_ref[...]
        b_run[...] = b0_ref[...]

    sides = [sides_ref[0:MINI], sides_ref[MINI : 2 * MINI]]
    left = lax.broadcasted_iota(jnp.int32, (HEAD, PAIR), 1) < HEAD
    tri = tri_ref[0:MINI]
    same_head = ones_ref[...]

    def one(at, carry):
        rows = pl.ds(at * MINI, MINI)
        queries = both_sequences(q_ref, rows, 0, width)
        keys = both_sequences(k_ref, rows, 0, width)
        targets = both_sequences(v_ref, rows, 0, width) - keys
        results = []
        for part in range(3):
            wide = slice(4 * PAIR * part, 4 * PAIR * (part + 1))
            thin = slice(PAIR * part, PAIR * (part + 1))
            gains, shifts = gain_ref[:, thin], shift_ref[:, thin]
            rate = rate_ref[at, :, thin]
            weight, offset = w_run[:, wide], b_run[:, thin]
            weight_low = weight.astype(low)
            w_ref[at, :, wide] = weight_low
            query_low, key_low = queries[:, wide].astype(low), keys[:, wide].astype(low)
            key_block, query_block = expand(key_low, sides), expand(query_low, sides)
            both = dot_nt(weight_low, jnp.concatenate([key_block, query_block], axis=0))
            hidden = both[:, :PAIR] + offset
            centred = hidden - mean_rows(hidden)
            inverse = lax.rsqrt(mean_rows(centred * centred) + epsilon)
            normed = centred * inverse
            target = to_feature(targets[:, wide], left)
            held = gains * normed + shifts - target
            residual = held * gains
            residual_mean = mean_rows(residual)
            cross = mean_rows(residual * normed)
            inner_grad = (residual - residual_mean - normed * cross) * inverse
            scaled = inner_grad * (rate * (1.0 / MINI))
            scaled_low = scaled.astype(low)
            w_run[:, wide] = weight - dot_nn(scaled_low, key_block)
            b_run[:, thin] = offset - dot_nn(scaled_low, same_head)
            scores = dot_nt(query_low, key_block) + 1.0
            mixing = (tri * rate * scores).astype(low)
            mixing_block = jnp.concatenate([mixing] * 8, axis=0) * same_head
            updated = both[:, PAIR:] + offset - dot_nt(inner_grad.astype(low), mixing_block)
            updated = updated - mean_rows(updated)
            updated_inverse = lax.rsqrt(mean_rows(updated * updated) + epsilon)
            updated = updated * updated_inverse
            results.append(to_rows(updated * gains + shifts, left))
            xh_ref[at, :, thin] = normed
            h_ref[at, :, thin] = held
            grs_ref[at, :, thin] = scaled
            xb_ref[at, :, thin] = updated
            stat_ref[at, 0:1, thin] = inverse
            stat_ref[at, 1:2, thin] = residual_mean
            stat_ref[at, 2:3, thin] = cross
            stat_ref[at, 3:4, thin] = updated_inverse
            score_ref[at, :, thin] = scores
        result = queries + jnp.concatenate(results, axis=1)
        out_ref[0, rows, :] = result[:, :width]
        out_ref[1, rows, :] = result[:, width:]
        return carry

    lax.fori_loop(0, steps, one, 0)


def ttt_backward_kernel(steps, q_ref, k_ref, dout_ref, rate_ref, w_ref, xh_ref, h_ref, grs_ref, xb_ref, stat_ref, score_ref,
                        gain_ref, sides_ref, tri_ref, ones_ref, dw_in, db_in, dgain_in, dshift_in, *outs):
    grad_ref, rdr_ref, dw_ref, db_ref, dgain_ref, dshift_ref = outs[-6:]
    width = 768

    @pl.when(pl.program_id(0) == 0)
    def _():
        dw_ref[...] = dw_in[...]
        db_ref[...] = db_in[...]
        dgain_ref[...] = dgain_in[...]
        dshift_ref[...] = dshift_in[...]

    sides = [sides_ref[0:MINI], sides_ref[MINI : 2 * MINI]]
    wide_sides = [jnp.concatenate([side] * 4, axis=0) for side in sides]
    left = lax.broadcasted_iota(jnp.int32, (HEAD, PAIR), 1) < HEAD
    tri = tri_ref[0:MINI]
    tri_turned = tri_ref[MINI : 2 * MINI]
    same_head = ones_ref[...]

    def block_of(weight):
        return jnp.concatenate([weight * wide_sides[0], weight * wide_sides[1]], axis=0)

    def one(step, carry):
        at = steps - 1 - step
        rows = pl.ds(at * MINI, MINI)
        queries = both_sequences(q_ref, rows, 0, width)
        keys = both_sequences(k_ref, rows, 0, width)
        douts = both_sequences(dout_ref, rows, 0, width)
        query_grads, key_grads, value_grads = [], [], []
        for part in range(3):
            wide = slice(4 * PAIR * part, 4 * PAIR * (part + 1))
            thin = slice(PAIR * part, PAIR * (part + 1))
            gains = gain_ref[:, thin]
            rate = rate_ref[at, :, thin]
            normed, held, scaled, updated = xh_ref[at, :, thin], h_ref[at, :, thin], grs_ref[at, :, thin], xb_ref[at, :, thin]
            inverse, residual_mean, cross, updated_inverse = (stat_ref[at, row : row + 1, thin] for row in range(4))
            scores = score_ref[at, :, thin]
            weight_low = w_ref[at, :, wide]
            dweight, doffset = dw_ref[:, wide], db_ref[:, thin]
            dweight_low = dweight.astype(low)
            query_low, key_low = queries[:, wide].astype(low), keys[:, wide].astype(low)
            key_block, query_block = expand(key_low, sides), expand(query_low, sides)
            mixing = (tri * rate * scores).astype(low)
            mixing_block = jnp.concatenate([mixing] * 8, axis=0) * same_head

            dout = to_feature(douts[:, wide], left)
            dupdated = dout * gains
            dupdated = updated_inverse * (dupdated - mean_rows(dupdated) - updated * mean_rows(dupdated * updated))
            dupdated_low = dupdated.astype(low)
            key_dw = dot_nt(dweight_low, key_block) + doffset
            grad_in = -dot_nn(dupdated_low, mixing_block) - (rate * (1.0 / MINI)) * key_dw
            rate_part = -jnp.sum(scaled * key_dw, axis=0, keepdims=True)
            residual = held * gains
            in_mean = mean_rows(grad_in)
            in_cross = mean_rows(grad_in * normed)
            in_held = inverse * (mean_rows(grad_in * residual) - residual_mean * in_mean - cross * in_cross)
            dresidual = inverse * (grad_in - in_mean - normed * in_cross)
            dtarget = dresidual * gains
            dnormed = dtarget * gains - inverse * (grad_in * cross + in_cross * residual)
            dhidden = inverse * (dnormed - mean_rows(dnormed) - normed * (mean_rows(dnormed * normed) + in_held))
            dhidden_low = dhidden.astype(low)
            dgain_ref[:, thin] += dout * updated + dresidual * (held + gains * normed)
            dshift_ref[:, thin] += dout + dtarget
            db_ref[:, thin] = doffset + dot_nn((dupdated + dhidden).astype(low), same_head)
            dw_ref[:, wide] = dweight + dot_nn(
                jnp.concatenate([dupdated_low, dhidden_low], axis=1), jnp.concatenate([query_block, key_block], axis=0)
            )
            dupdated_rows = to_rows(dupdated, left).astype(low)
            dhidden_rows = to_rows(dhidden, left).astype(low)
            scaled_rows = to_rows(-scaled, left).astype(low)
            dtarget_rows = to_rows(dtarget, left)
            dmix = dot_nt(dupdated_rows, expand(scaled_rows, sides)) * tri * MINI
            dmix_turned = dot_nt(scaled_rows, expand(dupdated_rows, sides)) * tri_turned * MINI
            rdr_ref[at, :, thin] = rate_part + jnp.sum(dmix * scores, axis=0, keepdims=True)
            dmix_low, dmix_turned_low = dmix.astype(low), dmix_turned.astype(low)
            for tile in range(4):
                block = block_of(tile_of(weight_low, tile))
                dblock = block_of(tile_of(dweight_low, tile))
                query_grads.append(
                    tile_of(douts[:, wide], tile)
                    + dot_nn(
                        jnp.concatenate([tile_of(dupdated_rows, tile), dmix_low], axis=1),
                        jnp.concatenate([block, tile_of(key_block, tile)], axis=0),
                    )
                )
                key_grads.append(
                    tile_of(dtarget_rows, tile)
                    + dot_nn(
                        jnp.concatenate([tile_of(dhidden_rows, tile), tile_of(scaled_rows, tile), dmix_turned_low], axis=1),
                        jnp.concatenate([block, dblock, tile_of(query_block, tile)], axis=0),
                    )
                )
                value_grads.append(-tile_of(dtarget_rows, tile))
        store_sequences(grad_ref, rows, 0, width, query_grads, low)
        store_sequences(grad_ref, rows, width, width, key_grads, low)
        store_sequences(grad_ref, rows, 2 * width, width, value_grads, low)
        return carry

    lax.fori_loop(0, steps, one, 0)


def ttt_constants():
    lane = np.arange(PAIR)
    row = np.arange(MINI)
    sides = np.concatenate([np.tile(lane < HEAD, (MINI, 1)), np.tile(lane >= HEAD, (MINI, 1))]).astype(np.float32)
    col = lane % MINI
    tri = np.where(col[None] <= row[:, None], 1.0 / (row[:, None] + 1.0), 0.0)
    tri_turned = np.where(row[:, None] <= col[None], 1.0 / (col[None] + 1.0), 0.0)
    ones = (lane[:, None] // MINI == lane[None] // MINI).astype(np.float32)
    return (
        jnp.asarray(sides, low),
        jnp.asarray(np.concatenate([tri, tri_turned]), full),
        jnp.asarray(ones, low),
    )


def spec(shape, index):
    return pl.BlockSpec(shape, index)


def ttt_forward(projected, rates, state, gains, shifts, steps=4):
    count = projected.shape[1] // MINI
    first, begin, end, before = 0, 0, count, None
    queries, keys, values = projected, projected, projected
    sides, tri, ones = ttt_constants()
    whole = lambda *shape: pl.BlockSpec(shape, lambda at: (0,) * len(shape))
    column = lambda place: pl.BlockSpec((2, steps * MINI, 768), lambda at, place=place: (0, first + at, place))
    part = column(0)
    saved = lambda *tail: pl.BlockSpec((steps,) + tail, lambda at: (at, 0, 0))
    made = lambda kind, *tail: jax.ShapeDtypeStruct((end - begin,) + tail, kind)
    extra = [] if before is None else [before]
    inputs = [queries, keys, values, rates, *state, gains, shifts, sides, tri, ones]
    out, *rest = pl.pallas_call(
        lambda *refs: ttt_forward_kernel(steps, *refs),
        grid=((end - begin) // steps,),
        in_specs=[column(0), column(1), column(2), pl.BlockSpec((steps, 1, 384), lambda at: (first + at, 0, 0)), whole(64, 1536), whole(64, 384),
                  whole(64, 384), whole(64, 384), whole(32, 128), whole(32, 128), whole(128, 128)]
        + [pl.BlockSpec(memory_space=pl.ANY)] * len(extra),
        out_specs=[part, saved(64, 1536), saved(64, 384), saved(64, 384), saved(64, 384), saved(64, 384), saved(8, 384),
                   saved(16, 384), whole(64, 1536), whole(64, 384)],
        out_shape=[jax.ShapeDtypeStruct((2, count * MINI, 768), full), made(low, 64, 1536), made(full, 64, 384), made(full, 64, 384),
                   made(full, 64, 384), made(full, 64, 384), made(full, 8, 384), made(full, 16, 384),
                   jax.ShapeDtypeStruct((64, 1536), full), jax.ShapeDtypeStruct((64, 384), full)],
        input_output_aliases={len(inputs): 0} if extra else {},
        compiler_params=pltpu.CompilerParams(vmem_limit_bytes=40 * 1024 * 1024),
        cost_estimate=pl.CostEstimate(flops=(end - begin) * 1_400_000_000, bytes_accessed=(end - begin) * 1_500_000, transcendentals=0),
        name="ttt_forward",
    )(*inputs, *extra)
    return out, rest[:7], rest[7:]


def ttt_backward(projected, dout, rates, saved_arrays, state, gains, begin, end, before, steps=4):
    count = projected.shape[1] // MINI
    first, blocks = begin // steps, (end - begin) // steps
    queries, keys = projected, projected
    sides, tri, ones = ttt_constants()
    whole = lambda *shape: pl.BlockSpec(shape, lambda at: (0,) * len(shape))
    part = lambda width, place=0: pl.BlockSpec((2, steps * MINI, width), lambda at: (0, first + blocks - 1 - at, place))
    saved = lambda *tail: pl.BlockSpec((steps,) + tail, lambda at: (first + blocks - 1 - at, 0, 0))
    made = lambda *tail: pl.BlockSpec((steps,) + tail, lambda at: (blocks - 1 - at, 0, 0))
    extra = [] if before is None else [before]
    inputs = [queries, keys, dout, rates, *saved_arrays, gains, sides, tri, ones, *state]
    states = [whole(64, 1536), whole(64, 384), whole(64, 384), whole(64, 384)]
    grad, rate_back, *state = pl.pallas_call(
        lambda *refs: ttt_backward_kernel(steps, *refs),
        grid=(blocks,),
        in_specs=[part(768), part(768, 1), part(768), saved(1, 384),
                  saved(64, 1536), saved(64, 384), saved(64, 384), saved(64, 384), saved(64, 384), saved(8, 384), saved(16, 384),
                  whole(64, 384), whole(32, 128), whole(32, 128), whole(128, 128)]
        + states + [pl.BlockSpec(memory_space=pl.ANY)] * len(extra),
        out_specs=[part(2304), made(1, 384)] + states,
        out_shape=[jax.ShapeDtypeStruct((2, count * MINI, 2304), low), jax.ShapeDtypeStruct((end - begin, 1, 384), full)]
        + [jax.ShapeDtypeStruct((64, 1536), full)] + [jax.ShapeDtypeStruct((64, 384), full)] * 3,
        input_output_aliases={len(inputs): 0} if extra else {},
        compiler_params=pltpu.CompilerParams(vmem_limit_bytes=40 * 1024 * 1024),
        cost_estimate=pl.CostEstimate(flops=(end - begin) * 2_000_000_000, bytes_accessed=(end - begin) * 1_500_000, transcendentals=0),
        name="ttt_backward",
    )(*inputs, *extra)
    return grad, rate_back, state


def silu_parts(gate):
    sigma = jax.nn.sigmoid(gate)
    return gate * sigma, sigma * (1.0 + gate * (1.0 - sigma))


def gelu_parts(values):
    slope = 0.7978845608028654
    turn = jnp.tanh(slope * (values + 0.044715 * values * values * values))
    half = 0.5 * (1.0 + turn)
    return values * half, half + 0.5 * values * (1.0 - turn * turn) * slope * (1.0 + 3 * 0.044715 * values * values)


def row_mean(values):
    return jnp.mean(values, axis=-1, keepdims=True)


def dot_tn(former, latter):
    return lax.dot_general(former, latter, (((0,), (0,)), ((), ())), preferred_element_type=full)


def exact_dot(former, latter):
    total = None
    for _ in range(3):
        part = former.astype(low)
        former = former - part.astype(full)
        term = dot_nn(part, latter)
        total = term if total is None else total + term
    return total


def constant_spec(*shape, at=0, buffers=None):
    index = lambda *steps: (0,) * (len(shape) - 1) + (at,)
    if buffers is None:
        return pl.BlockSpec(shape, index)
    return pl.BlockSpec(shape, index, pipeline_mode=pl.Buffered(buffers))


def call(kernel, name, grid, prefetch, in_specs, out_specs, out_shape, scratch, cost, arrays):
    return pl.pallas_call(
        kernel,
        grid_spec=pltpu.PrefetchScalarGridSpec(
            num_scalar_prefetch=prefetch, grid=grid, in_specs=in_specs, out_specs=out_specs, scratch_shapes=scratch
        ),
        out_shape=out_shape,
        compiler_params=pltpu.CompilerParams(vmem_limit_bytes=56 * 1024 * 1024),
        cost_estimate=pl.CostEstimate(flops=cost, bytes_accessed=cost // 500, transcendentals=0),
        name=name,
    )(*arrays)


ETA = 64
VECTORS = 80
BIAS = 96


def lane_table():
    lane = np.arange(384)
    part, side, tile, token = lane // 128, lane // 64 % 2, lane // 16 % 4, lane % 16
    pair = 4 * part + tile
    return token, pair // 6, 2 * (pair % 6) + side


def lane_constants():
    token, sequence, head = lane_table()
    table = np.zeros((32, 384), np.float32)
    table[:MINI] = token[None] == np.arange(MINI)[:, None]
    table[16], table[17] = sequence, token
    chosen = np.zeros((PAIR, 384), np.float32)
    chosen[ETA + head, np.arange(384)] = 1
    return jnp.asarray(table), jnp.asarray(chosen, low)


def project_kernel(length_ref, tokens_ref, w_ref, bias_ref, table_ref, chosen_ref,
                   proj_ref, normed_ref, rate_ref, rest_ref, wt_ref, b_ref, gain_ref, shift_ref, vec_ref):
    at = pl.program_id(0)
    wide = w_ref.shape[1] - PAIR

    @pl.when(at == 0)
    def _():
        small = w_ref[:, wide:].astype(full)
        turned = small.T
        wt_ref[:, :768] = turned[:HEAD]
        wt_ref[:, 768:] = turned[:HEAD]
        vec_ref[...] = turned[VECTORS : VECTORS + 8]
        for place, ref in enumerate((b_ref, gain_ref, shift_ref)):
            total = jnp.zeros((HEAD, 384), full)
            for head in range(12):
                column = small[HEAD * head : HEAD * (head + 1), VECTORS + place : VECTORS + place + 1]
                total = total + column * chosen_ref[ETA + head : ETA + head + 1].astype(full)
            ref[...] = total
        rate_ref[...] = jnp.zeros_like(rate_ref)
        rest_ref[...] = jnp.zeros_like(rest_ref)

    values = tokens_ref[...].astype(full)
    normed = (values * lax.rsqrt(row_mean(values * values) + epsilon) * vec_ref[3:4]).astype(low)
    normed_ref[...] = normed
    proj_ref[:, :wide] = dot_nn(normed, w_ref[:, :wide])
    last = dot_nn(normed, w_ref[:, wide:])
    proj_ref[:, wide:] = last
    spread = exact_dot(last + bias_ref[...], chosen_ref[...])
    blocks = spread.shape[0] // MINI
    spread = jnp.sum(spread.reshape(blocks, MINI, 384) * table_ref[:MINI][None], axis=1)
    sequence, token = table_ref[16:17], table_ref[17:18]
    mine = sequence == (at // 2).astype(full)
    sigma = jax.nn.sigmoid(spread)
    begin = (at % 2) * blocks
    block = lax.broadcasted_iota(jnp.int32, spread.shape, 0) + begin
    live = (block * MINI).astype(full) + token < length_ref[at // 2].astype(full)
    here = pl.ds(begin, blocks)
    rate_ref[here, 0, :] += jnp.where(live & mine, sigma * (1.0 / HEAD), 0.0)
    rest_ref[here, :] += jnp.where(mine, 1.0 - sigma, 0.0)


def project(lengths, tokens, whole, bias_row):
    rows, width = tokens.shape
    table, chosen = lane_constants()
    tile = rows // 4
    columns = whole.shape[1]
    row = lambda n: pl.BlockSpec((tile, n), lambda at, *_: (at, 0))
    shape = jax.ShapeDtypeStruct
    return call(
        project_kernel, "project", (4,), 1,
        [row(width), constant_spec(width, columns, buffers=1), constant_spec(1, PAIR), constant_spec(32, 384), constant_spec(PAIR, 384)],
        [row(columns), row(width), constant_spec(32, 1, 384), constant_spec(32, 384), constant_spec(64, 1536)]
        + [constant_spec(64, 384)] * 3 + [constant_spec(8, width)],
        [shape((rows, columns), full), shape((rows, width), low), shape((32, 1, 384), full), shape((32, 384), full),
         shape((64, 1536), full)] + [shape((64, 384), full)] * 3 + [shape((8, width), full)],
        [], 5_000_000_000, (lengths, tokens, whole, bias_row, table, chosen),
    )


def post_kernel(inner_ref, normed_ref, tokens_ref, w_gate_ref, w_out_ref, vec_ref, gate_ref, mixed_ref, first_ref, second_ref):
    gate = dot_nn(normed_ref[...], w_gate_ref[...])
    gate_ref[...] = gate
    inner = inner_ref[...]
    centred = inner - row_mean(inner)
    standard = centred * lax.rsqrt(row_mean(centred * centred) + epsilon)
    mixed = ((standard * vec_ref[4:5] + vec_ref[5:6]) * gelu_parts(gate)[0]).astype(low)
    mixed_ref[...] = mixed
    first = tokens_ref[...].astype(full) + dot_nn(mixed, w_out_ref[...])
    first_ref[...] = first
    second_ref[...] = (first * lax.rsqrt(row_mean(first * first) + epsilon) * vec_ref[6:7]).astype(low)


def post(inner, normed, tokens, fetched, vectors):
    rows, width = tokens.shape
    tile = rows // 4
    row = pl.BlockSpec((tile, width), lambda at: (at, 0))
    shape = jax.ShapeDtypeStruct
    return call(
        post_kernel, "post", (4,), 0,
        [row, row, row, constant_spec(width, width, at=0, buffers=1), constant_spec(width, width, at=1, buffers=1), constant_spec(8, width)],
        [row] * 4, [shape((rows, width), kind) for kind in (full, low, full, low)], [], 4_000_000_000,
        (inner, normed, tokens, fetched, fetched, vectors),
    )


def store_blocks(table_ref, out_ref, held_ref, block, first=0):
    if block % 8:
        out_ref[...] = held_ref[...].astype(out_ref.dtype)
        return
    for pair in range(held_ref.shape[0] // (2 * block)):
        rows = [held_ref[pl.ds(pl.multiple_of(table_ref[2 * pair + side] * block, 8), block), :] for side in range(2)]
        out_ref[2 * block * pair : 2 * block * (pair + 1), :] = jnp.concatenate(rows, axis=0).astype(out_ref.dtype)


def ffn_kernel(block, down_block, table_ref, place_ref, second_ref, first_ref, up_ref, w_gate_ref, w_up_ref, w_down_ref,
               out_ref, dsecond_ref, dboth_ref, ddown_ref, turned, total, act, both_low, held):
    at = pl.program_id(0)
    rows = second_ref.shape[0]
    tile = 256

    @pl.when(at == 0)
    def _():
        turned[...] = second_ref[...].T
        total[...] = first_ref[...]
        dsecond_ref[...] = jnp.zeros_like(dsecond_ref)

    w_gate, w_up, w_down = w_gate_ref[...], w_up_ref[...], w_down_ref[...]

    def one(place, carry):
        here = pl.ds(place * tile, tile)
        second, upstream = second_ref[here, :], up_ref[here, :]
        gate, up = dot_nn(second, w_gate), dot_nn(second, w_up)
        value, slope = silu_parts(gate)
        activated = (value * up).astype(low)
        act[here, :] = activated
        total[here, :] += dot_nn(activated, w_down)
        dact = dot_nt(upstream, w_down)
        dgate, dup = (dact * up * slope).astype(low), (dact * value).astype(low)
        both_low[here, : dgate.shape[1]] = dgate
        both_low[here, dgate.shape[1] :] = dup
        dsecond_ref[here, :] += dot_nt(dgate, w_gate) + dot_nt(dup, w_up)
        return carry

    lax.fori_loop(0, rows // tile, one, 0)
    held[...] = dot_nn(turned[...], both_low[...])
    store_blocks(table_ref, dboth_ref, held, block)
    ddown = dot_tn(act[...], up_ref[...]).astype(low)
    count = ddown.shape[0] // down_block
    for place in range(count):
        to = pl.multiple_of(place_ref[at * count + place] * down_block, 16)
        ddown_ref[pl.ds(to, down_block), :] = ddown[down_block * place : down_block * (place + 1)]

    @pl.when(at == pl.num_programs(0) - 1)
    def _():
        out_ref[...] = total[...].astype(low)


def ffn(table, inverse, second, first, upstream, fetched, w_down, devices, steps):
    rows, width = second.shape
    hidden = w_down.shape[0]
    size = hidden // steps
    begin = 2 * width // size
    shape = jax.ShapeDtypeStruct
    column = lambda first: pl.BlockSpec((width, size), lambda at, *_, first=first: (0, first + at))
    return call(
        lambda *refs: ffn_kernel(width // devices, hidden // devices, *refs), "ffn", (steps,), 2,
        [constant_spec(rows, width, buffers=1)] * 3 + [column(begin), column(begin + steps),
         pl.BlockSpec((size, width), lambda at, *_: (at, 0))],
        [constant_spec(rows, width, buffers=1), constant_spec(rows, width, buffers=1),
         pl.BlockSpec((width, 2 * size), lambda at, *_: (0, at)), constant_spec(hidden, width, buffers=1)],
        [shape((rows, width), low), shape((rows, width), full), shape((width, 2 * hidden), low), shape((hidden, width), low)],
        [pltpu.VMEM((width, rows), low), pltpu.VMEM((rows, width), full), pltpu.VMEM((rows, size), low),
         pltpu.VMEM((rows, 2 * size), low), pltpu.VMEM((width, 2 * size), full)],
        29_000_000_000, (table, inverse, second, first, upstream, fetched, fetched, w_down),
    )


def post_back_kernel(block, table_ref, dsecond_ref, first_ref, up_ref, inner_ref, gate_ref, mixed_ref, normed_ref, w_out_ref, vec_ref,
                     dfirst_ref, dgate_ref, dinner_ref, sums_ref, dout_ref, held):
    at = pl.program_id(0)

    @pl.when(at == 0)
    def _():
        sums_ref[...] = jnp.zeros_like(sums_ref)
        held[...] = jnp.zeros_like(held)

    width = first_ref.shape[1]
    first, dsecond = first_ref[...], dsecond_ref[...]
    scale = lax.rsqrt(row_mean(first * first) + epsilon)
    two_sum = jnp.sum(dsecond * first * scale, axis=0, keepdims=True)
    dsecond = dsecond * vec_ref[6:7]
    dfirst = up_ref[...].astype(full) + scale * dsecond - first * (scale * scale * scale * row_mean(first * dsecond))
    dfirst_ref[...] = dfirst
    dfirst_low = dfirst.astype(low)
    held[:, :width] += dot_tn(mixed_ref[...], dfirst_low)
    dmixed = dot_nt(dfirst_low, w_out_ref[...])
    inner = inner_ref[...]
    centred = inner - row_mean(inner)
    inverse = lax.rsqrt(row_mean(centred * centred) + epsilon)
    standard = centred * inverse
    value, slope = gelu_parts(gate_ref[...])
    dgate = (dmixed * (standard * vec_ref[4:5] + vec_ref[5:6]) * slope).astype(low)
    dgate_ref[...] = dgate
    held[:, width:] += dot_tn(normed_ref[...], dgate)
    dpost = dmixed * value
    sums_ref[4:5] += jnp.sum(dpost * standard, axis=0, keepdims=True)
    sums_ref[5:6] += jnp.sum(dpost, axis=0, keepdims=True)
    sums_ref[6:7] += two_sum
    dpost = dpost * vec_ref[4:5]
    dinner_ref[...] = inverse * (dpost - row_mean(dpost) - standard * row_mean(dpost * standard))

    @pl.when(at == pl.num_programs(0) - 1)
    def _():
        store_blocks(table_ref, dout_ref, held, block)


def post_back(table, dsecond, first, upstream, inner, gate, mixed, normed, fetched, vectors, devices):
    rows, width = first.shape
    tile = rows // 4
    row = pl.BlockSpec((tile, width), lambda at, *_: (at, 0))
    shape = jax.ShapeDtypeStruct
    return call(
        lambda *refs: post_back_kernel(width // devices, *refs), "post_back", (4,), 1,
        [row] * 7 + [constant_spec(width, width, at=1, buffers=1), constant_spec(8, width)],
        [row, row, row, constant_spec(8, width), constant_spec(width, 2 * width, buffers=1)],
        [shape((rows, width), full), shape((rows, width), low), shape((rows, width), full), shape((8, width), full),
         shape((width, 2 * width), low)],
        [pltpu.VMEM((width, 2 * width), full)], 5_000_000_000,
        (table, dsecond, first, upstream, inner, gate, mixed, normed, fetched, vectors),
    )


def weight_kernel(block, table_ref, normed_ref, grad_ref, out_ref, turned, held):
    @pl.when(pl.program_id(0) == 0)
    def _():
        turned[...] = normed_ref[...].T

    held[...] = dot_nn(turned[...], grad_ref[...])
    store_blocks(table_ref, out_ref, held, block)


def weight_grads(table, normed, grads, devices):
    rows, width = normed.shape
    columns = grads.shape[1]
    size = 384
    shape = jax.ShapeDtypeStruct
    return call(
        lambda *refs: weight_kernel(width // devices, *refs), "weight_grads", (columns // size,), 1,
        [constant_spec(rows, width, buffers=1), pl.BlockSpec((rows, size), lambda at, *_: (0, at))],
        pl.BlockSpec((width, size), lambda at, *_: (0, at)), shape((width, columns), low),
        [pltpu.VMEM((width, rows), low), pltpu.VMEM((width, size), full)], 4_000_000_000, (table, normed, grads),
    )


def finish_kernel(tokens_ref, dfirst_ref, dqkv_ref, dgate_ref, rate_ref, rest_ref, w_ref, w_gate_ref, vec_ref, table_ref, chosen_ref,
                  out_ref, dlog_ref, sums_ref):
    at = pl.program_id(0)
    wide = dqkv_ref.shape[1]

    @pl.when(at == 0)
    def _():
        sums_ref[...] = jnp.zeros_like(sums_ref)

    blocks = tokens_ref.shape[0] // MINI
    here = pl.ds((at % 2) * blocks, blocks)
    mine = (table_ref[16:17] == (at // 2).astype(full)).astype(full)
    dlog = rate_ref[here, 0, :] * rest_ref[here, :] * mine
    dlog = (dlog[:, None, :] * table_ref[:MINI][None]).reshape(blocks * MINI, 384).astype(low)
    dlog = dot_nt(dlog, chosen_ref[...]).astype(low)
    dlog_ref[...] = dlog
    dnormed = dot_nt(dqkv_ref[...], w_ref[:, :wide]) + dot_nt(dgate_ref[...], w_gate_ref[...]) + dot_nt(dlog, w_ref[:, wide:])
    values = tokens_ref[...].astype(full)
    scale = lax.rsqrt(row_mean(values * values) + epsilon)
    sums_ref[3:4] += jnp.sum(dnormed * values * scale, axis=0, keepdims=True)
    dnormed = dnormed * vec_ref[3:4]
    back = scale * dnormed - values * (scale * scale * scale * row_mean(values * dnormed))
    out_ref[...] = (dfirst_ref[...] + back).astype(low)


def finish(tokens, dfirst, dqkv, dgate, rate_back, rest, whole, fetched, vectors):
    rows, width = tokens.shape
    tile = rows // 4
    table, chosen = lane_constants()
    row = lambda n: pl.BlockSpec((tile, n), lambda at: (at, 0))
    shape = jax.ShapeDtypeStruct
    return call(
        finish_kernel, "finish", (4,), 0,
        [row(width), row(width), row(3 * width), row(width), constant_spec(32, 1, 384), constant_spec(32, 384),
         constant_spec(width, whole.shape[1], buffers=1), constant_spec(width, width, at=0, buffers=1), constant_spec(8, width),
         constant_spec(32, 384), constant_spec(PAIR, 384)],
        [row(width), row(PAIR), constant_spec(8, width)],
        [shape((rows, width), low), shape((rows, PAIR), low), shape((8, width), full)], [], 7_000_000_000,
        (tokens, dfirst, dqkv, dgate, rate_back, rest, whole, fetched, vectors, table, chosen),
    )


def pack_kernel(block, table_ref, normed_ref, dlog_ref, sums_ref, more_ref, dw_ref, db_ref, dgain_ref, dshift_ref, rate_ref, rest_ref,
                chosen_ref, out_ref, held):
    width = sums_ref.shape[1]
    eta = dot_tn(dlog_ref[...], normed_ref[...])
    inner = dw_ref[:, :width] + dw_ref[:, width:]
    rows = jnp.concatenate(
        [inner, eta[ETA : ETA + 16], sums_ref[...] + more_ref[...], jnp.zeros((PAIR - VECTORS - 8, width), full)], axis=0
    )
    lane = lax.broadcasted_iota(jnp.int32, (HEAD, PAIR), 1)
    chosen = chosen_ref[...].astype(full)
    bias = jnp.sum(rate_ref[:, 0, :] * rest_ref[...], axis=0, keepdims=True)
    held[...] = rows.T
    bias = jnp.sum(chosen * bias, axis=1, keepdims=True)
    square = jnp.broadcast_to(bias, (PAIR, PAIR)).T[:1]
    bias_row = pltpu.roll(square, BIAS - ETA, axis=1)
    bias_row = jnp.where((lane[:1] >= BIAS) & (lane[:1] < BIAS + 12), bias_row, 0.0)
    for head in range(12):
        here = pl.ds(HEAD * head, HEAD)
        mask = chosen[ETA + head : ETA + head + 1]
        total = held[here, :] + bias_row
        for place, (ref, share) in enumerate(((db_ref, 1.0 / MINI), (dgain_ref, 1.0), (dshift_ref, 1.0))):
            column = jnp.sum(ref[...] * mask, axis=1, keepdims=True) * share
            total = total + jnp.where(lane == VECTORS + place, column, 0.0)
        held[here, :] = total
    store_blocks(table_ref, out_ref, held, block)


def pack(table, normed, dlog, sums, more, state, rate_back, rest, devices):
    rows, width = normed.shape
    _, chosen = lane_constants()
    spec = lambda array: constant_spec(*array.shape, buffers=1)
    arrays = (normed, dlog, sums, more, *state, rate_back, rest, chosen)
    return call(
        lambda *refs: pack_kernel(width // devices, *refs), "pack", (1,), 1,
        [spec(array) for array in arrays], constant_spec(width, PAIR, buffers=1), jax.ShapeDtypeStruct((width, PAIR), full),
        [pltpu.VMEM((width, PAIR), full)], 1_000_000_000, (table, *arrays),
    )


class Links:
    def __init__(self, dp, fsdp):
        self.axes = ("dp", "fsdp")
        self.count = dp * fsdp
        self.core = fsdp
        self.far = fsdp // 2
        bits = [1 << place for place in reversed(range(self.count.bit_length() - 1))]
        self.others = [bit for bit in bits if bit != self.core]
        near = [bit for bit in self.others if bit != self.far]
        self.orders = [near, near[1:] + near[:1]]
        self.phases = len(near)
        self.me = lax.axis_index("dp") * fsdp + lax.axis_index("fsdp")
        self.side = (self.me // self.core) % 2

    def swap(self, values, bits):
        pairs = [(place, place ^ bits[(place // self.core) % 2]) for place in range(self.count)]
        return lax.ppermute(values, self.axes, pairs)

    def gather(self, own, behind, at):
        orders = [[self.far] + order for order in self.orders]
        held = own
        for phase in range(len(orders[0])):
            if phase == at:
                held, behind = tie(held, behind)
            bits = [order[phase] for order in orders]
            got = self.swap(held, bits)
            ones = [(self.me // bit) % 2 for bit in bits]
            mine = jnp.where(self.side == 0, ones[0], ones[1]) == 0
            held = jnp.stack([jnp.where(mine, held, got), jnp.where(mine, got, held)])
        got = self.swap(held, [self.core] * 2)
        mine = self.side == 0
        pair = [jnp.where(mine, held, got), jnp.where(mine, got, held)]
        placed = []
        for array, order in zip(pair, orders):
            have = order[::-1]
            placed.append(array.transpose([have.index(bit) for bit in self.others] + [len(have), len(have) + 1]))
        above = [bit for bit in self.others if bit > self.core]
        return jnp.stack(placed, axis=len(above)).reshape(-1, own.shape[-1]), behind

    def tables(self):
        half = []
        for side in range(2):
            masks = self.orders[side] + [self.far]
            half.append(np.array([sum(bit for at, bit in enumerate(masks) if place >> (len(masks) - 1 - at) & 1)
                                  for place in range(self.count // 2)], np.int32))
        keep = jnp.where(self.side == 0, half[0], half[1])
        send = jnp.where(self.side == 0, half[1], half[0])
        table = jnp.concatenate([self.me ^ keep, self.me ^ self.core ^ send]).astype(jnp.int32)
        places = jnp.arange(self.count, dtype=jnp.int32)
        inverse = jnp.sum(jnp.where(table[None] == places[:, None], places[None], 0), axis=1).astype(jnp.int32)
        return table, inverse

    def scatter(self, arrays, wires):
        steps = [[self.core] * 2] + [list(pair) for pair in zip(*self.orders)] + [[self.far] * 2]
        for bits in steps:
            halves = [array.shape[0] // 2 for array in arrays]
            got = [self.swap(array[half:].astype(wire), bits) for array, half, wire in zip(arrays, halves, wires)]
            arrays = [array[:half].astype(full) + other.astype(full) for array, half, other in zip(arrays, halves, got)]
            changed = yield arrays
            arrays = arrays if changed is None else changed


def tie(*groups):
    flat, tree = jax.tree.flatten(groups)
    return jax.tree.unflatten(tree, lax.optimization_barrier(flat))


def in_order(table, array, rows):
    if rows % 8 == 0:
        return array
    return array.reshape((-1, rows) + array.shape[1:])[table].reshape(array.shape)


def body(dp, fsdp, tokens, lengths, cotangent, mixer_in, w_eta, eta_bias, w_out, inner_w, inner_b, ttt_gain, ttt_shift,
         norm_one, post_gain, post_shift, w_gate_up, w_down, norm_two):
    links = Links(dp, fsdp)
    devices = dp * fsdp
    micro, slots, width = tokens.shape
    rows = micro * slots
    heads = eta_bias.shape[0]
    head = width // heads
    hidden = w_gate_up.shape[1] // 2
    device_rows = width // devices
    table, inverse = links.tables()
    zeros = lambda columns: jnp.zeros((device_rows, columns), low)

    vectors = jnp.stack([inner_b, ttt_gain, ttt_shift, norm_one, post_gain, post_shift, norm_two])
    vectors = dot_tn(vectors, jnp.eye(7, PAIR, VECTORS, dtype=low)).astype(low)
    small = jnp.concatenate([inner_w, w_eta, zeros(PAIR - ETA - heads)], axis=1) + vectors
    parts = 3
    share = device_rows // parts
    piece = width // parts
    own_down = w_down.reshape(-1, share, parts, piece).transpose(2, 1, 0, 3).reshape(device_rows, hidden)
    own_rest = jnp.concatenate([mixer_in[:, 3 * width :], w_out, w_gate_up, own_down], axis=1)
    own = jnp.concatenate([mixer_in[:, : 3 * width], small], axis=1)
    whole, own_rest = links.gather(own, own_rest, 3)
    fetched = lax.all_gather(own_rest, ("dp", "fsdp"), axis=0, tiled=True)
    whole_down = fetched[:, 2 * width + 2 * hidden :].reshape(devices, parts, share, -1, piece).transpose(0, 3, 2, 1, 4)
    whole_down = whole_down.reshape(hidden, width)

    places = lax.broadcasted_iota(jnp.int32, (micro, slots), 1)
    live = places < lengths
    upstream = jnp.where(live[..., None], cotangent, jnp.zeros_like(cotangent)).reshape(rows, width)
    inputs = tokens.reshape(rows, width)
    bias_row = jnp.pad(eta_bias.astype(full), (ETA, PAIR - ETA - heads)).reshape(1, PAIR)
    projected, normed, rate_lanes, rest_lanes, start_w, start_b, gain_lanes, shift_lanes, vec_rows = project(
        lengths.reshape(micro), inputs, whole, bias_row
    )
    projected = projected.reshape(micro, slots, -1)
    inner, saved, _ = ttt_forward(projected, rate_lanes, [start_w, start_b], gain_lanes, shift_lanes)
    inner = inner.reshape(rows, width)
    gate, mixed, first, second = post(inner, normed, inputs, fetched, vec_rows)
    block_out, dsecond, grad_both, grad_down = ffn(
        table, inverse, second, first, upstream, fetched, whole_down, devices, dp
    )
    large_phases = links.scatter([in_order(table, grad_both, device_rows), grad_down], [low] * 2)
    large = next(large_phases)
    dsecond, large = tie(dsecond, large)
    large = large_phases.send(large)
    dfirst, dgate, dinner, sums, grad_middle = post_back(
        table, dsecond, first, upstream, inner, gate, mixed, normed, fetched, vec_rows, devices
    )
    middle_phases = links.scatter([in_order(table, grad_middle, device_rows)], [low])
    middle = next(middle_phases)
    dinner, middle = tie(dinner, middle)
    middle = middle_phases.send(middle)
    dinner = dinner.reshape(micro, slots, width)
    state = [jnp.zeros((HEAD, 1536), full)] + [jnp.zeros((HEAD, 384), full)] * 3
    dqkv, rate_back = None, []
    cuts = [32, 20, 12, 8, 0]
    for end, begin in zip(cuts[:-1], cuts[1:]):
        dqkv, rate_part, state = ttt_backward(
            projected, dinner, rate_lanes, saved, state, gain_lanes, begin, end, dqkv
        )
        rate_back.insert(0, rate_part)
        state, dqkv, large, middle = tie(state, dqkv, large, middle)
        large = next_or(large_phases, large)
        middle = next_or(middle_phases, middle)
    large, middle = drain(large_phases, large), drain(middle_phases, middle)
    dqkv = dqkv.reshape(rows, 3 * width)
    rate_back = jnp.concatenate(rate_back, axis=0)
    grad_mixer = in_order(table, weight_grads(table, normed, dqkv, devices), device_rows)
    last_phases = links.scatter([grad_mixer], [low])
    last = next(last_phases)
    dfirst, last = tie(dfirst, last)
    last = last_phases.send(last)
    grad_tokens, dlog, more = finish(inputs, dfirst, dqkv, dgate, rate_back, rest_lanes, whole, fetched, vec_rows)
    dlog, last = tie(dlog, last)
    last = last_phases.send(last)
    small_grad = pack(table, normed, dlog, sums, more, state, rate_back, rest_lanes, devices)
    small_grad, last = tie(small_grad, last)
    small_phases = links.scatter([in_order(table, small_grad, device_rows)], [full])
    last, (out_small,) = drain(last_phases, last_phases.send(last)), drain(small_phases, next(small_phases))
    out_inner_b, out_gain, out_shift, out_norm_one, out_post_gain, out_post_shift, out_norm_two = (
        out_small[:, VECTORS + place] for place in range(7)
    )
    out_out, out_gate_in = middle[0][:, :width], middle[0][:, width:]
    return (
        block_out.reshape(tokens.shape),
        grad_tokens.reshape(tokens.shape),
        jnp.concatenate([last[0], out_gate_in], axis=1),
        out_small[:, ETA : ETA + heads],
        out_small[0, BIAS : BIAS + heads],
        out_out,
        out_small[:, :head],
        out_inner_b,
        out_gain,
        out_shift,
        out_norm_one,
        out_post_gain,
        out_post_shift,
        large[0].reshape(device_rows, dp, 2, -1).transpose(0, 2, 1, 3).reshape(device_rows, 2 * hidden),
        large[1],
        out_norm_two,
    )


def next_or(phases, arrays):
    try:
        return phases.send(arrays)
    except StopIteration:
        return arrays


def drain(phases, arrays):
    for later in phases:
        arrays = later
    return arrays


def solution(mesh):
    split = ("dp", "fsdp")
    row, vector, token = P(split, None), P(split), P(None, split, None)
    dp, fsdp = mesh.shape["dp"], mesh.shape["fsdp"]
    return jax.shard_map(
        lambda *arrays: body(dp, fsdp, *arrays),
        mesh=mesh,
        in_specs=(token, P(None, split), token, row, row, P(), row, row) + (vector,) * 6 + (row, row, vector),
        out_specs=(token, token, row, row, P(), row, row) + (vector,) * 6 + (row, row, vector),
        check_vma=False,
    )
```

```python
import jax
import jax.numpy as jnp
from jax import lax
from jax.experimental import pallas as pl
from jax.experimental.pallas import tpu as pltpu
from jax.sharding import PartitionSpec as P
import numpy as np

MINI = 16
HEAD = 64
PAIR = 2 * HEAD
epsilon = 1e-06
low = jnp.bfloat16
full = jnp.float32


def dot_nn(former, latter):
    return lax.dot_general(former, latter, (((1,), (0,)), ((), ())), preferred_element_type=full)


def dot_nt(former, latter):
    return lax.dot_general(former, latter, (((1,), (1,)), ((), ())), preferred_element_type=full)


def tile_of(rows, at):
    return rows[:, PAIR * at : PAIR * (at + 1)]


def key_row(group, side, tile):
    return HEAD * group + 32 * side + MINI * tile


def query_row(group, side, tile):
    return key_row(1 - group, side, tile)


def expand(rows, sides):
    zero = jnp.zeros((MINI, PAIR), rows.dtype)
    blocks = []
    for side in range(2):
        for at in range(2):
            kept = tile_of(rows, at) * sides[side]
            blocks.append(jnp.concatenate([kept if other == at else zero for other in range(2)], axis=1))
    return jnp.concatenate(blocks, axis=0)


def expand_both(queries, keys, sides):
    width = 2 * PAIR
    blocks = [(expand(keys[:, width * group : width * (group + 1)], sides), expand(queries[:, width * group : width * (group + 1)], sides))
              for group in range(2)]
    return blocks, (jnp.concatenate(blocks[0], axis=0), jnp.concatenate(blocks[1][::-1], axis=0))


def to_feature(rows, first_side, groups):
    tiles = [tile_of(rows, 2 * group + at) for group in groups for _ in range(2) for at in range(2)]
    stacked = jnp.concatenate(tiles, axis=0).T
    return jnp.where(first_side, stacked[:HEAD], stacked[HEAD:])


def to_rows(columns, left, place):
    turned = jnp.concatenate([columns, columns], axis=0).T
    pick = lambda group, side, at: turned[place(group, side, at) : place(group, side, at) + MINI]
    return jnp.concatenate([jnp.where(left, pick(group, 0, at), pick(group, 1, at)) for group in range(2) for at in range(2)], axis=1)


def exchange(values):
    half = [values[:, HEAD * at : HEAD * (at + 1)] for at in range(values.shape[1] // HEAD)]
    return jnp.concatenate([half[at ^ 1] for at in range(len(half))], axis=1)


def mean_rows(values):
    return jnp.sum(values, axis=0, keepdims=True) * (1.0 / values.shape[0])


def both_sequences(ref, rows, base, width):
    return jnp.concatenate([ref[0, rows, base : base + width], ref[1, rows, base : base + width]], axis=1)


def store_sequences(ref, rows, base, width, pieces, kind):
    whole = jnp.concatenate(pieces, axis=1)
    ref[0, rows, base : base + width] = whole[:, :width].astype(kind)
    ref[1, rows, base : base + width] = whole[:, width:].astype(kind)


def read_constants(low_ref, full_ref):
    sides = [low_ref[0:MINI], low_ref[MINI : 2 * MINI]]
    same, crossed = low_ref[32:160], low_ref[160:288]
    return sides, same, crossed, full_ref[0:MINI], full_ref[16:144], full_ref[144:272]


def lane_masks(rows=HEAD, width=3 * PAIR):
    lane = lax.broadcasted_iota(jnp.int32, (rows, width), 1)
    return lane % PAIR < HEAD, lane % HEAD < 32


PARTS = range(3)


def thin(part):
    return slice(PAIR * part, PAIR * (part + 1))


def wide(part):
    return slice(4 * PAIR * part, 4 * PAIR * (part + 1))


def lanes(pieces):
    return jnp.concatenate(pieces, axis=1)


def ttt_forward_kernel(steps, q_ref, k_ref, v_ref, rate_ref, w0_ref, b0_ref, gain_ref, shift_ref, low_ref, full_ref,
                       out_ref, w_ref, xh_ref, h_ref, grs_ref, xb_ref, stat_ref, score_ref, w_run, b_run, gain_query, shift_query):
    width = 768

    @pl.when(pl.program_id(0) == 0)
    def _():
        w_run[...] = w0_ref[...]
        b_run[...] = b0_ref[...]
        gain_query[...] = exchange(gain_ref[...])
        shift_query[...] = exchange(shift_ref[...])

    sides, same, crossed, tri, _, _ = read_constants(low_ref, full_ref)
    left, first_side = lane_masks()
    left_one, first_one = left[:, :PAIR], first_side[:, :PAIR]
    tri = lanes([tri] * 3)

    def begin(at):
        rows = slice(at * MINI, (at + 1) * MINI)
        queries = both_sequences(q_ref, rows, 0, width)
        keys = both_sequences(k_ref, rows, 0, width)
        targets = both_sequences(v_ref, rows, 0, width) - keys
        query_low, key_low = queries.astype(low), keys.astype(low)
        expanded = [expand_both(query_low[:, wide(part)], key_low[:, wide(part)], sides) for part in PARTS]
        target = lanes([to_feature(targets[:, wide(part)], first_one, (0, 1)) for part in PARTS])
        return rows, queries, query_low, expanded, target

    def multiply(at, started, weights):
        _, _, query_low, expanded, _ = started
        products = []
        for part in PARTS:
            weight_low = weights[part].astype(low)
            w_ref[at, :, wide(part)] = weight_low
            for group in range(2):
                here = slice(2 * PAIR * group, 2 * PAIR * (group + 1))
                rows = jnp.concatenate([weight_low[:, here], query_low[:, wide(part)][:, here]], axis=0)
                products.append(dot_nt(rows, expanded[part][1][group]))
        return lanes(products[::2]), lanes(products[1::2])

    def finish(at, started, kept):
        rows, queries = started[:2]
        inner_grad, mixing, updated = kept
        inner_grad_low = inner_grad.astype(low)
        moved = []
        for part in PARTS:
            mixing_block = jnp.concatenate([mixing[:, thin(part)]] * 8, axis=0) * crossed
            moved.append(dot_nt(inner_grad_low[:, thin(part)], mixing_block))
        updated = updated - lanes(moved)
        updated = updated - mean_rows(updated)
        updated_inverse = lax.rsqrt(mean_rows(updated * updated) + epsilon)
        updated = updated * updated_inverse
        xb_ref[at] = updated
        stat_ref[at, 3:4] = updated_inverse
        updated = updated * gain_query[...] + shift_query[...]
        result = queries + lanes([to_rows(updated[:, thin(part)], left_one[:MINI], query_row) for part in PARTS])
        out_ref[0, rows, :] = result[:, :width]
        out_ref[1, rows, :] = result[:, width:]

    weights = [w_run[:, wide(part)] for part in PARTS]
    offset = b_run[...]
    started = begin(0)
    pending = None
    for at in range(steps):
        first, second = multiply(at, started, weights)
        if pending is not None:
            finish(*pending)
        gains, shifts = gain_ref[...], shift_ref[...]
        rate = rate_ref[at]
        _, _, _, expanded, target = started
        hidden = jnp.where(left, first[:HEAD], second[:HEAD]) + offset
        scores = jnp.where(left[:MINI], first[HEAD:], second[HEAD:]) + 1.0
        updated = jnp.where(left, second[:HEAD], first[:HEAD]) + exchange(offset)
        centred = hidden - mean_rows(hidden)
        inverse = lax.rsqrt(mean_rows(centred * centred) + epsilon)
        normed = centred * inverse
        held = gains * normed + (shifts - target)
        residual = held * gains
        residual_mean = mean_rows(residual)
        cross = mean_rows(residual * normed)
        inner_grad = (residual - residual_mean - normed * cross) * inverse
        scaled = inner_grad * (rate * (1.0 / MINI))
        scaled_low = scaled.astype(low)
        scaled_other = exchange(scaled).astype(low)
        xh_ref[at] = normed
        h_ref[at] = held
        grs_ref[at] = scaled
        stat_ref[at, 0:1] = inverse
        stat_ref[at, 1:2] = residual_mean
        stat_ref[at, 2:3] = cross
        score_ref[at] = scores
        changed = []
        for part in PARTS:
            blocks = expanded[part][0]
            change = [dot_nn(scaled_low[:, thin(part)][:, :HEAD], blocks[0][0]),
                      dot_nn(scaled_other[:, thin(part)][:, :HEAD], blocks[1][0])]
            changed.append(weights[part] - lanes(change))
        weights = changed
        offset = offset - lanes([dot_nn(scaled_low[:, thin(part)], same) for part in PARTS])
        pending = (at, started, (inner_grad, (tri * rate * scores).astype(low), updated))
        if at + 1 < steps:
            started = begin(at + 1)
    finish(*pending)
    for part in PARTS:
        w_run[:, wide(part)] = weights[part]
    b_run[...] = offset


def ttt_backward_kernel(steps, q_ref, k_ref, dout_ref, rate_ref, w_ref, xh_ref, h_ref, grs_ref, xb_ref, stat_ref, score_ref,
                        gain_ref, low_ref, full_ref, *refs):
    states, refs = refs[:6], refs[6:]
    grad_ref, rdr_ref, dw_ref, db_ref, dgain_ref, dshift_ref, dgain_query_ref, dshift_query_ref, gain_query = refs[-9:]
    width = 768

    @pl.when(pl.program_id(0) == 0)
    def _():
        for state, ref in zip(states, (dw_ref, db_ref, dgain_ref, dshift_ref, dgain_query_ref, dshift_query_ref)):
            ref[...] = state[...]
        gain_query[...] = exchange(gain_ref[...])

    sides, same, crossed, tri, scale, scale_turned = read_constants(low_ref, full_ref)
    left, first_side = lane_masks()
    left_one, first_one = left[:, :PAIR], first_side[:, :PAIR]
    left_rows = left_one[:MINI]
    left_square = lax.broadcasted_iota(jnp.int32, (PAIR, PAIR), 1) < HEAD
    zero = jnp.zeros((MINI, PAIR), full)
    tri = lanes([tri] * 3)

    def begin(at):
        rows = slice(at * MINI, (at + 1) * MINI)
        query_low = both_sequences(q_ref, rows, 0, width).astype(low)
        key_low = both_sequences(k_ref, rows, 0, width).astype(low)
        douts = both_sequences(dout_ref, rows, 0, width)
        expanded = [expand_both(query_low[:, wide(part)], key_low[:, wide(part)], sides) for part in PARTS]
        mixing = (tri * rate_ref[at] * score_ref[at]).astype(low)
        dout = lanes([to_feature(douts[:, wide(part)], first_one, (1, 0)) for part in PARTS])
        updated = xb_ref[at]
        dupdated = dout * gain_query[...]
        dupdated = stat_ref[at, 3:4] * (dupdated - mean_rows(dupdated) - updated * mean_rows(dupdated * updated))
        dgain_query_ref[...] += dout * updated
        dshift_query_ref[...] += dout
        dupdated_low = dupdated.astype(low)
        mixed = []
        for part in PARTS:
            mixing_block = jnp.concatenate([mixing[:, thin(part)]] * 8, axis=0) * crossed
            mixed.append(dot_nn(dupdated_low[:, thin(part)], mixing_block))
        return rows, douts, expanded, dupdated, dupdated_low, lanes(mixed)

    def finish(at, started, kept):
        rows, douts, expanded, dupdated, dupdated_low, _ = started
        dhidden, dtarget, dweights_low, rate_part = kept
        scaled = -grs_ref[at]
        scaled_low = scaled.astype(low)
        scores = score_ref[at]
        none = jnp.zeros((HEAD, PAIR), low)
        turned_low, turned_query, query_rows, dmixes, dmixes_turned = [], [], [], [], []
        for part in PARTS:
            turned_low.append(jnp.concatenate([dhidden[:, thin(part)], scaled[:, thin(part)]], axis=0).T.astype(low))
            turned_query.append(jnp.concatenate([dupdated[:, thin(part)], dtarget[:, thin(part)]], axis=0).T)
            query_rows.append(jnp.where(left_square, turned_query[part], 0.0).astype(low))
        for part in PARTS:
            dmix = dot_nn(query_rows[part][:, :HEAD], scaled_low[:, thin(part)]) * scale
            dmix_turned = dot_nn(turned_low[part], jnp.concatenate([none, dupdated_low[:, thin(part)]], axis=0)) * scale_turned
            dmixes.append(sum(dmix[MINI * row : MINI * (row + 1)] for row in range(8)))
            dmixes_turned.append(sum(dmix_turned[MINI * row : MINI * (row + 1)] for row in range(8)))
        rdr_ref[at] = rate_part + jnp.sum(lanes(dmixes) * scores, axis=0, keepdims=True)
        query_grads, key_grads, value_grads = [], [], []
        for part in PARTS:
            weight_low = w_ref[at, :, wide(part)]
            for group in range(2):
                keep_key, keep_query = (left_rows, ~left_rows) if group == 0 else (~left_rows, left_rows)
                key_side = jnp.where(keep_query, dmixes_turned[part], zero).astype(low)
                query_side = jnp.where(keep_key, dmixes[part], zero).astype(low)
                extra = jnp.concatenate([key_side, key_side, query_side, query_side], axis=0)
                for at_tile in range(2):
                    tile = 2 * group + at_tile
                    place = [key_row(group, side, at_tile) for side in range(2)]
                    place_query = [query_row(group, side, at_tile) for side in range(2)]
                    held_rows = jnp.concatenate(
                        [turned_low[part][row : row + MINI] for row in place]
                        + [query_rows[part][row : row + MINI] for row in place_query],
                        axis=0,
                    )
                    product = dot_nn(
                        jnp.concatenate([held_rows, extra], axis=1),
                        jnp.concatenate(
                            [tile_of(weight_low, tile), tile_of(dweights_low[part], tile), tile_of(expanded[part][1][group], at_tile)],
                            axis=0,
                        ),
                    )
                    dvalue = jnp.where(
                        left_rows,
                        exchange(turned_query[part][place[0] : place[0] + MINI]),
                        turned_query[part][place[1] : place[1] + MINI],
                    )
                    key_grads.append(dvalue + jnp.where(left_rows, product[:MINI], product[MINI : 2 * MINI]))
                    query_grads.append(
                        tile_of(douts[:, wide(part)], tile) + jnp.where(left_rows, product[2 * MINI : 3 * MINI], product[3 * MINI :])
                    )
                    value_grads.append(-dvalue)
        store_sequences(grad_ref, rows, 0, width, query_grads, low)
        store_sequences(grad_ref, rows, width, width, key_grads, low)
        store_sequences(grad_ref, rows, 2 * width, width, value_grads, low)

    dweights = [dw_ref[:, wide(part)] for part in PARTS]
    doffset = db_ref[...]
    started = begin(steps - 1)
    pending = None
    for at in reversed(range(steps)):
        _, _, expanded, dupdated, _, mixed = started
        dweights_low = [dweight.astype(low) for dweight in dweights]
        key_dw = []
        for part in PARTS:
            blocks = expanded[part][0]
            key_dw.append(dot_nt(dweights_low[part][:, : 2 * PAIR], blocks[0][0]))
            key_dw.append(dot_nt(dweights_low[part][:, 2 * PAIR :], blocks[1][0]))
        key_dw = lanes(key_dw) + doffset
        if pending is not None:
            finish(*pending)
        upcoming = begin(at - 1) if at > 0 else None
        gains = gain_ref[...]
        rate = rate_ref[at]
        normed, held, scaled = xh_ref[at], h_ref[at], grs_ref[at]
        inverse, residual_mean, cross = (stat_ref[at, row : row + 1] for row in range(3))
        grad_in = -mixed - (rate * (1.0 / MINI)) * key_dw
        rate_part = -jnp.sum(scaled * key_dw, axis=0, keepdims=True)
        residual = held * gains
        in_mean = mean_rows(grad_in)
        in_cross = mean_rows(grad_in * normed)
        in_held = inverse * (mean_rows(grad_in * residual) - residual_mean * in_mean - cross * in_cross)
        dresidual = inverse * (grad_in - in_mean - normed * in_cross)
        dtarget = dresidual * gains
        dnormed = dtarget * gains - inverse * (grad_in * cross + in_cross * residual)
        dhidden = inverse * (dnormed - mean_rows(dnormed) - normed * (mean_rows(dnormed * normed) + in_held))
        dgain_ref[...] += dresidual * (held + gains * normed)
        dshift_ref[...] += dtarget
        to_first = jnp.where(left, dhidden, dupdated).astype(low)
        to_second = jnp.where(left, dupdated, dhidden).astype(low)
        changed = []
        for part in PARTS:
            pairs = expanded[part][1]
            change = [dot_nn(to_first[:, thin(part)], pairs[0]), dot_nn(to_second[:, thin(part)], pairs[1])]
            changed.append(dweights[part] + lanes(change))
        total_low = (exchange(dupdated) + dhidden).astype(low)
        doffset = doffset + lanes([dot_nn(total_low[:, thin(part)], same) for part in PARTS])
        dweights = changed
        pending = (at, started, (dhidden, dtarget, dweights_low, rate_part))
        started = upcoming
    finish(*pending)
    for part in PARTS:
        dw_ref[:, wide(part)] = dweights[part]
    db_ref[...] = doffset


def ttt_constants():
    lane = np.arange(PAIR)
    row = np.arange(MINI)
    sides = np.concatenate([np.tile(lane < HEAD, (MINI, 1)), np.tile(lane >= HEAD, (MINI, 1))])
    token = lane % MINI
    tri = np.where(token[None] <= row[:, None], 1.0 / (row[:, None] + 1.0), 0.0)
    same = lane[:, None] // MINI == lane[None] // MINI
    crossed = (lane[:, None] + HEAD) % PAIR // MINI == lane[None] // MINI
    scale = np.where(crossed & (token[None] <= token[:, None]), MINI / (token[:, None] + 1.0), 0.0)
    return (
        jnp.asarray(np.concatenate([sides, same, crossed]).astype(np.float32), low),
        jnp.asarray(np.concatenate([tri, scale, scale.T]), full),
    )


def ttt_forward(projected, rates, state, gains, shifts, steps=4):
    count = projected.shape[1] // MINI
    first, begin, end = 0, 0, count
    queries, keys, values = projected, projected, projected
    constants = ttt_constants()
    whole = lambda *shape: pl.BlockSpec(shape, lambda at: (0,) * len(shape))
    column = lambda place: pl.BlockSpec((2, steps * MINI, 768), lambda at, place=place: (0, first + at, place))
    part = column(0)
    saved = lambda *tail: pl.BlockSpec((steps,) + tail, lambda at: (at, 0, 0))
    made = lambda kind, *tail: jax.ShapeDtypeStruct((end - begin,) + tail, kind)
    inputs = [queries, keys, values, rates, *state, gains, shifts, *constants]
    out, *rest = pl.pallas_call(
        lambda *refs: ttt_forward_kernel(steps, *refs),
        grid=((end - begin) // steps,),
        in_specs=[column(0), column(1), column(2), pl.BlockSpec((steps, 1, 384), lambda at: (first + at, 0, 0)), whole(64, 1536), whole(64, 384),
                  whole(64, 384), whole(64, 384), whole(288, 128), whole(272, 128)],
        out_specs=[part, saved(64, 1536), saved(64, 384), saved(64, 384), saved(64, 384), saved(64, 384), saved(8, 384),
                   saved(16, 384)],
        out_shape=[jax.ShapeDtypeStruct((2, count * MINI, 768), full), made(low, 64, 1536), made(full, 64, 384), made(full, 64, 384),
                   made(full, 64, 384), made(full, 64, 384), made(full, 8, 384), made(full, 16, 384)],
        scratch_shapes=[pltpu.VMEM((64, 1536), full)] + [pltpu.VMEM((64, 384), full)] * 3,
        compiler_params=pltpu.CompilerParams(vmem_limit_bytes=60 * 1024 * 1024),
        cost_estimate=pl.CostEstimate(flops=(end - begin) * 1_400_000_000, bytes_accessed=(end - begin) * 1_500_000, transcendentals=0),
        name="ttt_forward",
    )(*inputs)
    return out, rest


def ttt_backward(projected, dout, rates, saved_arrays, state, gains, begin, end, before, steps=4):
    count = projected.shape[1] // MINI
    first, blocks = begin // steps, (end - begin) // steps
    queries, keys = projected, projected
    constants = ttt_constants()
    whole = lambda *shape: pl.BlockSpec(shape, lambda at: (0,) * len(shape))
    part = lambda width, place=0: pl.BlockSpec((2, steps * MINI, width), lambda at: (0, first + blocks - 1 - at, place))
    saved = lambda *tail: pl.BlockSpec((steps,) + tail, lambda at: (first + blocks - 1 - at, 0, 0))
    made = lambda *tail: pl.BlockSpec((steps,) + tail, lambda at: (blocks - 1 - at, 0, 0))
    extra = [] if before is None else [before]
    inputs = [queries, keys, dout, rates, *saved_arrays, gains, *constants, *state]
    states = [whole(64, 1536)] + [whole(64, 384)] * 5
    grad, rate_back, *state = pl.pallas_call(
        lambda *refs: ttt_backward_kernel(steps, *refs),
        grid=(blocks,),
        in_specs=[part(768), part(768, 1), part(768), saved(1, 384),
                  saved(64, 1536), saved(64, 384), saved(64, 384), saved(64, 384), saved(64, 384), saved(8, 384), saved(16, 384),
                  whole(64, 384), whole(288, 128), whole(272, 128)]
        + states + [pl.BlockSpec(memory_space=pl.ANY)] * len(extra),
        out_specs=[part(2304), made(1, 384)] + states,
        out_shape=[jax.ShapeDtypeStruct((2, count * MINI, 2304), low), jax.ShapeDtypeStruct((end - begin, 1, 384), full)]
        + [jax.ShapeDtypeStruct((64, 1536), full)] + [jax.ShapeDtypeStruct((64, 384), full)] * 5,
        scratch_shapes=[pltpu.VMEM((64, 384), full)],
        input_output_aliases={len(inputs): 0} if extra else {},
        compiler_params=pltpu.CompilerParams(vmem_limit_bytes=60 * 1024 * 1024),
        cost_estimate=pl.CostEstimate(flops=(end - begin) * 2_000_000_000, bytes_accessed=(end - begin) * 1_500_000, transcendentals=0),
        name="ttt_backward",
    )(*inputs, *extra)
    return grad, rate_back, state


def silu_parts(gate):
    sigma = jax.nn.sigmoid(gate)
    return gate * sigma, sigma * (1.0 + gate * (1.0 - sigma))


def gelu_parts(values):
    slope = 0.7978845608028654
    turn = jnp.tanh(slope * (values + 0.044715 * values * values * values))
    half = 0.5 * (1.0 + turn)
    return values * half, half + 0.5 * values * (1.0 - turn * turn) * slope * (1.0 + 3 * 0.044715 * values * values)


def row_mean(values):
    return jnp.mean(values, axis=-1, keepdims=True)


def dot_tn(former, latter):
    return lax.dot_general(former, latter, (((0,), (0,)), ((), ())), preferred_element_type=full)


def exact_dot(former, latter):
    total = None
    for _ in range(3):
        part = former.astype(low)
        former = former - part.astype(full)
        term = dot_nn(part, latter)
        total = term if total is None else total + term
    return total


def constant_spec(*shape, at=0, buffers=None):
    index = lambda *steps: (0,) * (len(shape) - 1) + (at,)
    if buffers is None:
        return pl.BlockSpec(shape, index)
    return pl.BlockSpec(shape, index, pipeline_mode=pl.Buffered(buffers))


def call(kernel, name, grid, prefetch, in_specs, out_specs, out_shape, scratch, cost, arrays):
    return pl.pallas_call(
        kernel,
        grid_spec=pltpu.PrefetchScalarGridSpec(
            num_scalar_prefetch=prefetch, grid=grid, in_specs=in_specs, out_specs=out_specs, scratch_shapes=scratch
        ),
        out_shape=out_shape,
        compiler_params=pltpu.CompilerParams(vmem_limit_bytes=60 * 1024 * 1024),
        cost_estimate=pl.CostEstimate(flops=cost, bytes_accessed=cost // 500, transcendentals=0),
        name=name,
    )(*arrays)


ETA = 64
VECTORS = 80
BIAS = 96


def lane_table():
    lane = np.arange(384)
    part, group, side, tile, token = lane // 128, lane // 64 % 2, lane // 32 % 2, lane // 16 % 2, lane % 16
    pair = 4 * part + 2 * group + tile
    return token, pair // 6, 2 * (pair % 6) + side


def lane_constants():
    token, sequence, head = lane_table()
    table = np.zeros((32, 384), np.float32)
    table[:MINI] = token[None] == np.arange(MINI)[:, None]
    table[16], table[17] = sequence, token
    chosen = np.zeros((PAIR, 384), np.float32)
    chosen[ETA + head, np.arange(384)] = 1
    return jnp.asarray(table), jnp.asarray(chosen, low)


def project_kernel(length_ref, tokens_ref, w_ref, small_ref, bias_ref, table_ref, chosen_ref,
                   proj_ref, normed_ref, rate_ref, rest_ref, wt_ref, b_ref, gain_ref, shift_ref, vec_ref):
    at = pl.program_id(0)
    split = 512 // tokens_ref.shape[0]
    wide = w_ref.shape[1]

    @pl.when(at == 0)
    def _():
        small = small_ref[...].astype(full)
        turned = small.T
        wt_ref[:, :768] = turned[:HEAD]
        wt_ref[:, 768:] = turned[:HEAD]
        vec_ref[...] = turned[VECTORS : VECTORS + 8]
        for place, ref in enumerate((b_ref, gain_ref, shift_ref)):
            total = jnp.zeros((HEAD, 384), full)
            for head in range(12):
                column = small[HEAD * head : HEAD * (head + 1), VECTORS + place : VECTORS + place + 1]
                total = total + column * chosen_ref[ETA + head : ETA + head + 1].astype(full)
            ref[...] = total
        rate_ref[...] = jnp.zeros_like(rate_ref)
        rest_ref[...] = jnp.zeros_like(rest_ref)

    values = tokens_ref[...].astype(full)
    normed = (values * lax.rsqrt(row_mean(values * values) + epsilon) * vec_ref[3:4]).astype(low)
    normed_ref[...] = normed
    proj_ref[...] = dot_nn(normed, w_ref[...])
    last = dot_nn(normed, small_ref[...])
    spread = exact_dot(last + bias_ref[...], chosen_ref[...])
    blocks = spread.shape[0] // MINI
    spread = jnp.sum(spread.reshape(blocks, MINI, 384) * table_ref[:MINI][None], axis=1)
    sequence, token = table_ref[16:17], table_ref[17:18]
    mine = sequence == (at // split).astype(full)
    sigma = jax.nn.sigmoid(spread)
    begin = (at % split) * blocks
    block = lax.broadcasted_iota(jnp.int32, spread.shape, 0) + begin
    live = (block * MINI).astype(full) + token < length_ref[at // split].astype(full)
    here = pl.ds(begin, blocks)
    rate_ref[here, 0, :] += jnp.where(live & mine, sigma * (1.0 / HEAD), 0.0)
    rest_ref[here, :] += jnp.where(mine, 1.0 - sigma, 0.0)


def project(lengths, tokens, whole, bias_row):
    rows, width = tokens.shape
    table, chosen = lane_constants()
    tile = rows // 2
    columns = 3 * width
    row = lambda n: pl.BlockSpec((tile, n), lambda at, *_: (at, 0))
    shape = jax.ShapeDtypeStruct
    return call(
        project_kernel, "project", (2,), 1,
        [row(width), constant_spec(width, columns, buffers=1), constant_spec(width, PAIR, at=5 * width // PAIR), constant_spec(1, PAIR), constant_spec(32, 384), constant_spec(PAIR, 384)],
        [row(columns), row(width), constant_spec(32, 1, 384), constant_spec(32, 384), constant_spec(64, 1536)]
        + [constant_spec(64, 384)] * 3 + [constant_spec(8, width)],
        [shape((rows, columns), full), shape((rows, width), low), shape((32, 1, 384), full), shape((32, 384), full),
         shape((64, 1536), full)] + [shape((64, 384), full)] * 3 + [shape((8, width), full)],
        [], 5_000_000_000, (lengths, tokens, whole, whole, bias_row, table, chosen),
    )


def post_kernel(inner_ref, normed_ref, tokens_ref, w_gate_ref, w_out_ref, vec_ref, gate_ref, mixed_ref, first_ref, second_ref):
    gate = dot_nn(normed_ref[...], w_gate_ref[...])
    gate_ref[...] = gate
    inner = inner_ref[...]
    centred = inner - row_mean(inner)
    standard = centred * lax.rsqrt(row_mean(centred * centred) + epsilon)
    mixed = ((standard * vec_ref[4:5] + vec_ref[5:6]) * gelu_parts(gate)[0]).astype(low)
    mixed_ref[...] = mixed
    first = tokens_ref[...].astype(full) + dot_nn(mixed, w_out_ref[...])
    first_ref[...] = first
    second_ref[...] = (first * lax.rsqrt(row_mean(first * first) + epsilon) * vec_ref[6:7]).astype(low)


def post(inner, normed, tokens, whole, vectors):
    rows, width = tokens.shape
    tile = rows // 4
    row = pl.BlockSpec((tile, width), lambda at: (at, 0))
    shape = jax.ShapeDtypeStruct
    return call(
        post_kernel, "post", (4,), 0,
        [row, row, row, constant_spec(width, width, at=3, buffers=1), constant_spec(width, width, at=4, buffers=1), constant_spec(8, width)],
        [row] * 4, [shape((rows, width), kind) for kind in (full, low, full, low)], [], 4_000_000_000,
        (inner, normed, tokens, whole, whole, vectors),
    )


def store_blocks(table_ref, sent_ref, kept_ref, held_ref, block):
    half = kept_ref.shape[0]
    if block % 8:
        kept_ref[...] = held_ref[:half].astype(kept_ref.dtype)
        sent_ref[...] = held_ref[half:].astype(sent_ref.dtype)
        return
    for pair in range(held_ref.shape[0] // (2 * block)):
        rows = [held_ref[pl.ds(pl.multiple_of(table_ref[2 * pair + side] * block, 8), block), :] for side in range(2)]
        begin = 2 * block * pair
        ref, begin = (kept_ref, begin) if begin < half else (sent_ref, begin - half)
        ref[begin : begin + 2 * block, :] = jnp.concatenate(rows, axis=0).astype(ref.dtype)


def ffn_kernel(block, down_block, table_ref, place_ref, second_ref, first_ref, up_ref, w_gate_ref, w_up_ref, w_down_ref,
               out_ref, dsecond_ref, both_sent_ref, both_kept_ref, down_sent_ref, down_kept_ref, turned, total, act, both_low, held):
    at = pl.program_id(0)
    rows = second_ref.shape[0]
    tile = 512

    @pl.when(at == 0)
    def _():
        turned[...] = second_ref[...].T
        total[...] = first_ref[...]
        dsecond_ref[...] = jnp.zeros_like(dsecond_ref)

    w_gate, w_up, w_down = w_gate_ref[...], w_up_ref[...], w_down_ref[...]

    def one(place, carry):
        here = pl.ds(place * tile, tile)
        second, upstream = second_ref[here, :], up_ref[here, :]
        gate, up = dot_nn(second, w_gate), dot_nn(second, w_up)
        value, slope = silu_parts(gate)
        activated = (value * up).astype(low)
        act[here, :] = activated
        total[here, :] += dot_nn(activated, w_down)
        dact = dot_nt(upstream, w_down)
        dgate, dup = (dact * up * slope).astype(low), (dact * value).astype(low)
        both_low[here, : dgate.shape[1]] = dgate
        both_low[here, dgate.shape[1] :] = dup
        dsecond_ref[here, :] += dot_nt(dgate, w_gate) + dot_nt(dup, w_up)
        return carry

    lax.fori_loop(0, rows // tile, one, 0)
    held[...] = dot_nn(turned[...], both_low[...])
    store_blocks(table_ref, both_sent_ref, both_kept_ref, held, block)
    ddown = dot_tn(act[...], up_ref[...]).astype(low)
    count = ddown.shape[0] // down_block
    half = down_kept_ref.shape[0]
    for place in range(count):
        to = pl.multiple_of(place_ref[at * count + place] * down_block, 16)
        rows_here = ddown[down_block * place : down_block * (place + 1)]

        @pl.when(to < half)
        def _():
            down_kept_ref[pl.ds(to, down_block), :] = rows_here

        @pl.when(to >= half)
        def _():
            down_sent_ref[pl.ds(to - half, down_block), :] = rows_here

    @pl.when(at == pl.num_programs(0) - 1)
    def _():
        out_ref[...] = total[...].astype(low)


def ffn(table, inverse, second, first, upstream, fetched, w_down, devices, steps):
    rows, width = second.shape
    hidden = w_down.shape[0]
    size = hidden // steps
    begin = 0
    shape = jax.ShapeDtypeStruct
    column = lambda first: pl.BlockSpec((width, size), lambda at, *_, first=first: (0, first + at))
    return call(
        lambda *refs: ffn_kernel(width // devices, hidden // devices, *refs), "ffn", (steps,), 2,
        [constant_spec(rows, width, buffers=1)] * 3 + [column(begin), column(begin + steps),
         pl.BlockSpec((size, width), lambda at, *_: (at, 0))],
        [constant_spec(rows, width, buffers=1), constant_spec(rows, width, buffers=1),
         *[pl.BlockSpec((width // 2, 2 * size), lambda at, *_: (0, at))] * 2, *[constant_spec(hidden // 2, width, buffers=1)] * 2],
        [shape((rows, width), low), shape((rows, width), full), *[shape((width // 2, 2 * hidden), low)] * 2,
         *[shape((hidden // 2, width), low)] * 2],
        [pltpu.VMEM((width, rows), low), pltpu.VMEM((rows, width), full), pltpu.VMEM((rows, size), low),
         pltpu.VMEM((rows, 2 * size), low), pltpu.VMEM((width, 2 * size), full)],
        29_000_000_000, (table, inverse, second, first, upstream, fetched, fetched, w_down),
    )


def post_back_kernel(dsecond_ref, first_ref, up_ref, inner_ref, gate_ref, w_out_ref, vec_ref,
                     dfirst_ref, dgate_ref, dinner_ref, dfirst_low_ref, sums_ref):
    @pl.when(pl.program_id(0) == 0)
    def _():
        sums_ref[...] = jnp.zeros_like(sums_ref)

    first, dsecond = first_ref[...], dsecond_ref[...]
    scale = lax.rsqrt(row_mean(first * first) + epsilon)
    sums_ref[6:7] += jnp.sum(dsecond * first * scale, axis=0, keepdims=True)
    dsecond = dsecond * vec_ref[6:7]
    dfirst = up_ref[...].astype(full) + scale * dsecond - first * (scale * scale * scale * row_mean(first * dsecond))
    dfirst_ref[...] = dfirst
    dfirst_low = dfirst.astype(low)
    dfirst_low_ref[...] = dfirst_low
    dmixed = dot_nt(dfirst_low, w_out_ref[...])
    inner = inner_ref[...]
    centred = inner - row_mean(inner)
    inverse = lax.rsqrt(row_mean(centred * centred) + epsilon)
    standard = centred * inverse
    value, slope = gelu_parts(gate_ref[...])
    dgate_ref[...] = (dmixed * (standard * vec_ref[4:5] + vec_ref[5:6]) * slope).astype(low)
    dpost = dmixed * value
    sums_ref[4:5] += jnp.sum(dpost * standard, axis=0, keepdims=True)
    sums_ref[5:6] += jnp.sum(dpost, axis=0, keepdims=True)
    dpost = dpost * vec_ref[4:5]
    dinner_ref[...] = inverse * (dpost - row_mean(dpost) - standard * row_mean(dpost * standard))


def post_back(dsecond, first, upstream, inner, gate, whole, vectors):
    rows, width = first.shape
    tile = rows // 4
    row = pl.BlockSpec((tile, width), lambda at: (at, 0))
    shape = jax.ShapeDtypeStruct
    return call(
        post_back_kernel, "post_back", (4,), 0,
        [row] * 5 + [constant_spec(width, width, at=4, buffers=1), constant_spec(8, width)],
        [row, row, row, row, constant_spec(8, width)],
        [shape((rows, width), full), shape((rows, width), low), shape((rows, width), full), shape((rows, width), low),
         shape((8, width), full)],
        [], 4_000_000_000, (dsecond, first, upstream, inner, gate, whole, vectors),
    )


def middle_kernel(block, table_ref, mixed_ref, dfirst_ref, normed_ref, dgate_ref, sent_ref, kept_ref, held):
    @pl.when(pl.program_id(0) == 0)
    def _():
        held[...] = dot_tn(mixed_ref[...], dfirst_ref[...])

    @pl.when(pl.program_id(0) == 1)
    def _():
        held[...] = dot_tn(normed_ref[...], dgate_ref[...])

    store_blocks(table_ref, sent_ref, kept_ref, held, block)


def middle_grads(table, mixed, dfirst, normed, dgate, devices):
    rows, width = normed.shape
    whole = constant_spec(rows, width, buffers=1)
    return call(
        lambda *refs: middle_kernel(width // devices, *refs), "middle_grads", (2,), 1,
        [whole] * 4, [pl.BlockSpec((width // 2, width), lambda at, *_: (0, at))] * 2,
        [jax.ShapeDtypeStruct((width // 2, 2 * width), low)] * 2, [pltpu.VMEM((width, width), full)], 3_000_000_000,
        (table, mixed, dfirst, normed, dgate),
    )


def weight_kernel(block, table_ref, shared_ref, normed_ref, grad_ref, sent_ref, kept_ref, last_sent_ref, last_kept_ref, turned, held):
    at = pl.program_id(0)
    last = pl.num_programs(0) - 1

    @pl.when(at == 0)
    def _():
        turned[...] = normed_ref[...].T

    held[...] = dot_nn(turned[...], grad_ref[...])

    @pl.when(at < last)
    def _():
        store_blocks(table_ref, sent_ref, kept_ref, held, block)

    @pl.when(at == last)
    def _():
        store_blocks(shared_ref, last_sent_ref, last_kept_ref, held, block)


def weight_grads(table, shared, normed, grads, devices):
    rows, width = normed.shape
    size = width
    shape = jax.ShapeDtypeStruct
    early = pl.BlockSpec((width // 2, size), lambda at, *_: (0, jnp.minimum(at, 1)))
    late = pl.BlockSpec((width // 2, size), lambda at, *_: (0, 0))
    return call(
        lambda *refs: weight_kernel(width // devices, *refs), "weight_grads", (3,), 2,
        [constant_spec(rows, width, buffers=1), pl.BlockSpec((rows, size), lambda at, *_: (0, at))],
        [early, early, late, late], [shape((width // 2, 2 * size), low)] * 2 + [shape((width // 2, size), low)] * 2,
        [pltpu.VMEM((width, rows), low), pltpu.VMEM((width, size), full)], 4_000_000_000, (table, shared, normed, grads),
    )


def finish_kernel(tokens_ref, dfirst_ref, dqkv_ref, dgate_ref, rate_ref, rest_ref, w_ref, small_ref, w_gate_ref, vec_ref, table_ref, chosen_ref,
                  out_ref, dlog_ref, sums_ref):
    at = pl.program_id(0)

    @pl.when(at == 0)
    def _():
        sums_ref[...] = jnp.zeros_like(sums_ref)

    blocks = tokens_ref.shape[0] // MINI
    here = pl.ds((at % 2) * blocks, blocks)
    mine = (table_ref[16:17] == (at // 2).astype(full)).astype(full)
    dlog = rate_ref[here, 0, :] * rest_ref[here, :] * mine
    dlog = (dlog[:, None, :] * table_ref[:MINI][None]).reshape(blocks * MINI, 384).astype(low)
    dlog = dot_nt(dlog, chosen_ref[...]).astype(low)
    dlog_ref[...] = dlog
    dnormed = dot_nt(dqkv_ref[...], w_ref[...]) + dot_nt(dgate_ref[...], w_gate_ref[...]) + dot_nt(dlog, small_ref[...])
    values = tokens_ref[...].astype(full)
    scale = lax.rsqrt(row_mean(values * values) + epsilon)
    sums_ref[3:4] += jnp.sum(dnormed * values * scale, axis=0, keepdims=True)
    dnormed = dnormed * vec_ref[3:4]
    back = scale * dnormed - values * (scale * scale * scale * row_mean(values * dnormed))
    out_ref[...] = (dfirst_ref[...] + back).astype(low)


def finish(tokens, dfirst, dqkv, dgate, rate_back, rest, whole, vectors):
    rows, width = tokens.shape
    tile = rows // 4
    table, chosen = lane_constants()
    row = lambda n: pl.BlockSpec((tile, n), lambda at: (at, 0))
    shape = jax.ShapeDtypeStruct
    return call(
        finish_kernel, "finish", (4,), 0,
        [row(width), row(width), row(3 * width), row(width), constant_spec(32, 1, 384), constant_spec(32, 384),
         constant_spec(width, 3 * width, buffers=1), constant_spec(width, PAIR, at=5 * width // PAIR, buffers=1),
         constant_spec(width, width, at=3, buffers=1), constant_spec(8, width),
         constant_spec(32, 384), constant_spec(PAIR, 384)],
        [row(width), row(PAIR), constant_spec(8, width)],
        [shape((rows, width), low), shape((rows, PAIR), low), shape((8, width), full)], [], 7_000_000_000,
        (tokens, dfirst, dqkv, dgate, rate_back, rest, whole, whole, whole, vectors, table, chosen),
    )


def pack_kernel(block, table_ref, normed_ref, dlog_ref, sums_ref, more_ref, dw_ref, db_ref, dgain_ref, dshift_ref, dgain_query_ref,
                dshift_query_ref, rate_ref, rest_ref,
                chosen_ref, sent_ref, kept_ref, held):
    width = sums_ref.shape[1]
    eta = dot_tn(dlog_ref[...], normed_ref[...])
    inner = dw_ref[:, :width] + dw_ref[:, width:]
    rows = jnp.concatenate(
        [inner, eta[ETA : ETA + 16], sums_ref[...] + more_ref[...], jnp.zeros((PAIR - VECTORS - 8, width), full)], axis=0
    )
    lane = lax.broadcasted_iota(jnp.int32, (HEAD, PAIR), 1)
    chosen = chosen_ref[...].astype(full)
    bias = jnp.sum(rate_ref[:, 0, :] * rest_ref[...], axis=0, keepdims=True)
    held[...] = rows.T
    bias = jnp.sum(chosen * bias, axis=1, keepdims=True)
    square = jnp.broadcast_to(bias, (PAIR, PAIR)).T[:1]
    bias_row = pltpu.roll(square, BIAS - ETA, axis=1)
    bias_row = jnp.where((lane[:1] >= BIAS) & (lane[:1] < BIAS + 12), bias_row, 0.0)

    lanes = [db_ref[...] * (1.0 / MINI), dgain_ref[...] + exchange(dgain_query_ref[...]), dshift_ref[...] + exchange(dshift_query_ref[...])]
    for head in range(12):
        here = pl.ds(HEAD * head, HEAD)
        mask = chosen[ETA + head : ETA + head + 1]
        total = held[here, :] + bias_row
        for place, values in enumerate(lanes):
            column = jnp.sum(values * mask, axis=1, keepdims=True)
            total = total + jnp.where(lane == VECTORS + place, column, 0.0)
        held[here, :] = total
    store_blocks(table_ref, sent_ref, kept_ref, held, block)


def pack(table, normed, dlog, sums, more, state, rate_back, rest, devices):
    rows, width = normed.shape
    _, chosen = lane_constants()
    spec = lambda array: constant_spec(*array.shape, buffers=1)
    arrays = (normed, dlog, sums, more, *state, rate_back, rest, chosen)
    return call(
        lambda *refs: pack_kernel(width // devices, *refs), "pack", (1,), 1,
        [spec(array) for array in arrays], [constant_spec(width // 2, PAIR, buffers=1)] * 2,
        [jax.ShapeDtypeStruct((width // 2, PAIR), full)] * 2,
        [pltpu.VMEM((width, PAIR), full)], 1_000_000_000, (table, *arrays),
    )


class Links:
    def __init__(self, dp, fsdp):
        self.axes = ("dp", "fsdp")
        self.count = dp * fsdp
        self.core = fsdp
        self.far = fsdp // 2
        bits = [1 << place for place in reversed(range(self.count.bit_length() - 1))]
        self.others = [bit for bit in bits if bit != self.core]
        near = [bit for bit in self.others if bit != self.far]
        turned = [near[turn:] + near[:turn] for turn in range(3)]
        self.orders = {"split": turned[:2], "shared": [turned[2]] * 2}
        self.me = lax.axis_index("dp") * fsdp + lax.axis_index("fsdp")
        self.side = (self.me // self.core) % 2

    def swap(self, values, bits):
        pairs = [(place, place ^ bits[(place // self.core) % 2]) for place in range(self.count)]
        return lax.ppermute(values, self.axes, pairs)

    def gather(self, pieces, kinds, behind, at):
        orders = [[[self.far] + order for order in self.orders[kind]] for kind in kinds]
        held = list(pieces)
        for phase in range(len(orders[0][0])):
            if phase == at:
                held, behind = tie(held, behind)
            for place, pair in enumerate(orders):
                bits = [order[phase] for order in pair]
                got = self.swap(held[place], bits)
                ones = [(self.me // bit) % 2 for bit in bits]
                mine = jnp.where(self.side == 0, ones[0], ones[1]) == 0
                held[place] = jnp.stack([jnp.where(mine, held[place], got), jnp.where(mine, got, held[place])])
        above = [bit for bit in self.others if bit > self.core]
        whole = []
        for array, pair in zip(held, orders):
            got = self.swap(array, [self.core] * 2)
            mine = self.side == 0
            cores = [jnp.where(mine, array, got), jnp.where(mine, got, array)]
            placed = []
            for half, order in zip(cores, pair):
                have = order[::-1]
                placed.append(half.transpose([have.index(bit) for bit in self.others] + [len(have), len(have) + 1]))
            whole.append(jnp.stack(placed, axis=len(above)).reshape(-1, array.shape[-1]))
        return jnp.concatenate(whole, axis=1), behind

    def tables(self, kind):
        half = []
        for side in range(2):
            masks = self.orders[kind][side] + [self.far]
            half.append(np.array([sum(bit for at, bit in enumerate(masks) if place >> (len(masks) - 1 - at) & 1)
                                  for place in range(self.count // 2)], np.int32))
        keep = jnp.where(self.side == 0, half[0], half[1])
        send = jnp.where(self.side == 0, half[1], half[0])
        table = jnp.concatenate([self.me ^ keep, self.me ^ self.core ^ send]).astype(jnp.int32)
        places = jnp.arange(self.count, dtype=jnp.int32)
        inverse = jnp.sum(jnp.where(table[None] == places[:, None], places[None], 0), axis=1).astype(jnp.int32)
        return table, inverse

    def scatter(self, arrays, kinds):
        steps = [[[self.core] * 2] + [list(pair) for pair in zip(*self.orders[kind])] + [[self.far] * 2] for kind in kinds]
        for place in range(len(steps[0])):
            later = []
            for (sent, kept), step in zip(arrays, steps):
                total = kept.astype(full) + self.swap(sent, step[place]).astype(full)
                half = total.shape[0] // 2
                kept = total[:half].astype(low) if place == 0 else total[:half]
                later.append((total[half:].astype(low), kept) if place + 1 < len(step) else total)
            changed = yield later
            arrays = later if changed is None else changed

    def scatter_small(self, array):
        bits = [self.core] + self.orders["shared"][0] + [self.far]
        while bits:
            now, bits = bits[:2], bits[2:]
            parts = array.reshape((1 << len(now), -1) + array.shape[1:])
            array = parts[0]
            for place in range(1, 1 << len(now)):
                mask = sum(bit for at, bit in enumerate(now) if place >> (len(now) - 1 - at) & 1)
                array = array + self.swap(parts[place], [mask] * 2)
            changed = yield array
            array = array if changed is None else changed


def tie(*groups):
    flat, tree = jax.tree.flatten(groups)
    return jax.tree.unflatten(tree, lax.optimization_barrier(flat))


def halves(array):
    half = array.shape[0] // 2
    return array[half:], array[:half]


def tie(*groups):
    flat, tree = jax.tree.flatten(groups)
    return jax.tree.unflatten(tree, lax.optimization_barrier(flat))


def in_order(table, pair, rows):
    if rows % 8 == 0:
        return pair
    whole = jnp.concatenate([pair[1], pair[0]], axis=0)
    return halves(whole.reshape((-1, rows) + whole.shape[1:])[table].reshape(whole.shape))


def body(dp, fsdp, tokens, lengths, cotangent, mixer_in, w_eta, eta_bias, w_out, inner_w, inner_b, ttt_gain, ttt_shift,
         norm_one, post_gain, post_shift, w_gate_up, w_down, norm_two):
    links = Links(dp, fsdp)
    devices = dp * fsdp
    micro, slots, width = tokens.shape
    rows = micro * slots
    heads = eta_bias.shape[0]
    head = width // heads
    hidden = w_gate_up.shape[1] // 2
    device_rows = width // devices
    table, _ = links.tables("split")
    shared, inverse = links.tables("shared")
    zeros = lambda columns: jnp.zeros((device_rows, columns), low)

    vectors = jnp.stack([inner_b, ttt_gain, ttt_shift, norm_one, post_gain, post_shift, norm_two])
    vectors = dot_tn(vectors, jnp.eye(7, PAIR, VECTORS, dtype=low)).astype(low)
    small = jnp.concatenate([inner_w, w_eta, zeros(PAIR - ETA - heads)], axis=1) + vectors
    parts = 3
    share = device_rows // parts
    piece = width // parts
    own_down = w_down.reshape(-1, share, parts, piece).transpose(2, 1, 0, 3).reshape(device_rows, hidden)
    own_rest = jnp.concatenate([w_gate_up, own_down], axis=1)
    cut = 21 * PAIR
    pieces = [mixer_in[:, :cut], jnp.concatenate([mixer_in[:, cut:], w_out, small], axis=1)]
    whole, own_rest = links.gather(pieces, ["split", "shared"], own_rest, 2)
    fetched = lax.all_gather(own_rest, ("dp", "fsdp"), axis=0, tiled=True)
    whole_down = fetched[:, 2 * hidden :].reshape(devices, parts, share, -1, piece).transpose(0, 3, 2, 1, 4)
    whole_down = whole_down.reshape(hidden, width)

    places = lax.broadcasted_iota(jnp.int32, (micro, slots), 1)
    live = places < lengths
    upstream = jnp.where(live[..., None], cotangent, jnp.zeros_like(cotangent)).reshape(rows, width)
    inputs = tokens.reshape(rows, width)
    bias_row = jnp.pad(eta_bias.astype(full), (ETA, PAIR - ETA - heads)).reshape(1, PAIR)
    projected, normed, rate_lanes, rest_lanes, start_w, start_b, gain_lanes, shift_lanes, vec_rows = project(
        lengths.reshape(micro), inputs, whole, bias_row
    )
    projected = projected.reshape(micro, slots, -1)
    inner, saved = ttt_forward(projected, rate_lanes, [start_w, start_b], gain_lanes, shift_lanes)
    inner = inner.reshape(rows, width)
    gate, mixed, first, second = post(inner, normed, inputs, whole, vec_rows)
    block_out, dsecond, both_sent, both_kept, down_sent, down_kept = ffn(
        table, inverse, second, first, upstream, fetched, whole_down, devices, dp
    )
    large_phases = links.scatter([in_order(table, (both_sent, both_kept), device_rows), (down_sent, down_kept)], ["split", "shared"])
    large = next(large_phases)
    dfirst, dgate, dinner, dfirst_low, sums = post_back(dsecond, first, upstream, inner, gate, whole, vec_rows)
    dfirst_low, large = tie(dfirst_low, large)
    large = large_phases.send(large)
    middle = middle_grads(table, mixed, dfirst_low, normed, dgate, devices)
    dinner, middle = tie(dinner, list(middle))
    middle_phases = links.scatter([in_order(table, tuple(middle), device_rows)], ["split"])
    middle = next(middle_phases)
    dinner = dinner.reshape(micro, slots, width)
    state = [jnp.zeros((HEAD, 1536), full)] + [jnp.zeros((HEAD, 384), full)] * 5
    dqkv, rate_back = None, []
    cuts = [32, 16, 8, 4, 0]
    for end, begin in zip(cuts[:-1], cuts[1:]):
        dqkv, rate_part, state = ttt_backward(
            projected, dinner, rate_lanes, saved, state, gain_lanes, begin, end, dqkv
        )
        rate_back.insert(0, rate_part)
        if begin > 0:
            state, dqkv, large, middle = tie(state, dqkv, large, middle)
            large, middle = next_or(large_phases, large), next_or(middle_phases, middle)
    dqkv = dqkv.reshape(rows, 3 * width)
    rate_back = jnp.concatenate(rate_back, axis=0)
    early_sent, early_kept, late_sent, late_kept = weight_grads(table, shared, normed, dqkv, devices)
    last = [in_order(table, (early_sent, early_kept), device_rows), in_order(shared, (late_sent, late_kept), device_rows)]
    last, large, middle = tie(last, large, middle)
    last_phases = links.scatter(last, ["split", "shared"])
    last, large, middle = next(last_phases), next_or(large_phases, large), next_or(middle_phases, middle)
    dfirst, last, large, middle = tie(dfirst, last, large, middle)
    last, large, middle = last_phases.send(last), next_or(large_phases, large), next_or(middle_phases, middle)
    grad_tokens, dlog, more = finish(inputs, dfirst, dqkv, dgate, rate_back, rest_lanes, whole, vec_rows)
    dlog, last, middle = tie(dlog, last, middle)
    last = last_phases.send(last)
    small_grad = pack(shared, normed, dlog, sums, more, state, rate_back, rest_lanes, devices)
    small_grad, last = tie(list(small_grad), last)
    small_sent, small_kept = in_order(shared, tuple(small_grad), device_rows)
    small_phases = links.scatter_small(jnp.concatenate([small_kept, small_sent], axis=0))
    out_small, last = next(small_phases), next_or(last_phases, last)
    out_small, last = tie(out_small, last)
    out_small, last = next_or(small_phases, out_small), next_or(last_phases, last)
    out_small, last = tie(out_small, last)
    out_small, last = drain(small_phases, out_small), drain(last_phases, last)
    large, middle = drain(large_phases, large), drain(middle_phases, middle)
    out_inner_b, out_gain, out_shift, out_norm_one, out_post_gain, out_post_shift, out_norm_two = (
        out_small[:, VECTORS + place] for place in range(7)
    )
    out_out, out_gate_in = middle[0][:, :width], middle[0][:, width:]
    return (
        block_out.reshape(tokens.shape),
        grad_tokens.reshape(tokens.shape),
        jnp.concatenate([*last, out_gate_in], axis=1),
        out_small[:, ETA : ETA + heads],
        out_small[0, BIAS : BIAS + heads],
        out_out,
        out_small[:, :head],
        out_inner_b,
        out_gain,
        out_shift,
        out_norm_one,
        out_post_gain,
        out_post_shift,
        large[0].reshape(device_rows, dp, 2, -1).transpose(0, 2, 1, 3).reshape(device_rows, 2 * hidden),
        large[1],
        out_norm_two,
    )


def next_or(phases, arrays):
    try:
        return phases.send(arrays)
    except StopIteration:
        return arrays


def drain(phases, arrays):
    try:
        while True:
            arrays = phases.send(arrays)
    except StopIteration:
        return arrays


def solution(mesh):
    split = ("dp", "fsdp")
    row, vector, token = P(split, None), P(split), P(None, split, None)
    dp, fsdp = mesh.shape["dp"], mesh.shape["fsdp"]
    return jax.shard_map(
        lambda *arrays: body(dp, fsdp, *arrays),
        mesh=mesh,
        in_specs=(token, P(None, split), token, row, row, P(), row, row) + (vector,) * 6 + (row, row, vector),
        out_specs=(token, token, row, row, P(), row, row) + (vector,) * 6 + (row, row, vector),
        check_vma=False,
    )
```

```python
import jax
import jax.numpy as jnp
from jax import lax
from jax.experimental import pallas as pl
from jax.experimental.pallas import tpu as pltpu
from jax.sharding import PartitionSpec as P
import numpy as np

MINI = 16
HEAD = 64
PAIR = 2 * HEAD
epsilon = 1e-06
low = jnp.bfloat16
full = jnp.float32


def dot_nn(former, latter):
    return lax.dot_general(former, latter, (((1,), (0,)), ((), ())), preferred_element_type=full)


def dot_nt(former, latter):
    return lax.dot_general(former, latter, (((1,), (1,)), ((), ())), preferred_element_type=full)


def tile_of(rows, at):
    return rows[:, PAIR * at : PAIR * (at + 1)]


def key_row(group, side, tile):
    return HEAD * group + 32 * side + MINI * tile


def query_row(group, side, tile):
    return key_row(1 - group, side, tile)


def expand(rows, sides):
    zero = jnp.zeros((MINI, PAIR), rows.dtype)
    blocks = []
    for side in range(2):
        for at in range(2):
            kept = tile_of(rows, at) * sides[side]
            blocks.append(jnp.concatenate([kept if other == at else zero for other in range(2)], axis=1))
    return jnp.concatenate(blocks, axis=0)


def expand_both(queries, keys, sides):
    width = 2 * PAIR
    blocks = [(expand(keys[:, width * group : width * (group + 1)], sides), expand(queries[:, width * group : width * (group + 1)], sides))
              for group in range(2)]
    return blocks, (jnp.concatenate(blocks[0], axis=0), jnp.concatenate(blocks[1][::-1], axis=0))


def to_feature(rows, first_side, groups):
    tiles = [tile_of(rows, 2 * group + at) for group in groups for _ in range(2) for at in range(2)]
    stacked = jnp.concatenate(tiles, axis=0).T
    return jnp.where(first_side, stacked[:HEAD], stacked[HEAD:])


def to_rows(columns, left, place):
    turned = jnp.concatenate([columns, columns], axis=0).T
    pick = lambda group, side, at: turned[place(group, side, at) : place(group, side, at) + MINI]
    return jnp.concatenate([jnp.where(left, pick(group, 0, at), pick(group, 1, at)) for group in range(2) for at in range(2)], axis=1)


def exchange(values):
    half = [values[:, HEAD * at : HEAD * (at + 1)] for at in range(values.shape[1] // HEAD)]
    return jnp.concatenate([half[at ^ 1] for at in range(len(half))], axis=1)


def mean_rows(values):
    return jnp.sum(values, axis=0, keepdims=True) * (1.0 / values.shape[0])


def both_sequences(ref, rows, base, width):
    return jnp.concatenate([ref[0, rows, base : base + width], ref[1, rows, base : base + width]], axis=1)


def store_sequences(ref, rows, base, width, pieces, kind):
    whole = jnp.concatenate(pieces, axis=1)
    ref[0, rows, base : base + width] = whole[:, :width].astype(kind)
    ref[1, rows, base : base + width] = whole[:, width:].astype(kind)


def read_constants(low_ref, full_ref):
    sides = [low_ref[0:MINI], low_ref[MINI : 2 * MINI]]
    same, crossed = low_ref[32:160], low_ref[160:288]
    return sides, same, crossed, full_ref[0:MINI], full_ref[16:144], full_ref[144:272]


def lane_masks(rows=HEAD, width=3 * PAIR):
    lane = lax.broadcasted_iota(jnp.int32, (rows, width), 1)
    return lane % PAIR < HEAD, lane % HEAD < 32


PARTS = range(3)


def thin(part):
    return slice(PAIR * part, PAIR * (part + 1))


def wide(part):
    return slice(4 * PAIR * part, 4 * PAIR * (part + 1))


def lanes(pieces):
    return jnp.concatenate(pieces, axis=1)


def ttt_forward_kernel(steps, q_ref, k_ref, v_ref, rate_ref, w0_ref, b0_ref, gain_ref, shift_ref, low_ref, full_ref,
                       out_ref, w_ref, xh_ref, h_ref, grs_ref, xb_ref, stat_ref, score_ref, w_run, b_run, gain_query, shift_query):
    width = 768

    @pl.when(pl.program_id(0) == 0)
    def _():
        w_run[...] = w0_ref[...]
        b_run[...] = b0_ref[...]
        gain_query[...] = exchange(gain_ref[...])
        shift_query[...] = exchange(shift_ref[...])

    sides, same, crossed, tri, _, _ = read_constants(low_ref, full_ref)
    left, first_side = lane_masks()
    left_one, first_one = left[:, :PAIR], first_side[:, :PAIR]
    tri = lanes([tri] * 3)

    def begin(at):
        rows = slice(at * MINI, (at + 1) * MINI)
        queries = both_sequences(q_ref, rows, 0, width)
        keys = both_sequences(k_ref, rows, 0, width)
        targets = both_sequences(v_ref, rows, 0, width) - keys
        query_low, key_low = queries.astype(low), keys.astype(low)
        expanded = [expand_both(query_low[:, wide(part)], key_low[:, wide(part)], sides) for part in PARTS]
        target = lanes([to_feature(targets[:, wide(part)], first_one, (0, 1)) for part in PARTS])
        return rows, queries, query_low, expanded, target

    def multiply(at, started, weights):
        _, _, query_low, expanded, _ = started
        products = []
        for part in PARTS:
            weight_low = weights[part].astype(low)
            w_ref[at, :, wide(part)] = weight_low
            for group in range(2):
                here = slice(2 * PAIR * group, 2 * PAIR * (group + 1))
                rows = jnp.concatenate([weight_low[:, here], query_low[:, wide(part)][:, here]], axis=0)
                products.append(dot_nt(rows, expanded[part][1][group]))
        return lanes(products[::2]), lanes(products[1::2])

    def finish(at, started, kept):
        rows, queries = started[:2]
        inner_grad, mixing, updated = kept
        inner_grad_low = inner_grad.astype(low)
        moved = []
        for part in PARTS:
            mixing_block = jnp.concatenate([mixing[:, thin(part)]] * 8, axis=0) * crossed
            moved.append(dot_nt(inner_grad_low[:, thin(part)], mixing_block))
        updated = updated - lanes(moved)
        updated = updated - mean_rows(updated)
        updated_inverse = lax.rsqrt(mean_rows(updated * updated) + epsilon)
        updated = updated * updated_inverse
        xb_ref[at] = updated
        stat_ref[at, 3:4] = updated_inverse
        updated = updated * gain_query[...] + shift_query[...]
        result = queries + lanes([to_rows(updated[:, thin(part)], left_one[:MINI], query_row) for part in PARTS])
        out_ref[0, rows, :] = result[:, :width]
        out_ref[1, rows, :] = result[:, width:]

    weights = [w_run[:, wide(part)] for part in PARTS]
    offset = b_run[...]
    started = begin(0)
    pending = None
    for at in range(steps):
        first, second = multiply(at, started, weights)
        if pending is not None:
            finish(*pending)
        gains, shifts = gain_ref[...], shift_ref[...]
        rate = rate_ref[at]
        _, _, _, expanded, target = started
        hidden = jnp.where(left, first[:HEAD], second[:HEAD]) + offset
        scores = jnp.where(left[:MINI], first[HEAD:], second[HEAD:]) + 1.0
        updated = jnp.where(left, second[:HEAD], first[:HEAD]) + exchange(offset)
        centred = hidden - mean_rows(hidden)
        inverse = lax.rsqrt(mean_rows(centred * centred) + epsilon)
        normed = centred * inverse
        held = gains * normed + (shifts - target)
        residual = held * gains
        residual_mean = mean_rows(residual)
        cross = mean_rows(residual * normed)
        inner_grad = (residual - residual_mean - normed * cross) * inverse
        scaled = inner_grad * (rate * (1.0 / MINI))
        scaled_low = scaled.astype(low)
        scaled_other = exchange(scaled).astype(low)
        xh_ref[at] = normed
        h_ref[at] = held
        grs_ref[at] = scaled
        stat_ref[at, 0:1] = inverse
        stat_ref[at, 1:2] = residual_mean
        stat_ref[at, 2:3] = cross
        score_ref[at] = scores
        changed = []
        for part in PARTS:
            blocks = expanded[part][0]
            change = [dot_nn(scaled_low[:, thin(part)][:, :HEAD], blocks[0][0]),
                      dot_nn(scaled_other[:, thin(part)][:, :HEAD], blocks[1][0])]
            changed.append(weights[part] - lanes(change))
        weights = changed
        offset = offset - lanes([dot_nn(scaled_low[:, thin(part)], same) for part in PARTS])
        pending = (at, started, (inner_grad, (tri * rate * scores).astype(low), updated))
        if at + 1 < steps:
            started = begin(at + 1)
    finish(*pending)
    for part in PARTS:
        w_run[:, wide(part)] = weights[part]
    b_run[...] = offset


def ttt_backward_kernel(steps, q_ref, k_ref, dout_ref, rate_ref, w_ref, xh_ref, h_ref, grs_ref, xb_ref, stat_ref, score_ref,
                        gain_ref, low_ref, full_ref, *refs):
    states, refs = refs[:6], refs[6:]
    grad_ref, rdr_ref, dw_ref, db_ref, dgain_ref, dshift_ref, dgain_query_ref, dshift_query_ref, gain_query = refs[-9:]
    width = 768

    @pl.when(pl.program_id(0) == 0)
    def _():
        for state, ref in zip(states, (dw_ref, db_ref, dgain_ref, dshift_ref, dgain_query_ref, dshift_query_ref)):
            ref[...] = state[...]
        gain_query[...] = exchange(gain_ref[...])

    sides, same, crossed, tri, scale, scale_turned = read_constants(low_ref, full_ref)
    left, first_side = lane_masks()
    left_one, first_one = left[:, :PAIR], first_side[:, :PAIR]
    left_rows = left_one[:MINI]
    left_square = lax.broadcasted_iota(jnp.int32, (PAIR, PAIR), 1) < HEAD
    zero = jnp.zeros((MINI, PAIR), full)
    tri = lanes([tri] * 3)

    def begin(at):
        rows = slice(at * MINI, (at + 1) * MINI)
        query_low = both_sequences(q_ref, rows, 0, width).astype(low)
        key_low = both_sequences(k_ref, rows, 0, width).astype(low)
        douts = both_sequences(dout_ref, rows, 0, width)
        expanded = [expand_both(query_low[:, wide(part)], key_low[:, wide(part)], sides) for part in PARTS]
        mixing = (tri * rate_ref[at] * score_ref[at]).astype(low)
        dout = lanes([to_feature(douts[:, wide(part)], first_one, (1, 0)) for part in PARTS])
        updated = xb_ref[at]
        dupdated = dout * gain_query[...]
        dupdated = stat_ref[at, 3:4] * (dupdated - mean_rows(dupdated) - updated * mean_rows(dupdated * updated))
        dgain_query_ref[...] += dout * updated
        dshift_query_ref[...] += dout
        dupdated_low = dupdated.astype(low)
        mixed = []
        for part in PARTS:
            mixing_block = jnp.concatenate([mixing[:, thin(part)]] * 8, axis=0) * crossed
            mixed.append(dot_nn(dupdated_low[:, thin(part)], mixing_block))
        return rows, douts, expanded, dupdated, dupdated_low, lanes(mixed)

    def finish(at, started, kept):
        rows, douts, expanded, dupdated, dupdated_low, _ = started
        dhidden, dtarget, dweights_low, rate_part = kept
        scaled = -grs_ref[at]
        scaled_low = scaled.astype(low)
        scores = score_ref[at]
        none = jnp.zeros((HEAD, PAIR), low)
        turned_low, turned_query, query_rows, dmixes, dmixes_turned = [], [], [], [], []
        for part in PARTS:
            turned_low.append(jnp.concatenate([dhidden[:, thin(part)], scaled[:, thin(part)]], axis=0).T.astype(low))
            turned_query.append(jnp.concatenate([dupdated[:, thin(part)], dtarget[:, thin(part)]], axis=0).T)
            query_rows.append(jnp.where(left_square, turned_query[part], 0.0).astype(low))
        for part in PARTS:
            dmix = dot_nn(query_rows[part][:, :HEAD], scaled_low[:, thin(part)]) * scale
            dmix_turned = dot_nn(turned_low[part], jnp.concatenate([none, dupdated_low[:, thin(part)]], axis=0)) * scale_turned
            dmixes.append(sum(dmix[MINI * row : MINI * (row + 1)] for row in range(8)))
            dmixes_turned.append(sum(dmix_turned[MINI * row : MINI * (row + 1)] for row in range(8)))
        rdr_ref[at] = rate_part + jnp.sum(lanes(dmixes) * scores, axis=0, keepdims=True)
        query_grads, key_grads, value_grads = [], [], []
        for part in PARTS:
            weight_low = w_ref[at, :, wide(part)]
            for group in range(2):
                keep_key, keep_query = (left_rows, ~left_rows) if group == 0 else (~left_rows, left_rows)
                key_side = jnp.where(keep_query, dmixes_turned[part], zero).astype(low)
                query_side = jnp.where(keep_key, dmixes[part], zero).astype(low)
                extra = jnp.concatenate([key_side, key_side, query_side, query_side], axis=0)
                for at_tile in range(2):
                    tile = 2 * group + at_tile
                    place = [key_row(group, side, at_tile) for side in range(2)]
                    place_query = [query_row(group, side, at_tile) for side in range(2)]
                    held_rows = jnp.concatenate(
                        [turned_low[part][row : row + MINI] for row in place]
                        + [query_rows[part][row : row + MINI] for row in place_query],
                        axis=0,
                    )
                    product = dot_nn(
                        jnp.concatenate([held_rows, extra], axis=1),
                        jnp.concatenate(
                            [tile_of(weight_low, tile), tile_of(dweights_low[part], tile), tile_of(expanded[part][1][group], at_tile)],
                            axis=0,
                        ),
                    )
                    dvalue = jnp.where(
                        left_rows,
                        exchange(turned_query[part][place[0] : place[0] + MINI]),
                        turned_query[part][place[1] : place[1] + MINI],
                    )
                    key_grads.append(dvalue + jnp.where(left_rows, product[:MINI], product[MINI : 2 * MINI]))
                    query_grads.append(
                        tile_of(douts[:, wide(part)], tile) + jnp.where(left_rows, product[2 * MINI : 3 * MINI], product[3 * MINI :])
                    )
                    value_grads.append(-dvalue)
        store_sequences(grad_ref, rows, 0, width, query_grads, low)
        store_sequences(grad_ref, rows, width, width, key_grads, low)
        store_sequences(grad_ref, rows, 2 * width, width, value_grads, low)

    dweights = [dw_ref[:, wide(part)] for part in PARTS]
    doffset = db_ref[...]
    started = begin(steps - 1)
    pending = None
    for at in reversed(range(steps)):
        _, _, expanded, dupdated, _, mixed = started
        dweights_low = [dweight.astype(low) for dweight in dweights]
        key_dw = []
        for part in PARTS:
            blocks = expanded[part][0]
            key_dw.append(dot_nt(dweights_low[part][:, : 2 * PAIR], blocks[0][0]))
            key_dw.append(dot_nt(dweights_low[part][:, 2 * PAIR :], blocks[1][0]))
        key_dw = lanes(key_dw) + doffset
        if pending is not None:
            finish(*pending)
        upcoming = begin(at - 1) if at > 0 else None
        gains = gain_ref[...]
        rate = rate_ref[at]
        normed, held, scaled = xh_ref[at], h_ref[at], grs_ref[at]
        inverse, residual_mean, cross = (stat_ref[at, row : row + 1] for row in range(3))
        grad_in = -mixed - (rate * (1.0 / MINI)) * key_dw
        rate_part = -jnp.sum(scaled * key_dw, axis=0, keepdims=True)
        residual = held * gains
        in_mean = mean_rows(grad_in)
        in_cross = mean_rows(grad_in * normed)
        in_held = inverse * (mean_rows(grad_in * residual) - residual_mean * in_mean - cross * in_cross)
        dresidual = inverse * (grad_in - in_mean - normed * in_cross)
        dtarget = dresidual * gains
        dnormed = dtarget * gains - inverse * (grad_in * cross + in_cross * residual)
        dhidden = inverse * (dnormed - mean_rows(dnormed) - normed * (mean_rows(dnormed * normed) + in_held))
        dgain_ref[...] += dresidual * (held + gains * normed)
        dshift_ref[...] += dtarget
        to_first = jnp.where(left, dhidden, dupdated).astype(low)
        to_second = jnp.where(left, dupdated, dhidden).astype(low)
        changed = []
        for part in PARTS:
            pairs = expanded[part][1]
            change = [dot_nn(to_first[:, thin(part)], pairs[0]), dot_nn(to_second[:, thin(part)], pairs[1])]
            changed.append(dweights[part] + lanes(change))
        total_low = (exchange(dupdated) + dhidden).astype(low)
        doffset = doffset + lanes([dot_nn(total_low[:, thin(part)], same) for part in PARTS])
        dweights = changed
        pending = (at, started, (dhidden, dtarget, dweights_low, rate_part))
        started = upcoming
    finish(*pending)
    for part in PARTS:
        dw_ref[:, wide(part)] = dweights[part]
    db_ref[...] = doffset


def ttt_constants():
    lane = np.arange(PAIR)
    row = np.arange(MINI)
    sides = np.concatenate([np.tile(lane < HEAD, (MINI, 1)), np.tile(lane >= HEAD, (MINI, 1))])
    token = lane % MINI
    tri = np.where(token[None] <= row[:, None], 1.0 / (row[:, None] + 1.0), 0.0)
    same = lane[:, None] // MINI == lane[None] // MINI
    crossed = (lane[:, None] + HEAD) % PAIR // MINI == lane[None] // MINI
    scale = np.where(crossed & (token[None] <= token[:, None]), MINI / (token[:, None] + 1.0), 0.0)
    return (
        jnp.asarray(np.concatenate([sides, same, crossed]).astype(np.float32), low),
        jnp.asarray(np.concatenate([tri, scale, scale.T]), full),
    )


def ttt_forward(projected, rates, state, gains, shifts, steps=4):
    count = projected.shape[1] // MINI
    first, begin, end = 0, 0, count
    queries, keys, values = projected, projected, projected
    constants = ttt_constants()
    whole = lambda *shape: pl.BlockSpec(shape, lambda at: (0,) * len(shape))
    column = lambda place: pl.BlockSpec((2, steps * MINI, 768), lambda at, place=place: (0, first + at, place))
    part = column(0)
    saved = lambda *tail: pl.BlockSpec((steps,) + tail, lambda at: (at, 0, 0))
    made = lambda kind, *tail: jax.ShapeDtypeStruct((end - begin,) + tail, kind)
    inputs = [queries, keys, values, rates, *state, gains, shifts, *constants]
    out, *rest = pl.pallas_call(
        lambda *refs: ttt_forward_kernel(steps, *refs),
        grid=((end - begin) // steps,),
        in_specs=[column(0), column(1), column(2), pl.BlockSpec((steps, 1, 384), lambda at: (first + at, 0, 0)), whole(64, 1536), whole(64, 384),
                  whole(64, 384), whole(64, 384), whole(288, 128), whole(272, 128)],
        out_specs=[part, saved(64, 1536), saved(64, 384), saved(64, 384), saved(64, 384), saved(64, 384), saved(8, 384),
                   saved(16, 384)],
        out_shape=[jax.ShapeDtypeStruct((2, count * MINI, 768), full), made(low, 64, 1536), made(full, 64, 384), made(full, 64, 384),
                   made(full, 64, 384), made(full, 64, 384), made(full, 8, 384), made(full, 16, 384)],
        scratch_shapes=[pltpu.VMEM((64, 1536), full)] + [pltpu.VMEM((64, 384), full)] * 3,
        compiler_params=pltpu.CompilerParams(vmem_limit_bytes=60 * 1024 * 1024),
        cost_estimate=pl.CostEstimate(flops=(end - begin) * 1_400_000_000, bytes_accessed=(end - begin) * 1_500_000, transcendentals=0),
        name="ttt_forward",
    )(*inputs)
    return out, rest


def ttt_backward(projected, dout, rates, saved_arrays, state, gains, begin, end, before, steps=4):
    count = projected.shape[1] // MINI
    first, blocks = begin // steps, (end - begin) // steps
    queries, keys = projected, projected
    constants = ttt_constants()
    whole = lambda *shape: pl.BlockSpec(shape, lambda at: (0,) * len(shape))
    part = lambda width, place=0: pl.BlockSpec((2, steps * MINI, width), lambda at: (0, first + blocks - 1 - at, place))
    saved = lambda *tail: pl.BlockSpec((steps,) + tail, lambda at: (first + blocks - 1 - at, 0, 0))
    made = lambda *tail: pl.BlockSpec((steps,) + tail, lambda at: (blocks - 1 - at, 0, 0))
    extra = [] if before is None else [before]
    inputs = [queries, keys, dout, rates, *saved_arrays, gains, *constants, *state]
    states = [whole(64, 1536)] + [whole(64, 384)] * 5
    grad, rate_back, *state = pl.pallas_call(
        lambda *refs: ttt_backward_kernel(steps, *refs),
        grid=(blocks,),
        in_specs=[part(768), part(768, 1), part(768), saved(1, 384),
                  saved(64, 1536), saved(64, 384), saved(64, 384), saved(64, 384), saved(64, 384), saved(8, 384), saved(16, 384),
                  whole(64, 384), whole(288, 128), whole(272, 128)]
        + states + [pl.BlockSpec(memory_space=pl.ANY)] * len(extra),
        out_specs=[part(2304), made(1, 384)] + states,
        out_shape=[jax.ShapeDtypeStruct((2, count * MINI, 2304), low), jax.ShapeDtypeStruct((end - begin, 1, 384), full)]
        + [jax.ShapeDtypeStruct((64, 1536), full)] + [jax.ShapeDtypeStruct((64, 384), full)] * 5,
        scratch_shapes=[pltpu.VMEM((64, 384), full)],
        input_output_aliases={len(inputs): 0} if extra else {},
        compiler_params=pltpu.CompilerParams(vmem_limit_bytes=60 * 1024 * 1024),
        cost_estimate=pl.CostEstimate(flops=(end - begin) * 2_000_000_000, bytes_accessed=(end - begin) * 1_500_000, transcendentals=0),
        name="ttt_backward",
    )(*inputs, *extra)
    return grad, rate_back, state


def silu_parts(gate):
    sigma = jax.nn.sigmoid(gate)
    return gate * sigma, sigma * (1.0 + gate * (1.0 - sigma))


def gelu_parts(values):
    slope = 0.7978845608028654
    turn = jnp.tanh(slope * (values + 0.044715 * values * values * values))
    half = 0.5 * (1.0 + turn)
    return values * half, half + 0.5 * values * (1.0 - turn * turn) * slope * (1.0 + 3 * 0.044715 * values * values)


def row_mean(values):
    return jnp.mean(values, axis=-1, keepdims=True)


def dot_tn(former, latter):
    return lax.dot_general(former, latter, (((0,), (0,)), ((), ())), preferred_element_type=full)


def exact_dot(former, latter):
    total = None
    for _ in range(3):
        part = former.astype(low)
        former = former - part.astype(full)
        term = dot_nn(part, latter)
        total = term if total is None else total + term
    return total


def constant_spec(*shape, at=0, buffers=None):
    index = lambda *steps: (0,) * (len(shape) - 1) + (at,)
    if buffers is None:
        return pl.BlockSpec(shape, index)
    return pl.BlockSpec(shape, index, pipeline_mode=pl.Buffered(buffers))


def call(kernel, name, grid, prefetch, in_specs, out_specs, out_shape, scratch, cost, arrays):
    return pl.pallas_call(
        kernel,
        grid_spec=pltpu.PrefetchScalarGridSpec(
            num_scalar_prefetch=prefetch, grid=grid, in_specs=in_specs, out_specs=out_specs, scratch_shapes=scratch
        ),
        out_shape=out_shape,
        compiler_params=pltpu.CompilerParams(vmem_limit_bytes=60 * 1024 * 1024),
        cost_estimate=pl.CostEstimate(flops=cost, bytes_accessed=cost // 500, transcendentals=0),
        name=name,
    )(*arrays)


ETA = 64
VECTORS = 80
BIAS = 96


def lane_table():
    lane = np.arange(384)
    part, group, side, tile, token = lane // 128, lane // 64 % 2, lane // 32 % 2, lane // 16 % 2, lane % 16
    pair = 4 * part + 2 * group + tile
    return token, pair // 6, 2 * (pair % 6) + side


def lane_constants():
    token, sequence, head = lane_table()
    table = np.zeros((32, 384), np.float32)
    table[:MINI] = token[None] == np.arange(MINI)[:, None]
    table[16], table[17] = sequence, token
    chosen = np.zeros((PAIR, 384), np.float32)
    chosen[ETA + head, np.arange(384)] = 1
    return jnp.asarray(table), jnp.asarray(chosen, low)


def block_copies(from_refs, table, to, columns, semaphores, first):
    started = []
    for place, ref in enumerate(from_refs):
        for item in range(ref.shape[0]):
            begin = pl.multiple_of(table[place * ref.shape[0] + item] * ref.shape[1], 16)
            target = to.at[pl.ds(begin, ref.shape[1]), columns]
            started.append(pltpu.make_async_copy(ref.at[item], target, semaphores.at[first + len(started)]))
    return started


def project_kernel(counts, length_ref, early_table_ref, late_table_ref, tokens_ref, bias_ref, table_ref, chosen_ref, *refs):
    early_refs, late_refs, refs = refs[: counts[0]], refs[counts[0] : sum(counts)], refs[sum(counts) :]
    whole_ref, proj_ref, normed_ref, rate_ref, rest_ref, wt_ref, b_ref, gain_ref, shift_ref, vec_ref, semaphores = refs
    at = pl.program_id(0)
    split = 512 // tokens_ref.shape[0]
    wide = proj_ref.shape[1]
    begin_small = whole_ref.shape[1] - PAIR
    cut = early_refs[0].shape[2]

    def copies():
        started = block_copies(early_refs, early_table_ref, whole_ref, slice(0, cut), semaphores, 0)
        return started + block_copies(late_refs, late_table_ref, whole_ref, slice(cut, whole_ref.shape[1]), semaphores, len(started))

    @pl.when(at == 0)
    def _():
        for copy in copies():
            copy.start()
        for copy in copies():
            copy.wait()
        small = whole_ref[:, begin_small:].astype(full)
        turned = small.T
        wt_ref[:, :768] = turned[:HEAD]
        wt_ref[:, 768:] = turned[:HEAD]
        vec_ref[...] = turned[VECTORS : VECTORS + 8]
        for place, ref in enumerate((b_ref, gain_ref, shift_ref)):
            total = jnp.zeros((HEAD, 384), full)
            for head in range(12):
                column = small[HEAD * head : HEAD * (head + 1), VECTORS + place : VECTORS + place + 1]
                total = total + column * chosen_ref[ETA + head : ETA + head + 1].astype(full)
            ref[...] = total
        rate_ref[...] = jnp.zeros_like(rate_ref)
        rest_ref[...] = jnp.zeros_like(rest_ref)

    values = tokens_ref[...].astype(full)
    normed = (values * lax.rsqrt(row_mean(values * values) + epsilon) * vec_ref[3:4]).astype(low)
    normed_ref[...] = normed
    proj_ref[...] = dot_nn(normed, whole_ref[:, :wide])
    last = dot_nn(normed, whole_ref[:, begin_small:])
    spread = exact_dot(last + bias_ref[...], chosen_ref[...])
    blocks = spread.shape[0] // MINI
    spread = jnp.sum(spread.reshape(blocks, MINI, 384) * table_ref[:MINI][None], axis=1)
    sequence, token = table_ref[16:17], table_ref[17:18]
    mine = sequence == (at // split).astype(full)
    sigma = jax.nn.sigmoid(spread)
    begin = (at % split) * blocks
    block = lax.broadcasted_iota(jnp.int32, spread.shape, 0) + begin
    live = (block * MINI).astype(full) + token < length_ref[at // split].astype(full)
    here = pl.ds(begin, blocks)
    rate_ref[here, 0, :] += jnp.where(live & mine, sigma * (1.0 / HEAD), 0.0)
    rest_ref[here, :] += jnp.where(mine, 1.0 - sigma, 0.0)


def project(lengths, tokens, early, late, bias_row):
    rows, width = tokens.shape
    table, chosen = lane_constants()
    tile = rows // 2
    columns = early[0][0].shape[2] + late[0][0].shape[2]
    counts = len(early[0]), len(late[0])
    row = lambda n: pl.BlockSpec((tile, n), lambda at, *_: (at, 0))
    shape = jax.ShapeDtypeStruct
    return call(
        lambda *refs: project_kernel(counts, *refs), "project", (2,), 3,
        [row(width), constant_spec(1, PAIR), constant_spec(32, 384), constant_spec(PAIR, 384)]
        + [pl.BlockSpec(memory_space=pl.ANY)] * sum(counts),
        [constant_spec(width, columns, buffers=1), row(3 * width), row(width), constant_spec(32, 1, 384), constant_spec(32, 384),
         constant_spec(64, 1536)] + [constant_spec(64, 384)] * 3 + [constant_spec(8, width)],
        [shape((width, columns), low), shape((rows, 3 * width), full), shape((rows, width), low), shape((32, 1, 384), full),
         shape((32, 384), full), shape((64, 1536), full)] + [shape((64, 384), full)] * 3 + [shape((8, width), full)],
        [pltpu.SemaphoreType.DMA((early[1].shape[0] + late[1].shape[0],))], 5_000_000_000,
        (lengths, early[1], late[1], tokens, bias_row, table, chosen, *early[0], *late[0]),
    )


def post_kernel(inner_ref, normed_ref, tokens_ref, w_gate_ref, w_out_ref, vec_ref, gate_ref, mixed_ref, first_ref, second_ref):
    gate = dot_nn(normed_ref[...], w_gate_ref[...])
    gate_ref[...] = gate
    inner = inner_ref[...]
    centred = inner - row_mean(inner)
    standard = centred * lax.rsqrt(row_mean(centred * centred) + epsilon)
    mixed = ((standard * vec_ref[4:5] + vec_ref[5:6]) * gelu_parts(gate)[0]).astype(low)
    mixed_ref[...] = mixed
    first = tokens_ref[...].astype(full) + dot_nn(mixed, w_out_ref[...])
    first_ref[...] = first
    second_ref[...] = (first * lax.rsqrt(row_mean(first * first) + epsilon) * vec_ref[6:7]).astype(low)


def post(inner, normed, tokens, whole, vectors):
    rows, width = tokens.shape
    tile = rows // 4
    row = pl.BlockSpec((tile, width), lambda at: (at, 0))
    shape = jax.ShapeDtypeStruct
    return call(
        post_kernel, "post", (4,), 0,
        [row, row, row, constant_spec(width, width, at=3, buffers=1), constant_spec(width, width, at=4, buffers=1), constant_spec(8, width)],
        [row] * 4, [shape((rows, width), kind) for kind in (full, low, full, low)], [], 4_000_000_000,
        (inner, normed, tokens, whole, whole, vectors),
    )


def store_blocks(table_ref, sent_ref, kept_ref, held_ref, block):
    half = kept_ref.shape[0]
    if block % 8:
        kept_ref[...] = held_ref[:half].astype(kept_ref.dtype)
        sent_ref[...] = held_ref[half:].astype(sent_ref.dtype)
        return
    for pair in range(held_ref.shape[0] // (2 * block)):
        rows = [held_ref[pl.ds(pl.multiple_of(table_ref[2 * pair + side] * block, 8), block), :] for side in range(2)]
        begin = 2 * block * pair
        ref, begin = (kept_ref, begin) if begin < half else (sent_ref, begin - half)
        ref[begin : begin + 2 * block, :] = jnp.concatenate(rows, axis=0).astype(ref.dtype)


def ffn_kernel(block, down_block, steps, counts, table_ref, shared_ref, both_table_ref, down_table_ref, second_ref, first_ref, up_ref, *refs):
    both_refs, refs = refs[: counts[0]], refs[counts[0] :]
    down_refs, refs = refs[: counts[1]], refs[counts[1] :]
    aligned = block % 8 == 0
    out_ref, dsecond_ref, sent_ref, kept_ref, *refs = refs
    natural_ref, refs = (None, refs) if aligned else (refs[0], refs[1:])
    turned, total, act, both_low, held, w_both, w_down_all, held_down, semaphores = refs
    at = pl.program_id(0)
    size = act.shape[1]
    hidden = w_down_all.shape[0]

    def copies():
        started = block_copies(both_refs, both_table_ref, w_both, slice(None), semaphores, 0)
        return started + block_copies(down_refs, down_table_ref, w_down_all, slice(None), semaphores, len(started))

    @pl.when(at == 0)
    def _():
        for copy in copies():
            copy.start()
        turned[...] = second_ref[...].T
        total[...] = first_ref[...]
        dsecond_ref[...] = jnp.zeros_like(dsecond_ref)
        for copy in copies():
            copy.wait()

    @pl.when(at < steps)
    def _():
        columns = pl.ds(pl.multiple_of(at * size, PAIR), size)
        w_gate, w_up = w_both[:, columns], w_both[:, pl.ds(pl.multiple_of(hidden + at * size, PAIR), size)]
        w_down = w_down_all[columns, :]
        second, upstream = second_ref[...], up_ref[...]
        cuts = [slice(begin, begin + size // 2) for begin in range(0, size, size // 2)]
        made = [(dot_nn(second, w_gate[:, cut]), dot_nn(second, w_up[:, cut]), dot_nt(upstream, w_down[cut])) for cut in cuts]
        for cut, (gate, up, dact) in zip(cuts, made):
            value, slope = silu_parts(gate)
            act[:, cut] = (value * up).astype(low)
            both_low[:, cut] = (dact * up * slope).astype(low)
            both_low[:, size + cut.start : size + cut.stop] = (dact * value).astype(low)
        total[...] += dot_nn(act[...], w_down)
        dsecond_ref[...] += dot_nt(both_low[:, :size], w_gate) + dot_nt(both_low[:, size:], w_up)
        ddown = dot_tn(act[...], upstream)
        held[...] = dot_nn(turned[...], both_low[...])
        if aligned:
            count = size // down_block
            third = ddown.shape[1] // 3
            for place in range(count):
                mine = ddown[down_block * place : down_block * (place + 1)]
                pieces = [jnp.concatenate([mine[8 * row : 8 * row + 8, third * part : third * (part + 1)] for row in range(down_block // 8)],
                                          axis=1) for part in range(3)]
                held_down[pl.ds(pl.multiple_of((at * count + place) * block, 8), block), :] = jnp.concatenate(pieces, axis=0)
        else:
            natural_ref[pl.ds(pl.multiple_of(at * size, 16), size), :] = ddown.astype(low)
        store_blocks(table_ref, sent_ref, kept_ref, held, block)

    @pl.when(at == steps - 1)
    def _():
        out_ref[...] = total[...].astype(low)

    if aligned:
        for extra in range(held_down.shape[1] // (2 * size)):

            @pl.when(at == steps + extra)
            def _():
                store_blocks(shared_ref, sent_ref, kept_ref, held_down.at[:, 2 * size * extra : 2 * size * (extra + 1)], block)


def ffn(table, shared, second, first, upstream, both, down, devices, steps):
    rows, width = second.shape
    hidden = down[0][0].shape[1] * down[1].shape[0]
    size = hidden // steps
    aligned = width // devices % 8 == 0
    columns = 3 * hidden if aligned else 2 * hidden
    shape = jax.ShapeDtypeStruct
    counts = len(both[0]), len(down[0])
    copies = both[1].shape[0] + down[1].shape[0]
    natural = [] if aligned else [(hidden, width)]
    return call(
        lambda *refs: ffn_kernel(width // devices, hidden // devices, steps, counts, *refs), "ffn", (columns // (2 * size),), 4,
        [constant_spec(rows, width, buffers=1)] * 3 + [pl.BlockSpec(memory_space=pl.ANY)] * sum(counts),
        [constant_spec(rows, width, buffers=1), constant_spec(rows, width, buffers=1),
         *[pl.BlockSpec((width // 2, 2 * size), lambda at, *_: (0, at))] * 2, *[constant_spec(*item, buffers=1) for item in natural]],
        [shape((rows, width), low), shape((rows, width), full), *[shape((width // 2, columns), low)] * 2,
         *[shape(item, low) for item in natural]],
        [pltpu.VMEM((width, rows), low), pltpu.VMEM((rows, width), full), pltpu.VMEM((rows, size), low),
         pltpu.VMEM((rows, 2 * size), low), pltpu.VMEM((width, 2 * size), full), pltpu.VMEM((width, 2 * hidden), low),
         pltpu.VMEM((hidden, width), low), pltpu.VMEM((width, hidden) if aligned else (8, PAIR), full),
         pltpu.SemaphoreType.DMA((copies,))],
        29_000_000_000, (table, shared, both[1], down[1], second, first, upstream, *both[0], *down[0]),
    )


def fold_kernel(counts, *refs):
    pairs, outs = refs[: 2 * sum(counts)], refs[2 * sum(counts) :]
    for group, count in enumerate(counts):
        sent_ref, kept_ref = outs[2 * group : 2 * group + 2]
        half = kept_ref.shape[0]
        begin = 0
        for _ in range(count):
            (kept, got), pairs = pairs[:2], pairs[2:]
            columns = slice(begin, begin + kept.shape[1])
            sent_ref[:, columns] = (kept[half:].astype(full) + got[half:].astype(full)).astype(low)
            kept_ref[:, columns] = kept[:half].astype(full) + got[:half].astype(full)
            begin = columns.stop


def fold(groups, steps):
    specs, arrays, outs, shapes = [], [], [], []
    for group in groups:
        rows = group[0][0].shape[0]
        width = 0
        for kept, got, first, columns in group:
            part = columns // steps
            specs += [pl.BlockSpec((rows, part), lambda at, begin=first // part: (0, begin + at))] * 2
            arrays += [kept, got]
            width += part
        outs += [pl.BlockSpec((rows // 2, width), lambda at: (0, at))] * 2
        shapes += [jax.ShapeDtypeStruct((rows // 2, width * steps), kind) for kind in (low, full)]
    results = call(
        lambda *refs: fold_kernel([len(group) for group in groups], *refs), "fold", (steps,), 0, specs, outs, shapes, [], 100_000_000, arrays
    )
    return [(results[place], results[place + 1]) for place in range(0, len(results), 2)]


def post_back_kernel(dsecond_ref, first_ref, up_ref, inner_ref, gate_ref, w_out_ref, vec_ref,
                     dfirst_ref, dgate_ref, dinner_ref, dfirst_low_ref, sums_ref):
    @pl.when(pl.program_id(0) == 0)
    def _():
        sums_ref[...] = jnp.zeros_like(sums_ref)

    first, dsecond = first_ref[...], dsecond_ref[...]
    scale = lax.rsqrt(row_mean(first * first) + epsilon)
    sums_ref[6:7] += jnp.sum(dsecond * first * scale, axis=0, keepdims=True)
    dsecond = dsecond * vec_ref[6:7]
    dfirst = up_ref[...].astype(full) + scale * dsecond - first * (scale * scale * scale * row_mean(first * dsecond))
    dfirst_ref[...] = dfirst
    dfirst_low = dfirst.astype(low)
    dfirst_low_ref[...] = dfirst_low
    dmixed = dot_nt(dfirst_low, w_out_ref[...])
    inner = inner_ref[...]
    centred = inner - row_mean(inner)
    inverse = lax.rsqrt(row_mean(centred * centred) + epsilon)
    standard = centred * inverse
    value, slope = gelu_parts(gate_ref[...])
    dgate_ref[...] = (dmixed * (standard * vec_ref[4:5] + vec_ref[5:6]) * slope).astype(low)
    dpost = dmixed * value
    sums_ref[4:5] += jnp.sum(dpost * standard, axis=0, keepdims=True)
    sums_ref[5:6] += jnp.sum(dpost, axis=0, keepdims=True)
    dpost = dpost * vec_ref[4:5]
    dinner_ref[...] = inverse * (dpost - row_mean(dpost) - standard * row_mean(dpost * standard))


def post_back(dsecond, first, upstream, inner, gate, whole, vectors):
    rows, width = first.shape
    tile = rows // 4
    row = pl.BlockSpec((tile, width), lambda at: (at, 0))
    shape = jax.ShapeDtypeStruct
    return call(
        post_back_kernel, "post_back", (4,), 0,
        [row] * 5 + [constant_spec(width, width, at=4, buffers=1), constant_spec(8, width)],
        [row, row, row, row, constant_spec(8, width)],
        [shape((rows, width), full), shape((rows, width), low), shape((rows, width), full), shape((rows, width), low),
         shape((8, width), full)],
        [], 4_000_000_000, (dsecond, first, upstream, inner, gate, whole, vectors),
    )


def middle_kernel(block, table_ref, mixed_ref, dfirst_ref, normed_ref, dgate_ref, sent_ref, kept_ref, held):
    @pl.when(pl.program_id(0) == 0)
    def _():
        held[...] = dot_tn(mixed_ref[...], dfirst_ref[...])

    @pl.when(pl.program_id(0) == 1)
    def _():
        held[...] = dot_tn(normed_ref[...], dgate_ref[...])

    store_blocks(table_ref, sent_ref, kept_ref, held, block)


def middle_grads(table, mixed, dfirst, normed, dgate, devices):
    rows, width = normed.shape
    whole = constant_spec(rows, width, buffers=1)
    return call(
        lambda *refs: middle_kernel(width // devices, *refs), "middle_grads", (2,), 1,
        [whole] * 4, [pl.BlockSpec((width // 2, width), lambda at, *_: (0, at))] * 2,
        [jax.ShapeDtypeStruct((width // 2, 2 * width), low)] * 2, [pltpu.VMEM((width, width), full)], 3_000_000_000,
        (table, mixed, dfirst, normed, dgate),
    )


def weight_kernel(block, table_ref, normed_ref, grad_ref, sent_ref, kept_ref, turned, held):
    @pl.when(pl.program_id(0) == 0)
    def _():
        turned[...] = normed_ref[...].T

    held[...] = dot_nn(turned[...], grad_ref[...])
    store_blocks(table_ref, sent_ref, kept_ref, held, block)


def weight_grads(table, normed, grads, devices):
    rows, width = normed.shape
    out = pl.BlockSpec((width // 2, width), lambda at, *_: (0, at))
    return call(
        lambda *refs: weight_kernel(width // devices, *refs), "weight_grads", (2,), 1,
        [constant_spec(rows, width, buffers=1), pl.BlockSpec((rows, width), lambda at, *_: (0, at))],
        [out, out], [jax.ShapeDtypeStruct((width // 2, 2 * width), low)] * 2,
        [pltpu.VMEM((width, rows), low), pltpu.VMEM((width, width), full)], 3_000_000_000, (table, normed, grads),
    )


def last_kernel(block, table_ref, normed_ref, grad_ref, sums_ref, dw_ref, db_ref, dgain_ref, dshift_ref, dgain_query_ref,
                dshift_query_ref, rate_ref, rest_ref, lane_ref, chosen_ref, sent_ref, kept_ref, dlog_ref, held):
    rows, width = normed_ref.shape
    turned = normed_ref[...].T
    held[:, :width] = dot_nn(turned, grad_ref[...])
    slots = rate_ref.shape[0] * MINI
    for sequence in range(rows // slots):
        mine = (lane_ref[16:17] == float(sequence)).astype(full)
        spread = rate_ref[:, 0, :] * rest_ref[...] * mine
        spread = (spread[:, None, :] * lane_ref[:MINI][None]).reshape(slots, 384).astype(low)
        dlog_ref[slots * sequence : slots * (sequence + 1)] = dot_nt(spread, chosen_ref[...]).astype(low)
    eta = dot_nn(turned, dlog_ref[...])
    inner = dw_ref[:, :width] + dw_ref[:, width:]
    fixed = jnp.concatenate(
        [inner, jnp.zeros((VECTORS - HEAD, width), full), sums_ref[...], jnp.zeros((PAIR - VECTORS - 8, width), full)], axis=0
    )
    lane = lax.broadcasted_iota(jnp.int32, (HEAD, PAIR), 1)
    chosen = chosen_ref[...].astype(full)
    bias = jnp.sum(rate_ref[:, 0, :] * rest_ref[...], axis=0, keepdims=True)
    held[:, width:] = eta + fixed.T
    bias = jnp.sum(chosen * bias, axis=1, keepdims=True)
    square = jnp.broadcast_to(bias, (PAIR, PAIR)).T[:1]
    bias_row = pltpu.roll(square, BIAS - ETA, axis=1)
    bias_row = jnp.where((lane[:1] >= BIAS) & (lane[:1] < BIAS + 12), bias_row, 0.0)
    lanes_of = [db_ref[...] * (1.0 / MINI), dgain_ref[...] + exchange(dgain_query_ref[...]), dshift_ref[...] + exchange(dshift_query_ref[...])]
    for head in range(12):
        here = pl.ds(HEAD * head, HEAD)
        mask = chosen[ETA + head : ETA + head + 1]
        total = held[here, width:] + bias_row
        for place, values in enumerate(lanes_of):
            column = jnp.sum(values * mask, axis=1, keepdims=True)
            total = total + jnp.where(lane == VECTORS + place, column, 0.0)
        held[here, width:] = total
    store_blocks(table_ref, sent_ref, kept_ref, held, block)


def last_grads(table, normed, grads, sums, state, rate_back, rest, devices):
    rows, width = normed.shape
    lane, chosen = lane_constants()
    spec = lambda array: constant_spec(*array.shape, buffers=1)
    others = (sums, *state, rate_back, rest, lane, chosen)
    shape = jax.ShapeDtypeStruct
    out = constant_spec(width // 2, width + PAIR, buffers=1)
    return call(
        lambda *refs: last_kernel(width // devices, *refs), "last_grads", (1,), 1,
        [spec(normed), constant_spec(rows, width, at=2, buffers=1)] + [spec(array) for array in others],
        [out, out, constant_spec(rows, PAIR, buffers=1)],
        [shape((width // 2, width + PAIR), low)] * 2 + [shape((rows, PAIR), low)],
        [pltpu.VMEM((width, width + PAIR), full)], 3_000_000_000, (table, normed, grads, *others),
    )


def finish_kernel(tokens_ref, dfirst_ref, dqkv_ref, dgate_ref, dlog_ref, w_ref, small_ref, w_gate_ref, vec_ref, out_ref):
    dnormed = dot_nt(dqkv_ref[...], w_ref[...]) + dot_nt(dgate_ref[...], w_gate_ref[...]) + dot_nt(dlog_ref[...], small_ref[...])
    values = tokens_ref[...].astype(full)
    scale = lax.rsqrt(row_mean(values * values) + epsilon)
    dnormed = dnormed * vec_ref[3:4]
    back = scale * dnormed - values * (scale * scale * scale * row_mean(values * dnormed))
    out_ref[...] = (dfirst_ref[...] + back).astype(low)


def finish(tokens, dfirst, dqkv, dgate, dlog, whole, vectors, at, before):
    rows, width = tokens.shape
    tile = rows // 2
    row = lambda n: pl.BlockSpec((tile, n), lambda step: (at, 0))
    arrays = [tokens, dfirst, dqkv, dgate, dlog, whole, whole, whole, vectors]
    extra = [] if before is None else [before]
    return pl.pallas_call(
        lambda *refs: finish_kernel(*refs[:9], refs[-1]),
        grid=(1,),
        in_specs=[row(width), row(width), row(3 * width), row(width), row(PAIR), constant_spec(width, 3 * width, buffers=1),
                  constant_spec(width, PAIR, at=5 * width // PAIR, buffers=1), constant_spec(width, width, at=3, buffers=1),
                  constant_spec(8, width)] + [pl.BlockSpec(memory_space=pl.ANY)] * len(extra),
        out_specs=row(width),
        out_shape=jax.ShapeDtypeStruct((rows, width), low),
        input_output_aliases={len(arrays): 0} if extra else {},
        compiler_params=pltpu.CompilerParams(vmem_limit_bytes=60 * 1024 * 1024),
        cost_estimate=pl.CostEstimate(flops=3_000_000_000, bytes_accessed=10_000_000, transcendentals=0),
        name="finish",
    )(*arrays, *extra)


class Links:
    def __init__(self, dp, fsdp):
        self.axes = ("dp", "fsdp")
        self.count = dp * fsdp
        self.core = fsdp
        self.far = fsdp // 2
        bits = [1 << place for place in reversed(range(self.count.bit_length() - 1))]
        self.others = [bit for bit in bits if bit != self.core]
        near = [bit for bit in reversed(self.others) if bit != self.far]
        near = near[:1] + near[:0:-1]
        turned = [near[turn:] + near[:turn] for turn in range(3)]
        self.orders = {"split": [turned[0], turned[2]], "shared": [turned[1]] * 2}
        self.phases = self.near = len(near)
        self.me = lax.axis_index("dp") * fsdp + lax.axis_index("fsdp")
        self.side = (self.me // self.core) % 2

    def swap(self, values, bits):
        pairs = [(place, place ^ bits[(place // self.core) % 2]) for place in range(self.count)]
        return lax.ppermute(values, self.axes, pairs)

    def one(self, bit):
        return (self.me // bit) % 2

    def join(self, held, bits):
        got = self.swap(held, bits)
        mine = jnp.where(self.side == 0, self.one(bits[0]), self.one(bits[1])) == 0
        return jnp.stack([jnp.where(mine, held, got), jnp.where(mine, got, held)])

    def gather(self, pieces, kinds):
        orders = [[[self.far] + order for order in self.orders[kind]] for kind in kinds]
        held = list(pieces)
        for phase in range(len(orders[0][0])):
            held = [self.join(array, [order[phase] for order in pair]) for array, pair in zip(held, orders)]
            changed = yield held
            held = held if changed is None else changed
        above = [bit for bit in self.others if bit > self.core]
        whole = []
        for array, pair in zip(held, orders):
            got = self.swap(array, [self.core] * 2)
            mine = self.side == 0
            cores = [jnp.where(mine, array, got), jnp.where(mine, got, array)]
            placed = []
            for half, order in zip(cores, pair):
                have = order[::-1]
                placed.append(half.transpose([have.index(bit) for bit in self.others] + [len(have), len(have) + 1]))
            whole.append(jnp.stack(placed, axis=len(above)).reshape(-1, array.shape[-1]))
        yield whole

    def gather_blocks(self, pieces, kinds, pairs, whole_last):
        held = list(pieces)
        orders = [self.orders[kind] for kind in kinds]
        count = self.phases

        def ready(array, place):
            rows = pieces[place].shape[0]
            if not pairs[place]:
                return array.reshape((-1, rows) + array.shape[-1:])
            turned = []
            stacked = array.ndim - 2
            for order in orders[place]:
                have = ([self.far] + order)[:stacked][::-1]
                at = have.index(1)
                turned.append(array.transpose([axis for axis in range(stacked) if axis != at] + [at, stacked, stacked + 1]))
            array = jnp.where(self.side == 0, turned[0], turned[1])
            return array.reshape((-1, 2 * rows) + array.shape[-1:])

        for phase in range(count):
            for place, pair in enumerate(orders):
                held[place] = self.join(held[place], [self.far] * 2 if phase == 0 else [order[phase - 1] for order in pair])
                if phase == count - 1 and not whole_last[place]:
                    held[place] = ready(held[place], place)
            changed = yield held
            held = held if changed is None else changed
        buffers = []
        for place, pair in enumerate(orders):
            last = [order[-1] for order in pair]
            if whole_last[place]:
                buffers.append([ready(self.join(held[place], last), place)])
            else:
                buffers.append([held[place], self.swap(held[place], last), self.swap(held[place], [self.core] * 2)])
        changed = yield buffers
        buffers = buffers if changed is None else changed
        buffers = [list(group) + [self.swap(group[0 if whole else 1], [self.core] * 2)] for group, whole in zip(buffers, whole_last)]

        def places(bits, device, unit):
            found = []
            clear = device & ~(sum(bits) + unit - 1)
            for place in range(1 << len(bits)):
                found.append((clear + sum(bit for at, bit in enumerate(bits) if place >> (len(bits) - 1 - at) & 1)) // unit)
            return jnp.stack(found)

        done = []
        for place, pair in enumerate(orders):
            unit = 2 if pairs[place] else 1
            table = []
            for core, last in ((0, 0), (self.core, 0)) if whole_last[place] else ((0, 0), (0, 1), (self.core, 0), (self.core, 1)):
                by_side = []
                for order in pair:
                    have = ([self.far] + order)[::-1] if whole_last[place] else ([self.far] + order[:-1])[::-1]
                    by_side.append(places([bit for bit in have if bit >= unit], self.me ^ core ^ (order[-1] if last else 0), unit))
                own = self.side if core == 0 else 1 - self.side
                table.append(jnp.where(own == 0, by_side[0], by_side[1]))
            done.append((buffers[place], jnp.concatenate(table).astype(jnp.int32)))
        yield done

    def table(self, kind):
        half = []
        for side in range(2):
            masks = self.orders[kind][side] + [self.far]
            half.append(np.array([sum(bit for at, bit in enumerate(masks) if place >> (len(masks) - 1 - at) & 1)
                                  for place in range(self.count // 2)], np.int32))
        keep = jnp.where(self.side == 0, half[0], half[1])
        send = jnp.where(self.side == 0, half[1], half[0])
        return jnp.concatenate([self.me ^ keep, self.me ^ self.core ^ send]).astype(jnp.int32)

    def exchange_cores(self, pair):
        return pair[1], self.swap(pair[0], [self.core] * 2)

    def step(self, groups, phase):
        done = []
        for (sent, kept), kind in zip(groups, ("split", "shared")):
            bits = [order[phase] for order in self.orders[kind]] if phase < self.near else [self.far] * 2
            done.append((kept, self.swap(sent, bits)))
        return done


def refold(groups, steps):
    return fold([[(kept, got, 0, kept.shape[1])] for kept, got in groups], steps)


def tie(*groups):
    flat, tree = jax.tree.flatten(groups)
    return jax.tree.unflatten(tree, lax.optimization_barrier(flat))


def halves(array):
    half = array.shape[0] // 2
    return array[half:], array[:half]


def tie(*groups):
    flat, tree = jax.tree.flatten(groups)
    return jax.tree.unflatten(tree, lax.optimization_barrier(flat))


def halves(array):
    half = array.shape[0] // 2
    return array[half:], array[:half]


def in_order(table, pair, rows):
    if rows % 8 == 0:
        return pair
    whole = jnp.concatenate([pair[1], pair[0]], axis=0)
    return halves(whole.reshape((-1, rows) + whole.shape[1:])[table].reshape(whole.shape))


def body(dp, fsdp, tokens, lengths, cotangent, mixer_in, w_eta, eta_bias, w_out, inner_w, inner_b, ttt_gain, ttt_shift,
         norm_one, post_gain, post_shift, w_gate_up, w_down, norm_two):
    links = Links(dp, fsdp)
    devices = dp * fsdp
    micro, slots, width = tokens.shape
    rows = micro * slots
    heads = eta_bias.shape[0]
    head = width // heads
    hidden = w_gate_up.shape[1] // 2
    device_rows = width // devices
    table, shared = links.table("split"), links.table("shared")
    zeros = lambda columns: jnp.zeros((device_rows, columns), low)

    vectors = jnp.stack([inner_b, ttt_gain, ttt_shift, norm_one, post_gain, post_shift, norm_two])
    vectors = dot_tn(vectors, jnp.eye(7, PAIR, VECTORS, dtype=low)).astype(low)
    small = jnp.concatenate([inner_w, w_eta, zeros(PAIR - ETA - heads)], axis=1) + vectors
    cut = 21 * PAIR
    pieces = [mixer_in[:, :cut], jnp.concatenate([mixer_in[:, cut:], w_out, small], axis=1)]
    rest = [w_gate_up, w_down]
    kinds = ["split", "shared"]
    aligned = device_rows % 8 == 0
    if aligned:
        mixer_phases = links.gather_blocks(pieces, kinds, [True, True], [False, True])
    else:
        mixer_phases = links.gather(pieces, kinds)
    places = lax.broadcasted_iota(jnp.int32, (micro, slots), 1)
    live = places < lengths
    upstream = jnp.where(live[..., None], cotangent, jnp.zeros_like(cotangent)).reshape(rows, width)
    held = next(mixer_phases)
    for _ in range(links.phases - 2):
        held = mixer_phases.send(held)
    held, rest, upstream = tie(held, rest, upstream)
    rest_phases = links.gather_blocks(rest, kinds, [True, False], [False, False]) if aligned else links.gather(rest, kinds)
    held, rest = mixer_phases.send(held), next(rest_phases)
    held, rest = tie(held, rest)
    held, rest = mixer_phases.send(held), rest_phases.send(rest)
    held, rest = tie(held, rest)
    held = mixer_phases.send(held)
    as_blocks = lambda arrays: [([array[None]], jnp.zeros((1,), jnp.int32)) for array in arrays]
    early, late = held if aligned else as_blocks(held)

    inputs = tokens.reshape(rows, width)
    bias_row = jnp.pad(eta_bias.astype(full), (ETA, PAIR - ETA - heads)).reshape(1, PAIR)
    early, late, rest = tie(early, late, rest)
    rest = rest_phases.send(rest)
    whole, projected, normed, rate_lanes, rest_lanes, start_w, start_b, gain_lanes, shift_lanes, vec_rows = project(
        lengths.reshape(micro), inputs, early, late, bias_row
    )
    projected = projected.reshape(micro, slots, -1)
    rate_lanes, rest = tie(rate_lanes, rest)
    rest = rest_phases.send(rest)
    inner, saved = ttt_forward(projected, rate_lanes, [start_w, start_b], gain_lanes, shift_lanes)
    inner = inner.reshape(rows, width)
    inner, rest = tie(inner, rest)
    rest = drain(rest_phases, rest)
    if not aligned:
        rest = as_blocks(rest)
    gate, mixed, first, second = post(inner, normed, inputs, whole, vec_rows)
    block_out, dsecond, large_sent, large_kept, *natural = ffn(table, shared, second, first, upstream, *rest, devices, dp)
    down_rows = hidden // devices
    unit = min(8, device_rows // 3)
    if not aligned:
        natural = natural[0].reshape(devices, -1, unit, 3, width // 3).transpose(0, 3, 2, 1, 4).reshape(width, hidden)
        pairs = in_order(table, (large_sent, large_kept), device_rows), in_order(shared, halves(natural), device_rows)
        large_sent, large_kept = (jnp.concatenate(pair, axis=1) for pair in zip(*pairs))
    large = links.exchange_cores((large_sent, large_kept))
    dfirst, dgate, dinner, dfirst_low, sums = post_back(dsecond, first, upstream, inner, gate, whole, vec_rows)
    middle = middle_grads(table, mixed, dfirst_low, normed, dgate, devices)
    middle = links.exchange_cores(in_order(table, tuple(middle), device_rows))
    dinner, large, middle = tie(dinner, large, middle)
    groups = fold([[(*large, 0, 2 * hidden), (*middle, 0, 2 * width)], [(*large, 2 * hidden, hidden)]], dp)
    dinner, groups = tie(dinner, groups)
    groups = links.step(groups, 0)
    dinner = dinner.reshape(micro, slots, width)
    state = [jnp.zeros((HEAD, 1536), full)] + [jnp.zeros((HEAD, 384), full)] * 5
    dqkv, rate_late, state = ttt_backward(projected, dinner, rate_lanes, saved, state, gain_lanes, 8, slots // MINI, None)
    dqkv, state, groups = tie(dqkv, state, groups)
    groups = refold(groups, dp)
    dqkv, state, groups = tie(dqkv, state, groups)
    groups = links.step(groups, 1)
    dqkv, rate_early, state = ttt_backward(projected, dinner, rate_lanes, saved, state, gain_lanes, 0, 8, dqkv)
    dqkv = dqkv.reshape(rows, 3 * width)
    rate_back = jnp.concatenate([rate_early, rate_late], axis=0)
    early = weight_grads(table, normed, dqkv, devices)
    dqkv, early, groups = tie(dqkv, list(early), groups)
    groups = refold(groups, dp)
    dqkv, early, groups = tie(dqkv, early, groups)
    for phase in range(2, links.near):
        groups = refold(groups, dp) if phase > 2 else groups
        groups = links.step(groups, phase)
    early = links.exchange_cores(in_order(table, tuple(early), device_rows))
    *late, dlog = last_grads(shared, normed, dqkv, sums, state, rate_back, rest_lanes, devices)
    late, dlog, early, groups = tie(list(late), dlog, early, groups)
    late = links.exchange_cores(in_order(shared, tuple(late), device_rows))
    groups = refold(groups, dp)
    late, groups = tie(late, groups)
    groups = links.step(groups, links.near)
    last = fold([[(*early, 0, 2 * width)], [(*late, 0, width + PAIR)]], 1)
    dlog, last = tie(dlog, last)
    last = links.step(last, 0)
    grad_tokens = None
    for half in range(2):
        grad_tokens = finish(inputs, dfirst, dqkv, dgate, dlog, whole, vec_rows, half, grad_tokens)
        grad_tokens, last = tie(grad_tokens, last)
        last = links.step(refold(last, 1), 1 + half)
    for phase in range(3, links.near + 1):
        last = links.step(refold(last, 1), phase)
    large, down = (kept + got.astype(full) for kept, got in groups)
    early, late = (kept + got.astype(full) for kept, got in last)
    part = hidden // dp
    large = large.reshape(device_rows, dp, -1)
    both = large[:, :, : 2 * part].reshape(device_rows, dp, 2, part).transpose(0, 2, 1, 3).reshape(device_rows, 2 * hidden)
    middle = large[:, :, 2 * part :].reshape(device_rows, 2 * width)
    out_small = late[:, width:]
    out_out, out_gate_in = middle[:, :width], middle[:, width:]
    out_mixer = jnp.concatenate([early, late[:, :width], out_gate_in], axis=1)
    out_eta = out_small[:, ETA : ETA + heads]
    out_norm_one = jnp.sum(mixer_in.astype(full) * out_mixer, axis=1) + jnp.sum(w_eta.astype(full) * out_eta, axis=1)
    out_norm_one = out_norm_one / norm_one.astype(full)
    out_inner_b, out_gain, out_shift, _, out_post_gain, out_post_shift, out_norm_two = (
        out_small[:, VECTORS + place] for place in range(7)
    )
    return (
        block_out.reshape(tokens.shape),
        grad_tokens.reshape(tokens.shape),
        out_mixer,
        out_eta,
        out_small[0, BIAS : BIAS + heads],
        out_out,
        out_small[:, :head],
        out_inner_b,
        out_gain,
        out_shift,
        out_norm_one,
        out_post_gain,
        out_post_shift,
        both,
        down.reshape(3, unit, -1, width // 3).transpose(2, 1, 0, 3).reshape(down_rows, width),
        out_norm_two,
    )


def drain(phases, arrays):
    try:
        while True:
            arrays = phases.send(arrays)
    except StopIteration:
        return arrays


def solution(mesh):
    split = ("dp", "fsdp")
    row, vector, token = P(split, None), P(split), P(None, split, None)
    dp, fsdp = mesh.shape["dp"], mesh.shape["fsdp"]
    return jax.shard_map(
        lambda *arrays: body(dp, fsdp, *arrays),
        mesh=mesh,
        in_specs=(token, P(None, split), token, row, row, P(), row, row) + (vector,) * 6 + (row, row, vector),
        out_specs=(token, token, row, row, P(), row, row) + (vector,) * 6 + (row, row, vector),
        check_vma=False,
    )
```

```python
import jax
import jax.numpy as jnp
from jax import lax
from jax.experimental import pallas as pl
from jax.experimental.pallas import tpu as pltpu
from jax.sharding import PartitionSpec as P
import numpy as np

MINI = 16
HEAD = 64
PAIR = 2 * HEAD
epsilon = 1e-06
low = jnp.bfloat16
full = jnp.float32


def dot_nn(former, latter):
    return lax.dot_general(former, latter, (((1,), (0,)), ((), ())), preferred_element_type=full)


def dot_nt(former, latter):
    return lax.dot_general(former, latter, (((1,), (1,)), ((), ())), preferred_element_type=full)


def tile_of(rows, at):
    return rows[:, PAIR * at : PAIR * (at + 1)]


def key_row(group, side, tile):
    return HEAD * group + 32 * side + MINI * tile


def query_row(group, side, tile):
    return key_row(1 - group, side, tile)


def expand(rows, sides):
    zero = jnp.zeros((MINI, PAIR), rows.dtype)
    blocks = []
    for side in range(2):
        for at in range(2):
            kept = tile_of(rows, at) * sides[side]
            blocks.append(jnp.concatenate([kept if other == at else zero for other in range(2)], axis=1))
    return jnp.concatenate(blocks, axis=0)


def expand_both(queries, keys, sides):
    width = 2 * PAIR
    blocks = [(expand(keys[:, width * group : width * (group + 1)], sides), expand(queries[:, width * group : width * (group + 1)], sides))
              for group in range(2)]
    return blocks, (jnp.concatenate(blocks[0], axis=0), jnp.concatenate(blocks[1][::-1], axis=0))


def to_feature(rows, first_side, groups):
    tiles = [tile_of(rows, 2 * group + at) for group in groups for _ in range(2) for at in range(2)]
    stacked = jnp.concatenate(tiles, axis=0).T
    return jnp.where(first_side, stacked[:HEAD], stacked[HEAD:])


def to_rows(columns, left, place):
    turned = jnp.concatenate([columns, columns], axis=0).T
    pick = lambda group, side, at: turned[place(group, side, at) : place(group, side, at) + MINI]
    return jnp.concatenate([jnp.where(left, pick(group, 0, at), pick(group, 1, at)) for group in range(2) for at in range(2)], axis=1)


def exchange(values):
    half = [values[:, HEAD * at : HEAD * (at + 1)] for at in range(values.shape[1] // HEAD)]
    return jnp.concatenate([half[at ^ 1] for at in range(len(half))], axis=1)


def mean_rows(values):
    return jnp.sum(values, axis=0, keepdims=True) * (1.0 / values.shape[0])


def both_sequences(ref, rows, base, width):
    return jnp.concatenate([ref[0, rows, base : base + width], ref[1, rows, base : base + width]], axis=1)


def store_sequences(ref, rows, base, width, pieces, kind):
    whole = jnp.concatenate(pieces, axis=1)
    ref[0, rows, base : base + width] = whole[:, :width].astype(kind)
    ref[1, rows, base : base + width] = whole[:, width:].astype(kind)


def read_constants(low_ref, full_ref):
    sides = [low_ref[0:MINI], low_ref[MINI : 2 * MINI]]
    same, crossed = low_ref[32:160], low_ref[160:288]
    return sides, same, crossed, full_ref[0:MINI], full_ref[16:144], full_ref[144:272]


def lane_masks(rows=HEAD, width=3 * PAIR):
    lane = lax.broadcasted_iota(jnp.int32, (rows, width), 1)
    return lane % PAIR < HEAD, lane % HEAD < 32


PARTS = range(3)


def thin(part):
    return slice(PAIR * part, PAIR * (part + 1))


def wide(part):
    return slice(4 * PAIR * part, 4 * PAIR * (part + 1))


def lanes(pieces):
    return jnp.concatenate(pieces, axis=1)


def ttt_forward_kernel(steps, q_ref, k_ref, v_ref, rate_ref, w0_ref, b0_ref, gain_ref, shift_ref, low_ref, full_ref,
                       out_ref, w_ref, xh_ref, h_ref, grs_ref, xb_ref, stat_ref, score_ref, w_run, b_run, gain_query, shift_query):
    width = 768

    @pl.when(pl.program_id(0) == 0)
    def _():
        w_run[...] = w0_ref[...]
        b_run[...] = b0_ref[...]
        gain_query[...] = exchange(gain_ref[...])
        shift_query[...] = exchange(shift_ref[...])

    sides, same, crossed, tri, _, _ = read_constants(low_ref, full_ref)
    left, first_side = lane_masks()
    left_one, first_one = left[:, :PAIR], first_side[:, :PAIR]
    tri = lanes([tri] * 3)

    def begin(at):
        rows = slice(at * MINI, (at + 1) * MINI)
        queries = both_sequences(q_ref, rows, 0, width)
        keys = both_sequences(k_ref, rows, 0, width)
        targets = both_sequences(v_ref, rows, 0, width) - keys
        query_low, key_low = queries.astype(low), keys.astype(low)
        expanded = [expand_both(query_low[:, wide(part)], key_low[:, wide(part)], sides) for part in PARTS]
        target = lanes([to_feature(targets[:, wide(part)], first_one, (0, 1)) for part in PARTS])
        return rows, queries, query_low, expanded, target

    def multiply(at, started, weights):
        _, _, query_low, expanded, _ = started
        products = []
        for part in PARTS:
            weight_low = weights[part].astype(low)
            w_ref[at, :, wide(part)] = weight_low
            for group in range(2):
                here = slice(2 * PAIR * group, 2 * PAIR * (group + 1))
                rows = jnp.concatenate([weight_low[:, here], query_low[:, wide(part)][:, here]], axis=0)
                products.append(dot_nt(rows, expanded[part][1][group]))
        return lanes(products[::2]), lanes(products[1::2])

    def finish(at, started, kept):
        rows, queries = started[:2]
        inner_grad, mixing, updated = kept
        inner_grad_low = inner_grad.astype(low)
        moved = []
        for part in PARTS:
            mixing_block = jnp.concatenate([mixing[:, thin(part)]] * 8, axis=0) * crossed
            moved.append(dot_nt(inner_grad_low[:, thin(part)], mixing_block))
        updated = updated - lanes(moved)
        updated = updated - mean_rows(updated)
        updated_inverse = lax.rsqrt(mean_rows(updated * updated) + epsilon)
        updated = updated * updated_inverse
        xb_ref[at] = updated
        stat_ref[at, 3:4] = updated_inverse
        updated = updated * gain_query[...] + shift_query[...]
        result = queries + lanes([to_rows(updated[:, thin(part)], left_one[:MINI], query_row) for part in PARTS])
        out_ref[0, rows, :] = result[:, :width]
        out_ref[1, rows, :] = result[:, width:]

    weights = [w_run[:, wide(part)] for part in PARTS]
    offset = b_run[...]
    started = begin(0)
    pending = None
    for at in range(steps):
        first, second = multiply(at, started, weights)
        if pending is not None:
            finish(*pending)
        gains, shifts = gain_ref[...], shift_ref[...]
        rate = rate_ref[at]
        _, _, _, expanded, target = started
        hidden = jnp.where(left, first[:HEAD], second[:HEAD]) + offset
        scores = jnp.where(left[:MINI], first[HEAD:], second[HEAD:]) + 1.0
        updated = jnp.where(left, second[:HEAD], first[:HEAD]) + exchange(offset)
        centred = hidden - mean_rows(hidden)
        inverse = lax.rsqrt(mean_rows(centred * centred) + epsilon)
        normed = centred * inverse
        held = gains * normed + (shifts - target)
        residual = held * gains
        residual_mean = mean_rows(residual)
        cross = mean_rows(residual * normed)
        inner_grad = (residual - residual_mean - normed * cross) * inverse
        scaled = inner_grad * (rate * (1.0 / MINI))
        scaled_low = scaled.astype(low)
        scaled_other = exchange(scaled).astype(low)
        xh_ref[at] = normed
        h_ref[at] = held
        grs_ref[at] = scaled
        stat_ref[at, 0:1] = inverse
        stat_ref[at, 1:2] = residual_mean
        stat_ref[at, 2:3] = cross
        score_ref[at] = scores
        changed = []
        for part in PARTS:
            blocks = expanded[part][0]
            change = [dot_nn(scaled_low[:, thin(part)][:, :HEAD], blocks[0][0]),
                      dot_nn(scaled_other[:, thin(part)][:, :HEAD], blocks[1][0])]
            changed.append(weights[part] - lanes(change))
        weights = changed
        offset = offset - lanes([dot_nn(scaled_low[:, thin(part)], same) for part in PARTS])
        pending = (at, started, (inner_grad, (tri * rate * scores).astype(low), updated))
        if at + 1 < steps:
            started = begin(at + 1)
    finish(*pending)
    for part in PARTS:
        w_run[:, wide(part)] = weights[part]
    b_run[...] = offset


def ttt_backward_kernel(steps, q_ref, k_ref, dout_ref, rate_ref, w_ref, xh_ref, h_ref, grs_ref, xb_ref, stat_ref, score_ref,
                        gain_ref, low_ref, full_ref, *refs):
    states, refs = refs[:6], refs[6:]
    grad_ref, rdr_ref, dw_ref, db_ref, dgain_ref, dshift_ref, dgain_query_ref, dshift_query_ref, gain_query = refs[-9:]
    width = 768

    @pl.when(pl.program_id(0) == 0)
    def _():
        for state, ref in zip(states, (dw_ref, db_ref, dgain_ref, dshift_ref, dgain_query_ref, dshift_query_ref)):
            ref[...] = state[...]
        gain_query[...] = exchange(gain_ref[...])

    sides, same, crossed, tri, scale, scale_turned = read_constants(low_ref, full_ref)
    left, first_side = lane_masks()
    left_one, first_one = left[:, :PAIR], first_side[:, :PAIR]
    left_rows = left_one[:MINI]
    left_square = lax.broadcasted_iota(jnp.int32, (PAIR, PAIR), 1) < HEAD
    zero = jnp.zeros((MINI, PAIR), full)
    tri = lanes([tri] * 3)

    def begin(at):
        rows = slice(at * MINI, (at + 1) * MINI)
        query_low = both_sequences(q_ref, rows, 0, width).astype(low)
        key_low = both_sequences(k_ref, rows, 0, width).astype(low)
        douts = both_sequences(dout_ref, rows, 0, width)
        expanded = [expand_both(query_low[:, wide(part)], key_low[:, wide(part)], sides) for part in PARTS]
        mixing = (tri * rate_ref[at] * score_ref[at]).astype(low)
        dout = lanes([to_feature(douts[:, wide(part)], first_one, (1, 0)) for part in PARTS])
        updated = xb_ref[at]
        dupdated = dout * gain_query[...]
        dupdated = stat_ref[at, 3:4] * (dupdated - mean_rows(dupdated) - updated * mean_rows(dupdated * updated))
        dgain_query_ref[...] += dout * updated
        dshift_query_ref[...] += dout
        dupdated_low = dupdated.astype(low)
        mixed = []
        for part in PARTS:
            mixing_block = jnp.concatenate([mixing[:, thin(part)]] * 8, axis=0) * crossed
            mixed.append(dot_nn(dupdated_low[:, thin(part)], mixing_block))
        return rows, douts, expanded, dupdated, dupdated_low, lanes(mixed)

    def finish(at, started, kept):
        rows, douts, expanded, dupdated, dupdated_low, _ = started
        dhidden, dtarget, dweights_low, rate_part = kept
        scaled = -grs_ref[at]
        scaled_low = scaled.astype(low)
        scores = score_ref[at]
        none = jnp.zeros((HEAD, PAIR), low)
        turned_low, turned_query, query_rows, dmixes, dmixes_turned = [], [], [], [], []
        for part in PARTS:
            turned_low.append(jnp.concatenate([dhidden[:, thin(part)], scaled[:, thin(part)]], axis=0).T.astype(low))
            turned_query.append(jnp.concatenate([dupdated[:, thin(part)], dtarget[:, thin(part)]], axis=0).T)
            query_rows.append(jnp.where(left_square, turned_query[part], 0.0).astype(low))
        for part in PARTS:
            dmix = dot_nn(query_rows[part][:, :HEAD], scaled_low[:, thin(part)]) * scale
            dmix_turned = dot_nn(turned_low[part], jnp.concatenate([none, dupdated_low[:, thin(part)]], axis=0)) * scale_turned
            dmixes.append(sum(dmix[MINI * row : MINI * (row + 1)] for row in range(8)))
            dmixes_turned.append(sum(dmix_turned[MINI * row : MINI * (row + 1)] for row in range(8)))
        rdr_ref[at] = rate_part + jnp.sum(lanes(dmixes) * scores, axis=0, keepdims=True)
        query_grads, key_grads, value_grads = [], [], []
        for part in PARTS:
            weight_low = w_ref[at, :, wide(part)]
            for group in range(2):
                keep_key, keep_query = (left_rows, ~left_rows) if group == 0 else (~left_rows, left_rows)
                key_side = jnp.where(keep_query, dmixes_turned[part], zero).astype(low)
                query_side = jnp.where(keep_key, dmixes[part], zero).astype(low)
                extra = jnp.concatenate([key_side, key_side, query_side, query_side], axis=0)
                for at_tile in range(2):
                    tile = 2 * group + at_tile
                    place = [key_row(group, side, at_tile) for side in range(2)]
                    place_query = [query_row(group, side, at_tile) for side in range(2)]
                    held_rows = jnp.concatenate(
                        [turned_low[part][row : row + MINI] for row in place]
                        + [query_rows[part][row : row + MINI] for row in place_query],
                        axis=0,
                    )
                    product = dot_nn(
                        jnp.concatenate([held_rows, extra], axis=1),
                        jnp.concatenate(
                            [tile_of(weight_low, tile), tile_of(dweights_low[part], tile), tile_of(expanded[part][1][group], at_tile)],
                            axis=0,
                        ),
                    )
                    dvalue = jnp.where(
                        left_rows,
                        exchange(turned_query[part][place[0] : place[0] + MINI]),
                        turned_query[part][place[1] : place[1] + MINI],
                    )
                    key_grads.append(dvalue + jnp.where(left_rows, product[:MINI], product[MINI : 2 * MINI]))
                    query_grads.append(
                        tile_of(douts[:, wide(part)], tile) + jnp.where(left_rows, product[2 * MINI : 3 * MINI], product[3 * MINI :])
                    )
                    value_grads.append(-dvalue)
        store_sequences(grad_ref, rows, 0, width, query_grads, low)
        store_sequences(grad_ref, rows, width, width, key_grads, low)
        store_sequences(grad_ref, rows, 2 * width, width, value_grads, low)

    dweights = [dw_ref[:, wide(part)] for part in PARTS]
    doffset = db_ref[...]
    started = begin(steps - 1)
    pending = None
    for at in reversed(range(steps)):
        _, _, expanded, dupdated, _, mixed = started
        dweights_low = [dweight.astype(low) for dweight in dweights]
        key_dw = []
        for part in PARTS:
            blocks = expanded[part][0]
            key_dw.append(dot_nt(dweights_low[part][:, : 2 * PAIR], blocks[0][0]))
            key_dw.append(dot_nt(dweights_low[part][:, 2 * PAIR :], blocks[1][0]))
        key_dw = lanes(key_dw) + doffset
        if pending is not None:
            finish(*pending)
        upcoming = begin(at - 1) if at > 0 else None
        gains = gain_ref[...]
        rate = rate_ref[at]
        normed, held, scaled = xh_ref[at], h_ref[at], grs_ref[at]
        inverse, residual_mean, cross = (stat_ref[at, row : row + 1] for row in range(3))
        grad_in = -mixed - (rate * (1.0 / MINI)) * key_dw
        rate_part = -jnp.sum(scaled * key_dw, axis=0, keepdims=True)
        residual = held * gains
        in_mean = mean_rows(grad_in)
        in_cross = mean_rows(grad_in * normed)
        in_held = inverse * (mean_rows(grad_in * residual) - residual_mean * in_mean - cross * in_cross)
        dresidual = inverse * (grad_in - in_mean - normed * in_cross)
        dtarget = dresidual * gains
        dnormed = dtarget * gains - inverse * (grad_in * cross + in_cross * residual)
        dhidden = inverse * (dnormed - mean_rows(dnormed) - normed * (mean_rows(dnormed * normed) + in_held))
        dgain_ref[...] += dresidual * (held + gains * normed)
        dshift_ref[...] += dtarget
        to_first = jnp.where(left, dhidden, dupdated).astype(low)
        to_second = jnp.where(left, dupdated, dhidden).astype(low)
        changed = []
        for part in PARTS:
            pairs = expanded[part][1]
            change = [dot_nn(to_first[:, thin(part)], pairs[0]), dot_nn(to_second[:, thin(part)], pairs[1])]
            changed.append(dweights[part] + lanes(change))
        total_low = (exchange(dupdated) + dhidden).astype(low)
        doffset = doffset + lanes([dot_nn(total_low[:, thin(part)], same) for part in PARTS])
        dweights = changed
        pending = (at, started, (dhidden, dtarget, dweights_low, rate_part))
        started = upcoming
    finish(*pending)
    for part in PARTS:
        dw_ref[:, wide(part)] = dweights[part]
    db_ref[...] = doffset


def ttt_constants():
    lane = np.arange(PAIR)
    row = np.arange(MINI)
    sides = np.concatenate([np.tile(lane < HEAD, (MINI, 1)), np.tile(lane >= HEAD, (MINI, 1))])
    token = lane % MINI
    tri = np.where(token[None] <= row[:, None], 1.0 / (row[:, None] + 1.0), 0.0)
    same = lane[:, None] // MINI == lane[None] // MINI
    crossed = (lane[:, None] + HEAD) % PAIR // MINI == lane[None] // MINI
    scale = np.where(crossed & (token[None] <= token[:, None]), MINI / (token[:, None] + 1.0), 0.0)
    return (
        jnp.asarray(np.concatenate([sides, same, crossed]).astype(np.float32), low),
        jnp.asarray(np.concatenate([tri, scale, scale.T]), full),
    )


def ttt_forward(projected, rates, state, gains, shifts, steps=4):
    count = projected.shape[1] // MINI
    first, begin, end = 0, 0, count
    queries, keys, values = projected, projected, projected
    constants = ttt_constants()
    whole = lambda *shape: pl.BlockSpec(shape, lambda at: (0,) * len(shape))
    column = lambda place: pl.BlockSpec((2, steps * MINI, 768), lambda at, place=place: (0, first + at, place))
    part = column(0)
    saved = lambda *tail: pl.BlockSpec((steps,) + tail, lambda at: (at, 0, 0))
    made = lambda kind, *tail: jax.ShapeDtypeStruct((end - begin,) + tail, kind)
    inputs = [queries, keys, values, rates, *state, gains, shifts, *constants]
    out, *rest = pl.pallas_call(
        lambda *refs: ttt_forward_kernel(steps, *refs),
        grid=((end - begin) // steps,),
        in_specs=[column(0), column(1), column(2), pl.BlockSpec((steps, 1, 384), lambda at: (first + at, 0, 0)), whole(64, 1536), whole(64, 384),
                  whole(64, 384), whole(64, 384), whole(288, 128), whole(272, 128)],
        out_specs=[part, saved(64, 1536), saved(64, 384), saved(64, 384), saved(64, 384), saved(64, 384), saved(8, 384),
                   saved(16, 384)],
        out_shape=[jax.ShapeDtypeStruct((2, count * MINI, 768), full), made(low, 64, 1536), made(full, 64, 384), made(full, 64, 384),
                   made(full, 64, 384), made(full, 64, 384), made(full, 8, 384), made(full, 16, 384)],
        scratch_shapes=[pltpu.VMEM((64, 1536), full)] + [pltpu.VMEM((64, 384), full)] * 3,
        compiler_params=pltpu.CompilerParams(vmem_limit_bytes=60 * 1024 * 1024),
        cost_estimate=pl.CostEstimate(flops=(end - begin) * 1_400_000_000, bytes_accessed=(end - begin) * 1_500_000, transcendentals=0),
        name="ttt_forward",
    )(*inputs)
    return out, rest


def ttt_backward(projected, dout, rates, saved_arrays, state, gains, begin, end, before, steps=4):
    count = projected.shape[1] // MINI
    first, blocks = begin // steps, (end - begin) // steps
    queries, keys = projected, projected
    constants = ttt_constants()
    whole = lambda *shape: pl.BlockSpec(shape, lambda at: (0,) * len(shape))
    part = lambda width, place=0: pl.BlockSpec((2, steps * MINI, width), lambda at: (0, first + blocks - 1 - at, place))
    saved = lambda *tail: pl.BlockSpec((steps,) + tail, lambda at: (first + blocks - 1 - at, 0, 0))
    made = lambda *tail: pl.BlockSpec((steps,) + tail, lambda at: (blocks - 1 - at, 0, 0))
    extra = [] if before is None else [before]
    inputs = [queries, keys, dout, rates, *saved_arrays, gains, *constants, *state]
    states = [whole(64, 1536)] + [whole(64, 384)] * 5
    grad, rate_back, *state = pl.pallas_call(
        lambda *refs: ttt_backward_kernel(steps, *refs),
        grid=(blocks,),
        in_specs=[part(768), part(768, 1), part(768), saved(1, 384),
                  saved(64, 1536), saved(64, 384), saved(64, 384), saved(64, 384), saved(64, 384), saved(8, 384), saved(16, 384),
                  whole(64, 384), whole(288, 128), whole(272, 128)]
        + states + [pl.BlockSpec(memory_space=pl.ANY)] * len(extra),
        out_specs=[part(2304), made(1, 384)] + states,
        out_shape=[jax.ShapeDtypeStruct((2, count * MINI, 2304), low), jax.ShapeDtypeStruct((end - begin, 1, 384), full)]
        + [jax.ShapeDtypeStruct((64, 1536), full)] + [jax.ShapeDtypeStruct((64, 384), full)] * 5,
        scratch_shapes=[pltpu.VMEM((64, 384), full)],
        input_output_aliases={len(inputs): 0} if extra else {},
        compiler_params=pltpu.CompilerParams(vmem_limit_bytes=60 * 1024 * 1024),
        cost_estimate=pl.CostEstimate(flops=(end - begin) * 2_000_000_000, bytes_accessed=(end - begin) * 1_500_000, transcendentals=0),
        name="ttt_backward",
    )(*inputs, *extra)
    return grad, rate_back, state


def silu_parts(gate):
    sigma = jax.nn.sigmoid(gate)
    return gate * sigma, sigma * (1.0 + gate * (1.0 - sigma))


def gelu_parts(values):
    slope = 0.7978845608028654
    turn = jnp.tanh(slope * (values + 0.044715 * values * values * values))
    half = 0.5 * (1.0 + turn)
    return values * half, half + 0.5 * values * (1.0 - turn * turn) * slope * (1.0 + 3 * 0.044715 * values * values)


def row_mean(values):
    return jnp.mean(values, axis=-1, keepdims=True)


def dot_tn(former, latter):
    return lax.dot_general(former, latter, (((0,), (0,)), ((), ())), preferred_element_type=full)


def exact_dot(former, latter):
    total = None
    for _ in range(3):
        part = former.astype(low)
        former = former - part.astype(full)
        term = dot_nn(part, latter)
        total = term if total is None else total + term
    return total


def constant_spec(*shape, at=0, buffers=None):
    index = lambda *steps: (0,) * (len(shape) - 1) + (at,)
    if buffers is None:
        return pl.BlockSpec(shape, index)
    return pl.BlockSpec(shape, index, pipeline_mode=pl.Buffered(buffers))


def call(kernel, name, grid, prefetch, in_specs, out_specs, out_shape, scratch, cost, arrays):
    return pl.pallas_call(
        kernel,
        grid_spec=pltpu.PrefetchScalarGridSpec(
            num_scalar_prefetch=prefetch, grid=grid, in_specs=in_specs, out_specs=out_specs, scratch_shapes=scratch
        ),
        out_shape=out_shape,
        compiler_params=pltpu.CompilerParams(vmem_limit_bytes=60 * 1024 * 1024),
        cost_estimate=pl.CostEstimate(flops=cost, bytes_accessed=cost // 500, transcendentals=0),
        name=name,
    )(*arrays)


ETA = 64
VECTORS = 80
BIAS = 96


def lane_table():
    lane = np.arange(384)
    part, group, side, tile, token = lane // 128, lane // 64 % 2, lane // 32 % 2, lane // 16 % 2, lane % 16
    pair = 4 * part + 2 * group + tile
    return token, pair // 6, 2 * (pair % 6) + side


def lane_constants():
    token, sequence, head = lane_table()
    table = np.zeros((32, 384), np.float32)
    table[:MINI] = token[None] == np.arange(MINI)[:, None]
    table[16], table[17] = sequence, token
    chosen = np.zeros((PAIR, 384), np.float32)
    chosen[ETA + head, np.arange(384)] = 1
    return jnp.asarray(table), jnp.asarray(chosen, low)


def block_copies(from_refs, table, to, columns, semaphores, first):
    started = []
    for place, ref in enumerate(from_refs):
        for item in range(ref.shape[0]):
            begin = pl.multiple_of(table[place * ref.shape[0] + item] * ref.shape[1], 16)
            target = to.at[pl.ds(begin, ref.shape[1]), columns]
            started.append(pltpu.make_async_copy(ref.at[item], target, semaphores.at[first + len(started)]))
    return started


def project_kernel(counts, length_ref, early_table_ref, late_table_ref, tokens_ref, bias_ref, table_ref, chosen_ref, *refs):
    early_refs, late_refs, refs = refs[: counts[0]], refs[counts[0] : sum(counts)], refs[sum(counts) :]
    whole_ref, proj_ref, normed_ref, rate_ref, rest_ref, wt_ref, b_ref, gain_ref, shift_ref, vec_ref, semaphores = refs
    at = pl.program_id(0)
    split = 512 // tokens_ref.shape[0]
    wide = proj_ref.shape[1]
    begin_small = whole_ref.shape[1] - PAIR
    cut = early_refs[0].shape[2]

    def copies():
        started = block_copies(early_refs, early_table_ref, whole_ref, slice(0, cut), semaphores, 0)
        return started + block_copies(late_refs, late_table_ref, whole_ref, slice(cut, whole_ref.shape[1]), semaphores, len(started))

    @pl.when(at == 0)
    def _():
        for copy in copies():
            copy.start()
        for copy in copies():
            copy.wait()
        small = whole_ref[:, begin_small:].astype(full)
        turned = small.T
        wt_ref[:, :768] = turned[:HEAD]
        wt_ref[:, 768:] = turned[:HEAD]
        vec_ref[...] = turned[VECTORS : VECTORS + 8]
        for place, ref in enumerate((b_ref, gain_ref, shift_ref)):
            total = jnp.zeros((HEAD, 384), full)
            for head in range(12):
                column = small[HEAD * head : HEAD * (head + 1), VECTORS + place : VECTORS + place + 1]
                total = total + column * chosen_ref[ETA + head : ETA + head + 1].astype(full)
            ref[...] = total
        rate_ref[...] = jnp.zeros_like(rate_ref)
        rest_ref[...] = jnp.zeros_like(rest_ref)

    values = tokens_ref[...].astype(full)
    normed = (values * lax.rsqrt(row_mean(values * values) + epsilon) * vec_ref[3:4]).astype(low)
    normed_ref[...] = normed
    proj_ref[...] = dot_nn(normed, whole_ref[:, :wide])
    last = dot_nn(normed, whole_ref[:, begin_small:])
    spread = exact_dot(last + bias_ref[...], chosen_ref[...])
    blocks = spread.shape[0] // MINI
    spread = jnp.sum(spread.reshape(blocks, MINI, 384) * table_ref[:MINI][None], axis=1)
    sequence, token = table_ref[16:17], table_ref[17:18]
    mine = sequence == (at // split).astype(full)
    sigma = jax.nn.sigmoid(spread)
    begin = (at % split) * blocks
    block = lax.broadcasted_iota(jnp.int32, spread.shape, 0) + begin
    live = (block * MINI).astype(full) + token < length_ref[at // split].astype(full)
    here = pl.ds(begin, blocks)
    rate_ref[here, 0, :] += jnp.where(live & mine, sigma * (1.0 / HEAD), 0.0)
    rest_ref[here, :] += jnp.where(mine, 1.0 - sigma, 0.0)


def project(lengths, tokens, early, late, bias_row):
    rows, width = tokens.shape
    table, chosen = lane_constants()
    tile = rows // 2
    columns = early[0][0].shape[2] + late[0][0].shape[2]
    counts = len(early[0]), len(late[0])
    row = lambda n: pl.BlockSpec((tile, n), lambda at, *_: (at, 0))
    shape = jax.ShapeDtypeStruct
    return call(
        lambda *refs: project_kernel(counts, *refs), "project", (2,), 3,
        [row(width), constant_spec(1, PAIR), constant_spec(32, 384), constant_spec(PAIR, 384)]
        + [pl.BlockSpec(memory_space=pl.ANY)] * sum(counts),
        [constant_spec(width, columns, buffers=1), row(3 * width), row(width), constant_spec(32, 1, 384), constant_spec(32, 384),
         constant_spec(64, 1536)] + [constant_spec(64, 384)] * 3 + [constant_spec(8, width)],
        [shape((width, columns), low), shape((rows, 3 * width), full), shape((rows, width), low), shape((32, 1, 384), full),
         shape((32, 384), full), shape((64, 1536), full)] + [shape((64, 384), full)] * 3 + [shape((8, width), full)],
        [pltpu.SemaphoreType.DMA((early[1].shape[0] + late[1].shape[0],))], 5_000_000_000,
        (lengths, early[1], late[1], tokens, bias_row, table, chosen, *early[0], *late[0]),
    )


def post_kernel(inner_ref, normed_ref, tokens_ref, w_gate_ref, w_out_ref, vec_ref, gate_ref, mixed_ref, first_ref, second_ref):
    gate = dot_nn(normed_ref[...], w_gate_ref[...])
    gate_ref[...] = gate
    inner = inner_ref[...]
    centred = inner - row_mean(inner)
    standard = centred * lax.rsqrt(row_mean(centred * centred) + epsilon)
    mixed = ((standard * vec_ref[4:5] + vec_ref[5:6]) * gelu_parts(gate)[0]).astype(low)
    mixed_ref[...] = mixed
    first = tokens_ref[...].astype(full) + dot_nn(mixed, w_out_ref[...])
    first_ref[...] = first
    second_ref[...] = (first * lax.rsqrt(row_mean(first * first) + epsilon) * vec_ref[6:7]).astype(low)


def post(inner, normed, tokens, whole, vectors):
    rows, width = tokens.shape
    tile = rows // 4
    row = pl.BlockSpec((tile, width), lambda at: (at, 0))
    shape = jax.ShapeDtypeStruct
    return call(
        post_kernel, "post", (4,), 0,
        [row, row, row, constant_spec(width, width, at=3, buffers=1), constant_spec(width, width, at=4, buffers=1), constant_spec(8, width)],
        [row] * 4, [shape((rows, width), kind) for kind in (full, low, full, low)], [], 4_000_000_000,
        (inner, normed, tokens, whole, whole, vectors),
    )


def store_blocks(table_ref, sent_ref, kept_ref, held_ref, block):
    half = kept_ref.shape[0]
    if block % 8:
        kept_ref[...] = held_ref[:half].astype(kept_ref.dtype)
        sent_ref[...] = held_ref[half:].astype(sent_ref.dtype)
        return
    for pair in range(held_ref.shape[0] // (2 * block)):
        rows = [held_ref[pl.ds(pl.multiple_of(table_ref[2 * pair + side] * block, 8), block), :] for side in range(2)]
        begin = 2 * block * pair
        ref, begin = (kept_ref, begin) if begin < half else (sent_ref, begin - half)
        ref[begin : begin + 2 * block, :] = jnp.concatenate(rows, axis=0).astype(ref.dtype)


def ffn_kernel(block, down_block, steps, counts, table_ref, shared_ref, both_table_ref, down_table_ref, second_ref, first_ref, up_ref, *refs):
    both_refs, refs = refs[: counts[0]], refs[counts[0] :]
    down_refs, refs = refs[: counts[1]], refs[counts[1] :]
    aligned = block % 8 == 0
    out_ref, dsecond_ref, sent_ref, kept_ref, *refs = refs
    natural_ref, refs = (None, refs) if aligned else (refs[0], refs[1:])
    turned, total, act, both_low, held, w_both, w_down_all, held_down, semaphores = refs
    at = pl.program_id(0)
    size = act.shape[1]
    hidden = w_down_all.shape[0]

    def copies():
        started = block_copies(both_refs, both_table_ref, w_both, slice(None), semaphores, 0)
        return started + block_copies(down_refs, down_table_ref, w_down_all, slice(None), semaphores, len(started))

    @pl.when(at == 0)
    def _():
        for copy in copies():
            copy.start()
        turned[...] = second_ref[...].T
        total[...] = first_ref[...]
        dsecond_ref[...] = jnp.zeros_like(dsecond_ref)
        for copy in copies():
            copy.wait()

    @pl.when(at < steps)
    def _():
        columns = pl.ds(pl.multiple_of(at * size, PAIR), size)
        w_gate, w_up = w_both[:, columns], w_both[:, pl.ds(pl.multiple_of(hidden + at * size, PAIR), size)]
        w_down = w_down_all[columns, :]
        second, upstream = second_ref[...], up_ref[...]
        cuts = [slice(begin, begin + size // 2) for begin in range(0, size, size // 2)]
        made = [(dot_nn(second, w_gate[:, cut]), dot_nn(second, w_up[:, cut]), dot_nt(upstream, w_down[cut])) for cut in cuts]
        for cut, (gate, up, dact) in zip(cuts, made):
            value, slope = silu_parts(gate)
            act[:, cut] = (value * up).astype(low)
            both_low[:, cut] = (dact * up * slope).astype(low)
            both_low[:, size + cut.start : size + cut.stop] = (dact * value).astype(low)
        total[...] += dot_nn(act[...], w_down)
        dsecond_ref[...] += dot_nt(both_low[:, :size], w_gate) + dot_nt(both_low[:, size:], w_up)
        ddown = dot_tn(act[...], upstream)
        held[...] = dot_nn(turned[...], both_low[...])
        if aligned:
            count = size // down_block
            third = ddown.shape[1] // 3
            for place in range(count):
                mine = ddown[down_block * place : down_block * (place + 1)]
                pieces = [jnp.concatenate([mine[8 * row : 8 * row + 8, third * part : third * (part + 1)] for row in range(down_block // 8)],
                                          axis=1) for part in range(3)]
                held_down[pl.ds(pl.multiple_of((at * count + place) * block, 8), block), :] = jnp.concatenate(pieces, axis=0)
        else:
            natural_ref[pl.ds(pl.multiple_of(at * size, 16), size), :] = ddown.astype(low)
        store_blocks(table_ref, sent_ref, kept_ref, held, block)

    @pl.when(at == steps - 1)
    def _():
        out_ref[...] = total[...].astype(low)

    if aligned:
        for extra in range(held_down.shape[1] // (2 * size)):

            @pl.when(at == steps + extra)
            def _():
                store_blocks(shared_ref, sent_ref, kept_ref, held_down.at[:, 2 * size * extra : 2 * size * (extra + 1)], block)


def ffn(table, shared, second, first, upstream, both, down, devices, steps):
    rows, width = second.shape
    hidden = down[0][0].shape[1] * down[1].shape[0]
    size = hidden // steps
    aligned = width // devices % 8 == 0
    columns = 3 * hidden if aligned else 2 * hidden
    shape = jax.ShapeDtypeStruct
    counts = len(both[0]), len(down[0])
    copies = both[1].shape[0] + down[1].shape[0]
    natural = [] if aligned else [(hidden, width)]
    return call(
        lambda *refs: ffn_kernel(width // devices, hidden // devices, steps, counts, *refs), "ffn", (columns // (2 * size),), 4,
        [constant_spec(rows, width, buffers=1)] * 3 + [pl.BlockSpec(memory_space=pl.ANY)] * sum(counts),
        [constant_spec(rows, width, buffers=1), constant_spec(rows, width, buffers=1),
         *[pl.BlockSpec((width // 2, 2 * size), lambda at, *_: (0, at))] * 2, *[constant_spec(*item, buffers=1) for item in natural]],
        [shape((rows, width), low), shape((rows, width), full), *[shape((width // 2, columns), low)] * 2,
         *[shape(item, low) for item in natural]],
        [pltpu.VMEM((width, rows), low), pltpu.VMEM((rows, width), full), pltpu.VMEM((rows, size), low),
         pltpu.VMEM((rows, 2 * size), low), pltpu.VMEM((width, 2 * size), full), pltpu.VMEM((width, 2 * hidden), low),
         pltpu.VMEM((hidden, width), low), pltpu.VMEM((width, hidden) if aligned else (8, PAIR), full),
         pltpu.SemaphoreType.DMA((copies,))],
        29_000_000_000, (table, shared, both[1], down[1], second, first, upstream, *both[0], *down[0]),
    )


def fold_kernel(counts, paired, *refs):
    pairs, outs = refs[: 2 * sum(counts)], refs[2 * sum(counts) :]
    for group, count in enumerate(counts):
        sent_ref, kept_ref = outs[2 * group : 2 * group + 2]
        half = kept_ref.shape[0]
        begin = 0
        for _ in range(count):
            (kept, got), pairs = pairs[:2], pairs[2:]
            plain = kept.shape[1] - (2 * paired if group + 1 == len(counts) else 0)
            columns = slice(begin, begin + plain)
            sent_ref[:, columns] = (kept[half:, :plain].astype(full) + got[half:, :plain].astype(full)).astype(low)
            kept_ref[:, columns] = (kept[:half, :plain].astype(full) + got[:half, :plain].astype(full)).astype(kept_ref.dtype)
            if plain < kept.shape[1]:
                total = kept[:, plain:].astype(full) + got[:, plain:].astype(full)
                total = total[:, :paired] + total[:, paired:]
                high = total[half:].astype(low)
                sent_ref[:, plain : plain + paired] = high
                sent_ref[:, plain + paired :] = (total[half:] - high.astype(full)).astype(low)
                kept_ref[:, plain : plain + paired] = total[:half]
                kept_ref[:, plain + paired :] = jnp.zeros_like(total[:half])
            begin += kept.shape[1]


def fold(groups, steps, paired=0, kind=full):
    specs, arrays, outs, shapes = [], [], [], []
    for group in groups:
        rows = group[0][0].shape[0]
        width = 0
        for kept, got, first, columns in group:
            part = columns // steps
            specs += [pl.BlockSpec((rows, part), lambda at, begin=first // part: (0, begin + at))] * 2
            arrays += [kept, got]
            width += part
        outs += [pl.BlockSpec((rows // 2, width), lambda at: (0, at))] * 2
        shapes += [jax.ShapeDtypeStruct((rows // 2, width * steps), out) for out in (low, kind)]
    results = call(
        lambda *refs: fold_kernel([len(group) for group in groups], paired, *refs), "fold", (steps,), 0, specs, outs, shapes, [],
        100_000_000, arrays,
    )
    return [(results[place], results[place + 1]) for place in range(0, len(results), 2)]


def post_back_kernel(dsecond_ref, first_ref, up_ref, inner_ref, gate_ref, w_out_ref, vec_ref,
                     dfirst_ref, dgate_ref, dinner_ref, dfirst_low_ref, sums_ref):
    @pl.when(pl.program_id(0) == 0)
    def _():
        sums_ref[...] = jnp.zeros_like(sums_ref)

    first, dsecond = first_ref[...], dsecond_ref[...]
    scale = lax.rsqrt(row_mean(first * first) + epsilon)
    sums_ref[6:7] += jnp.sum(dsecond * first * scale, axis=0, keepdims=True)
    dsecond = dsecond * vec_ref[6:7]
    dfirst = up_ref[...].astype(full) + scale * dsecond - first * (scale * scale * scale * row_mean(first * dsecond))
    dfirst_ref[...] = dfirst
    dfirst_low = dfirst.astype(low)
    dfirst_low_ref[...] = dfirst_low
    dmixed = dot_nt(dfirst_low, w_out_ref[...])
    inner = inner_ref[...]
    centred = inner - row_mean(inner)
    inverse = lax.rsqrt(row_mean(centred * centred) + epsilon)
    standard = centred * inverse
    value, slope = gelu_parts(gate_ref[...])
    dgate_ref[...] = (dmixed * (standard * vec_ref[4:5] + vec_ref[5:6]) * slope).astype(low)
    dpost = dmixed * value
    sums_ref[4:5] += jnp.sum(dpost * standard, axis=0, keepdims=True)
    sums_ref[5:6] += jnp.sum(dpost, axis=0, keepdims=True)
    dpost = dpost * vec_ref[4:5]
    dinner_ref[...] = inverse * (dpost - row_mean(dpost) - standard * row_mean(dpost * standard))


def post_back(dsecond, first, upstream, inner, gate, whole, vectors):
    rows, width = first.shape
    tile = rows // 4
    row = pl.BlockSpec((tile, width), lambda at: (at, 0))
    shape = jax.ShapeDtypeStruct
    return call(
        post_back_kernel, "post_back", (4,), 0,
        [row] * 5 + [constant_spec(width, width, at=4, buffers=1), constant_spec(8, width)],
        [row, row, row, row, constant_spec(8, width)],
        [shape((rows, width), full), shape((rows, width), low), shape((rows, width), full), shape((rows, width), low),
         shape((8, width), full)],
        [], 4_000_000_000, (dsecond, first, upstream, inner, gate, whole, vectors),
    )


def middle_kernel(block, table_ref, mixed_ref, dfirst_ref, normed_ref, dgate_ref, sent_ref, kept_ref, held):
    @pl.when(pl.program_id(0) == 0)
    def _():
        held[...] = dot_tn(mixed_ref[...], dfirst_ref[...])

    @pl.when(pl.program_id(0) == 1)
    def _():
        held[...] = dot_tn(normed_ref[...], dgate_ref[...])

    store_blocks(table_ref, sent_ref, kept_ref, held, block)


def middle_grads(table, mixed, dfirst, normed, dgate, devices):
    rows, width = normed.shape
    whole = constant_spec(rows, width, buffers=1)
    return call(
        lambda *refs: middle_kernel(width // devices, *refs), "middle_grads", (2,), 1,
        [whole] * 4, [pl.BlockSpec((width // 2, width), lambda at, *_: (0, at))] * 2,
        [jax.ShapeDtypeStruct((width // 2, 2 * width), low)] * 2, [pltpu.VMEM((width, width), full)], 3_000_000_000,
        (table, mixed, dfirst, normed, dgate),
    )


def weight_kernel(block, table_ref, normed_ref, grad_ref, sent_ref, kept_ref, turned, held):
    @pl.when(pl.program_id(0) == 0)
    def _():
        turned[...] = normed_ref[...].T

    held[...] = dot_nn(turned[...], grad_ref[...])
    store_blocks(table_ref, sent_ref, kept_ref, held, block)


def weight_grads(table, normed, grads, devices):
    rows, width = normed.shape
    out = pl.BlockSpec((width // 2, width), lambda at, *_: (0, at))
    return call(
        lambda *refs: weight_kernel(width // devices, *refs), "weight_grads", (2,), 1,
        [constant_spec(rows, width, buffers=1), pl.BlockSpec((rows, width), lambda at, *_: (0, at))],
        [out, out], [jax.ShapeDtypeStruct((width // 2, 2 * width), low)] * 2,
        [pltpu.VMEM((width, rows), low), pltpu.VMEM((width, width), full)], 3_000_000_000, (table, normed, grads),
    )


def last_kernel(block, table_ref, normed_ref, grad_ref, sums_ref, dw_ref, db_ref, dgain_ref, dshift_ref, dgain_query_ref,
                dshift_query_ref, rate_ref, rest_ref, lane_ref, chosen_ref, sent_ref, kept_ref, dlog_ref, held):
    rows, width = normed_ref.shape
    turned = normed_ref[...].T
    held[:, :width] = dot_nn(turned, grad_ref[...])
    slots = rate_ref.shape[0] * MINI
    for sequence in range(rows // slots):
        mine = (lane_ref[16:17] == float(sequence)).astype(full)
        spread = rate_ref[:, 0, :] * rest_ref[...] * mine
        spread = (spread[:, None, :] * lane_ref[:MINI][None]).reshape(slots, 384).astype(low)
        dlog_ref[slots * sequence : slots * (sequence + 1)] = dot_nt(spread, chosen_ref[...]).astype(low)
    eta = dot_nn(turned, dlog_ref[...])
    inner = dw_ref[:, :width] + dw_ref[:, width:]
    fixed = jnp.concatenate(
        [inner, jnp.zeros((VECTORS - HEAD, width), full), sums_ref[...], jnp.zeros((PAIR - VECTORS - 8, width), full)], axis=0
    )
    lane = lax.broadcasted_iota(jnp.int32, (HEAD, PAIR), 1)
    chosen = chosen_ref[...].astype(full)
    bias = jnp.sum(rate_ref[:, 0, :] * rest_ref[...], axis=0, keepdims=True)
    held[:, width : width + PAIR] = eta + fixed.T
    bias = jnp.sum(chosen * bias, axis=1, keepdims=True)
    square = jnp.broadcast_to(bias, (PAIR, PAIR)).T[:1]
    bias_row = pltpu.roll(square, BIAS - ETA, axis=1)
    bias_row = jnp.where((lane[:1] >= BIAS) & (lane[:1] < BIAS + 12), bias_row, 0.0)
    lanes_of = [db_ref[...] * (1.0 / MINI), dgain_ref[...] + exchange(dgain_query_ref[...]), dshift_ref[...] + exchange(dshift_query_ref[...])]
    for head in range(12):
        here = pl.ds(HEAD * head, HEAD)
        mask = chosen[ETA + head : ETA + head + 1]
        total = held[here, width : width + PAIR] + bias_row
        for place, values in enumerate(lanes_of):
            column = jnp.sum(values * mask, axis=1, keepdims=True)
            total = total + jnp.where(lane == VECTORS + place, column, 0.0)
        high = total.astype(low).astype(full)
        held[here, width : width + PAIR] = high
        held[here, width + PAIR :] = total - high
    store_blocks(table_ref, sent_ref, kept_ref, held, block)


def last_grads(table, normed, grads, sums, state, rate_back, rest, devices):
    rows, width = normed.shape
    lane, chosen = lane_constants()
    spec = lambda array: constant_spec(*array.shape, buffers=1)
    others = (sums, *state, rate_back, rest, lane, chosen)
    shape = jax.ShapeDtypeStruct
    out = constant_spec(width // 2, width + 2 * PAIR, buffers=1)
    return call(
        lambda *refs: last_kernel(width // devices, *refs), "last_grads", (1,), 1,
        [spec(normed), constant_spec(rows, width, at=2, buffers=1)] + [spec(array) for array in others],
        [out, out, constant_spec(rows, PAIR, buffers=1)],
        [shape((width // 2, width + 2 * PAIR), low)] * 2 + [shape((rows, PAIR), low)],
        [pltpu.VMEM((width, width + 2 * PAIR), full)], 3_000_000_000, (table, normed, grads, *others),
    )


def finish_kernel(tokens_ref, dfirst_ref, dqkv_ref, dgate_ref, dlog_ref, w_ref, small_ref, w_gate_ref, vec_ref, out_ref):
    dnormed = dot_nt(dqkv_ref[...], w_ref[...]) + dot_nt(dgate_ref[...], w_gate_ref[...]) + dot_nt(dlog_ref[...], small_ref[...])
    values = tokens_ref[...].astype(full)
    scale = lax.rsqrt(row_mean(values * values) + epsilon)
    dnormed = dnormed * vec_ref[3:4]
    back = scale * dnormed - values * (scale * scale * scale * row_mean(values * dnormed))
    out_ref[...] = (dfirst_ref[...] + back).astype(low)


def finish(tokens, dfirst, dqkv, dgate, dlog, whole, vectors, at, before):
    rows, width = tokens.shape
    tile = rows // 2
    row = lambda n: pl.BlockSpec((tile, n), lambda step: (at, 0))
    arrays = [tokens, dfirst, dqkv, dgate, dlog, whole, whole, whole, vectors]
    extra = [] if before is None else [before]
    return pl.pallas_call(
        lambda *refs: finish_kernel(*refs[:9], refs[-1]),
        grid=(1,),
        in_specs=[row(width), row(width), row(3 * width), row(width), row(PAIR), constant_spec(width, 3 * width, buffers=1),
                  constant_spec(width, PAIR, at=5 * width // PAIR, buffers=1), constant_spec(width, width, at=3, buffers=1),
                  constant_spec(8, width)] + [pl.BlockSpec(memory_space=pl.ANY)] * len(extra),
        out_specs=row(width),
        out_shape=jax.ShapeDtypeStruct((rows, width), low),
        input_output_aliases={len(arrays): 0} if extra else {},
        compiler_params=pltpu.CompilerParams(vmem_limit_bytes=60 * 1024 * 1024),
        cost_estimate=pl.CostEstimate(flops=3_000_000_000, bytes_accessed=10_000_000, transcendentals=0),
        name="finish",
    )(*arrays, *extra)


class Links:
    def __init__(self, dp, fsdp):
        self.axes = ("dp", "fsdp")
        self.count = dp * fsdp
        self.core = fsdp
        self.far = fsdp // 2
        bits = [1 << place for place in reversed(range(self.count.bit_length() - 1))]
        self.others = [bit for bit in bits if bit != self.core]
        near = [bit for bit in reversed(self.others) if bit != self.far]
        near = near[:1] + near[:0:-1]
        turned = [near[turn:] + near[:turn] for turn in range(3)]
        self.orders = {"split": [turned[0], turned[2]], "shared": [turned[1]] * 2}
        self.phases = self.near = len(near)
        self.me = lax.axis_index("dp") * fsdp + lax.axis_index("fsdp")
        self.side = (self.me // self.core) % 2

    def swap(self, values, bits):
        pairs = [(place, place ^ bits[(place // self.core) % 2]) for place in range(self.count)]
        return lax.ppermute(values, self.axes, pairs)

    def one(self, bit):
        return (self.me // bit) % 2

    def join(self, held, bits):
        got = self.swap(held, bits)
        mine = jnp.where(self.side == 0, self.one(bits[0]), self.one(bits[1])) == 0
        return jnp.stack([jnp.where(mine, held, got), jnp.where(mine, got, held)])

    def gather(self, pieces, kinds):
        orders = [[[self.far] + order for order in self.orders[kind]] for kind in kinds]
        held = list(pieces)
        for phase in range(len(orders[0][0])):
            held = [self.join(array, [order[phase] for order in pair]) for array, pair in zip(held, orders)]
            changed = yield held
            held = held if changed is None else changed
        above = [bit for bit in self.others if bit > self.core]
        whole = []
        for array, pair in zip(held, orders):
            got = self.swap(array, [self.core] * 2)
            mine = self.side == 0
            cores = [jnp.where(mine, array, got), jnp.where(mine, got, array)]
            placed = []
            for half, order in zip(cores, pair):
                have = order[::-1]
                placed.append(half.transpose([have.index(bit) for bit in self.others] + [len(have), len(have) + 1]))
            whole.append(jnp.stack(placed, axis=len(above)).reshape(-1, array.shape[-1]))
        yield whole

    def gather_blocks(self, pieces, kinds, pairs, whole_last):
        held = list(pieces)
        orders = [self.orders[kind] for kind in kinds]
        count = self.phases

        def ready(array, place):
            rows = pieces[place].shape[0]
            if not pairs[place]:
                return array.reshape((-1, rows) + array.shape[-1:])
            turned = []
            stacked = array.ndim - 2
            for order in orders[place]:
                have = ([self.far] + order)[:stacked][::-1]
                at = have.index(1)
                turned.append(array.transpose([axis for axis in range(stacked) if axis != at] + [at, stacked, stacked + 1]))
            array = jnp.where(self.side == 0, turned[0], turned[1])
            return array.reshape((-1, 2 * rows) + array.shape[-1:])

        for phase in range(count):
            for place, pair in enumerate(orders):
                held[place] = self.join(held[place], [self.far] * 2 if phase == 0 else [order[phase - 1] for order in pair])
                if phase == count - 1 and not whole_last[place]:
                    held[place] = ready(held[place], place)
            changed = yield held
            held = held if changed is None else changed
        buffers = []
        for place, pair in enumerate(orders):
            last = [order[-1] for order in pair]
            if whole_last[place]:
                buffers.append([ready(self.join(held[place], last), place)])
            else:
                buffers.append([held[place], self.swap(held[place], last), self.swap(held[place], [self.core] * 2)])
        changed = yield buffers
        buffers = buffers if changed is None else changed
        buffers = [list(group) + [self.swap(group[0 if whole else 1], [self.core] * 2)] for group, whole in zip(buffers, whole_last)]

        def places(bits, device, unit):
            found = []
            clear = device & ~(sum(bits) + unit - 1)
            for place in range(1 << len(bits)):
                found.append((clear + sum(bit for at, bit in enumerate(bits) if place >> (len(bits) - 1 - at) & 1)) // unit)
            return jnp.stack(found)

        done = []
        for place, pair in enumerate(orders):
            unit = 2 if pairs[place] else 1
            table = []
            for core, last in ((0, 0), (self.core, 0)) if whole_last[place] else ((0, 0), (0, 1), (self.core, 0), (self.core, 1)):
                by_side = []
                for order in pair:
                    have = ([self.far] + order)[::-1] if whole_last[place] else ([self.far] + order[:-1])[::-1]
                    by_side.append(places([bit for bit in have if bit >= unit], self.me ^ core ^ (order[-1] if last else 0), unit))
                own = self.side if core == 0 else 1 - self.side
                table.append(jnp.where(own == 0, by_side[0], by_side[1]))
            done.append((buffers[place], jnp.concatenate(table).astype(jnp.int32)))
        yield done

    def table(self, kind):
        half = []
        for side in range(2):
            masks = self.orders[kind][side] + [self.far]
            half.append(np.array([sum(bit for at, bit in enumerate(masks) if place >> (len(masks) - 1 - at) & 1)
                                  for place in range(self.count // 2)], np.int32))
        keep = jnp.where(self.side == 0, half[0], half[1])
        send = jnp.where(self.side == 0, half[1], half[0])
        return jnp.concatenate([self.me ^ keep, self.me ^ self.core ^ send]).astype(jnp.int32)

    def exchange_cores(self, pair):
        return pair[1], self.swap(pair[0], [self.core] * 2)

    def step(self, groups, phase):
        done = []
        for (sent, kept), kind in zip(groups, ("split", "shared")):
            bits = [order[phase] for order in self.orders[kind]] if phase < self.near else [self.far] * 2
            done.append((kept, self.swap(sent, bits)))
        return done


def refold(groups, steps, paired=0):
    return fold([[(kept, got, 0, kept.shape[1])] for kept, got in groups], steps, paired)


def tie(*groups):
    flat, tree = jax.tree.flatten(groups)
    return jax.tree.unflatten(tree, lax.optimization_barrier(flat))


def halves(array):
    half = array.shape[0] // 2
    return array[half:], array[:half]


def tie(*groups):
    flat, tree = jax.tree.flatten(groups)
    return jax.tree.unflatten(tree, lax.optimization_barrier(flat))


def halves(array):
    half = array.shape[0] // 2
    return array[half:], array[:half]


def in_order(table, pair, rows):
    if rows % 8 == 0:
        return pair
    whole = jnp.concatenate([pair[1], pair[0]], axis=0)
    return halves(whole.reshape((-1, rows) + whole.shape[1:])[table].reshape(whole.shape))


def body(dp, fsdp, tokens, lengths, cotangent, mixer_in, w_eta, eta_bias, w_out, inner_w, inner_b, ttt_gain, ttt_shift,
         norm_one, post_gain, post_shift, w_gate_up, w_down, norm_two):
    links = Links(dp, fsdp)
    devices = dp * fsdp
    micro, slots, width = tokens.shape
    rows = micro * slots
    heads = eta_bias.shape[0]
    head = width // heads
    hidden = w_gate_up.shape[1] // 2
    device_rows = width // devices
    table, shared = links.table("split"), links.table("shared")
    zeros = lambda columns: jnp.zeros((device_rows, columns), low)

    vectors = jnp.stack([inner_b, ttt_gain, ttt_shift, norm_one, post_gain, post_shift, norm_two])
    vectors = dot_tn(vectors, jnp.eye(7, PAIR, VECTORS, dtype=low)).astype(low)
    small = jnp.concatenate([inner_w, w_eta, zeros(PAIR - ETA - heads)], axis=1) + vectors
    cut = 21 * PAIR
    pieces = [mixer_in[:, :cut], jnp.concatenate([mixer_in[:, cut:], w_out, small], axis=1)]
    rest = [w_gate_up, w_down]
    kinds = ["split", "shared"]
    aligned = device_rows % 8 == 0
    if aligned:
        mixer_phases = links.gather_blocks(pieces, kinds, [True, True], [False, True])
    else:
        mixer_phases = links.gather(pieces, kinds)
    places = lax.broadcasted_iota(jnp.int32, (micro, slots), 1)
    live = places < lengths
    upstream = jnp.where(live[..., None], cotangent, jnp.zeros_like(cotangent)).reshape(rows, width)
    held = next(mixer_phases)
    for _ in range(links.phases - 2):
        held = mixer_phases.send(held)
    state = [jnp.zeros((HEAD, 1536), full), jnp.zeros((HEAD, 384), full)]
    held, rest, upstream, state = tie(held, rest, upstream, state)
    zero_state = [state[0]] + [state[1]] * 5
    rest_phases = links.gather_blocks(rest, kinds, [True, False], [False, False]) if aligned else links.gather(rest, kinds)
    held, rest = mixer_phases.send(held), next(rest_phases)
    held, rest = tie(held, rest)
    held, rest = mixer_phases.send(held), rest_phases.send(rest)
    held, rest = tie(held, rest)
    held = mixer_phases.send(held)
    as_blocks = lambda arrays: [([array[None]], jnp.zeros((1,), jnp.int32)) for array in arrays]
    early, late = held if aligned else as_blocks(held)

    inputs = tokens.reshape(rows, width)
    bias_row = jnp.pad(eta_bias.astype(full), (ETA, PAIR - ETA - heads)).reshape(1, PAIR)
    early, late, rest = tie(early, late, rest)
    rest = rest_phases.send(rest)
    whole, projected, normed, rate_lanes, rest_lanes, start_w, start_b, gain_lanes, shift_lanes, vec_rows = project(
        lengths.reshape(micro), inputs, early, late, bias_row
    )
    projected = projected.reshape(micro, slots, -1)
    rate_lanes, rest = tie(rate_lanes, rest)
    rest = rest_phases.send(rest)
    inner, saved = ttt_forward(projected, rate_lanes, [start_w, start_b], gain_lanes, shift_lanes)
    inner = inner.reshape(rows, width)
    inner, rest = tie(inner, rest)
    rest = drain(rest_phases, rest)
    if not aligned:
        rest = as_blocks(rest)
    gate, mixed, first, second = post(inner, normed, inputs, whole, vec_rows)
    block_out, dsecond, large_sent, large_kept, *natural = ffn(table, shared, second, first, upstream, *rest, devices, dp)
    down_rows = hidden // devices
    unit = min(8, device_rows // 3)
    if not aligned:
        natural = natural[0].reshape(devices, -1, unit, 3, width // 3).transpose(0, 3, 2, 1, 4).reshape(width, hidden)
        pairs = in_order(table, (large_sent, large_kept), device_rows), in_order(shared, halves(natural), device_rows)
        large_sent, large_kept = (jnp.concatenate(pair, axis=1) for pair in zip(*pairs))
    large = links.exchange_cores((large_sent, large_kept))
    dfirst, dgate, dinner, dfirst_low, sums = post_back(dsecond, first, upstream, inner, gate, whole, vec_rows)
    middle = middle_grads(table, mixed, dfirst_low, normed, dgate, devices)
    middle = links.exchange_cores(in_order(table, tuple(middle), device_rows))
    dinner, large, middle = tie(dinner, large, middle)
    groups = fold([[(*large, 0, 2 * hidden), (*middle, 0, 2 * width)], [(*large, 2 * hidden, hidden)]], dp, 0, low)
    dinner, groups = tie(dinner, groups)
    groups = links.step(groups, 0)
    dinner = dinner.reshape(micro, slots, width)
    dqkv, rate_late, state = ttt_backward(projected, dinner, rate_lanes, saved, zero_state, gain_lanes, 4, slots // MINI, None)
    dqkv, state, groups = tie(dqkv, state, groups)
    groups = refold(groups, 2)
    dqkv, state, groups = tie(dqkv, state, groups)
    groups = links.step(groups, 1)
    dqkv, rate_early, state = ttt_backward(projected, dinner, rate_lanes, saved, state, gain_lanes, 0, 4, dqkv)
    dqkv = dqkv.reshape(rows, 3 * width)
    rate_back = jnp.concatenate([rate_early, rate_late], axis=0)
    early = weight_grads(table, normed, dqkv, devices)
    dqkv, early, groups = tie(dqkv, list(early), groups)
    groups = refold(groups, 2)
    dqkv, early, groups = tie(dqkv, early, groups)
    for phase in range(2, links.near):
        groups = refold(groups, 2) if phase > 2 else groups
        groups = links.step(groups, phase)
    early = links.exchange_cores(in_order(table, tuple(early), device_rows))
    *late, dlog = last_grads(shared, normed, dqkv, sums, state, rate_back, rest_lanes, devices)
    late, dlog, early, groups = tie(list(late), dlog, early, groups)
    late = links.exchange_cores(in_order(shared, tuple(late), device_rows))
    groups = refold(groups, 2)
    late, groups = tie(late, groups)
    groups = links.step(groups, links.near)
    last = fold([[(*early, 0, 2 * width)], [(*late, 0, width + 2 * PAIR)]], 1, PAIR)
    dlog, last = tie(dlog, last)
    last = links.step(last, 0)
    grad_tokens = None
    for half in range(2):
        grad_tokens = finish(inputs, dfirst, dqkv, dgate, dlog, whole, vec_rows, half, grad_tokens)
        grad_tokens, last = tie(grad_tokens, last)
        last = links.step(refold(last, 1, PAIR), 1 + half)
    for phase in range(3, links.near + 1):
        last = links.step(refold(last, 1, PAIR), phase)
    large, down = (kept + got.astype(full) for kept, got in groups)
    early, late = (kept + got.astype(full) for kept, got in last)
    part = hidden // dp
    large = large.reshape(device_rows, dp, -1)
    both = large[:, :, : 2 * part].reshape(device_rows, dp, 2, part).transpose(0, 2, 1, 3).reshape(device_rows, 2 * hidden)
    middle = large[:, :, 2 * part :].reshape(device_rows, 2 * width)
    out_small = late[:, width : width + PAIR] + late[:, width + PAIR :]
    out_out, out_gate_in = middle[:, :width], middle[:, width:]
    out_mixer = jnp.concatenate([early, late[:, :width], out_gate_in], axis=1)
    out_eta = out_small[:, ETA : ETA + heads]
    out_norm_one = jnp.sum(mixer_in.astype(full) * out_mixer, axis=1) + jnp.sum(w_eta.astype(full) * out_eta, axis=1)
    out_norm_one = out_norm_one / norm_one.astype(full)
    out_inner_b, out_gain, out_shift, _, out_post_gain, out_post_shift, out_norm_two = (
        out_small[:, VECTORS + place] for place in range(7)
    )
    return (
        block_out.reshape(tokens.shape),
        grad_tokens.reshape(tokens.shape),
        out_mixer,
        out_eta,
        out_small[0, BIAS : BIAS + heads],
        out_out,
        out_small[:, :head],
        out_inner_b,
        out_gain,
        out_shift,
        out_norm_one,
        out_post_gain,
        out_post_shift,
        both,
        down.reshape(3, unit, -1, width // 3).transpose(2, 1, 0, 3).reshape(down_rows, width),
        out_norm_two,
    )


def drain(phases, arrays):
    try:
        while True:
            arrays = phases.send(arrays)
    except StopIteration:
        return arrays


def solution(mesh):
    split = ("dp", "fsdp")
    row, vector, token = P(split, None), P(split), P(None, split, None)
    dp, fsdp = mesh.shape["dp"], mesh.shape["fsdp"]
    return jax.shard_map(
        lambda *arrays: body(dp, fsdp, *arrays),
        mesh=mesh,
        in_specs=(token, P(None, split), token, row, row, P(), row, row) + (vector,) * 6 + (row, row, vector),
        out_specs=(token, token, row, row, P(), row, row) + (vector,) * 6 + (row, row, vector),
        check_vma=False,
    )
```

```python
import jax
import jax.numpy as jnp
from jax import lax
from jax.experimental import pallas as pl
from jax.experimental.pallas import tpu as pltpu
from jax.sharding import PartitionSpec as P
import numpy as np

MINI = 16
HEAD = 64
PAIR = 2 * HEAD
epsilon = 1e-06
low = jnp.bfloat16
full = jnp.float32


def dot_nn(former, latter):
    return lax.dot_general(former, latter, (((1,), (0,)), ((), ())), preferred_element_type=full)


def dot_nt(former, latter):
    return lax.dot_general(former, latter, (((1,), (1,)), ((), ())), preferred_element_type=full)


def tile_of(rows, at):
    return rows[:, PAIR * at : PAIR * (at + 1)]


def key_row(group, side, tile):
    return HEAD * group + 32 * side + MINI * tile


def query_row(group, side, tile):
    return key_row(1 - group, side, tile)


def expand(rows, sides):
    zero = jnp.zeros((MINI, PAIR), rows.dtype)
    blocks = []
    for side in range(2):
        for at in range(2):
            kept = tile_of(rows, at) * sides[side]
            blocks.append(jnp.concatenate([kept if other == at else zero for other in range(2)], axis=1))
    return jnp.concatenate(blocks, axis=0)


def expand_both(queries, keys, sides):
    width = 2 * PAIR
    blocks = [(expand(keys[:, width * group : width * (group + 1)], sides), expand(queries[:, width * group : width * (group + 1)], sides))
              for group in range(2)]
    return blocks, (jnp.concatenate(blocks[0], axis=0), jnp.concatenate(blocks[1][::-1], axis=0))


def to_feature(rows, first_side, groups):
    tiles = [tile_of(rows, 2 * group + at) for group in groups for _ in range(2) for at in range(2)]
    stacked = jnp.concatenate(tiles, axis=0).T
    return jnp.where(first_side, stacked[:HEAD], stacked[HEAD:])


def to_rows(columns, left, place):
    turned = jnp.concatenate([columns, columns], axis=0).T
    pick = lambda group, side, at: turned[place(group, side, at) : place(group, side, at) + MINI]
    return jnp.concatenate([jnp.where(left, pick(group, 0, at), pick(group, 1, at)) for group in range(2) for at in range(2)], axis=1)


def exchange(values):
    half = [values[:, HEAD * at : HEAD * (at + 1)] for at in range(values.shape[1] // HEAD)]
    return jnp.concatenate([half[at ^ 1] for at in range(len(half))], axis=1)


def mean_rows(values):
    return jnp.sum(values, axis=0, keepdims=True) * (1.0 / values.shape[0])


def both_sequences(ref, rows, base, width):
    return jnp.concatenate([ref[0, rows, base : base + width], ref[1, rows, base : base + width]], axis=1)


def store_sequences(ref, rows, base, width, pieces, kind):
    whole = jnp.concatenate(pieces, axis=1)
    ref[0, rows, base : base + width] = whole[:, :width].astype(kind)
    ref[1, rows, base : base + width] = whole[:, width:].astype(kind)


def read_constants(low_ref, full_ref):
    sides = [low_ref[0:MINI], low_ref[MINI : 2 * MINI]]
    same, crossed = low_ref[32:160], low_ref[160:288]
    return sides, same, crossed, full_ref[0:MINI], full_ref[16:144], full_ref[144:272]


def lane_masks(rows=HEAD, width=3 * PAIR):
    lane = lax.broadcasted_iota(jnp.int32, (rows, width), 1)
    return lane % PAIR < HEAD, lane % HEAD < 32


PARTS = range(3)


def thin(part):
    return slice(PAIR * part, PAIR * (part + 1))


def wide(part):
    return slice(4 * PAIR * part, 4 * PAIR * (part + 1))


def lanes(pieces):
    return jnp.concatenate(pieces, axis=1)


def ttt_forward_kernel(steps, q_ref, k_ref, v_ref, rate_ref, w0_ref, b0_ref, gain_ref, shift_ref, low_ref, full_ref,
                       out_ref, w_ref, xh_ref, h_ref, grs_ref, xb_ref, stat_ref, score_ref, w_run, b_run, gain_query, shift_query):
    width = 768

    @pl.when(pl.program_id(0) == 0)
    def _():
        w_run[...] = w0_ref[...]
        b_run[...] = b0_ref[...]
        gain_query[...] = exchange(gain_ref[...])
        shift_query[...] = exchange(shift_ref[...])

    sides, same, crossed, tri, _, _ = read_constants(low_ref, full_ref)
    left, first_side = lane_masks()
    left_one, first_one = left[:, :PAIR], first_side[:, :PAIR]
    tri = lanes([tri] * 3)

    def begin(at):
        rows = slice(at * MINI, (at + 1) * MINI)
        queries = both_sequences(q_ref, rows, 0, width)
        keys = both_sequences(k_ref, rows, 0, width)
        targets = both_sequences(v_ref, rows, 0, width) - keys
        query_low, key_low = queries.astype(low), keys.astype(low)
        expanded = [expand_both(query_low[:, wide(part)], key_low[:, wide(part)], sides) for part in PARTS]
        target = lanes([to_feature(targets[:, wide(part)], first_one, (0, 1)) for part in PARTS])
        return rows, queries, query_low, expanded, target

    def multiply(at, started, weights):
        _, _, query_low, expanded, _ = started
        products = []
        for part in PARTS:
            weight_low = weights[part].astype(low)
            w_ref[at, :, wide(part)] = weight_low
            for group in range(2):
                here = slice(2 * PAIR * group, 2 * PAIR * (group + 1))
                rows = jnp.concatenate([weight_low[:, here], query_low[:, wide(part)][:, here]], axis=0)
                products.append(dot_nt(rows, expanded[part][1][group]))
        return lanes(products[::2]), lanes(products[1::2])

    def finish(at, started, kept):
        rows, queries = started[:2]
        inner_grad, mixing, updated = kept
        inner_grad_low = inner_grad.astype(low)
        moved = []
        for part in PARTS:
            mixing_block = jnp.concatenate([mixing[:, thin(part)]] * 8, axis=0) * crossed
            moved.append(dot_nt(inner_grad_low[:, thin(part)], mixing_block))
        updated = updated - lanes(moved)
        updated = updated - mean_rows(updated)
        updated_inverse = lax.rsqrt(mean_rows(updated * updated) + epsilon)
        updated = updated * updated_inverse
        xb_ref[at] = updated
        stat_ref[at, 3:4] = updated_inverse
        updated = updated * gain_query[...] + shift_query[...]
        result = queries + lanes([to_rows(updated[:, thin(part)], left_one[:MINI], query_row) for part in PARTS])
        out_ref[0, rows, :] = result[:, :width]
        out_ref[1, rows, :] = result[:, width:]

    weights = [w_run[:, wide(part)] for part in PARTS]
    offset = b_run[...]
    started = begin(0)
    pending = None
    for at in range(steps):
        first, second = multiply(at, started, weights)
        if pending is not None:
            finish(*pending)
        gains, shifts = gain_ref[...], shift_ref[...]
        rate = rate_ref[at]
        _, _, _, expanded, target = started
        hidden = jnp.where(left, first[:HEAD], second[:HEAD]) + offset
        scores = jnp.where(left[:MINI], first[HEAD:], second[HEAD:]) + 1.0
        updated = jnp.where(left, second[:HEAD], first[:HEAD]) + exchange(offset)
        centred = hidden - mean_rows(hidden)
        inverse = lax.rsqrt(mean_rows(centred * centred) + epsilon)
        normed = centred * inverse
        held = gains * normed + (shifts - target)
        residual = held * gains
        residual_mean = mean_rows(residual)
        cross = mean_rows(residual * normed)
        inner_grad = (residual - residual_mean - normed * cross) * inverse
        scaled = inner_grad * (rate * (1.0 / MINI))
        scaled_low = scaled.astype(low)
        scaled_other = exchange(scaled).astype(low)
        xh_ref[at] = normed
        h_ref[at] = held
        grs_ref[at] = scaled
        stat_ref[at, 0:1] = inverse
        stat_ref[at, 1:2] = residual_mean
        stat_ref[at, 2:3] = cross
        score_ref[at] = scores
        changed = []
        for part in PARTS:
            blocks = expanded[part][0]
            change = [dot_nn(scaled_low[:, thin(part)][:, :HEAD], blocks[0][0]),
                      dot_nn(scaled_other[:, thin(part)][:, :HEAD], blocks[1][0])]
            changed.append(weights[part] - lanes(change))
        weights = changed
        offset = offset - lanes([dot_nn(scaled_low[:, thin(part)], same) for part in PARTS])
        pending = (at, started, (inner_grad, (tri * rate * scores).astype(low), updated))
        if at + 1 < steps:
            started = begin(at + 1)
    finish(*pending)
    for part in PARTS:
        w_run[:, wide(part)] = weights[part]
    b_run[...] = offset


def ttt_backward_kernel(steps, carried, q_ref, k_ref, dout_ref, rate_ref, w_ref, xh_ref, h_ref, grs_ref, xb_ref, stat_ref, score_ref,
                        gain_ref, low_ref, full_ref, *refs):
    states, refs = (refs[:6], refs[6:]) if carried else (None, refs)
    grad_ref, rdr_ref, dw_ref, db_ref, dgain_ref, dshift_ref, dgain_query_ref, dshift_query_ref, gain_query = refs[-9:]
    width = 768

    @pl.when(pl.program_id(0) == 0)
    def _():
        for place, ref in enumerate((dw_ref, db_ref, dgain_ref, dshift_ref, dgain_query_ref, dshift_query_ref)):
            ref[...] = states[place][...] if carried else jnp.zeros_like(ref)
        gain_query[...] = exchange(gain_ref[...])

    sides, same, crossed, tri, scale, scale_turned = read_constants(low_ref, full_ref)
    left, first_side = lane_masks()
    left_one, first_one = left[:, :PAIR], first_side[:, :PAIR]
    left_rows = left_one[:MINI]
    left_square = lax.broadcasted_iota(jnp.int32, (PAIR, PAIR), 1) < HEAD
    zero = jnp.zeros((MINI, PAIR), full)
    tri = lanes([tri] * 3)

    def begin(at):
        rows = slice(at * MINI, (at + 1) * MINI)
        query_low = both_sequences(q_ref, rows, 0, width).astype(low)
        key_low = both_sequences(k_ref, rows, 0, width).astype(low)
        douts = both_sequences(dout_ref, rows, 0, width)
        expanded = [expand_both(query_low[:, wide(part)], key_low[:, wide(part)], sides) for part in PARTS]
        mixing = (tri * rate_ref[at] * score_ref[at]).astype(low)
        dout = lanes([to_feature(douts[:, wide(part)], first_one, (1, 0)) for part in PARTS])
        updated = xb_ref[at]
        dupdated = dout * gain_query[...]
        dupdated = stat_ref[at, 3:4] * (dupdated - mean_rows(dupdated) - updated * mean_rows(dupdated * updated))
        dgain_query_ref[...] += dout * updated
        dshift_query_ref[...] += dout
        dupdated_low = dupdated.astype(low)
        mixed = []
        for part in PARTS:
            mixing_block = jnp.concatenate([mixing[:, thin(part)]] * 8, axis=0) * crossed
            mixed.append(dot_nn(dupdated_low[:, thin(part)], mixing_block))
        return rows, douts, expanded, dupdated, dupdated_low, lanes(mixed)

    def finish(at, started, kept):
        rows, douts, expanded, dupdated, dupdated_low, _ = started
        dhidden, dtarget, dweights_low, rate_part = kept
        scaled = -grs_ref[at]
        scaled_low = scaled.astype(low)
        scores = score_ref[at]
        none = jnp.zeros((HEAD, PAIR), low)
        turned_low, turned_query, query_rows, dmixes, dmixes_turned = [], [], [], [], []
        for part in PARTS:
            turned_low.append(jnp.concatenate([dhidden[:, thin(part)], scaled[:, thin(part)]], axis=0).T.astype(low))
            turned_query.append(jnp.concatenate([dupdated[:, thin(part)], dtarget[:, thin(part)]], axis=0).T)
            query_rows.append(jnp.where(left_square, turned_query[part], 0.0).astype(low))
        for part in PARTS:
            dmix = dot_nn(query_rows[part][:, :HEAD], scaled_low[:, thin(part)]) * scale
            dmix_turned = dot_nn(turned_low[part], jnp.concatenate([none, dupdated_low[:, thin(part)]], axis=0)) * scale_turned
            dmixes.append(sum(dmix[MINI * row : MINI * (row + 1)] for row in range(8)))
            dmixes_turned.append(sum(dmix_turned[MINI * row : MINI * (row + 1)] for row in range(8)))
        rdr_ref[at] = rate_part + jnp.sum(lanes(dmixes) * scores, axis=0, keepdims=True)
        query_grads, key_grads, value_grads = [], [], []
        for part in PARTS:
            weight_low = w_ref[at, :, wide(part)]
            for group in range(2):
                keep_key, keep_query = (left_rows, ~left_rows) if group == 0 else (~left_rows, left_rows)
                key_side = jnp.where(keep_query, dmixes_turned[part], zero).astype(low)
                query_side = jnp.where(keep_key, dmixes[part], zero).astype(low)
                extra = jnp.concatenate([key_side, key_side, query_side, query_side], axis=0)
                for at_tile in range(2):
                    tile = 2 * group + at_tile
                    place = [key_row(group, side, at_tile) for side in range(2)]
                    place_query = [query_row(group, side, at_tile) for side in range(2)]
                    held_rows = jnp.concatenate(
                        [turned_low[part][row : row + MINI] for row in place]
                        + [query_rows[part][row : row + MINI] for row in place_query],
                        axis=0,
                    )
                    product = dot_nn(
                        jnp.concatenate([held_rows, extra], axis=1),
                        jnp.concatenate(
                            [tile_of(weight_low, tile), tile_of(dweights_low[part], tile), tile_of(expanded[part][1][group], at_tile)],
                            axis=0,
                        ),
                    )
                    dvalue = jnp.where(
                        left_rows,
                        exchange(turned_query[part][place[0] : place[0] + MINI]),
                        turned_query[part][place[1] : place[1] + MINI],
                    )
                    key_grads.append(dvalue + jnp.where(left_rows, product[:MINI], product[MINI : 2 * MINI]))
                    query_grads.append(
                        tile_of(douts[:, wide(part)], tile) + jnp.where(left_rows, product[2 * MINI : 3 * MINI], product[3 * MINI :])
                    )
                    value_grads.append(-dvalue)
        store_sequences(grad_ref, rows, 0, width, query_grads, low)
        store_sequences(grad_ref, rows, width, width, key_grads, low)
        store_sequences(grad_ref, rows, 2 * width, width, value_grads, low)

    dweights = [dw_ref[:, wide(part)] for part in PARTS]
    doffset = db_ref[...]
    started = begin(steps - 1)
    pending = None
    for at in reversed(range(steps)):
        _, _, expanded, dupdated, _, mixed = started
        dweights_low = [dweight.astype(low) for dweight in dweights]
        key_dw = []
        for part in PARTS:
            blocks = expanded[part][0]
            key_dw.append(dot_nt(dweights_low[part][:, : 2 * PAIR], blocks[0][0]))
            key_dw.append(dot_nt(dweights_low[part][:, 2 * PAIR :], blocks[1][0]))
        key_dw = lanes(key_dw) + doffset
        if pending is not None:
            finish(*pending)
        upcoming = begin(at - 1) if at > 0 else None
        gains = gain_ref[...]
        rate = rate_ref[at]
        normed, held, scaled = xh_ref[at], h_ref[at], grs_ref[at]
        inverse, residual_mean, cross = (stat_ref[at, row : row + 1] for row in range(3))
        grad_in = -mixed - (rate * (1.0 / MINI)) * key_dw
        rate_part = -jnp.sum(scaled * key_dw, axis=0, keepdims=True)
        residual = held * gains
        in_mean = mean_rows(grad_in)
        in_cross = mean_rows(grad_in * normed)
        in_held = inverse * (mean_rows(grad_in * residual) - residual_mean * in_mean - cross * in_cross)
        dresidual = inverse * (grad_in - in_mean - normed * in_cross)
        dtarget = dresidual * gains
        dnormed = dtarget * gains - inverse * (grad_in * cross + in_cross * residual)
        dhidden = inverse * (dnormed - mean_rows(dnormed) - normed * (mean_rows(dnormed * normed) + in_held))
        dgain_ref[...] += dresidual * (held + gains * normed)
        dshift_ref[...] += dtarget
        to_first = jnp.where(left, dhidden, dupdated).astype(low)
        to_second = jnp.where(left, dupdated, dhidden).astype(low)
        changed = []
        for part in PARTS:
            pairs = expanded[part][1]
            change = [dot_nn(to_first[:, thin(part)], pairs[0]), dot_nn(to_second[:, thin(part)], pairs[1])]
            changed.append(dweights[part] + lanes(change))
        total_low = (exchange(dupdated) + dhidden).astype(low)
        doffset = doffset + lanes([dot_nn(total_low[:, thin(part)], same) for part in PARTS])
        dweights = changed
        pending = (at, started, (dhidden, dtarget, dweights_low, rate_part))
        started = upcoming
    finish(*pending)
    for part in PARTS:
        dw_ref[:, wide(part)] = dweights[part]
    db_ref[...] = doffset


def ttt_constants():
    lane = np.arange(PAIR)
    row = np.arange(MINI)
    sides = np.concatenate([np.tile(lane < HEAD, (MINI, 1)), np.tile(lane >= HEAD, (MINI, 1))])
    token = lane % MINI
    tri = np.where(token[None] <= row[:, None], 1.0 / (row[:, None] + 1.0), 0.0)
    same = lane[:, None] // MINI == lane[None] // MINI
    crossed = (lane[:, None] + HEAD) % PAIR // MINI == lane[None] // MINI
    scale = np.where(crossed & (token[None] <= token[:, None]), MINI / (token[:, None] + 1.0), 0.0)
    return (
        jnp.asarray(np.concatenate([sides, same, crossed]).astype(np.float32), low),
        jnp.asarray(np.concatenate([tri, scale, scale.T]), full),
    )


def ttt_forward(projected, rates, state, gains, shifts, steps=4):
    count = projected.shape[1] // MINI
    first, begin, end = 0, 0, count
    queries, keys, values = projected, projected, projected
    constants = ttt_constants()
    whole = lambda *shape: pl.BlockSpec(shape, lambda at: (0,) * len(shape))
    column = lambda place: pl.BlockSpec((2, steps * MINI, 768), lambda at, place=place: (0, first + at, place))
    part = column(0)
    saved = lambda *tail: pl.BlockSpec((steps,) + tail, lambda at: (at, 0, 0))
    made = lambda kind, *tail: jax.ShapeDtypeStruct((end - begin,) + tail, kind)
    inputs = [queries, keys, values, rates, *state, gains, shifts, *constants]
    out, *rest = pl.pallas_call(
        lambda *refs: ttt_forward_kernel(steps, *refs),
        grid=((end - begin) // steps,),
        in_specs=[column(0), column(1), column(2), pl.BlockSpec((steps, 1, 384), lambda at: (first + at, 0, 0)), whole(64, 1536), whole(64, 384),
                  whole(64, 384), whole(64, 384), whole(288, 128), whole(272, 128)],
        out_specs=[part, saved(64, 1536), saved(64, 384), saved(64, 384), saved(64, 384), saved(64, 384), saved(8, 384),
                   saved(16, 384)],
        out_shape=[jax.ShapeDtypeStruct((2, count * MINI, 768), full), made(low, 64, 1536), made(full, 64, 384), made(full, 64, 384),
                   made(full, 64, 384), made(full, 64, 384), made(full, 8, 384), made(full, 16, 384)],
        scratch_shapes=[pltpu.VMEM((64, 1536), full)] + [pltpu.VMEM((64, 384), full)] * 3,
        compiler_params=pltpu.CompilerParams(vmem_limit_bytes=60 * 1024 * 1024),
        cost_estimate=pl.CostEstimate(flops=(end - begin) * 1_400_000_000, bytes_accessed=(end - begin) * 1_500_000, transcendentals=0),
        name="ttt_forward",
    )(*inputs)
    return out, rest


def ttt_backward(projected, dout, rates, saved_arrays, state, gains, begin, end, before, steps=4):
    count = projected.shape[1] // MINI
    first, blocks = begin // steps, (end - begin) // steps
    queries, keys = projected, projected
    constants = ttt_constants()
    whole = lambda *shape: pl.BlockSpec(shape, lambda at: (0,) * len(shape))
    part = lambda width, place=0: pl.BlockSpec((2, steps * MINI, width), lambda at: (0, first + blocks - 1 - at, place))
    saved = lambda *tail: pl.BlockSpec((steps,) + tail, lambda at: (first + blocks - 1 - at, 0, 0))
    made = lambda *tail: pl.BlockSpec((steps,) + tail, lambda at: (blocks - 1 - at, 0, 0))
    extra = [] if before is None else [before]
    inputs = [queries, keys, dout, rates, *saved_arrays, gains, *constants, *(state or [])]
    states = [whole(64, 1536)] + [whole(64, 384)] * 5
    grad, rate_back, *sums = pl.pallas_call(
        lambda *refs: ttt_backward_kernel(steps, state is not None, *refs),
        grid=(blocks,),
        in_specs=[part(768), part(768, 1), part(768), saved(1, 384),
                  saved(64, 1536), saved(64, 384), saved(64, 384), saved(64, 384), saved(64, 384), saved(8, 384), saved(16, 384),
                  whole(64, 384), whole(288, 128), whole(272, 128)]
        + (states if state else []) + [pl.BlockSpec(memory_space=pl.ANY)] * len(extra),
        out_specs=[part(2304), made(1, 384)] + states,
        out_shape=[jax.ShapeDtypeStruct((2, count * MINI, 2304), low), jax.ShapeDtypeStruct((end - begin, 1, 384), full)]
        + [jax.ShapeDtypeStruct((64, 1536), full)] + [jax.ShapeDtypeStruct((64, 384), full)] * 5,
        scratch_shapes=[pltpu.VMEM((64, 384), full)],
        input_output_aliases={len(inputs): 0} if extra else {},
        compiler_params=pltpu.CompilerParams(vmem_limit_bytes=60 * 1024 * 1024),
        cost_estimate=pl.CostEstimate(flops=(end - begin) * 2_000_000_000, bytes_accessed=(end - begin) * 1_500_000, transcendentals=0),
        name="ttt_backward",
    )(*inputs, *extra)
    return grad, rate_back, sums


def silu_parts(gate):
    sigma = jax.nn.sigmoid(gate)
    return gate * sigma, sigma * (1.0 + gate * (1.0 - sigma))


def gelu_parts(values):
    slope = 0.7978845608028654
    turn = jnp.tanh(slope * (values + 0.044715 * values * values * values))
    half = 0.5 * (1.0 + turn)
    return values * half, half + 0.5 * values * (1.0 - turn * turn) * slope * (1.0 + 3 * 0.044715 * values * values)


def row_mean(values):
    return jnp.mean(values, axis=-1, keepdims=True)


def dot_tn(former, latter):
    return lax.dot_general(former, latter, (((0,), (0,)), ((), ())), preferred_element_type=full)


def exact_dot(former, latter):
    total = None
    for _ in range(3):
        part = former.astype(low)
        former = former - part.astype(full)
        term = dot_nn(part, latter)
        total = term if total is None else total + term
    return total


def constant_spec(*shape, at=0, buffers=None):
    index = lambda *steps: (0,) * (len(shape) - 1) + (at,)
    if buffers is None:
        return pl.BlockSpec(shape, index)
    return pl.BlockSpec(shape, index, pipeline_mode=pl.Buffered(buffers))


def call(kernel, name, grid, prefetch, in_specs, out_specs, out_shape, scratch, cost, arrays):
    return pl.pallas_call(
        kernel,
        grid_spec=pltpu.PrefetchScalarGridSpec(
            num_scalar_prefetch=prefetch, grid=grid, in_specs=in_specs, out_specs=out_specs, scratch_shapes=scratch
        ),
        out_shape=out_shape,
        compiler_params=pltpu.CompilerParams(vmem_limit_bytes=60 * 1024 * 1024),
        cost_estimate=pl.CostEstimate(flops=cost, bytes_accessed=cost // 500, transcendentals=0),
        name=name,
    )(*arrays)


ETA = 64
VECTORS = 80
BIAS = 96


def lane_table():
    lane = np.arange(384)
    part, group, side, tile, token = lane // 128, lane // 64 % 2, lane // 32 % 2, lane // 16 % 2, lane % 16
    pair = 4 * part + 2 * group + tile
    return token, pair // 6, 2 * (pair % 6) + side


def lane_constants():
    token, sequence, head = lane_table()
    table = np.zeros((32, 384), np.float32)
    table[:MINI] = token[None] == np.arange(MINI)[:, None]
    table[16], table[17] = sequence, token
    chosen = np.zeros((PAIR, 384), np.float32)
    chosen[ETA + head, np.arange(384)] = 1
    return jnp.asarray(table), jnp.asarray(chosen, low)


def block_copies(from_refs, table, to, columns, semaphores, first):
    started = []
    for place, ref in enumerate(from_refs):
        for item in range(ref.shape[0]):
            begin = pl.multiple_of(table[place * ref.shape[0] + item] * ref.shape[1], 16)
            target = to.at[pl.ds(begin, ref.shape[1]), columns]
            started.append(pltpu.make_async_copy(ref.at[item], target, semaphores.at[first + len(started)]))
    return started


def project_kernel(counts, length_ref, early_table_ref, late_table_ref, tokens_ref, bias_ref, table_ref, chosen_ref, *refs):
    early_refs, late_refs, refs = refs[: counts[0]], refs[counts[0] : sum(counts)], refs[sum(counts) :]
    whole_ref, proj_ref, normed_ref, rate_ref, rest_ref, wt_ref, b_ref, gain_ref, shift_ref, vec_ref, semaphores = refs
    at = pl.program_id(0)
    split = 512 // tokens_ref.shape[0]
    wide = proj_ref.shape[1]
    begin_small = whole_ref.shape[1] - PAIR
    cut = early_refs[0].shape[2]

    def copies():
        started = block_copies(early_refs, early_table_ref, whole_ref, slice(0, cut), semaphores, 0)
        return started + block_copies(late_refs, late_table_ref, whole_ref, slice(cut, whole_ref.shape[1]), semaphores, len(started))

    @pl.when(at == 0)
    def _():
        for copy in copies():
            copy.start()
        for copy in copies():
            copy.wait()
        small = whole_ref[:, begin_small:].astype(full)
        turned = small.T
        wt_ref[:, :768] = turned[:HEAD]
        wt_ref[:, 768:] = turned[:HEAD]
        vec_ref[...] = turned[VECTORS : VECTORS + 8]
        for place, ref in enumerate((b_ref, gain_ref, shift_ref)):
            total = jnp.zeros((HEAD, 384), full)
            for head in range(12):
                column = small[HEAD * head : HEAD * (head + 1), VECTORS + place : VECTORS + place + 1]
                total = total + column * chosen_ref[ETA + head : ETA + head + 1].astype(full)
            ref[...] = total
        rate_ref[...] = jnp.zeros_like(rate_ref)
        rest_ref[...] = jnp.zeros_like(rest_ref)

    values = tokens_ref[...].astype(full)
    normed = (values * lax.rsqrt(row_mean(values * values) + epsilon) * vec_ref[3:4]).astype(low)
    normed_ref[...] = normed
    proj_ref[...] = dot_nn(normed, whole_ref[:, :wide])
    last = dot_nn(normed, whole_ref[:, begin_small:])
    spread = exact_dot(last + bias_ref[...], chosen_ref[...])
    blocks = spread.shape[0] // MINI
    spread = jnp.sum(spread.reshape(blocks, MINI, 384) * table_ref[:MINI][None], axis=1)
    sequence, token = table_ref[16:17], table_ref[17:18]
    mine = sequence == (at // split).astype(full)
    sigma = jax.nn.sigmoid(spread)
    begin = (at % split) * blocks
    block = lax.broadcasted_iota(jnp.int32, spread.shape, 0) + begin
    live = (block * MINI).astype(full) + token < length_ref[at // split].astype(full)
    here = pl.ds(begin, blocks)
    rate_ref[here, 0, :] += jnp.where(live & mine, sigma * (1.0 / HEAD), 0.0)
    rest_ref[here, :] += jnp.where(mine, 1.0 - sigma, 0.0)


def project(lengths, tokens, early, late, bias_row):
    rows, width = tokens.shape
    table, chosen = lane_constants()
    tile = rows // 2
    columns = early[0][0].shape[2] + late[0][0].shape[2]
    counts = len(early[0]), len(late[0])
    row = lambda n: pl.BlockSpec((tile, n), lambda at, *_: (at, 0))
    shape = jax.ShapeDtypeStruct
    return call(
        lambda *refs: project_kernel(counts, *refs), "project", (2,), 3,
        [row(width), constant_spec(1, PAIR), constant_spec(32, 384), constant_spec(PAIR, 384)]
        + [pl.BlockSpec(memory_space=pl.ANY)] * sum(counts),
        [constant_spec(width, columns, buffers=1), row(3 * width), row(width), constant_spec(32, 1, 384), constant_spec(32, 384),
         constant_spec(64, 1536)] + [constant_spec(64, 384)] * 3 + [constant_spec(8, width)],
        [shape((width, columns), low), shape((rows, 3 * width), full), shape((rows, width), low), shape((32, 1, 384), full),
         shape((32, 384), full), shape((64, 1536), full)] + [shape((64, 384), full)] * 3 + [shape((8, width), full)],
        [pltpu.SemaphoreType.DMA((early[1].shape[0] + late[1].shape[0],))], 5_000_000_000,
        (lengths, early[1], late[1], tokens, bias_row, table, chosen, *early[0], *late[0]),
    )


def post_kernel(inner_ref, normed_ref, tokens_ref, w_gate_ref, w_out_ref, vec_ref, gate_ref, mixed_ref, first_ref, second_ref):
    gate = dot_nn(normed_ref[...], w_gate_ref[...])
    gate_ref[...] = gate
    inner = inner_ref[...]
    centred = inner - row_mean(inner)
    standard = centred * lax.rsqrt(row_mean(centred * centred) + epsilon)
    mixed = ((standard * vec_ref[4:5] + vec_ref[5:6]) * gelu_parts(gate)[0]).astype(low)
    mixed_ref[...] = mixed
    first = tokens_ref[...].astype(full) + dot_nn(mixed, w_out_ref[...])
    first_ref[...] = first
    second_ref[...] = (first * lax.rsqrt(row_mean(first * first) + epsilon) * vec_ref[6:7]).astype(low)


def post(inner, normed, tokens, whole, vectors):
    rows, width = tokens.shape
    tile = rows // 4
    row = pl.BlockSpec((tile, width), lambda at: (at, 0))
    shape = jax.ShapeDtypeStruct
    return call(
        post_kernel, "post", (4,), 0,
        [row, row, row, constant_spec(width, width, at=3, buffers=1), constant_spec(width, width, at=4, buffers=1), constant_spec(8, width)],
        [row] * 4, [shape((rows, width), kind) for kind in (full, low, full, low)], [], 4_000_000_000,
        (inner, normed, tokens, whole, whole, vectors),
    )


def store_blocks(table_ref, sent_ref, kept_ref, held_ref, block):
    half = kept_ref.shape[0]
    if block % 8:
        kept_ref[...] = held_ref[:half].astype(kept_ref.dtype)
        sent_ref[...] = held_ref[half:].astype(sent_ref.dtype)
        return
    for pair in range(held_ref.shape[0] // (2 * block)):
        rows = [held_ref[pl.ds(pl.multiple_of(table_ref[2 * pair + side] * block, 8), block), :] for side in range(2)]
        begin = 2 * block * pair
        ref, begin = (kept_ref, begin) if begin < half else (sent_ref, begin - half)
        ref[begin : begin + 2 * block, :] = jnp.concatenate(rows, axis=0).astype(ref.dtype)


def ffn_kernel(block, down_block, steps, counts, table_ref, shared_ref, both_table_ref, down_table_ref, second_ref, first_ref, up_ref, *refs):
    both_refs, refs = refs[: counts[0]], refs[counts[0] :]
    down_refs, refs = refs[: counts[1]], refs[counts[1] :]
    aligned = block % 8 == 0
    out_ref, dsecond_ref, sent_ref, kept_ref, *refs = refs
    natural_ref, refs = (None, refs) if aligned else (refs[0], refs[1:])
    turned, total, act, both_low, held, w_both, w_down_all, held_down, semaphores = refs
    at = pl.program_id(0)
    size = act.shape[1]
    hidden = w_down_all.shape[0]

    def copies():
        started = block_copies(both_refs, both_table_ref, w_both, slice(None), semaphores, 0)
        return started + block_copies(down_refs, down_table_ref, w_down_all, slice(None), semaphores, len(started))

    @pl.when(at == 0)
    def _():
        for copy in copies():
            copy.start()
        turned[...] = second_ref[...].T
        total[...] = first_ref[...]
        dsecond_ref[...] = jnp.zeros_like(dsecond_ref)
        for copy in copies():
            copy.wait()

    @pl.when(at < steps)
    def _():
        columns = pl.ds(pl.multiple_of(at * size, PAIR), size)
        w_gate, w_up = w_both[:, columns], w_both[:, pl.ds(pl.multiple_of(hidden + at * size, PAIR), size)]
        w_down = w_down_all[columns, :]
        second, upstream = second_ref[...], up_ref[...]
        cuts = [slice(begin, begin + size // 2) for begin in range(0, size, size // 2)]
        made = [(dot_nn(second, w_gate[:, cut]), dot_nn(second, w_up[:, cut]), dot_nt(upstream, w_down[cut])) for cut in cuts]
        for cut, (gate, up, dact) in zip(cuts, made):
            value, slope = silu_parts(gate)
            act[:, cut] = (value * up).astype(low)
            both_low[:, cut] = (dact * up * slope).astype(low)
            both_low[:, size + cut.start : size + cut.stop] = (dact * value).astype(low)
        total[...] += dot_nn(act[...], w_down)
        dsecond_ref[...] += dot_nt(both_low[:, :size], w_gate) + dot_nt(both_low[:, size:], w_up)
        ddown = dot_tn(act[...], upstream)
        held[...] = dot_nn(turned[...], both_low[...])
        if aligned:
            count = size // down_block
            third = ddown.shape[1] // 3
            for place in range(count):
                mine = ddown[down_block * place : down_block * (place + 1)]
                pieces = [jnp.concatenate([mine[8 * row : 8 * row + 8, third * part : third * (part + 1)] for row in range(down_block // 8)],
                                          axis=1) for part in range(3)]
                held_down[pl.ds(pl.multiple_of((at * count + place) * block, 8), block), :] = jnp.concatenate(pieces, axis=0)
        else:
            natural_ref[pl.ds(pl.multiple_of(at * size, 16), size), :] = ddown.astype(low)
        store_blocks(table_ref, sent_ref, kept_ref, held, block)

    @pl.when(at == steps - 1)
    def _():
        out_ref[...] = total[...].astype(low)

    if aligned:
        for extra in range(held_down.shape[1] // (2 * size)):

            @pl.when(at == steps + extra)
            def _():
                store_blocks(shared_ref, sent_ref, kept_ref, held_down.at[:, 2 * size * extra : 2 * size * (extra + 1)], block)


def ffn(table, shared, second, first, upstream, both, down, devices, steps):
    rows, width = second.shape
    hidden = down[0][0].shape[1] * down[1].shape[0]
    size = hidden // steps
    aligned = width // devices % 8 == 0
    columns = 3 * hidden if aligned else 2 * hidden
    shape = jax.ShapeDtypeStruct
    counts = len(both[0]), len(down[0])
    copies = both[1].shape[0] + down[1].shape[0]
    natural = [] if aligned else [(hidden, width)]
    return call(
        lambda *refs: ffn_kernel(width // devices, hidden // devices, steps, counts, *refs), "ffn", (columns // (2 * size),), 4,
        [constant_spec(rows, width, buffers=1)] * 3 + [pl.BlockSpec(memory_space=pl.ANY)] * sum(counts),
        [constant_spec(rows, width, buffers=1), constant_spec(rows, width, buffers=1),
         *[pl.BlockSpec((width // 2, 2 * size), lambda at, *_: (0, at))] * 2, *[constant_spec(*item, buffers=1) for item in natural]],
        [shape((rows, width), low), shape((rows, width), full), *[shape((width // 2, columns), low)] * 2,
         *[shape(item, low) for item in natural]],
        [pltpu.VMEM((width, rows), low), pltpu.VMEM((rows, width), full), pltpu.VMEM((rows, size), low),
         pltpu.VMEM((rows, 2 * size), low), pltpu.VMEM((width, 2 * size), full), pltpu.VMEM((width, 2 * hidden), low),
         pltpu.VMEM((hidden, width), low), pltpu.VMEM((width, hidden) if aligned else (8, PAIR), full),
         pltpu.SemaphoreType.DMA((copies,))],
        29_000_000_000, (table, shared, both[1], down[1], second, first, upstream, *both[0], *down[0]),
    )


def fold_kernel(layout, last, paired, *refs):
    outs = refs[sum(sum(members) + extra for members, extra in layout) :]
    for group, (members, extra) in enumerate(layout):
        mine, refs = refs[: sum(members) + extra], refs[sum(members) + extra :]
        totals = []
        for count in members:
            totals.append(sum(ref[...].astype(full) for ref in mine[:count]))
            mine = mine[count:]
        total = jnp.concatenate(totals, axis=1) if len(totals) > 1 else totals[0]
        for ref in mine:
            total = total + ref[...].astype(full)
        if paired and group + 1 == len(layout):
            plain = total.shape[1] - 2 * paired
            tail = total[:, plain : plain + paired] + total[:, plain + paired :]
            high = tail.astype(low).astype(full)
            total = jnp.concatenate([total[:, :plain], high, tail - high], axis=1)
        if last:
            half = total.shape[0] // 2
            outs[2 * group][...] = total[half:].astype(low)
            outs[2 * group + 1][...] = total[:half]
        else:
            outs[group][...] = total.astype(low)


def fold(groups, rows, steps, paired=0):
    last = rows // 2 % MINI != 0
    size, place = (rows, 0) if last else (rows // 2, 1)
    specs, arrays, outs, shapes, layout = [], [], [], [], []
    for members, extra in groups:
        width = 0
        for addends, first, columns in members:
            part = columns // steps
            specs += [pl.BlockSpec((size, part), lambda at, begin=first // part: (place, begin + at))] * len(addends)
            arrays += addends
            width += part
        specs += [pl.BlockSpec((size, width), lambda at: (place, at))] * len(extra)
        arrays += extra
        layout.append(([len(addends) for addends, _, _ in members], len(extra)))
        outs += [pl.BlockSpec((rows // 2, width), lambda at: (0, at))] * (2 if last else 1)
        shapes += [jax.ShapeDtypeStruct((rows // 2, width * steps), kind) for kind in ((low, full) if last else (low,))]
    results = call(
        lambda *refs: fold_kernel(layout, last, paired, *refs), "fold", (steps,), 0, specs, outs, shapes, [], 100_000_000, arrays
    )
    return [(results[2 * group], results[2 * group + 1]) for group in range(len(groups))] if last else list(results)


class Scatter:
    def __init__(self, links, groups, rows, steps, paired=0):
        self.links, self.steps, self.paired = links, steps, paired
        self.groups = [(members, []) for members in groups]
        self.rows, self.phase, self.kept, self.sent = rows, 0, None, None

    def fold(self):
        if self.kept is None:
            made = fold(self.groups, self.rows, self.steps, self.paired)
            if self.rows // 2 % MINI:
                self.sent, self.kept = [sent for sent, _ in made], [kept for _, kept in made]
            else:
                self.sent = made
        else:
            half = self.rows // 2
            totals = [kept + got.astype(full) for kept, got in zip(self.kept, self.got)]
            self.sent, self.kept = [total[half:].astype(low) for total in totals], [total[:half] for total in totals]
        self.rows //= 2

    def send(self):
        links, phase = self.links, self.phase
        self.got = []
        for sent, kind in zip(self.sent, ("split", "shared")):
            bits = [order[phase] for order in links.orders[kind]] if phase < links.near else [links.far] * 2
            self.got.append(links.swap(sent, bits))
        self.phase += 1
        if self.kept is None:
            self.groups = [(members, extra + [got]) for (members, extra), got in zip(self.groups, self.got)]

    def tied(self, *others):
        state = (self.sent, self.kept, self.got, self.groups) if self.phase else (self.sent,)
        arrays, tree = jax.tree.flatten(state)
        numbers = [place for place, array in enumerate(arrays) if not isinstance(array, int)]
        out = tie(*others, [arrays[place] for place in numbers])
        for place, array in zip(numbers, out[-1]):
            arrays[place] = array
        state = jax.tree.unflatten(tree, arrays)
        self.sent = state[0]
        if len(state) > 1:
            self.kept, self.got, self.groups = state[1:]
        return out[:-1] if len(others) > 1 else out[0]

    def result(self):
        while self.phase <= self.links.near:
            self.fold()
            self.send()
        return [kept + got.astype(full) for kept, got in zip(self.kept, self.got)]


def post_back_kernel(dsecond_ref, first_ref, up_ref, inner_ref, gate_ref, w_out_ref, vec_ref,
                     dfirst_ref, dgate_ref, dinner_ref, dfirst_low_ref, sums_ref):
    @pl.when(pl.program_id(0) == 0)
    def _():
        sums_ref[...] = jnp.zeros_like(sums_ref)

    first, dsecond = first_ref[...], dsecond_ref[...]
    scale = lax.rsqrt(row_mean(first * first) + epsilon)
    sums_ref[6:7] += jnp.sum(dsecond * first * scale, axis=0, keepdims=True)
    dsecond = dsecond * vec_ref[6:7]
    dfirst = up_ref[...].astype(full) + scale * dsecond - first * (scale * scale * scale * row_mean(first * dsecond))
    dfirst_ref[...] = dfirst
    dfirst_low = dfirst.astype(low)
    dfirst_low_ref[...] = dfirst_low
    dmixed = dot_nt(dfirst_low, w_out_ref[...])
    inner = inner_ref[...]
    centred = inner - row_mean(inner)
    inverse = lax.rsqrt(row_mean(centred * centred) + epsilon)
    standard = centred * inverse
    value, slope = gelu_parts(gate_ref[...])
    dgate_ref[...] = (dmixed * (standard * vec_ref[4:5] + vec_ref[5:6]) * slope).astype(low)
    dpost = dmixed * value
    sums_ref[4:5] += jnp.sum(dpost * standard, axis=0, keepdims=True)
    sums_ref[5:6] += jnp.sum(dpost, axis=0, keepdims=True)
    dpost = dpost * vec_ref[4:5]
    dinner_ref[...] = inverse * (dpost - row_mean(dpost) - standard * row_mean(dpost * standard))


def post_back(dsecond, first, upstream, inner, gate, whole, vectors):
    rows, width = first.shape
    tile = rows // 4
    row = pl.BlockSpec((tile, width), lambda at: (at, 0))
    shape = jax.ShapeDtypeStruct
    return call(
        post_back_kernel, "post_back", (4,), 0,
        [row] * 5 + [constant_spec(width, width, at=4, buffers=1), constant_spec(8, width)],
        [row, row, row, row, constant_spec(8, width)],
        [shape((rows, width), full), shape((rows, width), low), shape((rows, width), full), shape((rows, width), low),
         shape((8, width), full)],
        [], 4_000_000_000, (dsecond, first, upstream, inner, gate, whole, vectors),
    )


def middle_kernel(block, table_ref, mixed_ref, dfirst_ref, normed_ref, dgate_ref, sent_ref, kept_ref, held):
    @pl.when(pl.program_id(0) == 0)
    def _():
        held[...] = dot_tn(mixed_ref[...], dfirst_ref[...])

    @pl.when(pl.program_id(0) == 1)
    def _():
        held[...] = dot_tn(normed_ref[...], dgate_ref[...])

    store_blocks(table_ref, sent_ref, kept_ref, held, block)


def middle_grads(table, mixed, dfirst, normed, dgate, devices):
    rows, width = normed.shape
    whole = constant_spec(rows, width, buffers=1)
    return call(
        lambda *refs: middle_kernel(width // devices, *refs), "middle_grads", (2,), 1,
        [whole] * 4, [pl.BlockSpec((width // 2, width), lambda at, *_: (0, at))] * 2,
        [jax.ShapeDtypeStruct((width // 2, 2 * width), low)] * 2, [pltpu.VMEM((width, width), full)], 3_000_000_000,
        (table, mixed, dfirst, normed, dgate),
    )


def weight_kernel(block, table_ref, normed_ref, grad_ref, sent_ref, kept_ref, turned, held):
    @pl.when(pl.program_id(0) == 0)
    def _():
        turned[...] = normed_ref[...].T

    held[...] = dot_nn(turned[...], grad_ref[...])
    store_blocks(table_ref, sent_ref, kept_ref, held, block)


def weight_grads(table, normed, grads, devices):
    rows, width = normed.shape
    out = pl.BlockSpec((width // 2, width), lambda at, *_: (0, at))
    return call(
        lambda *refs: weight_kernel(width // devices, *refs), "weight_grads", (2,), 1,
        [constant_spec(rows, width, buffers=1), pl.BlockSpec((rows, width), lambda at, *_: (0, at))],
        [out, out], [jax.ShapeDtypeStruct((width // 2, 2 * width), low)] * 2,
        [pltpu.VMEM((width, rows), low), pltpu.VMEM((width, width), full)], 3_000_000_000, (table, normed, grads),
    )


def last_kernel(block, table_ref, normed_ref, grad_ref, sums_ref, dw_ref, db_ref, dgain_ref, dshift_ref, dgain_query_ref,
                dshift_query_ref, rate_ref, rest_ref, lane_ref, chosen_ref, sent_ref, kept_ref, dlog_ref, held):
    rows, width = normed_ref.shape
    turned = normed_ref[...].T
    held[:, :width] = dot_nn(turned, grad_ref[...])
    slots = rate_ref.shape[0] * MINI
    for sequence in range(rows // slots):
        mine = (lane_ref[16:17] == float(sequence)).astype(full)
        spread = rate_ref[:, 0, :] * rest_ref[...] * mine
        spread = (spread[:, None, :] * lane_ref[:MINI][None]).reshape(slots, 384).astype(low)
        dlog_ref[slots * sequence : slots * (sequence + 1)] = dot_nt(spread, chosen_ref[...]).astype(low)
    eta = dot_nn(turned, dlog_ref[...])
    inner = dw_ref[:, :width] + dw_ref[:, width:]
    fixed = jnp.concatenate(
        [inner, jnp.zeros((VECTORS - HEAD, width), full), sums_ref[...], jnp.zeros((PAIR - VECTORS - 8, width), full)], axis=0
    )
    lane = lax.broadcasted_iota(jnp.int32, (HEAD, PAIR), 1)
    chosen = chosen_ref[...].astype(full)
    bias = jnp.sum(rate_ref[:, 0, :] * rest_ref[...], axis=0, keepdims=True)
    held[:, width : width + PAIR] = eta + fixed.T
    bias = jnp.sum(chosen * bias, axis=1, keepdims=True)
    square = jnp.broadcast_to(bias, (PAIR, PAIR)).T[:1]
    bias_row = pltpu.roll(square, BIAS - ETA, axis=1)
    bias_row = jnp.where((lane[:1] >= BIAS) & (lane[:1] < BIAS + 12), bias_row, 0.0)
    lanes_of = [db_ref[...] * (1.0 / MINI), dgain_ref[...] + exchange(dgain_query_ref[...]), dshift_ref[...] + exchange(dshift_query_ref[...])]
    for head in range(12):
        here = pl.ds(HEAD * head, HEAD)
        mask = chosen[ETA + head : ETA + head + 1]
        total = held[here, width : width + PAIR] + bias_row
        for place, values in enumerate(lanes_of):
            column = jnp.sum(values * mask, axis=1, keepdims=True)
            total = total + jnp.where(lane == VECTORS + place, column, 0.0)
        high = total.astype(low).astype(full)
        held[here, width : width + PAIR] = high
        held[here, width + PAIR :] = total - high
    store_blocks(table_ref, sent_ref, kept_ref, held, block)


def last_grads(table, normed, grads, sums, state, rate_back, rest, devices):
    rows, width = normed.shape
    lane, chosen = lane_constants()
    spec = lambda array: constant_spec(*array.shape, buffers=1)
    others = (sums, *state, rate_back, rest, lane, chosen)
    shape = jax.ShapeDtypeStruct
    out = constant_spec(width // 2, width + 2 * PAIR, buffers=1)
    return call(
        lambda *refs: last_kernel(width // devices, *refs), "last_grads", (1,), 1,
        [spec(normed), constant_spec(rows, width, at=2, buffers=1)] + [spec(array) for array in others],
        [out, out, constant_spec(rows, PAIR, buffers=1)],
        [shape((width // 2, width + 2 * PAIR), low)] * 2 + [shape((rows, PAIR), low)],
        [pltpu.VMEM((width, width + 2 * PAIR), full)], 3_000_000_000, (table, normed, grads, *others),
    )


def finish_kernel(tokens_ref, dfirst_ref, dqkv_ref, dgate_ref, dlog_ref, w_ref, small_ref, w_gate_ref, vec_ref, out_ref):
    dnormed = dot_nt(dqkv_ref[...], w_ref[...]) + dot_nt(dgate_ref[...], w_gate_ref[...]) + dot_nt(dlog_ref[...], small_ref[...])
    values = tokens_ref[...].astype(full)
    scale = lax.rsqrt(row_mean(values * values) + epsilon)
    dnormed = dnormed * vec_ref[3:4]
    back = scale * dnormed - values * (scale * scale * scale * row_mean(values * dnormed))
    out_ref[...] = (dfirst_ref[...] + back).astype(low)


def finish(tokens, dfirst, dqkv, dgate, dlog, whole, vectors, at, before):
    rows, width = tokens.shape
    tile = rows // 2
    row = lambda n: pl.BlockSpec((tile, n), lambda step: (at, 0))
    arrays = [tokens, dfirst, dqkv, dgate, dlog, whole, whole, whole, vectors]
    extra = [] if before is None else [before]
    return pl.pallas_call(
        lambda *refs: finish_kernel(*refs[:9], refs[-1]),
        grid=(1,),
        in_specs=[row(width), row(width), row(3 * width), row(width), row(PAIR), constant_spec(width, 3 * width, buffers=1),
                  constant_spec(width, PAIR, at=5 * width // PAIR, buffers=1), constant_spec(width, width, at=3, buffers=1),
                  constant_spec(8, width)] + [pl.BlockSpec(memory_space=pl.ANY)] * len(extra),
        out_specs=row(width),
        out_shape=jax.ShapeDtypeStruct((rows, width), low),
        input_output_aliases={len(arrays): 0} if extra else {},
        compiler_params=pltpu.CompilerParams(vmem_limit_bytes=60 * 1024 * 1024),
        cost_estimate=pl.CostEstimate(flops=3_000_000_000, bytes_accessed=10_000_000, transcendentals=0),
        name="finish",
    )(*arrays, *extra)


class Links:
    def __init__(self, dp, fsdp):
        self.axes = ("dp", "fsdp")
        self.count = dp * fsdp
        self.core = fsdp
        self.far = fsdp // 2
        bits = [1 << place for place in reversed(range(self.count.bit_length() - 1))]
        self.others = [bit for bit in bits if bit != self.core]
        near = [bit for bit in reversed(self.others) if bit != self.far]
        near = near[:1] + near[:0:-1]
        turned = [near[turn:] + near[:turn] for turn in range(3)]
        self.orders = {"split": [turned[0], turned[2]], "shared": [turned[1]] * 2}
        self.phases = self.near = len(near)
        self.me = lax.axis_index("dp") * fsdp + lax.axis_index("fsdp")
        self.side = (self.me // self.core) % 2

    def swap(self, values, bits):
        pairs = [(place, place ^ bits[(place // self.core) % 2]) for place in range(self.count)]
        return lax.ppermute(values, self.axes, pairs)

    def one(self, bit):
        return (self.me // bit) % 2

    def join(self, held, bits):
        got = self.swap(held, bits)
        mine = jnp.where(self.side == 0, self.one(bits[0]), self.one(bits[1])) == 0
        return jnp.stack([jnp.where(mine, held, got), jnp.where(mine, got, held)])

    def gather(self, pieces, kinds):
        orders = [[[self.far] + order for order in self.orders[kind]] for kind in kinds]
        held = list(pieces)
        for phase in range(len(orders[0][0])):
            held = [self.join(array, [order[phase] for order in pair]) for array, pair in zip(held, orders)]
            changed = yield held
            held = held if changed is None else changed
        above = [bit for bit in self.others if bit > self.core]
        whole = []
        for array, pair in zip(held, orders):
            got = self.swap(array, [self.core] * 2)
            mine = self.side == 0
            cores = [jnp.where(mine, array, got), jnp.where(mine, got, array)]
            placed = []
            for half, order in zip(cores, pair):
                have = order[::-1]
                placed.append(half.transpose([have.index(bit) for bit in self.others] + [len(have), len(have) + 1]))
            whole.append(jnp.stack(placed, axis=len(above)).reshape(-1, array.shape[-1]))
        yield whole

    def gather_blocks(self, pieces, kinds, pairs, whole_last):
        held = list(pieces)
        orders = [self.orders[kind] for kind in kinds]
        count = self.phases

        def ready(array, place):
            rows = pieces[place].shape[0]
            if not pairs[place]:
                return array.reshape((-1, rows) + array.shape[-1:])
            turned = []
            stacked = array.ndim - 2
            for order in orders[place]:
                have = ([self.far] + order)[:stacked][::-1]
                at = have.index(1)
                turned.append(array.transpose([axis for axis in range(stacked) if axis != at] + [at, stacked, stacked + 1]))
            array = jnp.where(self.side == 0, turned[0], turned[1])
            return array.reshape((-1, 2 * rows) + array.shape[-1:])

        for phase in range(count):
            for place, pair in enumerate(orders):
                held[place] = self.join(held[place], [self.far] * 2 if phase == 0 else [order[phase - 1] for order in pair])
                if phase == count - 1 and not whole_last[place]:
                    held[place] = ready(held[place], place)
            changed = yield held
            held = held if changed is None else changed
        buffers = []
        for place, pair in enumerate(orders):
            last = [order[-1] for order in pair]
            if whole_last[place]:
                buffers.append([ready(self.join(held[place], last), place)])
            else:
                buffers.append([held[place], self.swap(held[place], last), self.swap(held[place], [self.core] * 2)])
        changed = yield buffers
        buffers = buffers if changed is None else changed
        buffers = [list(group) + [self.swap(group[0 if whole else 1], [self.core] * 2)] for group, whole in zip(buffers, whole_last)]

        def places(bits, device, unit):
            found = []
            clear = device & ~(sum(bits) + unit - 1)
            for place in range(1 << len(bits)):
                found.append((clear + sum(bit for at, bit in enumerate(bits) if place >> (len(bits) - 1 - at) & 1)) // unit)
            return jnp.stack(found)

        done = []
        for place, pair in enumerate(orders):
            unit = 2 if pairs[place] else 1
            table = []
            for core, last in ((0, 0), (self.core, 0)) if whole_last[place] else ((0, 0), (0, 1), (self.core, 0), (self.core, 1)):
                by_side = []
                for order in pair:
                    have = ([self.far] + order)[::-1] if whole_last[place] else ([self.far] + order[:-1])[::-1]
                    by_side.append(places([bit for bit in have if bit >= unit], self.me ^ core ^ (order[-1] if last else 0), unit))
                own = self.side if core == 0 else 1 - self.side
                table.append(jnp.where(own == 0, by_side[0], by_side[1]))
            done.append((buffers[place], jnp.concatenate(table).astype(jnp.int32)))
        yield done

    def table(self, kind):
        half = []
        for side in range(2):
            masks = self.orders[kind][side] + [self.far]
            half.append(np.array([sum(bit for at, bit in enumerate(masks) if place >> (len(masks) - 1 - at) & 1)
                                  for place in range(self.count // 2)], np.int32))
        keep = jnp.where(self.side == 0, half[0], half[1])
        send = jnp.where(self.side == 0, half[1], half[0])
        return jnp.concatenate([self.me ^ keep, self.me ^ self.core ^ send]).astype(jnp.int32)

    def exchange_cores(self, pair):
        return pair[1], self.swap(pair[0], [self.core] * 2)


def tie(*groups):
    flat, tree = jax.tree.flatten(groups)
    return jax.tree.unflatten(tree, lax.optimization_barrier(flat))


def halves(array):
    half = array.shape[0] // 2
    return array[half:], array[:half]


def tie(*groups):
    flat, tree = jax.tree.flatten(groups)
    return jax.tree.unflatten(tree, lax.optimization_barrier(flat))


def halves(array):
    half = array.shape[0] // 2
    return array[half:], array[:half]


def in_order(table, pair, rows):
    if rows % 8 == 0:
        return pair
    whole = jnp.concatenate([pair[1], pair[0]], axis=0)
    return halves(whole.reshape((-1, rows) + whole.shape[1:])[table].reshape(whole.shape))


def body(dp, fsdp, tokens, lengths, cotangent, mixer_in, w_eta, eta_bias, w_out, inner_w, inner_b, ttt_gain, ttt_shift,
         norm_one, post_gain, post_shift, w_gate_up, w_down, norm_two):
    links = Links(dp, fsdp)
    devices = dp * fsdp
    micro, slots, width = tokens.shape
    rows = micro * slots
    heads = eta_bias.shape[0]
    head = width // heads
    hidden = w_gate_up.shape[1] // 2
    device_rows = width // devices
    table, shared = links.table("split"), links.table("shared")
    zeros = lambda columns: jnp.zeros((device_rows, columns), low)

    vectors = jnp.stack([inner_b, ttt_gain, ttt_shift, norm_one, post_gain, post_shift, norm_two])
    vectors = dot_tn(vectors, jnp.eye(7, PAIR, VECTORS, dtype=low)).astype(low)
    small = jnp.concatenate([inner_w, w_eta, zeros(PAIR - ETA - heads)], axis=1) + vectors
    cut = 21 * PAIR
    pieces = [mixer_in[:, :cut], jnp.concatenate([mixer_in[:, cut:], w_out, small], axis=1)]
    rest = [w_gate_up, w_down]
    kinds = ["split", "shared"]
    aligned = device_rows % 8 == 0
    if aligned:
        mixer_phases = links.gather_blocks(pieces, kinds, [True, True], [False, True])
    else:
        mixer_phases = links.gather(pieces, kinds)
    places = lax.broadcasted_iota(jnp.int32, (micro, slots), 1)
    live = places < lengths
    upstream = jnp.where(live[..., None], cotangent, jnp.zeros_like(cotangent)).reshape(rows, width)
    held = next(mixer_phases)
    for _ in range(links.phases - 2):
        held = mixer_phases.send(held)
    held, rest, upstream = tie(held, rest, upstream)
    rest_phases = links.gather_blocks(rest, kinds, [True, False], [False, False]) if aligned else links.gather(rest, kinds)
    held, rest = mixer_phases.send(held), next(rest_phases)
    held, rest = tie(held, rest)
    held, rest = mixer_phases.send(held), rest_phases.send(rest)
    held = mixer_phases.send(held)
    as_blocks = lambda arrays: [([array[None]], jnp.zeros((1,), jnp.int32)) for array in arrays]
    early, late = held if aligned else as_blocks(held)

    inputs = tokens.reshape(rows, width)
    bias_row = jnp.pad(eta_bias.astype(full), (ETA, PAIR - ETA - heads)).reshape(1, PAIR)
    early, late, rest = tie(early, late, rest)
    rest = rest_phases.send(rest)
    whole, projected, normed, rate_lanes, rest_lanes, start_w, start_b, gain_lanes, shift_lanes, vec_rows = project(
        lengths.reshape(micro), inputs, early, late, bias_row
    )
    projected = projected.reshape(micro, slots, -1)
    rate_lanes, rest = tie(rate_lanes, rest)
    rest = rest_phases.send(rest)
    inner, saved = ttt_forward(projected, rate_lanes, [start_w, start_b], gain_lanes, shift_lanes)
    inner = inner.reshape(rows, width)
    inner, rest = tie(inner, rest)
    rest = drain(rest_phases, rest)
    if not aligned:
        rest = as_blocks(rest)
    gate, mixed, first, second = post(inner, normed, inputs, whole, vec_rows)
    block_out, dsecond, large_sent, large_kept, *natural = ffn(table, shared, second, first, upstream, *rest, devices, dp)
    down_rows = hidden // devices
    unit = min(8, device_rows // 3)
    if not aligned:
        natural = natural[0].reshape(devices, -1, unit, 3, width // 3).transpose(0, 3, 2, 1, 4).reshape(width, hidden)
        pairs = in_order(table, (large_sent, large_kept), device_rows), in_order(shared, halves(natural), device_rows)
        large_sent, large_kept = (jnp.concatenate(pair, axis=1) for pair in zip(*pairs))
    large = links.exchange_cores((large_sent, large_kept))
    dfirst, dgate, dinner, dfirst_low, sums = post_back(dsecond, first, upstream, inner, gate, whole, vec_rows)
    middle = middle_grads(table, mixed, dfirst_low, normed, dgate, devices)
    middle = links.exchange_cores(in_order(table, tuple(middle), device_rows))
    dinner, large, middle = tie(dinner, large, middle)
    large, middle = list(large), list(middle)
    whole_rows = width // 2
    first_sum = Scatter(
        links, [[(large, 0, 2 * hidden), (middle, 0, 2 * width)], [(large, 2 * hidden, hidden)]], whole_rows, 2
    )
    first_sum.fold()
    dinner = first_sum.tied(dinner)
    first_sum.send()
    dinner = dinner.reshape(micro, slots, width)
    dqkv, rate_late, state = ttt_backward(projected, dinner, rate_lanes, saved, None, gain_lanes, 4, slots // MINI, None)
    dqkv, state = first_sum.tied(dqkv, state)
    first_sum.fold()
    dqkv, state = first_sum.tied(dqkv, state)
    first_sum.send()
    dqkv, rate_early, state = ttt_backward(projected, dinner, rate_lanes, saved, state, gain_lanes, 0, 4, dqkv)
    dqkv = dqkv.reshape(rows, 3 * width)
    rate_back = jnp.concatenate([rate_early, rate_late], axis=0)
    early = weight_grads(table, normed, dqkv, devices)
    dqkv, early = first_sum.tied(dqkv, list(early))
    first_sum.fold()
    dqkv, early = first_sum.tied(dqkv, early)
    first_sum.send()
    early = links.exchange_cores(in_order(table, tuple(early), device_rows))
    *late, dlog = last_grads(shared, normed, dqkv, sums, state, rate_back, rest_lanes, devices)
    late, dlog, early = first_sum.tied(list(late), dlog, early)
    late = links.exchange_cores(in_order(shared, tuple(late), device_rows))
    first_sum.fold()
    late = first_sum.tied(late)
    first_sum.send()
    second_sum = Scatter(
        links, [[(list(early), 0, 2 * width)], [(list(late), 0, width + 2 * PAIR)]], whole_rows, 1, PAIR
    )
    second_sum.fold()
    dlog = second_sum.tied(dlog)
    second_sum.send()
    grad_tokens = None
    for half in range(2):
        grad_tokens = finish(inputs, dfirst, dqkv, dgate, dlog, whole, vec_rows, half, grad_tokens)
        grad_tokens = second_sum.tied(grad_tokens)
        second_sum.fold()
        second_sum.send()
    early, late = second_sum.result()
    large, down = first_sum.result()
    part = hidden // dp
    large = large.reshape(device_rows, 2, -1)
    both = large[:, :, :hidden].reshape(device_rows, dp, 2, part).transpose(0, 2, 1, 3).reshape(device_rows, 2 * hidden)
    middle = large[:, :, hidden:].reshape(device_rows, 2 * width)
    out_small = late[:, width : width + PAIR] + late[:, width + PAIR :]
    out_out, out_gate_in = middle[:, :width], middle[:, width:]
    out_mixer = jnp.concatenate([early, late[:, :width], out_gate_in], axis=1)
    out_eta = out_small[:, ETA : ETA + heads]
    out_norm_one = jnp.sum(mixer_in.astype(full) * out_mixer, axis=1) + jnp.sum(w_eta.astype(full) * out_eta, axis=1)
    out_norm_one = out_norm_one / norm_one.astype(full)
    out_inner_b, out_gain, out_shift, _, out_post_gain, out_post_shift, out_norm_two = (
        out_small[:, VECTORS + place] for place in range(7)
    )
    return (
        block_out.reshape(tokens.shape),
        grad_tokens.reshape(tokens.shape),
        out_mixer,
        out_eta,
        out_small[0, BIAS : BIAS + heads],
        out_out,
        out_small[:, :head],
        out_inner_b,
        out_gain,
        out_shift,
        out_norm_one,
        out_post_gain,
        out_post_shift,
        both,
        down.reshape(3, unit, -1, width // 3).transpose(2, 1, 0, 3).reshape(down_rows, width),
        out_norm_two,
    )


def drain(phases, arrays):
    try:
        while True:
            arrays = phases.send(arrays)
    except StopIteration:
        return arrays


def solution(mesh):
    split = ("dp", "fsdp")
    row, vector, token = P(split, None), P(split), P(None, split, None)
    dp, fsdp = mesh.shape["dp"], mesh.shape["fsdp"]
    return jax.shard_map(
        lambda *arrays: body(dp, fsdp, *arrays),
        mesh=mesh,
        in_specs=(token, P(None, split), token, row, row, P(), row, row) + (vector,) * 6 + (row, row, vector),
        out_specs=(token, token, row, row, P(), row, row) + (vector,) * 6 + (row, row, vector),
        check_vma=False,
    )
```

```python
import jax
import jax.numpy as jnp
from jax import lax
from jax.experimental import pallas as pl
from jax.experimental.pallas import tpu as pltpu
from jax.sharding import PartitionSpec as P
import numpy as np

MINI = 16
HEAD = 64
PAIR = 2 * HEAD
epsilon = 1e-06
low = jnp.bfloat16
full = jnp.float32


def dot_nn(former, latter):
    return lax.dot_general(former, latter, (((1,), (0,)), ((), ())), preferred_element_type=full)


def dot_nt(former, latter):
    return lax.dot_general(former, latter, (((1,), (1,)), ((), ())), preferred_element_type=full)


def tile_of(rows, at):
    return rows[:, PAIR * at : PAIR * (at + 1)]


def key_row(group, side, tile):
    return HEAD * group + 32 * side + MINI * tile


def query_row(group, side, tile):
    return key_row(1 - group, side, tile)


def expand(rows, sides):
    zero = jnp.zeros((MINI, PAIR), rows.dtype)
    blocks = []
    for side in range(2):
        for at in range(2):
            kept = tile_of(rows, at) * sides[side]
            blocks.append(jnp.concatenate([kept if other == at else zero for other in range(2)], axis=1))
    return jnp.concatenate(blocks, axis=0)


def expand_both(queries, keys, sides):
    width = 2 * PAIR
    blocks = [(expand(keys[:, width * group : width * (group + 1)], sides), expand(queries[:, width * group : width * (group + 1)], sides))
              for group in range(2)]
    return blocks, (jnp.concatenate(blocks[0], axis=0), jnp.concatenate(blocks[1][::-1], axis=0))


def to_feature(rows, first_side, groups):
    tiles = [tile_of(rows, 2 * group + at) for group in groups for _ in range(2) for at in range(2)]
    stacked = jnp.concatenate(tiles, axis=0).T
    return jnp.where(first_side, stacked[:HEAD], stacked[HEAD:])


def to_rows(columns, left, place):
    turned = jnp.concatenate([columns, columns], axis=0).T
    pick = lambda group, side, at: turned[place(group, side, at) : place(group, side, at) + MINI]
    return jnp.concatenate([jnp.where(left, pick(group, 0, at), pick(group, 1, at)) for group in range(2) for at in range(2)], axis=1)


def exchange(values):
    half = [values[:, HEAD * at : HEAD * (at + 1)] for at in range(values.shape[1] // HEAD)]
    return jnp.concatenate([half[at ^ 1] for at in range(len(half))], axis=1)


def mean_rows(values):
    return jnp.sum(values, axis=0, keepdims=True) * (1.0 / values.shape[0])


def both_sequences(ref, rows, base, width):
    return jnp.concatenate([ref[0, rows, base : base + width], ref[1, rows, base : base + width]], axis=1)


def store_sequences(ref, rows, base, width, pieces, kind):
    whole = jnp.concatenate(pieces, axis=1)
    ref[0, rows, base : base + width] = whole[:, :width].astype(kind)
    ref[1, rows, base : base + width] = whole[:, width:].astype(kind)


def read_constants(low_ref, full_ref):
    sides = [low_ref[0:MINI], low_ref[MINI : 2 * MINI]]
    same, crossed = low_ref[32:160], low_ref[160:288]
    return sides, same, crossed, full_ref[0:MINI], full_ref[16:144], full_ref[144:272]


def lane_masks(rows=HEAD, width=3 * PAIR):
    lane = lax.broadcasted_iota(jnp.int32, (rows, width), 1)
    return lane % PAIR < HEAD, lane % HEAD < 32


PARTS = range(3)


def thin(part):
    return slice(PAIR * part, PAIR * (part + 1))


def wide(part):
    return slice(4 * PAIR * part, 4 * PAIR * (part + 1))


def lanes(pieces):
    return jnp.concatenate(pieces, axis=1)


def ttt_forward_kernel(steps, q_ref, k_ref, v_ref, rate_ref, w0_ref, b0_ref, gain_ref, shift_ref, low_ref, full_ref,
                       out_ref, w_ref, xh_ref, h_ref, grs_ref, xb_ref, stat_ref, score_ref, w_run, b_run, gain_query, shift_query):
    width = 768

    @pl.when(pl.program_id(0) == 0)
    def _():
        w_run[...] = w0_ref[...]
        b_run[...] = b0_ref[...]
        gain_query[...] = exchange(gain_ref[...])
        shift_query[...] = exchange(shift_ref[...])

    sides, same, crossed, tri, _, _ = read_constants(low_ref, full_ref)
    left, first_side = lane_masks()
    left_one, first_one = left[:, :PAIR], first_side[:, :PAIR]
    tri = lanes([tri] * 3)

    def begin(at):
        rows = slice(at * MINI, (at + 1) * MINI)
        queries = both_sequences(q_ref, rows, 0, width)
        keys = both_sequences(k_ref, rows, 0, width)
        targets = both_sequences(v_ref, rows, 0, width) - keys
        query_low, key_low = queries.astype(low), keys.astype(low)
        expanded = [expand_both(query_low[:, wide(part)], key_low[:, wide(part)], sides) for part in PARTS]
        target = lanes([to_feature(targets[:, wide(part)], first_one, (0, 1)) for part in PARTS])
        return rows, queries, query_low, expanded, target

    def multiply(at, started, weights):
        _, _, query_low, expanded, _ = started
        products = []
        for part in PARTS:
            weight_low = weights[part].astype(low)
            w_ref[at, :, wide(part)] = weight_low
            for group in range(2):
                here = slice(2 * PAIR * group, 2 * PAIR * (group + 1))
                rows = jnp.concatenate([weight_low[:, here], query_low[:, wide(part)][:, here]], axis=0)
                products.append(dot_nt(rows, expanded[part][1][group]))
        return lanes(products[::2]), lanes(products[1::2])

    def finish(at, started, kept):
        rows, queries = started[:2]
        inner_grad, mixing, updated = kept
        inner_grad_low = inner_grad.astype(low)
        moved = []
        for part in PARTS:
            mixing_block = jnp.concatenate([mixing[:, thin(part)]] * 8, axis=0) * crossed
            moved.append(dot_nt(inner_grad_low[:, thin(part)], mixing_block))
        updated = updated - lanes(moved)
        updated = updated - mean_rows(updated)
        updated_inverse = lax.rsqrt(mean_rows(updated * updated) + epsilon)
        updated = updated * updated_inverse
        xb_ref[at] = updated
        stat_ref[at, 3:4] = updated_inverse
        updated = updated * gain_query[...] + shift_query[...]
        result = queries + lanes([to_rows(updated[:, thin(part)], left_one[:MINI], query_row) for part in PARTS])
        out_ref[0, rows, :] = result[:, :width]
        out_ref[1, rows, :] = result[:, width:]

    weights = [w_run[:, wide(part)] for part in PARTS]
    offset = b_run[...]
    started = begin(0)
    pending = None
    for at in range(steps):
        first, second = multiply(at, started, weights)
        if pending is not None:
            finish(*pending)
        gains, shifts = gain_ref[...], shift_ref[...]
        rate = rate_ref[at]
        _, _, _, expanded, target = started
        hidden = jnp.where(left, first[:HEAD], second[:HEAD]) + offset
        scores = jnp.where(left[:MINI], first[HEAD:], second[HEAD:]) + 1.0
        updated = jnp.where(left, second[:HEAD], first[:HEAD]) + exchange(offset)
        centred = hidden - mean_rows(hidden)
        inverse = lax.rsqrt(mean_rows(centred * centred) + epsilon)
        normed = centred * inverse
        held = gains * normed + (shifts - target)
        residual = held * gains
        residual_mean = mean_rows(residual)
        cross = mean_rows(residual * normed)
        inner_grad = (residual - residual_mean - normed * cross) * inverse
        scaled = inner_grad * (rate * (1.0 / MINI))
        scaled_low = scaled.astype(low)
        scaled_other = exchange(scaled).astype(low)
        xh_ref[at] = normed
        h_ref[at] = held
        grs_ref[at] = scaled
        stat_ref[at, 0:1] = inverse
        stat_ref[at, 1:2] = residual_mean
        stat_ref[at, 2:3] = cross
        score_ref[at] = scores
        changed = []
        for part in PARTS:
            blocks = expanded[part][0]
            change = [dot_nn(scaled_low[:, thin(part)][:, :HEAD], blocks[0][0]),
                      dot_nn(scaled_other[:, thin(part)][:, :HEAD], blocks[1][0])]
            changed.append(weights[part] - lanes(change))
        weights = changed
        offset = offset - lanes([dot_nn(scaled_low[:, thin(part)], same) for part in PARTS])
        pending = (at, started, (inner_grad, (tri * rate * scores).astype(low), updated))
        if at + 1 < steps:
            started = begin(at + 1)
    finish(*pending)
    for part in PARTS:
        w_run[:, wide(part)] = weights[part]
    b_run[...] = offset


def ttt_backward_kernel(steps, carried, q_ref, k_ref, dout_ref, rate_ref, w_ref, xh_ref, h_ref, grs_ref, xb_ref, stat_ref, score_ref,
                        gain_ref, low_ref, full_ref, *refs):
    states, refs = (refs[:6], refs[6:]) if carried else (None, refs)
    grad_ref, rdr_ref, dw_ref, db_ref, dgain_ref, dshift_ref, dgain_query_ref, dshift_query_ref, gain_query = refs[-9:]
    width = 768

    @pl.when(pl.program_id(0) == 0)
    def _():
        for place, ref in enumerate((dw_ref, db_ref, dgain_ref, dshift_ref, dgain_query_ref, dshift_query_ref)):
            ref[...] = states[place][...] if carried else jnp.zeros_like(ref)
        gain_query[...] = exchange(gain_ref[...])

    sides, same, crossed, tri, scale, scale_turned = read_constants(low_ref, full_ref)
    left, first_side = lane_masks()
    left_one, first_one = left[:, :PAIR], first_side[:, :PAIR]
    left_rows = left_one[:MINI]
    left_square = lax.broadcasted_iota(jnp.int32, (PAIR, PAIR), 1) < HEAD
    zero = jnp.zeros((MINI, PAIR), full)
    tri = lanes([tri] * 3)

    def begin(at):
        rows = slice(at * MINI, (at + 1) * MINI)
        query_low = both_sequences(q_ref, rows, 0, width).astype(low)
        key_low = both_sequences(k_ref, rows, 0, width).astype(low)
        douts = both_sequences(dout_ref, rows, 0, width)
        expanded = [expand_both(query_low[:, wide(part)], key_low[:, wide(part)], sides) for part in PARTS]
        mixing = (tri * rate_ref[at] * score_ref[at]).astype(low)
        dout = lanes([to_feature(douts[:, wide(part)], first_one, (1, 0)) for part in PARTS])
        updated = xb_ref[at]
        dupdated = dout * gain_query[...]
        dupdated = stat_ref[at, 3:4] * (dupdated - mean_rows(dupdated) - updated * mean_rows(dupdated * updated))
        dgain_query_ref[...] += dout * updated
        dshift_query_ref[...] += dout
        dupdated_low = dupdated.astype(low)
        mixed = []
        for part in PARTS:
            mixing_block = jnp.concatenate([mixing[:, thin(part)]] * 8, axis=0) * crossed
            mixed.append(dot_nn(dupdated_low[:, thin(part)], mixing_block))
        return rows, douts, expanded, dupdated, dupdated_low, lanes(mixed)

    def finish(at, started, kept):
        rows, douts, expanded, dupdated, dupdated_low, _ = started
        dhidden, dtarget, dweights_low, rate_part = kept
        scaled = -grs_ref[at]
        scaled_low = scaled.astype(low)
        scores = score_ref[at]
        none = jnp.zeros((HEAD, PAIR), low)
        turned_low, turned_query, query_rows, dmixes, dmixes_turned = [], [], [], [], []
        for part in PARTS:
            turned_low.append(jnp.concatenate([dhidden[:, thin(part)], scaled[:, thin(part)]], axis=0).T.astype(low))
            turned_query.append(jnp.concatenate([dupdated[:, thin(part)], dtarget[:, thin(part)]], axis=0).T)
            query_rows.append(jnp.where(left_square, turned_query[part], 0.0).astype(low))
        for part in PARTS:
            dmix = dot_nn(query_rows[part][:, :HEAD], scaled_low[:, thin(part)]) * scale
            dmix_turned = dot_nn(turned_low[part], jnp.concatenate([none, dupdated_low[:, thin(part)]], axis=0)) * scale_turned
            dmixes.append(sum(dmix[MINI * row : MINI * (row + 1)] for row in range(8)))
            dmixes_turned.append(sum(dmix_turned[MINI * row : MINI * (row + 1)] for row in range(8)))
        rdr_ref[at] = rate_part + jnp.sum(lanes(dmixes) * scores, axis=0, keepdims=True)
        query_grads, key_grads, value_grads = [], [], []
        for part in PARTS:
            weight_low = w_ref[at, :, wide(part)]
            for group in range(2):
                keep_key, keep_query = (left_rows, ~left_rows) if group == 0 else (~left_rows, left_rows)
                key_side = jnp.where(keep_query, dmixes_turned[part], zero).astype(low)
                query_side = jnp.where(keep_key, dmixes[part], zero).astype(low)
                extra = jnp.concatenate([key_side, key_side, query_side, query_side], axis=0)
                for at_tile in range(2):
                    tile = 2 * group + at_tile
                    place = [key_row(group, side, at_tile) for side in range(2)]
                    place_query = [query_row(group, side, at_tile) for side in range(2)]
                    held_rows = jnp.concatenate(
                        [turned_low[part][row : row + MINI] for row in place]
                        + [query_rows[part][row : row + MINI] for row in place_query],
                        axis=0,
                    )
                    product = dot_nn(
                        jnp.concatenate([held_rows, extra], axis=1),
                        jnp.concatenate(
                            [tile_of(weight_low, tile), tile_of(dweights_low[part], tile), tile_of(expanded[part][1][group], at_tile)],
                            axis=0,
                        ),
                    )
                    dvalue = jnp.where(
                        left_rows,
                        exchange(turned_query[part][place[0] : place[0] + MINI]),
                        turned_query[part][place[1] : place[1] + MINI],
                    )
                    key_grads.append(dvalue + jnp.where(left_rows, product[:MINI], product[MINI : 2 * MINI]))
                    query_grads.append(
                        tile_of(douts[:, wide(part)], tile) + jnp.where(left_rows, product[2 * MINI : 3 * MINI], product[3 * MINI :])
                    )
                    value_grads.append(-dvalue)
        store_sequences(grad_ref, rows, 0, width, query_grads, low)
        store_sequences(grad_ref, rows, width, width, key_grads, low)
        store_sequences(grad_ref, rows, 2 * width, width, value_grads, low)

    dweights = [dw_ref[:, wide(part)] for part in PARTS]
    doffset = db_ref[...]
    started = begin(steps - 1)
    pending = None
    for at in reversed(range(steps)):
        _, _, expanded, dupdated, _, mixed = started
        dweights_low = [dweight.astype(low) for dweight in dweights]
        key_dw = []
        for part in PARTS:
            blocks = expanded[part][0]
            key_dw.append(dot_nt(dweights_low[part][:, : 2 * PAIR], blocks[0][0]))
            key_dw.append(dot_nt(dweights_low[part][:, 2 * PAIR :], blocks[1][0]))
        key_dw = lanes(key_dw) + doffset
        if pending is not None:
            finish(*pending)
        upcoming = begin(at - 1) if at > 0 else None
        gains = gain_ref[...]
        rate = rate_ref[at]
        normed, held, scaled = xh_ref[at], h_ref[at], grs_ref[at]
        inverse, residual_mean, cross = (stat_ref[at, row : row + 1] for row in range(3))
        grad_in = -mixed - (rate * (1.0 / MINI)) * key_dw
        rate_part = -jnp.sum(scaled * key_dw, axis=0, keepdims=True)
        residual = held * gains
        in_mean = mean_rows(grad_in)
        in_cross = mean_rows(grad_in * normed)
        in_held = inverse * (mean_rows(grad_in * residual) - residual_mean * in_mean - cross * in_cross)
        dresidual = inverse * (grad_in - in_mean - normed * in_cross)
        dtarget = dresidual * gains
        dnormed = dtarget * gains - inverse * (grad_in * cross + in_cross * residual)
        dhidden = inverse * (dnormed - mean_rows(dnormed) - normed * (mean_rows(dnormed * normed) + in_held))
        dgain_ref[...] += dresidual * (held + gains * normed)
        dshift_ref[...] += dtarget
        to_first = jnp.where(left, dhidden, dupdated).astype(low)
        to_second = jnp.where(left, dupdated, dhidden).astype(low)
        changed = []
        for part in PARTS:
            pairs = expanded[part][1]
            change = [dot_nn(to_first[:, thin(part)], pairs[0]), dot_nn(to_second[:, thin(part)], pairs[1])]
            changed.append(dweights[part] + lanes(change))
        total_low = (exchange(dupdated) + dhidden).astype(low)
        doffset = doffset + lanes([dot_nn(total_low[:, thin(part)], same) for part in PARTS])
        dweights = changed
        pending = (at, started, (dhidden, dtarget, dweights_low, rate_part))
        started = upcoming
    finish(*pending)
    for part in PARTS:
        dw_ref[:, wide(part)] = dweights[part]
    db_ref[...] = doffset


def ttt_constants():
    lane = np.arange(PAIR)
    row = np.arange(MINI)
    sides = np.concatenate([np.tile(lane < HEAD, (MINI, 1)), np.tile(lane >= HEAD, (MINI, 1))])
    token = lane % MINI
    tri = np.where(token[None] <= row[:, None], 1.0 / (row[:, None] + 1.0), 0.0)
    same = lane[:, None] // MINI == lane[None] // MINI
    crossed = (lane[:, None] + HEAD) % PAIR // MINI == lane[None] // MINI
    scale = np.where(crossed & (token[None] <= token[:, None]), MINI / (token[:, None] + 1.0), 0.0)
    return (
        jnp.asarray(np.concatenate([sides, same, crossed]).astype(np.float32), low),
        jnp.asarray(np.concatenate([tri, scale, scale.T]), full),
    )


def ttt_forward(projected, rates, state, gains, shifts, steps=4):
    count = projected.shape[1] // MINI
    first, begin, end = 0, 0, count
    queries, keys, values = projected, projected, projected
    constants = ttt_constants()
    whole = lambda *shape: pl.BlockSpec(shape, lambda at: (0,) * len(shape))
    column = lambda place: pl.BlockSpec((2, steps * MINI, 768), lambda at, place=place: (0, first + at, place))
    part = column(0)
    saved = lambda *tail: pl.BlockSpec((steps,) + tail, lambda at: (at, 0, 0))
    made = lambda kind, *tail: jax.ShapeDtypeStruct((end - begin,) + tail, kind)
    inputs = [queries, keys, values, rates, *state, gains, shifts, *constants]
    out, *rest = pl.pallas_call(
        lambda *refs: ttt_forward_kernel(steps, *refs),
        grid=((end - begin) // steps,),
        in_specs=[column(0), column(1), column(2), pl.BlockSpec((steps, 1, 384), lambda at: (first + at, 0, 0)), whole(64, 1536), whole(64, 384),
                  whole(64, 384), whole(64, 384), whole(288, 128), whole(272, 128)],
        out_specs=[part, saved(64, 1536), saved(64, 384), saved(64, 384), saved(64, 384), saved(64, 384), saved(8, 384),
                   saved(16, 384)],
        out_shape=[jax.ShapeDtypeStruct((2, count * MINI, 768), full), made(low, 64, 1536), made(full, 64, 384), made(full, 64, 384),
                   made(full, 64, 384), made(full, 64, 384), made(full, 8, 384), made(full, 16, 384)],
        scratch_shapes=[pltpu.VMEM((64, 1536), full)] + [pltpu.VMEM((64, 384), full)] * 3,
        compiler_params=pltpu.CompilerParams(vmem_limit_bytes=60 * 1024 * 1024),
        cost_estimate=pl.CostEstimate(flops=(end - begin) * 1_400_000_000, bytes_accessed=(end - begin) * 1_500_000, transcendentals=0),
        name="ttt_forward",
    )(*inputs)
    return out, rest


def ttt_backward(projected, dout, rates, saved_arrays, state, gains, begin, end, before, steps=4):
    count = projected.shape[1] // MINI
    first, blocks = begin // steps, (end - begin) // steps
    queries, keys = projected, projected
    constants = ttt_constants()
    whole = lambda *shape: pl.BlockSpec(shape, lambda at: (0,) * len(shape))
    part = lambda width, place=0: pl.BlockSpec((2, steps * MINI, width), lambda at: (0, first + blocks - 1 - at, place))
    saved = lambda *tail: pl.BlockSpec((steps,) + tail, lambda at: (first + blocks - 1 - at, 0, 0))
    made = lambda *tail: pl.BlockSpec((steps,) + tail, lambda at: (blocks - 1 - at, 0, 0))
    extra = [] if before is None else [before]
    inputs = [queries, keys, dout, rates, *saved_arrays, gains, *constants, *(state or [])]
    states = [whole(64, 1536)] + [whole(64, 384)] * 5
    grad, rate_back, *sums = pl.pallas_call(
        lambda *refs: ttt_backward_kernel(steps, state is not None, *refs),
        grid=(blocks,),
        in_specs=[part(768), part(768, 1), part(768), saved(1, 384),
                  saved(64, 1536), saved(64, 384), saved(64, 384), saved(64, 384), saved(64, 384), saved(8, 384), saved(16, 384),
                  whole(64, 384), whole(288, 128), whole(272, 128)]
        + (states if state else []) + [pl.BlockSpec(memory_space=pl.ANY)] * len(extra),
        out_specs=[part(2304), made(1, 384)] + states,
        out_shape=[jax.ShapeDtypeStruct((2, count * MINI, 2304), low), jax.ShapeDtypeStruct((end - begin, 1, 384), full)]
        + [jax.ShapeDtypeStruct((64, 1536), full)] + [jax.ShapeDtypeStruct((64, 384), full)] * 5,
        scratch_shapes=[pltpu.VMEM((64, 384), full)],
        input_output_aliases={len(inputs): 0} if extra else {},
        compiler_params=pltpu.CompilerParams(vmem_limit_bytes=60 * 1024 * 1024),
        cost_estimate=pl.CostEstimate(flops=(end - begin) * 2_000_000_000, bytes_accessed=(end - begin) * 1_500_000, transcendentals=0),
        name="ttt_backward",
    )(*inputs, *extra)
    return grad, rate_back, sums


def silu_parts(gate):
    sigma = jax.nn.sigmoid(gate)
    return gate * sigma, sigma * (1.0 + gate * (1.0 - sigma))


def gelu_parts(values):
    slope = 0.7978845608028654
    turn = jnp.tanh(slope * (values + 0.044715 * values * values * values))
    half = 0.5 * (1.0 + turn)
    return values * half, half + 0.5 * values * (1.0 - turn * turn) * slope * (1.0 + 3 * 0.044715 * values * values)


def row_mean(values):
    return jnp.mean(values, axis=-1, keepdims=True)


def dot_tn(former, latter):
    return lax.dot_general(former, latter, (((0,), (0,)), ((), ())), preferred_element_type=full)


def exact_dot(former, latter):
    total = None
    for _ in range(3):
        part = former.astype(low)
        former = former - part.astype(full)
        term = dot_nn(part, latter)
        total = term if total is None else total + term
    return total


def constant_spec(*shape, at=0, buffers=None):
    index = lambda *steps: (0,) * (len(shape) - 1) + (at,)
    if buffers is None:
        return pl.BlockSpec(shape, index)
    return pl.BlockSpec(shape, index, pipeline_mode=pl.Buffered(buffers))


def call(kernel, name, grid, prefetch, in_specs, out_specs, out_shape, scratch, cost, arrays):
    return pl.pallas_call(
        kernel,
        grid_spec=pltpu.PrefetchScalarGridSpec(
            num_scalar_prefetch=prefetch, grid=grid, in_specs=in_specs, out_specs=out_specs, scratch_shapes=scratch
        ),
        out_shape=out_shape,
        compiler_params=pltpu.CompilerParams(vmem_limit_bytes=60 * 1024 * 1024),
        cost_estimate=pl.CostEstimate(flops=cost, bytes_accessed=cost // 500, transcendentals=0),
        name=name,
    )(*arrays)


ETA = 64
VECTORS = 80
BIAS = 96


def lane_table():
    lane = np.arange(384)
    part, group, side, tile, token = lane // 128, lane // 64 % 2, lane // 32 % 2, lane // 16 % 2, lane % 16
    pair = 4 * part + 2 * group + tile
    return token, pair // 6, 2 * (pair % 6) + side


def lane_constants():
    token, sequence, head = lane_table()
    table = np.zeros((32, 384), np.float32)
    table[:MINI] = token[None] == np.arange(MINI)[:, None]
    table[16], table[17] = sequence, token
    chosen = np.zeros((PAIR, 384), np.float32)
    chosen[ETA + head, np.arange(384)] = 1
    return jnp.asarray(table), jnp.asarray(chosen, low)


def block_copies(from_refs, table, to, columns, semaphores, first):
    started = []
    for place, ref in enumerate(from_refs):
        for item in range(ref.shape[0]):
            begin = pl.multiple_of(table[place * ref.shape[0] + item] * ref.shape[1], 16)
            target = to.at[pl.ds(begin, ref.shape[1]), columns]
            started.append(pltpu.make_async_copy(ref.at[item], target, semaphores.at[first + len(started)]))
    return started


def project_kernel(counts, length_ref, early_table_ref, late_table_ref, tokens_ref, bias_ref, table_ref, chosen_ref, *refs):
    early_refs, late_refs, refs = refs[: counts[0]], refs[counts[0] : sum(counts)], refs[sum(counts) :]
    whole_ref, proj_ref, normed_ref, rate_ref, rest_ref, wt_ref, b_ref, gain_ref, shift_ref, vec_ref, semaphores = refs
    at = pl.program_id(0)
    split = 512 // tokens_ref.shape[0]
    wide = proj_ref.shape[1]
    begin_small = whole_ref.shape[1] - PAIR
    cut = early_refs[0].shape[2]

    def copies():
        started = block_copies(early_refs, early_table_ref, whole_ref, slice(0, cut), semaphores, 0)
        return started + block_copies(late_refs, late_table_ref, whole_ref, slice(cut, whole_ref.shape[1]), semaphores, len(started))

    @pl.when(at == 0)
    def _():
        for copy in copies():
            copy.start()
        for copy in copies():
            copy.wait()
        small = whole_ref[:, begin_small:].astype(full)
        turned = small.T
        wt_ref[:, :768] = turned[:HEAD]
        wt_ref[:, 768:] = turned[:HEAD]
        vec_ref[...] = turned[VECTORS : VECTORS + 8]
        for place, ref in enumerate((b_ref, gain_ref, shift_ref)):
            total = jnp.zeros((HEAD, 384), full)
            for head in range(12):
                column = small[HEAD * head : HEAD * (head + 1), VECTORS + place : VECTORS + place + 1]
                total = total + column * chosen_ref[ETA + head : ETA + head + 1].astype(full)
            ref[...] = total
        rate_ref[...] = jnp.zeros_like(rate_ref)
        rest_ref[...] = jnp.zeros_like(rest_ref)

    values = tokens_ref[...].astype(full)
    normed = (values * lax.rsqrt(row_mean(values * values) + epsilon) * vec_ref[3:4]).astype(low)
    normed_ref[...] = normed
    proj_ref[...] = dot_nn(normed, whole_ref[:, :wide])
    last = dot_nn(normed, whole_ref[:, begin_small:])
    spread = exact_dot(last + bias_ref[...], chosen_ref[...])
    blocks = spread.shape[0] // MINI
    spread = jnp.sum(spread.reshape(blocks, MINI, 384) * table_ref[:MINI][None], axis=1)
    sequence, token = table_ref[16:17], table_ref[17:18]
    mine = sequence == (at // split).astype(full)
    sigma = jax.nn.sigmoid(spread)
    begin = (at % split) * blocks
    block = lax.broadcasted_iota(jnp.int32, spread.shape, 0) + begin
    live = (block * MINI).astype(full) + token < length_ref[at // split].astype(full)
    here = pl.ds(begin, blocks)
    rate_ref[here, 0, :] += jnp.where(live & mine, sigma * (1.0 / HEAD), 0.0)
    rest_ref[here, :] += jnp.where(mine, 1.0 - sigma, 0.0)


def project(lengths, tokens, early, late, bias_row):
    rows, width = tokens.shape
    table, chosen = lane_constants()
    tile = rows // 2
    columns = early[0][0].shape[2] + late[0][0].shape[2]
    counts = len(early[0]), len(late[0])
    row = lambda n: pl.BlockSpec((tile, n), lambda at, *_: (at, 0))
    shape = jax.ShapeDtypeStruct
    return call(
        lambda *refs: project_kernel(counts, *refs), "project", (2,), 3,
        [row(width), constant_spec(1, PAIR), constant_spec(32, 384), constant_spec(PAIR, 384)]
        + [pl.BlockSpec(memory_space=pl.ANY)] * sum(counts),
        [constant_spec(width, columns, buffers=1), row(3 * width), row(width), constant_spec(32, 1, 384), constant_spec(32, 384),
         constant_spec(64, 1536)] + [constant_spec(64, 384)] * 3 + [constant_spec(8, width)],
        [shape((width, columns), low), shape((rows, 3 * width), full), shape((rows, width), low), shape((32, 1, 384), full),
         shape((32, 384), full), shape((64, 1536), full)] + [shape((64, 384), full)] * 3 + [shape((8, width), full)],
        [pltpu.SemaphoreType.DMA((early[1].shape[0] + late[1].shape[0],))], 5_000_000_000,
        (lengths, early[1], late[1], tokens, bias_row, table, chosen, *early[0], *late[0]),
    )


def post_kernel(inner_ref, normed_ref, tokens_ref, w_gate_ref, w_out_ref, vec_ref, gate_ref, mixed_ref, first_ref, second_ref):
    gate = dot_nn(normed_ref[...], w_gate_ref[...])
    gate_ref[...] = gate
    inner = inner_ref[...]
    centred = inner - row_mean(inner)
    standard = centred * lax.rsqrt(row_mean(centred * centred) + epsilon)
    mixed = ((standard * vec_ref[4:5] + vec_ref[5:6]) * gelu_parts(gate)[0]).astype(low)
    mixed_ref[...] = mixed
    first = tokens_ref[...].astype(full) + dot_nn(mixed, w_out_ref[...])
    first_ref[...] = first
    second_ref[...] = (first * lax.rsqrt(row_mean(first * first) + epsilon) * vec_ref[6:7]).astype(low)


def post(inner, normed, tokens, whole, vectors):
    rows, width = tokens.shape
    tile = rows // 4
    row = pl.BlockSpec((tile, width), lambda at: (at, 0))
    shape = jax.ShapeDtypeStruct
    return call(
        post_kernel, "post", (4,), 0,
        [row, row, row, constant_spec(width, width, at=3, buffers=1), constant_spec(width, width, at=4, buffers=1), constant_spec(8, width)],
        [row] * 4, [shape((rows, width), kind) for kind in (full, low, full, low)], [], 4_000_000_000,
        (inner, normed, tokens, whole, whole, vectors),
    )


def store_blocks(table_ref, sent_ref, kept_ref, held_ref, block):
    half = kept_ref.shape[0]
    if block % 8:
        kept_ref[...] = held_ref[:half].astype(kept_ref.dtype)
        sent_ref[...] = held_ref[half:].astype(sent_ref.dtype)
        return
    for pair in range(held_ref.shape[0] // (2 * block)):
        rows = [held_ref[pl.ds(pl.multiple_of(table_ref[2 * pair + side] * block, 8), block), :] for side in range(2)]
        begin = 2 * block * pair
        ref, begin = (kept_ref, begin) if begin < half else (sent_ref, begin - half)
        ref[begin : begin + 2 * block, :] = jnp.concatenate(rows, axis=0).astype(ref.dtype)


def ffn_kernel(block, down_block, steps, counts, table_ref, shared_ref, both_table_ref, down_table_ref, second_ref, first_ref, up_ref, *refs):
    both_refs, refs = refs[: counts[0]], refs[counts[0] :]
    down_refs, refs = refs[: counts[1]], refs[counts[1] :]
    aligned = block % 8 == 0
    out_ref, dsecond_ref, sent_ref, kept_ref, *refs = refs
    natural_ref, refs = (None, refs) if aligned else (refs[0], refs[1:])
    turned, total, act, both_low, held, w_both, w_down_all, held_down, semaphores = refs
    at = pl.program_id(0)
    size = act.shape[1]
    hidden = w_down_all.shape[0]

    def copies():
        started = block_copies(both_refs, both_table_ref, w_both, slice(None), semaphores, 0)
        return started + block_copies(down_refs, down_table_ref, w_down_all, slice(None), semaphores, len(started))

    @pl.when(at == 0)
    def _():
        for copy in copies():
            copy.start()
        turned[...] = second_ref[...].T
        total[...] = first_ref[...]
        dsecond_ref[...] = jnp.zeros_like(dsecond_ref)
        for copy in copies():
            copy.wait()

    @pl.when(at < steps)
    def _():
        columns = pl.ds(pl.multiple_of(at * size, PAIR), size)
        w_gate, w_up = w_both[:, columns], w_both[:, pl.ds(pl.multiple_of(hidden + at * size, PAIR), size)]
        w_down = w_down_all[columns, :]
        second, upstream = second_ref[...], up_ref[...]
        cuts = [slice(begin, begin + size // 2) for begin in range(0, size, size // 2)]
        made = [(dot_nn(second, w_gate[:, cut]), dot_nn(second, w_up[:, cut]), dot_nt(upstream, w_down[cut])) for cut in cuts]
        for cut, (gate, up, dact) in zip(cuts, made):
            value, slope = silu_parts(gate)
            act[:, cut] = (value * up).astype(low)
            both_low[:, cut] = (dact * up * slope).astype(low)
            both_low[:, size + cut.start : size + cut.stop] = (dact * value).astype(low)
        total[...] += dot_nn(act[...], w_down)
        dsecond_ref[...] += dot_nt(both_low[:, :size], w_gate) + dot_nt(both_low[:, size:], w_up)
        ddown = dot_tn(act[...], upstream)
        held[...] = dot_nn(turned[...], both_low[...])
        if aligned:
            count = size // down_block
            third = ddown.shape[1] // 3
            for place in range(count):
                mine = ddown[down_block * place : down_block * (place + 1)]
                pieces = [jnp.concatenate([mine[8 * row : 8 * row + 8, third * part : third * (part + 1)] for row in range(down_block // 8)],
                                          axis=1) for part in range(3)]
                held_down[pl.ds(pl.multiple_of((at * count + place) * block, 8), block), :] = jnp.concatenate(pieces, axis=0)
        else:
            natural_ref[pl.ds(pl.multiple_of(at * size, 16), size), :] = ddown.astype(low)
        store_blocks(table_ref, sent_ref, kept_ref, held, block)

    @pl.when(at == steps - 1)
    def _():
        out_ref[...] = total[...].astype(low)

    if aligned:
        for extra in range(held_down.shape[1] // (2 * size)):

            @pl.when(at == steps + extra)
            def _():
                store_blocks(shared_ref, sent_ref, kept_ref, held_down.at[:, 2 * size * extra : 2 * size * (extra + 1)], block)


def ffn(table, shared, second, first, upstream, both, down, devices, steps):
    rows, width = second.shape
    hidden = down[0][0].shape[1] * down[1].shape[0]
    size = hidden // steps
    aligned = width // devices % 8 == 0
    columns = 3 * hidden if aligned else 2 * hidden
    shape = jax.ShapeDtypeStruct
    counts = len(both[0]), len(down[0])
    copies = both[1].shape[0] + down[1].shape[0]
    natural = [] if aligned else [(hidden, width)]
    return call(
        lambda *refs: ffn_kernel(width // devices, hidden // devices, steps, counts, *refs), "ffn", (columns // (2 * size),), 4,
        [constant_spec(rows, width, buffers=1)] * 3 + [pl.BlockSpec(memory_space=pl.ANY)] * sum(counts),
        [constant_spec(rows, width, buffers=1), constant_spec(rows, width, buffers=1),
         *[pl.BlockSpec((width // 2, 2 * size), lambda at, *_: (0, at))] * 2, *[constant_spec(*item, buffers=1) for item in natural]],
        [shape((rows, width), low), shape((rows, width), full), *[shape((width // 2, columns), low)] * 2,
         *[shape(item, low) for item in natural]],
        [pltpu.VMEM((width, rows), low), pltpu.VMEM((rows, width), full), pltpu.VMEM((rows, size), low),
         pltpu.VMEM((rows, 2 * size), low), pltpu.VMEM((width, 2 * size), full), pltpu.VMEM((width, 2 * hidden), low),
         pltpu.VMEM((hidden, width), low), pltpu.VMEM((width, hidden) if aligned else (8, PAIR), full),
         pltpu.SemaphoreType.DMA((copies,))],
        29_000_000_000, (table, shared, both[1], down[1], second, first, upstream, *both[0], *down[0]),
    )


def fold_kernel(layout, last, paired, *refs):
    outs = refs[sum(sum(members) + extra for members, extra in layout) :]
    for group, (members, extra) in enumerate(layout):
        mine, refs = refs[: sum(members) + extra], refs[sum(members) + extra :]
        totals = []
        for count in members:
            totals.append(sum(ref[...].astype(full) for ref in mine[:count]))
            mine = mine[count:]
        total = jnp.concatenate(totals, axis=1) if len(totals) > 1 else totals[0]
        for ref in mine:
            total = total + ref[...].astype(full)
        if paired and group + 1 == len(layout):
            plain = total.shape[1] - 2 * paired
            tail = total[:, plain : plain + paired] + total[:, plain + paired :]
            high = tail.astype(low).astype(full)
            total = jnp.concatenate([total[:, :plain], high, tail - high], axis=1)
        if last:
            half = total.shape[0] // 2
            outs[2 * group][...] = total[half:].astype(low)
            outs[2 * group + 1][...] = total[:half]
        else:
            outs[group][...] = total.astype(low)


def fold(groups, rows, steps, paired=0):
    last = rows // 2 % MINI != 0
    size, place = (rows, 0) if last else (rows // 2, 1)
    specs, arrays, outs, shapes, layout = [], [], [], [], []
    for members, extra in groups:
        width = 0
        for addends, first, columns in members:
            part = columns // steps
            specs += [pl.BlockSpec((size, part), lambda at, begin=first // part: (place, begin + at))] * len(addends)
            arrays += addends
            width += part
        specs += [pl.BlockSpec((size, width), lambda at: (place, at))] * len(extra)
        arrays += extra
        layout.append(([len(addends) for addends, _, _ in members], len(extra)))
        outs += [pl.BlockSpec((rows // 2, width), lambda at: (0, at))] * (2 if last else 1)
        shapes += [jax.ShapeDtypeStruct((rows // 2, width * steps), kind) for kind in ((low, full) if last else (low,))]
    results = call(
        lambda *refs: fold_kernel(layout, last, paired, *refs), "fold", (steps,), 0, specs, outs, shapes, [], 100_000_000, arrays
    )
    return [(results[2 * group], results[2 * group + 1]) for group in range(len(groups))] if last else list(results)


class Scatter:
    def __init__(self, links, groups, rows, steps, paired=0):
        self.links, self.steps, self.paired = links, steps, paired
        self.groups = [(members, []) for members in groups]
        self.rows, self.phase, self.kept, self.sent = rows, 0, None, None

    def fold(self):
        if self.kept is None:
            made = fold(self.groups, self.rows, self.steps, self.paired)
            if self.rows // 2 % MINI:
                self.sent, self.kept = [sent for sent, _ in made], [kept for _, kept in made]
            else:
                self.sent = made
        else:
            half = self.rows // 2
            totals = [kept + got.astype(full) for kept, got in zip(self.kept, self.got)]
            self.sent, self.kept = [total[half:].astype(low) for total in totals], [total[:half] for total in totals]
        self.rows //= 2

    def send(self):
        links, phase = self.links, self.phase
        self.got = []
        for sent, kind in zip(self.sent, ("split", "shared")):
            bits = [order[phase] for order in links.orders[kind]] if phase < links.near else [links.far] * 2
            self.got.append(links.swap(sent, bits))
        self.phase += 1
        if self.kept is None:
            self.groups = [(members, extra + [got]) for (members, extra), got in zip(self.groups, self.got)]

    def tied(self, *others):
        state = (self.sent, self.kept, self.got, self.groups) if self.phase else (self.sent,)
        arrays, tree = jax.tree.flatten(state)
        numbers = [place for place, array in enumerate(arrays) if not isinstance(array, int)]
        out = tie(*others, [arrays[place] for place in numbers])
        for place, array in zip(numbers, out[-1]):
            arrays[place] = array
        state = jax.tree.unflatten(tree, arrays)
        self.sent = state[0]
        if len(state) > 1:
            self.kept, self.got, self.groups = state[1:]
        return out[:-1] if len(others) > 1 else out[0]

    def result(self):
        while self.phase <= self.links.near:
            self.fold()
            self.send()
        return [kept + got.astype(full) for kept, got in zip(self.kept, self.got)]


def post_back_kernel(dsecond_ref, first_ref, up_ref, inner_ref, gate_ref, w_out_ref, vec_ref,
                     dfirst_ref, dgate_ref, dinner_ref, dfirst_low_ref, sums_ref):
    @pl.when(pl.program_id(0) == 0)
    def _():
        sums_ref[...] = jnp.zeros_like(sums_ref)

    first, dsecond = first_ref[...], dsecond_ref[...]
    scale = lax.rsqrt(row_mean(first * first) + epsilon)
    sums_ref[6:7] += jnp.sum(dsecond * first * scale, axis=0, keepdims=True)
    dsecond = dsecond * vec_ref[6:7]
    dfirst = up_ref[...].astype(full) + scale * dsecond - first * (scale * scale * scale * row_mean(first * dsecond))
    dfirst_ref[...] = dfirst
    dfirst_low = dfirst.astype(low)
    dfirst_low_ref[...] = dfirst_low
    dmixed = dot_nt(dfirst_low, w_out_ref[...])
    inner = inner_ref[...]
    centred = inner - row_mean(inner)
    inverse = lax.rsqrt(row_mean(centred * centred) + epsilon)
    standard = centred * inverse
    value, slope = gelu_parts(gate_ref[...])
    dgate_ref[...] = (dmixed * (standard * vec_ref[4:5] + vec_ref[5:6]) * slope).astype(low)
    dpost = dmixed * value
    sums_ref[4:5] += jnp.sum(dpost * standard, axis=0, keepdims=True)
    sums_ref[5:6] += jnp.sum(dpost, axis=0, keepdims=True)
    dpost = dpost * vec_ref[4:5]
    dinner_ref[...] = inverse * (dpost - row_mean(dpost) - standard * row_mean(dpost * standard))


def post_back(dsecond, first, upstream, inner, gate, whole, vectors):
    rows, width = first.shape
    tile = rows // 4
    row = pl.BlockSpec((tile, width), lambda at: (at, 0))
    shape = jax.ShapeDtypeStruct
    return call(
        post_back_kernel, "post_back", (4,), 0,
        [row] * 5 + [constant_spec(width, width, at=4, buffers=1), constant_spec(8, width)],
        [row, row, row, row, constant_spec(8, width)],
        [shape((rows, width), full), shape((rows, width), low), shape((rows, width), full), shape((rows, width), low),
         shape((8, width), full)],
        [], 4_000_000_000, (dsecond, first, upstream, inner, gate, whole, vectors),
    )


def middle_kernel(block, table_ref, mixed_ref, dfirst_ref, normed_ref, dgate_ref, sent_ref, kept_ref, held):
    @pl.when(pl.program_id(0) == 0)
    def _():
        held[...] = dot_tn(mixed_ref[...], dfirst_ref[...])

    @pl.when(pl.program_id(0) == 1)
    def _():
        held[...] = dot_tn(normed_ref[...], dgate_ref[...])

    store_blocks(table_ref, sent_ref, kept_ref, held, block)


def middle_grads(table, mixed, dfirst, normed, dgate, devices):
    rows, width = normed.shape
    whole = constant_spec(rows, width, buffers=1)
    return call(
        lambda *refs: middle_kernel(width // devices, *refs), "middle_grads", (2,), 1,
        [whole] * 4, [pl.BlockSpec((width // 2, width), lambda at, *_: (0, at))] * 2,
        [jax.ShapeDtypeStruct((width // 2, 2 * width), low)] * 2, [pltpu.VMEM((width, width), full)], 3_000_000_000,
        (table, mixed, dfirst, normed, dgate),
    )


def weight_kernel(block, table_ref, normed_ref, grad_ref, sent_ref, kept_ref, turned, held):
    @pl.when(pl.program_id(0) == 0)
    def _():
        turned[...] = normed_ref[...].T

    held[...] = dot_nn(turned[...], grad_ref[...])
    store_blocks(table_ref, sent_ref, kept_ref, held, block)


def weight_grads(table, normed, grads, devices):
    rows, width = normed.shape
    out = pl.BlockSpec((width // 2, width), lambda at, *_: (0, at))
    return call(
        lambda *refs: weight_kernel(width // devices, *refs), "weight_grads", (2,), 1,
        [constant_spec(rows, width, buffers=1), pl.BlockSpec((rows, width), lambda at, *_: (0, at))],
        [out, out], [jax.ShapeDtypeStruct((width // 2, 2 * width), low)] * 2,
        [pltpu.VMEM((width, rows), low), pltpu.VMEM((width, width), full)], 3_000_000_000, (table, normed, grads),
    )


def last_kernel(block, table_ref, normed_ref, grad_ref, sums_ref, dw_ref, db_ref, dgain_ref, dshift_ref, dgain_query_ref,
                dshift_query_ref, rate_ref, rest_ref, lane_ref, chosen_ref, sent_ref, kept_ref, dlog_ref, held):
    rows, width = normed_ref.shape
    turned = normed_ref[...].T
    held[:, :width] = dot_nn(turned, grad_ref[...])
    slots = rate_ref.shape[0] * MINI
    for sequence in range(rows // slots):
        mine = (lane_ref[16:17] == float(sequence)).astype(full)
        spread = rate_ref[:, 0, :] * rest_ref[...] * mine
        spread = (spread[:, None, :] * lane_ref[:MINI][None]).reshape(slots, 384).astype(low)
        dlog_ref[slots * sequence : slots * (sequence + 1)] = dot_nt(spread, chosen_ref[...]).astype(low)
    eta = dot_nn(turned, dlog_ref[...])
    inner = dw_ref[:, :width] + dw_ref[:, width:]
    fixed = jnp.concatenate(
        [inner, jnp.zeros((VECTORS - HEAD, width), full), sums_ref[...], jnp.zeros((PAIR - VECTORS - 8, width), full)], axis=0
    )
    lane = lax.broadcasted_iota(jnp.int32, (HEAD, PAIR), 1)
    chosen = chosen_ref[...].astype(full)
    bias = jnp.sum(rate_ref[:, 0, :] * rest_ref[...], axis=0, keepdims=True)
    held[:, width : width + PAIR] = eta + fixed.T
    bias = jnp.sum(chosen * bias, axis=1, keepdims=True)
    square = jnp.broadcast_to(bias, (PAIR, PAIR)).T[:1]
    bias_row = pltpu.roll(square, BIAS - ETA, axis=1)
    bias_row = jnp.where((lane[:1] >= BIAS) & (lane[:1] < BIAS + 12), bias_row, 0.0)
    lanes_of = [db_ref[...] * (1.0 / MINI), dgain_ref[...] + exchange(dgain_query_ref[...]), dshift_ref[...] + exchange(dshift_query_ref[...])]
    for head in range(12):
        here = pl.ds(HEAD * head, HEAD)
        mask = chosen[ETA + head : ETA + head + 1]
        total = held[here, width : width + PAIR] + bias_row
        for place, values in enumerate(lanes_of):
            column = jnp.sum(values * mask, axis=1, keepdims=True)
            total = total + jnp.where(lane == VECTORS + place, column, 0.0)
        high = total.astype(low).astype(full)
        held[here, width : width + PAIR] = high
        held[here, width + PAIR :] = total - high
    store_blocks(table_ref, sent_ref, kept_ref, held, block)


def last_grads(table, normed, grads, sums, state, rate_back, rest, devices):
    rows, width = normed.shape
    lane, chosen = lane_constants()
    spec = lambda array: constant_spec(*array.shape, buffers=1)
    others = (sums, *state, rate_back, rest, lane, chosen)
    shape = jax.ShapeDtypeStruct
    out = constant_spec(width // 2, width + 2 * PAIR, buffers=1)
    return call(
        lambda *refs: last_kernel(width // devices, *refs), "last_grads", (1,), 1,
        [spec(normed), constant_spec(rows, width, at=2, buffers=1)] + [spec(array) for array in others],
        [out, out, constant_spec(rows, PAIR, buffers=1)],
        [shape((width // 2, width + 2 * PAIR), low)] * 2 + [shape((rows, PAIR), low)],
        [pltpu.VMEM((width, width + 2 * PAIR), full)], 3_000_000_000, (table, normed, grads, *others),
    )


def finish_kernel(tokens_ref, dfirst_ref, dqkv_ref, dgate_ref, dlog_ref, w_ref, small_ref, w_gate_ref, vec_ref, out_ref):
    dnormed = dot_nt(dqkv_ref[...], w_ref[...]) + dot_nt(dgate_ref[...], w_gate_ref[...]) + dot_nt(dlog_ref[...], small_ref[...])
    values = tokens_ref[...].astype(full)
    scale = lax.rsqrt(row_mean(values * values) + epsilon)
    dnormed = dnormed * vec_ref[3:4]
    back = scale * dnormed - values * (scale * scale * scale * row_mean(values * dnormed))
    out_ref[...] = (dfirst_ref[...] + back).astype(low)


def finish(tokens, dfirst, dqkv, dgate, dlog, whole, vectors, at, before):
    rows, width = tokens.shape
    tile = rows // 2
    row = lambda n: pl.BlockSpec((tile, n), lambda step: (at, 0))
    arrays = [tokens, dfirst, dqkv, dgate, dlog, whole, whole, whole, vectors]
    extra = [] if before is None else [before]
    return pl.pallas_call(
        lambda *refs: finish_kernel(*refs[:9], refs[-1]),
        grid=(1,),
        in_specs=[row(width), row(width), row(3 * width), row(width), row(PAIR), constant_spec(width, 3 * width, buffers=1),
                  constant_spec(width, PAIR, at=5 * width // PAIR, buffers=1), constant_spec(width, width, at=3, buffers=1),
                  constant_spec(8, width)] + [pl.BlockSpec(memory_space=pl.ANY)] * len(extra),
        out_specs=row(width),
        out_shape=jax.ShapeDtypeStruct((rows, width), low),
        input_output_aliases={len(arrays): 0} if extra else {},
        compiler_params=pltpu.CompilerParams(vmem_limit_bytes=60 * 1024 * 1024),
        cost_estimate=pl.CostEstimate(flops=3_000_000_000, bytes_accessed=10_000_000, transcendentals=0),
        name="finish",
    )(*arrays, *extra)


class Links:
    def __init__(self, dp, fsdp):
        self.axes = ("dp", "fsdp")
        self.count = dp * fsdp
        self.core = fsdp
        self.far = fsdp // 2
        bits = [1 << place for place in reversed(range(self.count.bit_length() - 1))]
        self.others = [bit for bit in bits if bit != self.core]
        near = [bit for bit in reversed(self.others) if bit != self.far]
        near = near[:1] + near[:0:-1]
        turned = [near[turn:] + near[:turn] for turn in range(3)]
        self.orders = {"split": [turned[0], turned[2]], "shared": [turned[1]] * 2}
        self.phases = self.near = len(near)
        self.me = lax.axis_index("dp") * fsdp + lax.axis_index("fsdp")
        self.side = (self.me // self.core) % 2

    def swap(self, values, bits):
        pairs = [(place, place ^ bits[(place // self.core) % 2]) for place in range(self.count)]
        return lax.ppermute(values, self.axes, pairs)

    def one(self, bit):
        return (self.me // bit) % 2

    def join(self, held, bits):
        got = self.swap(held, bits)
        mine = jnp.where(self.side == 0, self.one(bits[0]), self.one(bits[1])) == 0
        return jnp.stack([jnp.where(mine, held, got), jnp.where(mine, got, held)])

    def gather(self, pieces, kinds):
        orders = [[[self.far] + order for order in self.orders[kind]] for kind in kinds]
        held = list(pieces)
        for phase in range(len(orders[0][0])):
            held = [self.join(array, [order[phase] for order in pair]) for array, pair in zip(held, orders)]
            changed = yield held
            held = held if changed is None else changed
        above = [bit for bit in self.others if bit > self.core]
        whole = []
        for array, pair in zip(held, orders):
            got = self.swap(array, [self.core] * 2)
            mine = self.side == 0
            cores = [jnp.where(mine, array, got), jnp.where(mine, got, array)]
            placed = []
            for half, order in zip(cores, pair):
                have = order[::-1]
                placed.append(half.transpose([have.index(bit) for bit in self.others] + [len(have), len(have) + 1]))
            whole.append(jnp.stack(placed, axis=len(above)).reshape(-1, array.shape[-1]))
        yield whole

    def gather_blocks(self, pieces, kinds, pairs, whole_last):
        held = list(pieces)
        orders = [self.orders[kind] for kind in kinds]
        count = self.phases

        def ready(array, place):
            rows = pieces[place].shape[0]
            if not pairs[place]:
                return array.reshape((-1, rows) + array.shape[-1:])
            turned = []
            stacked = array.ndim - 2
            for order in orders[place]:
                have = ([self.far] + order)[:stacked][::-1]
                at = have.index(1)
                turned.append(array.transpose([axis for axis in range(stacked) if axis != at] + [at, stacked, stacked + 1]))
            array = jnp.where(self.side == 0, turned[0], turned[1])
            return array.reshape((-1, 2 * rows) + array.shape[-1:])

        for phase in range(count):
            for place, pair in enumerate(orders):
                held[place] = self.join(held[place], [self.far] * 2 if phase == 0 else [order[phase - 1] for order in pair])
                if phase == count - 1 and not whole_last[place]:
                    held[place] = ready(held[place], place)
            changed = yield held
            held = held if changed is None else changed
        buffers = []
        for place, pair in enumerate(orders):
            last = [order[-1] for order in pair]
            if whole_last[place]:
                buffers.append([ready(self.join(held[place], last), place)])
            else:
                buffers.append([held[place], self.swap(held[place], last), self.swap(held[place], [self.core] * 2)])
        changed = yield buffers
        buffers = buffers if changed is None else changed
        buffers = [list(group) + [self.swap(group[0 if whole else 1], [self.core] * 2)] for group, whole in zip(buffers, whole_last)]

        def places(bits, device, unit):
            found = []
            clear = device & ~(sum(bits) + unit - 1)
            for place in range(1 << len(bits)):
                found.append((clear + sum(bit for at, bit in enumerate(bits) if place >> (len(bits) - 1 - at) & 1)) // unit)
            return jnp.stack(found)

        done = []
        for place, pair in enumerate(orders):
            unit = 2 if pairs[place] else 1
            table = []
            for core, last in ((0, 0), (self.core, 0)) if whole_last[place] else ((0, 0), (0, 1), (self.core, 0), (self.core, 1)):
                by_side = []
                for order in pair:
                    have = ([self.far] + order)[::-1] if whole_last[place] else ([self.far] + order[:-1])[::-1]
                    by_side.append(places([bit for bit in have if bit >= unit], self.me ^ core ^ (order[-1] if last else 0), unit))
                own = self.side if core == 0 else 1 - self.side
                table.append(jnp.where(own == 0, by_side[0], by_side[1]))
            done.append((buffers[place], jnp.concatenate(table).astype(jnp.int32)))
        yield done

    def table(self, kind):
        half = []
        for side in range(2):
            masks = self.orders[kind][side] + [self.far]
            half.append(np.array([sum(bit for at, bit in enumerate(masks) if place >> (len(masks) - 1 - at) & 1)
                                  for place in range(self.count // 2)], np.int32))
        keep = jnp.where(self.side == 0, half[0], half[1])
        send = jnp.where(self.side == 0, half[1], half[0])
        return jnp.concatenate([self.me ^ keep, self.me ^ self.core ^ send]).astype(jnp.int32)

    def exchange_cores(self, pair):
        return pair[1], self.swap(pair[0], [self.core] * 2)


def tie(*groups):
    flat, tree = jax.tree.flatten(groups)
    return jax.tree.unflatten(tree, lax.optimization_barrier(flat))


def halves(array):
    half = array.shape[0] // 2
    return array[half:], array[:half]


def tie(*groups):
    flat, tree = jax.tree.flatten(groups)
    return jax.tree.unflatten(tree, lax.optimization_barrier(flat))


def halves(array):
    half = array.shape[0] // 2
    return array[half:], array[:half]


def in_order(table, pair, rows):
    if rows % 8 == 0:
        return pair
    whole = jnp.concatenate([pair[1], pair[0]], axis=0)
    return halves(whole.reshape((-1, rows) + whole.shape[1:])[table].reshape(whole.shape))


def body(dp, fsdp, tokens, lengths, cotangent, mixer_in, w_eta, eta_bias, w_out, inner_w, inner_b, ttt_gain, ttt_shift,
         norm_one, post_gain, post_shift, w_gate_up, w_down, norm_two):
    links = Links(dp, fsdp)
    devices = dp * fsdp
    micro, slots, width = tokens.shape
    rows = micro * slots
    heads = eta_bias.shape[0]
    head = width // heads
    hidden = w_gate_up.shape[1] // 2
    device_rows = width // devices
    table, shared = links.table("split"), links.table("shared")
    zeros = lambda columns: jnp.zeros((device_rows, columns), low)

    vectors = jnp.stack([inner_b, ttt_gain, ttt_shift, norm_one, post_gain, post_shift, norm_two])
    vectors = dot_tn(vectors, jnp.eye(7, PAIR, VECTORS, dtype=low)).astype(low)
    small = jnp.concatenate([inner_w, w_eta, zeros(PAIR - ETA - heads)], axis=1) + vectors
    cut = 21 * PAIR
    pieces = [mixer_in[:, :cut], jnp.concatenate([mixer_in[:, cut:], w_out, small], axis=1)]
    rest = [w_gate_up, w_down]
    kinds = ["split", "shared"]
    aligned = device_rows % 8 == 0
    if aligned:
        mixer_phases = links.gather_blocks(pieces, kinds, [True, True], [False, True])
    else:
        mixer_phases = links.gather(pieces, kinds)
    places = lax.broadcasted_iota(jnp.int32, (micro, slots), 1)
    live = places < lengths
    upstream = jnp.where(live[..., None], cotangent, jnp.zeros_like(cotangent)).reshape(rows, width)
    held = next(mixer_phases)
    for _ in range(links.phases - 2):
        held = mixer_phases.send(held)
    held, rest, upstream = tie(held, rest, upstream)
    rest_phases = links.gather_blocks(rest, kinds, [True, False], [False, False]) if aligned else links.gather(rest, kinds)
    held, rest = mixer_phases.send(held), next(rest_phases)
    held, rest = mixer_phases.send(held), rest_phases.send(rest)
    held = mixer_phases.send(held)
    as_blocks = lambda arrays: [([array[None]], jnp.zeros((1,), jnp.int32)) for array in arrays]
    early, late = held if aligned else as_blocks(held)

    inputs = tokens.reshape(rows, width)
    bias_row = jnp.pad(eta_bias.astype(full), (ETA, PAIR - ETA - heads)).reshape(1, PAIR)
    early, late, rest = tie(early, late, rest)
    rest = rest_phases.send(rest)
    whole, projected, normed, rate_lanes, rest_lanes, start_w, start_b, gain_lanes, shift_lanes, vec_rows = project(
        lengths.reshape(micro), inputs, early, late, bias_row
    )
    projected = projected.reshape(micro, slots, -1)
    rate_lanes, rest = tie(rate_lanes, rest)
    rest = rest_phases.send(rest)
    inner, saved = ttt_forward(projected, rate_lanes, [start_w, start_b], gain_lanes, shift_lanes)
    inner = inner.reshape(rows, width)
    inner, rest = tie(inner, rest)
    rest = drain(rest_phases, rest)
    if not aligned:
        rest = as_blocks(rest)
    gate, mixed, first, second = post(inner, normed, inputs, whole, vec_rows)
    block_out, dsecond, large_sent, large_kept, *natural = ffn(table, shared, second, first, upstream, *rest, devices, dp)
    down_rows = hidden // devices
    unit = min(8, device_rows // 3)
    if not aligned:
        natural = natural[0].reshape(devices, -1, unit, 3, width // 3).transpose(0, 3, 2, 1, 4).reshape(width, hidden)
        pairs = in_order(table, (large_sent, large_kept), device_rows), in_order(shared, halves(natural), device_rows)
        large_sent, large_kept = (jnp.concatenate(pair, axis=1) for pair in zip(*pairs))
    large = links.exchange_cores((large_sent, large_kept))
    dfirst, dgate, dinner, dfirst_low, sums = post_back(dsecond, first, upstream, inner, gate, whole, vec_rows)
    middle = middle_grads(table, mixed, dfirst_low, normed, dgate, devices)
    middle = links.exchange_cores(in_order(table, tuple(middle), device_rows))
    dinner, large, middle = tie(dinner, large, middle)
    large, middle = list(large), list(middle)
    whole_rows = width // 2
    first_sum = Scatter(
        links, [[(large, 0, 2 * hidden), (middle, 0, 2 * width)], [(large, 2 * hidden, hidden)]], whole_rows, 2
    )
    first_sum.fold()
    dinner = first_sum.tied(dinner)
    first_sum.send()
    dinner = dinner.reshape(micro, slots, width)
    dqkv, rate_late, state = ttt_backward(projected, dinner, rate_lanes, saved, None, gain_lanes, 4, slots // MINI, None)
    dqkv, state = first_sum.tied(dqkv, state)
    first_sum.fold()
    dqkv, state = first_sum.tied(dqkv, state)
    first_sum.send()
    dqkv, rate_early, state = ttt_backward(projected, dinner, rate_lanes, saved, state, gain_lanes, 0, 4, dqkv)
    dqkv = dqkv.reshape(rows, 3 * width)
    rate_back = jnp.concatenate([rate_early, rate_late], axis=0)
    early = weight_grads(table, normed, dqkv, devices)
    dqkv, early = first_sum.tied(dqkv, list(early))
    first_sum.fold()
    dqkv, early = first_sum.tied(dqkv, early)
    first_sum.send()
    early = links.exchange_cores(in_order(table, tuple(early), device_rows))
    *late, dlog = last_grads(shared, normed, dqkv, sums, state, rate_back, rest_lanes, devices)
    late, dlog, early = first_sum.tied(list(late), dlog, early)
    late = links.exchange_cores(in_order(shared, tuple(late), device_rows))
    first_sum.fold()
    late = first_sum.tied(late)
    first_sum.send()
    second_sum = Scatter(
        links, [[(list(early), 0, 2 * width)], [(list(late), 0, width + 2 * PAIR)]], whole_rows, 1, PAIR
    )
    second_sum.fold()
    dlog = second_sum.tied(dlog)
    second_sum.send()
    grad_tokens = None
    for half in range(2):
        grad_tokens = finish(inputs, dfirst, dqkv, dgate, dlog, whole, vec_rows, half, grad_tokens)
        grad_tokens = second_sum.tied(grad_tokens)
        second_sum.fold()
        second_sum.send()
    early, late = second_sum.result()
    large, down = first_sum.result()
    part = hidden // dp
    large = large.reshape(device_rows, 2, -1)
    both = large[:, :, :hidden].reshape(device_rows, dp, 2, part).transpose(0, 2, 1, 3).reshape(device_rows, 2 * hidden)
    middle = large[:, :, hidden:].reshape(device_rows, 2 * width)
    out_small = late[:, width : width + PAIR] + late[:, width + PAIR :]
    out_out, out_gate_in = middle[:, :width], middle[:, width:]
    out_mixer = jnp.concatenate([early, late[:, :width], out_gate_in], axis=1)
    out_eta = out_small[:, ETA : ETA + heads]
    out_norm_one = jnp.sum(mixer_in.astype(full) * out_mixer, axis=1) + jnp.sum(w_eta.astype(full) * out_eta, axis=1)
    out_norm_one = out_norm_one / norm_one.astype(full)
    out_inner_b, out_gain, out_shift, _, out_post_gain, out_post_shift, out_norm_two = (
        out_small[:, VECTORS + place] for place in range(7)
    )
    return (
        block_out.reshape(tokens.shape),
        grad_tokens.reshape(tokens.shape),
        out_mixer,
        out_eta,
        out_small[0, BIAS : BIAS + heads],
        out_out,
        out_small[:, :head],
        out_inner_b,
        out_gain,
        out_shift,
        out_norm_one,
        out_post_gain,
        out_post_shift,
        both,
        down.reshape(3, unit, -1, width // 3).transpose(2, 1, 0, 3).reshape(down_rows, width),
        out_norm_two,
    )


def drain(phases, arrays):
    try:
        while True:
            arrays = phases.send(arrays)
    except StopIteration:
        return arrays


def solution(mesh):
    split = ("dp", "fsdp")
    row, vector, token = P(split, None), P(split), P(None, split, None)
    dp, fsdp = mesh.shape["dp"], mesh.shape["fsdp"]
    return jax.shard_map(
        lambda *arrays: body(dp, fsdp, *arrays),
        mesh=mesh,
        in_specs=(token, P(None, split), token, row, row, P(), row, row) + (vector,) * 6 + (row, row, vector),
        out_specs=(token, token, row, row, P(), row, row) + (vector,) * 6 + (row, row, vector),
        check_vma=False,
    )
```

```python
import jax
import jax.numpy as jnp
from jax import lax
from jax.experimental import pallas as pl
from jax.experimental.pallas import tpu as pltpu
from jax.sharding import PartitionSpec as P
import numpy as np

MINI = 16
HEAD = 64
PAIR = 2 * HEAD
epsilon = 1e-06
low = jnp.bfloat16
full = jnp.float32


def dot_nn(former, latter):
    return lax.dot_general(former, latter, (((1,), (0,)), ((), ())), preferred_element_type=full)


def dot_nt(former, latter):
    return lax.dot_general(former, latter, (((1,), (1,)), ((), ())), preferred_element_type=full)


def tile_of(rows, at):
    return rows[:, PAIR * at : PAIR * (at + 1)]


def key_row(group, side, tile):
    return HEAD * group + 32 * side + MINI * tile


def query_row(group, side, tile):
    return key_row(1 - group, side, tile)


def expand(rows, sides):
    zero = jnp.zeros((MINI, PAIR), rows.dtype)
    blocks = []
    for side in range(2):
        for at in range(2):
            kept = tile_of(rows, at) * sides[side]
            blocks.append(jnp.concatenate([kept if other == at else zero for other in range(2)], axis=1))
    return jnp.concatenate(blocks, axis=0)


def expand_both(queries, keys, sides):
    width = 2 * PAIR
    blocks = [(expand(keys[:, width * group : width * (group + 1)], sides), expand(queries[:, width * group : width * (group + 1)], sides))
              for group in range(2)]
    return blocks, (jnp.concatenate(blocks[0], axis=0), jnp.concatenate(blocks[1][::-1], axis=0))


def to_feature(rows, first_side, groups):
    tiles = [tile_of(rows, 2 * group + at) for group in groups for _ in range(2) for at in range(2)]
    stacked = jnp.concatenate(tiles, axis=0).T
    return jnp.where(first_side, stacked[:HEAD], stacked[HEAD:])


def to_rows(columns, left, place):
    turned = jnp.concatenate([columns, columns], axis=0).T
    pick = lambda group, side, at: turned[place(group, side, at) : place(group, side, at) + MINI]
    return jnp.concatenate([jnp.where(left, pick(group, 0, at), pick(group, 1, at)) for group in range(2) for at in range(2)], axis=1)


def exchange(values):
    half = [values[:, HEAD * at : HEAD * (at + 1)] for at in range(values.shape[1] // HEAD)]
    return jnp.concatenate([half[at ^ 1] for at in range(len(half))], axis=1)


def mean_rows(values):
    return jnp.sum(values, axis=0, keepdims=True) * (1.0 / values.shape[0])


def both_sequences(ref, rows, base, width):
    return jnp.concatenate([ref[0, rows, base : base + width], ref[1, rows, base : base + width]], axis=1)


def store_sequences(ref, rows, base, width, pieces, kind):
    whole = jnp.concatenate(pieces, axis=1)
    ref[0, rows, base : base + width] = whole[:, :width].astype(kind)
    ref[1, rows, base : base + width] = whole[:, width:].astype(kind)


def read_constants(low_ref, full_ref):
    sides = [low_ref[0:MINI], low_ref[MINI : 2 * MINI]]
    same, crossed = low_ref[32:160], low_ref[160:288]
    return sides, same, crossed, full_ref[0:MINI], full_ref[16:144], full_ref[144:272]


def lane_masks(rows=HEAD, width=3 * PAIR):
    lane = lax.broadcasted_iota(jnp.int32, (rows, width), 1)
    return lane % PAIR < HEAD, lane % HEAD < 32


PARTS = range(3)


def thin(part):
    return slice(PAIR * part, PAIR * (part + 1))


def wide(part):
    return slice(4 * PAIR * part, 4 * PAIR * (part + 1))


def lanes(pieces):
    return jnp.concatenate(pieces, axis=1)


def ttt_forward_kernel(steps, q_ref, k_ref, v_ref, rate_ref, w0_ref, b0_ref, gain_ref, shift_ref, low_ref, full_ref,
                       out_ref, w_ref, xh_ref, h_ref, grs_ref, xb_ref, stat_ref, score_ref, w_run, b_run, gain_query, shift_query):
    width = 768

    @pl.when(pl.program_id(0) == 0)
    def _():
        w_run[...] = w0_ref[...]
        b_run[...] = b0_ref[...]
        gain_query[...] = exchange(gain_ref[...])
        shift_query[...] = exchange(shift_ref[...])

    sides, same, crossed, tri, _, _ = read_constants(low_ref, full_ref)
    left, first_side = lane_masks()
    left_one, first_one = left[:, :PAIR], first_side[:, :PAIR]
    tri = lanes([tri] * 3)

    def begin(at):
        rows = slice(at * MINI, (at + 1) * MINI)
        queries = both_sequences(q_ref, rows, 0, width)
        keys = both_sequences(k_ref, rows, 0, width)
        targets = both_sequences(v_ref, rows, 0, width) - keys
        query_low, key_low = queries.astype(low), keys.astype(low)
        expanded = [expand_both(query_low[:, wide(part)], key_low[:, wide(part)], sides) for part in PARTS]
        target = lanes([to_feature(targets[:, wide(part)], first_one, (0, 1)) for part in PARTS])
        return rows, queries, query_low, expanded, target

    def multiply(at, started, weights):
        _, _, query_low, expanded, _ = started
        products = []
        for part in PARTS:
            weight_low = weights[part].astype(low)
            w_ref[at, :, wide(part)] = weight_low
            for group in range(2):
                here = slice(2 * PAIR * group, 2 * PAIR * (group + 1))
                rows = jnp.concatenate([weight_low[:, here], query_low[:, wide(part)][:, here]], axis=0)
                products.append(dot_nt(rows, expanded[part][1][group]))
        return lanes(products[::2]), lanes(products[1::2])

    def finish(at, started, kept):
        rows, queries = started[:2]
        inner_grad, mixing, updated = kept
        inner_grad_low = inner_grad.astype(low)
        moved = []
        for part in PARTS:
            mixing_block = jnp.concatenate([mixing[:, thin(part)]] * 8, axis=0) * crossed
            moved.append(dot_nt(inner_grad_low[:, thin(part)], mixing_block))
        updated = updated - lanes(moved)
        updated = updated - mean_rows(updated)
        updated_inverse = lax.rsqrt(mean_rows(updated * updated) + epsilon)
        updated = updated * updated_inverse
        xb_ref[at] = updated
        stat_ref[at, 3:4] = updated_inverse
        updated = updated * gain_query[...] + shift_query[...]
        result = queries + lanes([to_rows(updated[:, thin(part)], left_one[:MINI], query_row) for part in PARTS])
        out_ref[0, rows, :] = result[:, :width]
        out_ref[1, rows, :] = result[:, width:]

    weights = [w_run[:, wide(part)] for part in PARTS]
    offset = b_run[...]
    started = begin(0)
    pending = None
    for at in range(steps):
        first, second = multiply(at, started, weights)
        if pending is not None:
            finish(*pending)
        gains, shifts = gain_ref[...], shift_ref[...]
        rate = rate_ref[at]
        _, _, _, expanded, target = started
        hidden = jnp.where(left, first[:HEAD], second[:HEAD]) + offset
        scores = jnp.where(left[:MINI], first[HEAD:], second[HEAD:]) + 1.0
        updated = jnp.where(left, second[:HEAD], first[:HEAD]) + exchange(offset)
        centred = hidden - mean_rows(hidden)
        inverse = lax.rsqrt(mean_rows(centred * centred) + epsilon)
        normed = centred * inverse
        held = gains * normed + (shifts - target)
        residual = held * gains
        residual_mean = mean_rows(residual)
        cross = mean_rows(residual * normed)
        inner_grad = (residual - residual_mean - normed * cross) * inverse
        scaled = inner_grad * (rate * (1.0 / MINI))
        scaled_low = scaled.astype(low)
        scaled_other = exchange(scaled).astype(low)
        xh_ref[at] = normed
        h_ref[at] = held
        grs_ref[at] = scaled
        stat_ref[at, 0:1] = inverse
        stat_ref[at, 1:2] = residual_mean
        stat_ref[at, 2:3] = cross
        score_ref[at] = scores
        changed = []
        for part in PARTS:
            blocks = expanded[part][0]
            change = [dot_nn(scaled_low[:, thin(part)][:, :HEAD], blocks[0][0]),
                      dot_nn(scaled_other[:, thin(part)][:, :HEAD], blocks[1][0])]
            changed.append(weights[part] - lanes(change))
        weights = changed
        offset = offset - lanes([dot_nn(scaled_low[:, thin(part)], same) for part in PARTS])
        pending = (at, started, (inner_grad, (tri * rate * scores).astype(low), updated))
        if at + 1 < steps:
            started = begin(at + 1)
    finish(*pending)
    for part in PARTS:
        w_run[:, wide(part)] = weights[part]
    b_run[...] = offset


def ttt_backward_kernel(steps, carried, q_ref, k_ref, dout_ref, rate_ref, w_ref, xh_ref, h_ref, grs_ref, xb_ref, stat_ref, score_ref,
                        gain_ref, low_ref, full_ref, *refs):
    states, refs = (refs[:6], refs[6:]) if carried else (None, refs)
    grad_ref, rdr_ref, dw_ref, db_ref, dgain_ref, dshift_ref, dgain_query_ref, dshift_query_ref, gain_query = refs[-9:]
    width = 768

    @pl.when(pl.program_id(0) == 0)
    def _():
        for place, ref in enumerate((dw_ref, db_ref, dgain_ref, dshift_ref, dgain_query_ref, dshift_query_ref)):
            ref[...] = states[place][...] if carried else jnp.zeros_like(ref)
        gain_query[...] = exchange(gain_ref[...])

    sides, same, crossed, tri, scale, scale_turned = read_constants(low_ref, full_ref)
    left, first_side = lane_masks()
    left_one, first_one = left[:, :PAIR], first_side[:, :PAIR]
    left_rows = left_one[:MINI]
    left_square = lax.broadcasted_iota(jnp.int32, (PAIR, PAIR), 1) < HEAD
    zero = jnp.zeros((MINI, PAIR), full)
    tri = lanes([tri] * 3)

    def begin(at):
        rows = slice(at * MINI, (at + 1) * MINI)
        query_low = both_sequences(q_ref, rows, 0, width).astype(low)
        key_low = both_sequences(k_ref, rows, 0, width).astype(low)
        douts = both_sequences(dout_ref, rows, 0, width)
        expanded = [expand_both(query_low[:, wide(part)], key_low[:, wide(part)], sides) for part in PARTS]
        mixing = (tri * rate_ref[at] * score_ref[at]).astype(low)
        dout = lanes([to_feature(douts[:, wide(part)], first_one, (1, 0)) for part in PARTS])
        updated = xb_ref[at]
        dupdated = dout * gain_query[...]
        dupdated = stat_ref[at, 3:4] * (dupdated - mean_rows(dupdated) - updated * mean_rows(dupdated * updated))
        dgain_query_ref[...] += dout * updated
        dshift_query_ref[...] += dout
        dupdated_low = dupdated.astype(low)
        mixed = []
        for part in PARTS:
            mixing_block = jnp.concatenate([mixing[:, thin(part)]] * 8, axis=0) * crossed
            mixed.append(dot_nn(dupdated_low[:, thin(part)], mixing_block))
        return rows, douts, expanded, dupdated, dupdated_low, lanes(mixed)

    def finish(at, started, kept):
        rows, douts, expanded, dupdated, dupdated_low, _ = started
        dhidden, dtarget, dweights_low, rate_part = kept
        scaled = -grs_ref[at]
        scaled_low = scaled.astype(low)
        scores = score_ref[at]
        none = jnp.zeros((HEAD, PAIR), low)
        turned_low, turned_query, query_rows, dmixes, dmixes_turned = [], [], [], [], []
        for part in PARTS:
            turned_low.append(jnp.concatenate([dhidden[:, thin(part)], scaled[:, thin(part)]], axis=0).T.astype(low))
            turned_query.append(jnp.concatenate([dupdated[:, thin(part)], dtarget[:, thin(part)]], axis=0).T)
            query_rows.append(jnp.where(left_square, turned_query[part], 0.0).astype(low))
        for part in PARTS:
            dmix = dot_nn(query_rows[part][:, :HEAD], scaled_low[:, thin(part)]) * scale
            dmix_turned = dot_nn(turned_low[part], jnp.concatenate([none, dupdated_low[:, thin(part)]], axis=0)) * scale_turned
            dmixes.append(sum(dmix[MINI * row : MINI * (row + 1)] for row in range(8)))
            dmixes_turned.append(sum(dmix_turned[MINI * row : MINI * (row + 1)] for row in range(8)))
        rdr_ref[at] = rate_part + jnp.sum(lanes(dmixes) * scores, axis=0, keepdims=True)
        query_grads, key_grads, value_grads = [], [], []
        for part in PARTS:
            weight_low = w_ref[at, :, wide(part)]
            for group in range(2):
                keep_key, keep_query = (left_rows, ~left_rows) if group == 0 else (~left_rows, left_rows)
                key_side = jnp.where(keep_query, dmixes_turned[part], zero).astype(low)
                query_side = jnp.where(keep_key, dmixes[part], zero).astype(low)
                extra = jnp.concatenate([key_side, key_side, query_side, query_side], axis=0)
                for at_tile in range(2):
                    tile = 2 * group + at_tile
                    place = [key_row(group, side, at_tile) for side in range(2)]
                    place_query = [query_row(group, side, at_tile) for side in range(2)]
                    held_rows = jnp.concatenate(
                        [turned_low[part][row : row + MINI] for row in place]
                        + [query_rows[part][row : row + MINI] for row in place_query],
                        axis=0,
                    )
                    product = dot_nn(
                        jnp.concatenate([held_rows, extra], axis=1),
                        jnp.concatenate(
                            [tile_of(weight_low, tile), tile_of(dweights_low[part], tile), tile_of(expanded[part][1][group], at_tile)],
                            axis=0,
                        ),
                    )
                    dvalue = jnp.where(
                        left_rows,
                        exchange(turned_query[part][place[0] : place[0] + MINI]),
                        turned_query[part][place[1] : place[1] + MINI],
                    )
                    key_grads.append(dvalue + jnp.where(left_rows, product[:MINI], product[MINI : 2 * MINI]))
                    query_grads.append(
                        tile_of(douts[:, wide(part)], tile) + jnp.where(left_rows, product[2 * MINI : 3 * MINI], product[3 * MINI :])
                    )
                    value_grads.append(-dvalue)
        store_sequences(grad_ref, rows, 0, width, query_grads, low)
        store_sequences(grad_ref, rows, width, width, key_grads, low)
        store_sequences(grad_ref, rows, 2 * width, width, value_grads, low)

    dweights = [dw_ref[:, wide(part)] for part in PARTS]
    doffset = db_ref[...]
    started = begin(steps - 1)
    pending = None
    for at in reversed(range(steps)):
        _, _, expanded, dupdated, _, mixed = started
        dweights_low = [dweight.astype(low) for dweight in dweights]
        key_dw = []
        for part in PARTS:
            blocks = expanded[part][0]
            key_dw.append(dot_nt(dweights_low[part][:, : 2 * PAIR], blocks[0][0]))
            key_dw.append(dot_nt(dweights_low[part][:, 2 * PAIR :], blocks[1][0]))
        key_dw = lanes(key_dw) + doffset
        if pending is not None:
            finish(*pending)
        upcoming = begin(at - 1) if at > 0 else None
        gains = gain_ref[...]
        rate = rate_ref[at]
        normed, held, scaled = xh_ref[at], h_ref[at], grs_ref[at]
        inverse, residual_mean, cross = (stat_ref[at, row : row + 1] for row in range(3))
        grad_in = -mixed - (rate * (1.0 / MINI)) * key_dw
        rate_part = -jnp.sum(scaled * key_dw, axis=0, keepdims=True)
        residual = held * gains
        in_mean = mean_rows(grad_in)
        in_cross = mean_rows(grad_in * normed)
        in_held = inverse * (mean_rows(grad_in * residual) - residual_mean * in_mean - cross * in_cross)
        dresidual = inverse * (grad_in - in_mean - normed * in_cross)
        dtarget = dresidual * gains
        dnormed = dtarget * gains - inverse * (grad_in * cross + in_cross * residual)
        dhidden = inverse * (dnormed - mean_rows(dnormed) - normed * (mean_rows(dnormed * normed) + in_held))
        dgain_ref[...] += dresidual * (held + gains * normed)
        dshift_ref[...] += dtarget
        to_first = jnp.where(left, dhidden, dupdated).astype(low)
        to_second = jnp.where(left, dupdated, dhidden).astype(low)
        changed = []
        for part in PARTS:
            pairs = expanded[part][1]
            change = [dot_nn(to_first[:, thin(part)], pairs[0]), dot_nn(to_second[:, thin(part)], pairs[1])]
            changed.append(dweights[part] + lanes(change))
        total_low = (exchange(dupdated) + dhidden).astype(low)
        doffset = doffset + lanes([dot_nn(total_low[:, thin(part)], same) for part in PARTS])
        dweights = changed
        pending = (at, started, (dhidden, dtarget, dweights_low, rate_part))
        started = upcoming
    finish(*pending)
    for part in PARTS:
        dw_ref[:, wide(part)] = dweights[part]
    db_ref[...] = doffset


def ttt_constants():
    lane = np.arange(PAIR)
    row = np.arange(MINI)
    sides = np.concatenate([np.tile(lane < HEAD, (MINI, 1)), np.tile(lane >= HEAD, (MINI, 1))])
    token = lane % MINI
    tri = np.where(token[None] <= row[:, None], 1.0 / (row[:, None] + 1.0), 0.0)
    same = lane[:, None] // MINI == lane[None] // MINI
    crossed = (lane[:, None] + HEAD) % PAIR // MINI == lane[None] // MINI
    scale = np.where(crossed & (token[None] <= token[:, None]), MINI / (token[:, None] + 1.0), 0.0)
    return (
        jnp.asarray(np.concatenate([sides, same, crossed]).astype(np.float32), low),
        jnp.asarray(np.concatenate([tri, scale, scale.T]), full),
    )


def ttt_forward(projected, rates, state, gains, shifts, steps=4):
    count = projected.shape[1] // MINI
    first, begin, end = 0, 0, count
    queries, keys, values = projected, projected, projected
    constants = ttt_constants()
    whole = lambda *shape: pl.BlockSpec(shape, lambda at: (0,) * len(shape))
    column = lambda place: pl.BlockSpec((2, steps * MINI, 768), lambda at, place=place: (0, first + at, place))
    part = column(0)
    saved = lambda *tail: pl.BlockSpec((steps,) + tail, lambda at: (at, 0, 0))
    made = lambda kind, *tail: jax.ShapeDtypeStruct((end - begin,) + tail, kind)
    inputs = [queries, keys, values, rates, *state, gains, shifts, *constants]
    out, *rest = pl.pallas_call(
        lambda *refs: ttt_forward_kernel(steps, *refs),
        grid=((end - begin) // steps,),
        in_specs=[column(0), column(1), column(2), pl.BlockSpec((steps, 1, 384), lambda at: (first + at, 0, 0)), whole(64, 1536), whole(64, 384),
                  whole(64, 384), whole(64, 384), whole(288, 128), whole(272, 128)],
        out_specs=[part, saved(64, 1536), saved(64, 384), saved(64, 384), saved(64, 384), saved(64, 384), saved(8, 384),
                   saved(16, 384)],
        out_shape=[jax.ShapeDtypeStruct((2, count * MINI, 768), full), made(low, 64, 1536), made(full, 64, 384), made(full, 64, 384),
                   made(full, 64, 384), made(full, 64, 384), made(full, 8, 384), made(full, 16, 384)],
        scratch_shapes=[pltpu.VMEM((64, 1536), full)] + [pltpu.VMEM((64, 384), full)] * 3,
        compiler_params=pltpu.CompilerParams(vmem_limit_bytes=60 * 1024 * 1024),
        cost_estimate=pl.CostEstimate(flops=(end - begin) * 1_400_000_000, bytes_accessed=(end - begin) * 1_500_000, transcendentals=0),
        name="ttt_forward",
    )(*inputs)
    return out, rest


def ttt_backward(projected, dout, rates, saved_arrays, state, gains, begin, end, before, steps=4):
    count = projected.shape[1] // MINI
    first, blocks = begin // steps, (end - begin) // steps
    queries, keys = projected, projected
    constants = ttt_constants()
    whole = lambda *shape: pl.BlockSpec(shape, lambda at: (0,) * len(shape))
    part = lambda width, place=0: pl.BlockSpec((2, steps * MINI, width), lambda at: (0, first + blocks - 1 - at, place))
    saved = lambda *tail: pl.BlockSpec((steps,) + tail, lambda at: (first + blocks - 1 - at, 0, 0))
    made = lambda *tail: pl.BlockSpec((steps,) + tail, lambda at: (blocks - 1 - at, 0, 0))
    extra = [] if before is None else [before]
    inputs = [queries, keys, dout, rates, *saved_arrays, gains, *constants, *(state or [])]
    states = [whole(64, 1536)] + [whole(64, 384)] * 5
    grad, rate_back, *sums = pl.pallas_call(
        lambda *refs: ttt_backward_kernel(steps, state is not None, *refs),
        grid=(blocks,),
        in_specs=[part(768), part(768, 1), part(768), saved(1, 384),
                  saved(64, 1536), saved(64, 384), saved(64, 384), saved(64, 384), saved(64, 384), saved(8, 384), saved(16, 384),
                  whole(64, 384), whole(288, 128), whole(272, 128)]
        + (states if state else []) + [pl.BlockSpec(memory_space=pl.ANY)] * len(extra),
        out_specs=[part(2304), made(1, 384)] + states,
        out_shape=[jax.ShapeDtypeStruct((2, count * MINI, 2304), low), jax.ShapeDtypeStruct((end - begin, 1, 384), full)]
        + [jax.ShapeDtypeStruct((64, 1536), full)] + [jax.ShapeDtypeStruct((64, 384), full)] * 5,
        scratch_shapes=[pltpu.VMEM((64, 384), full)],
        input_output_aliases={len(inputs): 0} if extra else {},
        compiler_params=pltpu.CompilerParams(vmem_limit_bytes=60 * 1024 * 1024),
        cost_estimate=pl.CostEstimate(flops=(end - begin) * 2_000_000_000, bytes_accessed=(end - begin) * 1_500_000, transcendentals=0),
        name="ttt_backward",
    )(*inputs, *extra)
    return grad, rate_back, sums


def silu_parts(gate):
    sigma = jax.nn.sigmoid(gate)
    return gate * sigma, sigma * (1.0 + gate * (1.0 - sigma))


def gelu_parts(values):
    slope = 0.7978845608028654
    turn = jnp.tanh(slope * (values + 0.044715 * values * values * values))
    half = 0.5 * (1.0 + turn)
    return values * half, half + 0.5 * values * (1.0 - turn * turn) * slope * (1.0 + 3 * 0.044715 * values * values)


def row_mean(values):
    return jnp.mean(values, axis=-1, keepdims=True)


def dot_tn(former, latter):
    return lax.dot_general(former, latter, (((0,), (0,)), ((), ())), preferred_element_type=full)


def exact_dot(former, latter):
    total = None
    for _ in range(3):
        part = former.astype(low)
        former = former - part.astype(full)
        term = dot_nn(part, latter)
        total = term if total is None else total + term
    return total


def constant_spec(*shape, at=0, buffers=None):
    index = lambda *steps: (0,) * (len(shape) - 1) + (at,)
    if buffers is None:
        return pl.BlockSpec(shape, index)
    return pl.BlockSpec(shape, index, pipeline_mode=pl.Buffered(buffers))


def call(kernel, name, grid, prefetch, in_specs, out_specs, out_shape, scratch, cost, arrays):
    return pl.pallas_call(
        kernel,
        grid_spec=pltpu.PrefetchScalarGridSpec(
            num_scalar_prefetch=prefetch, grid=grid, in_specs=in_specs, out_specs=out_specs, scratch_shapes=scratch
        ),
        out_shape=out_shape,
        compiler_params=pltpu.CompilerParams(vmem_limit_bytes=60 * 1024 * 1024),
        cost_estimate=pl.CostEstimate(flops=cost, bytes_accessed=cost // 500, transcendentals=0),
        name=name,
    )(*arrays)


ETA = 64
VECTORS = 80
BIAS = 96


def lane_table():
    lane = np.arange(384)
    part, group, side, tile, token = lane // 128, lane // 64 % 2, lane // 32 % 2, lane // 16 % 2, lane % 16
    pair = 4 * part + 2 * group + tile
    return token, pair // 6, 2 * (pair % 6) + side


def lane_constants():
    token, sequence, head = lane_table()
    table = np.zeros((32, 384), np.float32)
    table[:MINI] = token[None] == np.arange(MINI)[:, None]
    table[16], table[17] = sequence, token
    chosen = np.zeros((PAIR, 384), np.float32)
    chosen[ETA + head, np.arange(384)] = 1
    return jnp.asarray(table), jnp.asarray(chosen, low)


def block_copies(from_refs, table, to, columns, semaphores, first):
    started = []
    for place, ref in enumerate(from_refs):
        for item in range(ref.shape[0]):
            begin = pl.multiple_of(table[place * ref.shape[0] + item] * ref.shape[1], 16)
            target = to.at[pl.ds(begin, ref.shape[1]), columns]
            started.append(pltpu.make_async_copy(ref.at[item], target, semaphores.at[first + len(started)]))
    return started


def project_kernel(counts, length_ref, early_table_ref, late_table_ref, tokens_ref, bias_ref, table_ref, chosen_ref, *refs):
    early_refs, late_refs, refs = refs[: counts[0]], refs[counts[0] : sum(counts)], refs[sum(counts) :]
    whole_ref, proj_ref, normed_ref, rate_ref, rest_ref, wt_ref, b_ref, gain_ref, shift_ref, vec_ref, semaphores = refs
    at = pl.program_id(0)
    split = 512 // tokens_ref.shape[0]
    wide = proj_ref.shape[1]
    begin_small = whole_ref.shape[1] - PAIR
    cut = early_refs[0].shape[2]

    def copies():
        started = block_copies(early_refs, early_table_ref, whole_ref, slice(0, cut), semaphores, 0)
        return started + block_copies(late_refs, late_table_ref, whole_ref, slice(cut, whole_ref.shape[1]), semaphores, len(started))

    @pl.when(at == 0)
    def _():
        for copy in copies():
            copy.start()
        for copy in copies():
            copy.wait()
        small = whole_ref[:, begin_small:].astype(full)
        turned = small.T
        wt_ref[:, :768] = turned[:HEAD]
        wt_ref[:, 768:] = turned[:HEAD]
        vec_ref[...] = turned[VECTORS : VECTORS + 8]
        for place, ref in enumerate((b_ref, gain_ref, shift_ref)):
            total = jnp.zeros((HEAD, 384), full)
            for head in range(12):
                column = small[HEAD * head : HEAD * (head + 1), VECTORS + place : VECTORS + place + 1]
                total = total + column * chosen_ref[ETA + head : ETA + head + 1].astype(full)
            ref[...] = total
        rate_ref[...] = jnp.zeros_like(rate_ref)
        rest_ref[...] = jnp.zeros_like(rest_ref)

    values = tokens_ref[...].astype(full)
    normed = (values * lax.rsqrt(row_mean(values * values) + epsilon) * vec_ref[3:4]).astype(low)
    normed_ref[...] = normed
    proj_ref[...] = dot_nn(normed, whole_ref[:, :wide])
    last = dot_nn(normed, whole_ref[:, begin_small:])
    spread = exact_dot(last + bias_ref[...], chosen_ref[...])
    blocks = spread.shape[0] // MINI
    spread = jnp.sum(spread.reshape(blocks, MINI, 384) * table_ref[:MINI][None], axis=1)
    sequence, token = table_ref[16:17], table_ref[17:18]
    mine = sequence == (at // split).astype(full)
    sigma = jax.nn.sigmoid(spread)
    begin = (at % split) * blocks
    block = lax.broadcasted_iota(jnp.int32, spread.shape, 0) + begin
    live = (block * MINI).astype(full) + token < length_ref[at // split].astype(full)
    here = pl.ds(begin, blocks)
    rate_ref[here, 0, :] += jnp.where(live & mine, sigma * (1.0 / HEAD), 0.0)
    rest_ref[here, :] += jnp.where(mine, 1.0 - sigma, 0.0)


def project(lengths, tokens, early, late, bias_row):
    rows, width = tokens.shape
    table, chosen = lane_constants()
    tile = rows // 2
    columns = early[0][0].shape[2] + late[0][0].shape[2]
    counts = len(early[0]), len(late[0])
    row = lambda n: pl.BlockSpec((tile, n), lambda at, *_: (at, 0))
    shape = jax.ShapeDtypeStruct
    return call(
        lambda *refs: project_kernel(counts, *refs), "project", (2,), 3,
        [row(width), constant_spec(1, PAIR), constant_spec(32, 384), constant_spec(PAIR, 384)]
        + [pl.BlockSpec(memory_space=pl.ANY)] * sum(counts),
        [constant_spec(width, columns, buffers=1), row(3 * width), row(width), constant_spec(32, 1, 384), constant_spec(32, 384),
         constant_spec(64, 1536)] + [constant_spec(64, 384)] * 3 + [constant_spec(8, width)],
        [shape((width, columns), low), shape((rows, 3 * width), full), shape((rows, width), low), shape((32, 1, 384), full),
         shape((32, 384), full), shape((64, 1536), full)] + [shape((64, 384), full)] * 3 + [shape((8, width), full)],
        [pltpu.SemaphoreType.DMA((early[1].shape[0] + late[1].shape[0],))], 5_000_000_000,
        (lengths, early[1], late[1], tokens, bias_row, table, chosen, *early[0], *late[0]),
    )


def post_kernel(inner_ref, normed_ref, tokens_ref, w_gate_ref, w_out_ref, vec_ref, gate_ref, mixed_ref, first_ref, second_ref):
    gate = dot_nn(normed_ref[...], w_gate_ref[...])
    gate_ref[...] = gate
    inner = inner_ref[...]
    centred = inner - row_mean(inner)
    standard = centred * lax.rsqrt(row_mean(centred * centred) + epsilon)
    mixed = ((standard * vec_ref[4:5] + vec_ref[5:6]) * gelu_parts(gate)[0]).astype(low)
    mixed_ref[...] = mixed
    first = tokens_ref[...].astype(full) + dot_nn(mixed, w_out_ref[...])
    first_ref[...] = first
    second_ref[...] = (first * lax.rsqrt(row_mean(first * first) + epsilon) * vec_ref[6:7]).astype(low)


def post(inner, normed, tokens, whole, vectors):
    rows, width = tokens.shape
    tile = rows // 2
    row = pl.BlockSpec((tile, width), lambda at: (at, 0))
    shape = jax.ShapeDtypeStruct
    return call(
        post_kernel, "post", (2,), 0,
        [row, row, row, constant_spec(width, width, at=3, buffers=1), constant_spec(width, width, at=4, buffers=1), constant_spec(8, width)],
        [row] * 4, [shape((rows, width), kind) for kind in (full, low, full, low)], [], 4_000_000_000,
        (inner, normed, tokens, whole, whole, vectors),
    )


def store_blocks(table_ref, sent_ref, kept_ref, held_ref, block):
    half = kept_ref.shape[0]
    if block % 8:
        kept_ref[...] = held_ref[:half].astype(kept_ref.dtype)
        sent_ref[...] = held_ref[half:].astype(sent_ref.dtype)
        return
    for pair in range(held_ref.shape[0] // (2 * block)):
        rows = [held_ref[pl.ds(pl.multiple_of(table_ref[2 * pair + side] * block, 8), block), :] for side in range(2)]
        begin = 2 * block * pair
        ref, begin = (kept_ref, begin) if begin < half else (sent_ref, begin - half)
        ref[begin : begin + 2 * block, :] = jnp.concatenate(rows, axis=0).astype(ref.dtype)


def ffn_kernel(block, down_block, steps, counts, table_ref, shared_ref, both_table_ref, down_table_ref, second_ref, first_ref, up_ref, *refs):
    both_refs, refs = refs[: counts[0]], refs[counts[0] :]
    down_refs, refs = refs[: counts[1]], refs[counts[1] :]
    aligned = block % 8 == 0
    out_ref, dsecond_ref, sent_ref, kept_ref, *refs = refs
    natural_ref, refs = (None, refs) if aligned else (refs[0], refs[1:])
    turned, total, act, both_low, held, w_both, w_down_all, held_down, semaphores = refs
    at = pl.program_id(0)
    size = act.shape[1]
    hidden = w_down_all.shape[0]

    def copies():
        started = block_copies(both_refs, both_table_ref, w_both, slice(None), semaphores, 0)
        return started + block_copies(down_refs, down_table_ref, w_down_all, slice(None), semaphores, len(started))

    @pl.when(at == 0)
    def _():
        for copy in copies():
            copy.start()
        turned[...] = second_ref[...].T
        total[...] = first_ref[...]
        dsecond_ref[...] = jnp.zeros_like(dsecond_ref)
        for copy in copies():
            copy.wait()

    @pl.when(at < steps)
    def _():
        columns = pl.ds(pl.multiple_of(at * size, PAIR), size)
        w_gate, w_up = w_both[:, columns], w_both[:, pl.ds(pl.multiple_of(hidden + at * size, PAIR), size)]
        w_down = w_down_all[columns, :]
        second, upstream = second_ref[...], up_ref[...]
        cuts = [slice(begin, begin + size // 2) for begin in range(0, size, size // 2)]
        made = [(dot_nn(second, w_gate[:, cut]), dot_nn(second, w_up[:, cut]), dot_nt(upstream, w_down[cut])) for cut in cuts]
        for cut, (gate, up, dact) in zip(cuts, made):
            value, slope = silu_parts(gate)
            act[:, cut] = (value * up).astype(low)
            both_low[:, cut] = (dact * up * slope).astype(low)
            both_low[:, size + cut.start : size + cut.stop] = (dact * value).astype(low)
        total[...] += dot_nn(act[...], w_down)
        dsecond_ref[...] += dot_nt(both_low[:, :size], w_gate) + dot_nt(both_low[:, size:], w_up)
        ddown = dot_tn(act[...], upstream)
        held[...] = dot_nn(turned[...], both_low[...])
        if aligned:
            count = size // down_block
            third = ddown.shape[1] // 3
            for place in range(count):
                mine = ddown[down_block * place : down_block * (place + 1)]
                pieces = [jnp.concatenate([mine[8 * row : 8 * row + 8, third * part : third * (part + 1)] for row in range(down_block // 8)],
                                          axis=1) for part in range(3)]
                held_down[pl.ds(pl.multiple_of((at * count + place) * block, 8), block), :] = jnp.concatenate(pieces, axis=0)
        else:
            natural_ref[pl.ds(pl.multiple_of(at * size, 16), size), :] = ddown.astype(low)
        store_blocks(table_ref, sent_ref, kept_ref, held, block)

    @pl.when(at == steps - 1)
    def _():
        out_ref[...] = total[...].astype(low)

    if aligned:
        for extra in range(held_down.shape[1] // (2 * size)):

            @pl.when(at == steps + extra)
            def _():
                store_blocks(shared_ref, sent_ref, kept_ref, held_down.at[:, 2 * size * extra : 2 * size * (extra + 1)], block)


def ffn(table, shared, second, first, upstream, both, down, devices, steps):
    rows, width = second.shape
    hidden = down[0][0].shape[1] * down[1].shape[0]
    size = hidden // steps
    aligned = width // devices % 8 == 0
    columns = 3 * hidden if aligned else 2 * hidden
    shape = jax.ShapeDtypeStruct
    counts = len(both[0]), len(down[0])
    copies = both[1].shape[0] + down[1].shape[0]
    natural = [] if aligned else [(hidden, width)]
    return call(
        lambda *refs: ffn_kernel(width // devices, hidden // devices, steps, counts, *refs), "ffn", (columns // (2 * size),), 4,
        [constant_spec(rows, width, buffers=1)] * 3 + [pl.BlockSpec(memory_space=pl.ANY)] * sum(counts),
        [constant_spec(rows, width, buffers=1), constant_spec(rows, width, buffers=1),
         *[pl.BlockSpec((width // 2, 2 * size), lambda at, *_: (0, at))] * 2, *[constant_spec(*item, buffers=1) for item in natural]],
        [shape((rows, width), low), shape((rows, width), full), *[shape((width // 2, columns), low)] * 2,
         *[shape(item, low) for item in natural]],
        [pltpu.VMEM((width, rows), low), pltpu.VMEM((rows, width), full), pltpu.VMEM((rows, size), low),
         pltpu.VMEM((rows, 2 * size), low), pltpu.VMEM((width, 2 * size), full), pltpu.VMEM((width, 2 * hidden), low),
         pltpu.VMEM((hidden, width), low), pltpu.VMEM((width, hidden) if aligned else (8, PAIR), full),
         pltpu.SemaphoreType.DMA((copies,))],
        29_000_000_000, (table, shared, both[1], down[1], second, first, upstream, *both[0], *down[0]),
    )


def fold_kernel(layout, last, paired, *refs):
    outs = refs[sum(sum(members) + extra for members, extra in layout) :]
    for group, (members, extra) in enumerate(layout):
        mine, refs = refs[: sum(members) + extra], refs[sum(members) + extra :]
        totals = []
        for count in members:
            totals.append(sum(ref[...].astype(full) for ref in mine[:count]))
            mine = mine[count:]
        total = jnp.concatenate(totals, axis=1) if len(totals) > 1 else totals[0]
        for ref in mine:
            total = total + ref[...].astype(full)
        if paired and group + 1 == len(layout):
            plain = total.shape[1] - 2 * paired
            tail = total[:, plain : plain + paired] + total[:, plain + paired :]
            high = tail.astype(low).astype(full)
            total = jnp.concatenate([total[:, :plain], high, tail - high], axis=1)
        if last:
            half = total.shape[0] // 2
            outs[2 * group][...] = total[half:].astype(low)
            outs[2 * group + 1][...] = total[:half]
        else:
            outs[group][...] = total.astype(low)


def fold(groups, rows, steps, paired=0):
    last = rows // 2 % MINI != 0
    size, place = (rows, 0) if last else (rows // 2, 1)
    specs, arrays, outs, shapes, layout = [], [], [], [], []
    for members, extra in groups:
        width = 0
        for addends, first, columns in members:
            part = columns // steps
            specs += [pl.BlockSpec((size, part), lambda at, begin=first // part: (place, begin + at))] * len(addends)
            arrays += addends
            width += part
        specs += [pl.BlockSpec((size, width), lambda at: (place, at))] * len(extra)
        arrays += extra
        layout.append(([len(addends) for addends, _, _ in members], len(extra)))
        outs += [pl.BlockSpec((rows // 2, width), lambda at: (0, at))] * (2 if last else 1)
        shapes += [jax.ShapeDtypeStruct((rows // 2, width * steps), kind) for kind in ((low, full) if last else (low,))]
    results = call(
        lambda *refs: fold_kernel(layout, last, paired, *refs), "fold", (steps,), 0, specs, outs, shapes, [], 100_000_000, arrays
    )
    return [(results[2 * group], results[2 * group + 1]) for group in range(len(groups))] if last else list(results)


class Scatter:
    def __init__(self, links, groups, rows, steps, paired=0):
        self.links, self.steps, self.paired = links, steps, paired
        self.groups = [(members, []) for members in groups]
        self.rows, self.phase, self.kept, self.sent = rows, 0, None, None

    def fold(self):
        if self.kept is None:
            made = fold(self.groups, self.rows, self.steps, self.paired)
            if self.rows // 2 % MINI:
                self.sent, self.kept = [sent for sent, _ in made], [kept for _, kept in made]
            else:
                self.sent = made
        else:
            half = self.rows // 2
            totals = [kept + got.astype(full) for kept, got in zip(self.kept, self.got)]
            self.sent, self.kept = [total[half:].astype(low) for total in totals], [total[:half] for total in totals]
        self.rows //= 2

    def send(self):
        links, phase = self.links, self.phase
        self.got = []
        for sent, kind in zip(self.sent, ("split", "shared")):
            bits = [order[phase] for order in links.orders[kind]] if phase < links.near else [links.far] * 2
            self.got.append(links.swap(sent, bits))
        self.phase += 1
        if self.kept is None:
            self.groups = [(members, extra + [got]) for (members, extra), got in zip(self.groups, self.got)]

    def tied(self, *others):
        state = (self.sent, self.kept, self.got, self.groups) if self.phase else (self.sent,)
        arrays, tree = jax.tree.flatten(state)
        numbers = [place for place, array in enumerate(arrays) if not isinstance(array, int)]
        out = tie(*others, [arrays[place] for place in numbers])
        for place, array in zip(numbers, out[-1]):
            arrays[place] = array
        state = jax.tree.unflatten(tree, arrays)
        self.sent = state[0]
        if len(state) > 1:
            self.kept, self.got, self.groups = state[1:]
        return out[:-1] if len(others) > 1 else out[0]

    def result(self):
        while self.phase <= self.links.near:
            self.fold()
            self.send()
        return [kept + got.astype(full) for kept, got in zip(self.kept, self.got)]


def post_back_kernel(dsecond_ref, first_ref, up_ref, inner_ref, gate_ref, w_out_ref, vec_ref,
                     dfirst_ref, dgate_ref, dinner_ref, dfirst_low_ref, sums_ref):
    @pl.when(pl.program_id(0) == 0)
    def _():
        sums_ref[...] = jnp.zeros_like(sums_ref)

    first, dsecond = first_ref[...], dsecond_ref[...]
    scale = lax.rsqrt(row_mean(first * first) + epsilon)
    sums_ref[6:7] += jnp.sum(dsecond * first * scale, axis=0, keepdims=True)
    dsecond = dsecond * vec_ref[6:7]
    dfirst = up_ref[...].astype(full) + scale * dsecond - first * (scale * scale * scale * row_mean(first * dsecond))
    dfirst_ref[...] = dfirst
    dfirst_low = dfirst.astype(low)
    dfirst_low_ref[...] = dfirst_low
    dmixed = dot_nt(dfirst_low, w_out_ref[...])
    inner = inner_ref[...]
    centred = inner - row_mean(inner)
    inverse = lax.rsqrt(row_mean(centred * centred) + epsilon)
    standard = centred * inverse
    value, slope = gelu_parts(gate_ref[...])
    dgate_ref[...] = (dmixed * (standard * vec_ref[4:5] + vec_ref[5:6]) * slope).astype(low)
    dpost = dmixed * value
    sums_ref[4:5] += jnp.sum(dpost * standard, axis=0, keepdims=True)
    sums_ref[5:6] += jnp.sum(dpost, axis=0, keepdims=True)
    dpost = dpost * vec_ref[4:5]
    dinner_ref[...] = inverse * (dpost - row_mean(dpost) - standard * row_mean(dpost * standard))


def post_back(dsecond, first, upstream, inner, gate, whole, vectors):
    rows, width = first.shape
    tile = rows // 4
    row = pl.BlockSpec((tile, width), lambda at: (at, 0))
    shape = jax.ShapeDtypeStruct
    return call(
        post_back_kernel, "post_back", (4,), 0,
        [row] * 5 + [constant_spec(width, width, at=4, buffers=1), constant_spec(8, width)],
        [row, row, row, row, constant_spec(8, width)],
        [shape((rows, width), full), shape((rows, width), low), shape((rows, width), full), shape((rows, width), low),
         shape((8, width), full)],
        [], 4_000_000_000, (dsecond, first, upstream, inner, gate, whole, vectors),
    )


def middle_kernel(block, table_ref, mixed_ref, dfirst_ref, normed_ref, dgate_ref, sent_ref, kept_ref, held):
    @pl.when(pl.program_id(0) == 0)
    def _():
        held[...] = dot_tn(mixed_ref[...], dfirst_ref[...])

    @pl.when(pl.program_id(0) == 1)
    def _():
        held[...] = dot_tn(normed_ref[...], dgate_ref[...])

    store_blocks(table_ref, sent_ref, kept_ref, held, block)


def middle_grads(table, mixed, dfirst, normed, dgate, devices):
    rows, width = normed.shape
    whole = constant_spec(rows, width, buffers=1)
    return call(
        lambda *refs: middle_kernel(width // devices, *refs), "middle_grads", (2,), 1,
        [whole] * 4, [pl.BlockSpec((width // 2, width), lambda at, *_: (0, at))] * 2,
        [jax.ShapeDtypeStruct((width // 2, 2 * width), low)] * 2, [pltpu.VMEM((width, width), full)], 3_000_000_000,
        (table, mixed, dfirst, normed, dgate),
    )


def weight_kernel(block, table_ref, normed_ref, grad_ref, sent_ref, kept_ref, turned, held):
    @pl.when(pl.program_id(0) == 0)
    def _():
        turned[...] = normed_ref[...].T

    held[...] = dot_nn(turned[...], grad_ref[...])
    store_blocks(table_ref, sent_ref, kept_ref, held, block)


def weight_grads(table, normed, grads, devices):
    rows, width = normed.shape
    out = pl.BlockSpec((width // 2, width), lambda at, *_: (0, at))
    return call(
        lambda *refs: weight_kernel(width // devices, *refs), "weight_grads", (2,), 1,
        [constant_spec(rows, width, buffers=1), pl.BlockSpec((rows, width), lambda at, *_: (0, at))],
        [out, out], [jax.ShapeDtypeStruct((width // 2, 2 * width), low)] * 2,
        [pltpu.VMEM((width, rows), low), pltpu.VMEM((width, width), full)], 3_000_000_000, (table, normed, grads),
    )


def last_kernel(block, table_ref, normed_ref, grad_ref, sums_ref, dw_ref, db_ref, dgain_ref, dshift_ref, dgain_query_ref,
                dshift_query_ref, rate_ref, rest_ref, lane_ref, chosen_ref, sent_ref, kept_ref, dlog_ref, held):
    rows, width = normed_ref.shape
    turned = normed_ref[...].T
    held[:, :width] = dot_nn(turned, grad_ref[...])
    slots = rate_ref.shape[0] * MINI
    for sequence in range(rows // slots):
        mine = (lane_ref[16:17] == float(sequence)).astype(full)
        spread = rate_ref[:, 0, :] * rest_ref[...] * mine
        spread = (spread[:, None, :] * lane_ref[:MINI][None]).reshape(slots, 384).astype(low)
        dlog_ref[slots * sequence : slots * (sequence + 1)] = dot_nt(spread, chosen_ref[...]).astype(low)
    eta = dot_nn(turned, dlog_ref[...])
    inner = dw_ref[:, :width] + dw_ref[:, width:]
    fixed = jnp.concatenate(
        [inner, jnp.zeros((VECTORS - HEAD, width), full), sums_ref[...], jnp.zeros((PAIR - VECTORS - 8, width), full)], axis=0
    )
    lane = lax.broadcasted_iota(jnp.int32, (HEAD, PAIR), 1)
    chosen = chosen_ref[...].astype(full)
    bias = jnp.sum(rate_ref[:, 0, :] * rest_ref[...], axis=0, keepdims=True)
    held[:, width : width + PAIR] = eta + fixed.T
    bias = jnp.sum(chosen * bias, axis=1, keepdims=True)
    square = jnp.broadcast_to(bias, (PAIR, PAIR)).T[:1]
    bias_row = pltpu.roll(square, BIAS - ETA, axis=1)
    bias_row = jnp.where((lane[:1] >= BIAS) & (lane[:1] < BIAS + 12), bias_row, 0.0)
    lanes_of = [db_ref[...] * (1.0 / MINI), dgain_ref[...] + exchange(dgain_query_ref[...]), dshift_ref[...] + exchange(dshift_query_ref[...])]
    for head in range(12):
        here = pl.ds(HEAD * head, HEAD)
        mask = chosen[ETA + head : ETA + head + 1]
        total = held[here, width : width + PAIR] + bias_row
        for place, values in enumerate(lanes_of):
            column = jnp.sum(values * mask, axis=1, keepdims=True)
            total = total + jnp.where(lane == VECTORS + place, column, 0.0)
        high = total.astype(low).astype(full)
        held[here, width : width + PAIR] = high
        held[here, width + PAIR :] = total - high
    store_blocks(table_ref, sent_ref, kept_ref, held, block)


def last_grads(table, normed, grads, sums, state, rate_back, rest, devices):
    rows, width = normed.shape
    lane, chosen = lane_constants()
    spec = lambda array: constant_spec(*array.shape, buffers=1)
    others = (sums, *state, rate_back, rest, lane, chosen)
    shape = jax.ShapeDtypeStruct
    out = constant_spec(width // 2, width + 2 * PAIR, buffers=1)
    return call(
        lambda *refs: last_kernel(width // devices, *refs), "last_grads", (1,), 1,
        [spec(normed), constant_spec(rows, width, at=2, buffers=1)] + [spec(array) for array in others],
        [out, out, constant_spec(rows, PAIR, buffers=1)],
        [shape((width // 2, width + 2 * PAIR), low)] * 2 + [shape((rows, PAIR), low)],
        [pltpu.VMEM((width, width + 2 * PAIR), full)], 3_000_000_000, (table, normed, grads, *others),
    )


def finish_kernel(tokens_ref, dfirst_ref, dqkv_ref, dgate_ref, dlog_ref, w_ref, small_ref, w_gate_ref, vec_ref, out_ref):
    dnormed = dot_nt(dqkv_ref[...], w_ref[...]) + dot_nt(dgate_ref[...], w_gate_ref[...]) + dot_nt(dlog_ref[...], small_ref[...])
    values = tokens_ref[...].astype(full)
    scale = lax.rsqrt(row_mean(values * values) + epsilon)
    dnormed = dnormed * vec_ref[3:4]
    back = scale * dnormed - values * (scale * scale * scale * row_mean(values * dnormed))
    out_ref[...] = (dfirst_ref[...] + back).astype(low)


def finish(tokens, dfirst, dqkv, dgate, dlog, whole, vectors, at, before):
    rows, width = tokens.shape
    tile = rows // 2
    row = lambda n: pl.BlockSpec((tile, n), lambda step: (at, 0))
    arrays = [tokens, dfirst, dqkv, dgate, dlog, whole, whole, whole, vectors]
    extra = [] if before is None else [before]
    return pl.pallas_call(
        lambda *refs: finish_kernel(*refs[:9], refs[-1]),
        grid=(1,),
        in_specs=[row(width), row(width), row(3 * width), row(width), row(PAIR), constant_spec(width, 3 * width, buffers=1),
                  constant_spec(width, PAIR, at=5 * width // PAIR, buffers=1), constant_spec(width, width, at=3, buffers=1),
                  constant_spec(8, width)] + [pl.BlockSpec(memory_space=pl.ANY)] * len(extra),
        out_specs=row(width),
        out_shape=jax.ShapeDtypeStruct((rows, width), low),
        input_output_aliases={len(arrays): 0} if extra else {},
        compiler_params=pltpu.CompilerParams(vmem_limit_bytes=60 * 1024 * 1024),
        cost_estimate=pl.CostEstimate(flops=3_000_000_000, bytes_accessed=10_000_000, transcendentals=0),
        name="finish",
    )(*arrays, *extra)


class Links:
    def __init__(self, dp, fsdp):
        self.axes = ("dp", "fsdp")
        self.count = dp * fsdp
        self.core = fsdp
        self.far = fsdp // 2
        bits = [1 << place for place in reversed(range(self.count.bit_length() - 1))]
        self.others = [bit for bit in bits if bit != self.core]
        near = [bit for bit in reversed(self.others) if bit != self.far]
        near = near[:1] + near[:0:-1]
        turned = [near[turn:] + near[:turn] for turn in range(3)]
        self.orders = {"split": [turned[0], turned[2]], "shared": [turned[1]] * 2}
        self.phases = self.near = len(near)
        self.me = lax.axis_index("dp") * fsdp + lax.axis_index("fsdp")
        self.side = (self.me // self.core) % 2

    def swap(self, values, bits):
        pairs = [(place, place ^ bits[(place // self.core) % 2]) for place in range(self.count)]
        return lax.ppermute(values, self.axes, pairs)

    def one(self, bit):
        return (self.me // bit) % 2

    def join(self, held, bits):
        got = self.swap(held, bits)
        mine = jnp.where(self.side == 0, self.one(bits[0]), self.one(bits[1])) == 0
        return jnp.stack([jnp.where(mine, held, got), jnp.where(mine, got, held)])

    def gather(self, pieces, kinds):
        orders = [[[self.far] + order for order in self.orders[kind]] for kind in kinds]
        held = list(pieces)
        for phase in range(len(orders[0][0])):
            held = [self.join(array, [order[phase] for order in pair]) for array, pair in zip(held, orders)]
            changed = yield held
            held = held if changed is None else changed
        above = [bit for bit in self.others if bit > self.core]
        whole = []
        for array, pair in zip(held, orders):
            got = self.swap(array, [self.core] * 2)
            mine = self.side == 0
            cores = [jnp.where(mine, array, got), jnp.where(mine, got, array)]
            placed = []
            for half, order in zip(cores, pair):
                have = order[::-1]
                placed.append(half.transpose([have.index(bit) for bit in self.others] + [len(have), len(have) + 1]))
            whole.append(jnp.stack(placed, axis=len(above)).reshape(-1, array.shape[-1]))
        yield whole

    def gather_blocks(self, pieces, kinds, pairs, whole_last):
        held = list(pieces)
        orders = [self.orders[kind] for kind in kinds]
        count = self.phases

        def ready(array, place):
            rows = pieces[place].shape[0]
            if not pairs[place]:
                return array.reshape((-1, rows) + array.shape[-1:])
            turned = []
            stacked = array.ndim - 2
            for order in orders[place]:
                have = ([self.far] + order)[:stacked][::-1]
                at = have.index(1)
                turned.append(array.transpose([axis for axis in range(stacked) if axis != at] + [at, stacked, stacked + 1]))
            array = jnp.where(self.side == 0, turned[0], turned[1])
            return array.reshape((-1, 2 * rows) + array.shape[-1:])

        for phase in range(count):
            for place, pair in enumerate(orders):
                held[place] = self.join(held[place], [self.far] * 2 if phase == 0 else [order[phase - 1] for order in pair])
                if phase == count - 1 and not whole_last[place]:
                    held[place] = ready(held[place], place)
            changed = yield held
            held = held if changed is None else changed
        buffers = []
        for place, pair in enumerate(orders):
            last = [order[-1] for order in pair]
            if whole_last[place]:
                buffers.append([ready(self.join(held[place], last), place)])
            else:
                buffers.append([held[place], self.swap(held[place], last), self.swap(held[place], [self.core] * 2)])
        changed = yield buffers
        buffers = buffers if changed is None else changed
        buffers = [list(group) + [self.swap(group[0 if whole else 1], [self.core] * 2)] for group, whole in zip(buffers, whole_last)]

        def places(bits, device, unit):
            found = []
            clear = device & ~(sum(bits) + unit - 1)
            for place in range(1 << len(bits)):
                found.append((clear + sum(bit for at, bit in enumerate(bits) if place >> (len(bits) - 1 - at) & 1)) // unit)
            return jnp.stack(found)

        done = []
        for place, pair in enumerate(orders):
            unit = 2 if pairs[place] else 1
            table = []
            for core, last in ((0, 0), (self.core, 0)) if whole_last[place] else ((0, 0), (0, 1), (self.core, 0), (self.core, 1)):
                by_side = []
                for order in pair:
                    have = ([self.far] + order)[::-1] if whole_last[place] else ([self.far] + order[:-1])[::-1]
                    by_side.append(places([bit for bit in have if bit >= unit], self.me ^ core ^ (order[-1] if last else 0), unit))
                own = self.side if core == 0 else 1 - self.side
                table.append(jnp.where(own == 0, by_side[0], by_side[1]))
            done.append((buffers[place], jnp.concatenate(table).astype(jnp.int32)))
        yield done

    def table(self, kind):
        half = []
        for side in range(2):
            masks = self.orders[kind][side] + [self.far]
            half.append(np.array([sum(bit for at, bit in enumerate(masks) if place >> (len(masks) - 1 - at) & 1)
                                  for place in range(self.count // 2)], np.int32))
        keep = jnp.where(self.side == 0, half[0], half[1])
        send = jnp.where(self.side == 0, half[1], half[0])
        return jnp.concatenate([self.me ^ keep, self.me ^ self.core ^ send]).astype(jnp.int32)

    def exchange_cores(self, pair):
        return pair[1], self.swap(pair[0], [self.core] * 2)


def tie(*groups):
    flat, tree = jax.tree.flatten(groups)
    return jax.tree.unflatten(tree, lax.optimization_barrier(flat))


def halves(array):
    half = array.shape[0] // 2
    return array[half:], array[:half]


def tie(*groups):
    flat, tree = jax.tree.flatten(groups)
    return jax.tree.unflatten(tree, lax.optimization_barrier(flat))


def halves(array):
    half = array.shape[0] // 2
    return array[half:], array[:half]


def in_order(table, pair, rows):
    if rows % 8 == 0:
        return pair
    whole = jnp.concatenate([pair[1], pair[0]], axis=0)
    return halves(whole.reshape((-1, rows) + whole.shape[1:])[table].reshape(whole.shape))


def body(dp, fsdp, tokens, lengths, cotangent, mixer_in, w_eta, eta_bias, w_out, inner_w, inner_b, ttt_gain, ttt_shift,
         norm_one, post_gain, post_shift, w_gate_up, w_down, norm_two):
    links = Links(dp, fsdp)
    devices = dp * fsdp
    micro, slots, width = tokens.shape
    rows = micro * slots
    heads = eta_bias.shape[0]
    head = width // heads
    hidden = w_gate_up.shape[1] // 2
    device_rows = width // devices
    table, shared = links.table("split"), links.table("shared")
    zeros = lambda columns: jnp.zeros((device_rows, columns), low)

    vectors = jnp.stack([inner_b, ttt_gain, ttt_shift, norm_one, post_gain, post_shift, norm_two])
    vectors = dot_tn(vectors, jnp.eye(7, PAIR, VECTORS, dtype=low)).astype(low)
    small = jnp.concatenate([inner_w, w_eta, zeros(PAIR - ETA - heads)], axis=1) + vectors
    cut = 22 * PAIR
    pieces = [mixer_in[:, :cut], jnp.concatenate([mixer_in[:, cut:], w_out, small], axis=1)]
    rest = [w_gate_up, w_down]
    kinds = ["split", "shared"]
    aligned = device_rows % 8 == 0
    if aligned:
        mixer_phases = links.gather_blocks(pieces, kinds, [True, True], [False, True])
    else:
        mixer_phases = links.gather(pieces, kinds)
    places = lax.broadcasted_iota(jnp.int32, (micro, slots), 1)
    live = places < lengths
    upstream = jnp.where(live[..., None], cotangent, jnp.zeros_like(cotangent)).reshape(rows, width)
    held = next(mixer_phases)
    for _ in range(links.phases - 2):
        held = mixer_phases.send(held)
    held, rest, upstream = tie(held, rest, upstream)
    rest_phases = links.gather_blocks(rest, kinds, [True, False], [False, False]) if aligned else links.gather(rest, kinds)
    held, rest = mixer_phases.send(held), next(rest_phases)
    held, rest = mixer_phases.send(held), rest_phases.send(rest)
    held = mixer_phases.send(held)
    as_blocks = lambda arrays: [([array[None]], jnp.zeros((1,), jnp.int32)) for array in arrays]
    early, late = held if aligned else as_blocks(held)

    inputs = tokens.reshape(rows, width)
    bias_row = jnp.pad(eta_bias.astype(full), (ETA, PAIR - ETA - heads)).reshape(1, PAIR)
    early, late, rest = tie(early, late, rest)
    rest = rest_phases.send(rest)
    whole, projected, normed, rate_lanes, rest_lanes, start_w, start_b, gain_lanes, shift_lanes, vec_rows = project(
        lengths.reshape(micro), inputs, early, late, bias_row
    )
    projected = projected.reshape(micro, slots, -1)
    rate_lanes, rest = tie(rate_lanes, rest)
    rest = rest_phases.send(rest)
    inner, saved = ttt_forward(projected, rate_lanes, [start_w, start_b], gain_lanes, shift_lanes)
    inner = inner.reshape(rows, width)
    inner, rest = tie(inner, rest)
    rest = drain(rest_phases, rest)
    if not aligned:
        rest = as_blocks(rest)
    gate, mixed, first, second = post(inner, normed, inputs, whole, vec_rows)
    block_out, dsecond, large_sent, large_kept, *natural = ffn(table, shared, second, first, upstream, *rest, devices, dp)
    down_rows = hidden // devices
    unit = min(8, device_rows // 3)
    if not aligned:
        natural = natural[0].reshape(devices, -1, unit, 3, width // 3).transpose(0, 3, 2, 1, 4).reshape(width, hidden)
        pairs = in_order(table, (large_sent, large_kept), device_rows), in_order(shared, halves(natural), device_rows)
        large_sent, large_kept = (jnp.concatenate(pair, axis=1) for pair in zip(*pairs))
    large = links.exchange_cores((large_sent, large_kept))
    dfirst, dgate, dinner, dfirst_low, sums = post_back(dsecond, first, upstream, inner, gate, whole, vec_rows)
    middle = middle_grads(table, mixed, dfirst_low, normed, dgate, devices)
    middle = links.exchange_cores(in_order(table, tuple(middle), device_rows))
    dinner, large, middle = tie(dinner, large, middle)
    large, middle = list(large), list(middle)
    whole_rows = width // 2
    first_sum = Scatter(
        links, [[(large, 0, 2 * hidden), (middle, 0, 2 * width)], [(large, 2 * hidden, hidden)]], whole_rows, 2
    )
    first_sum.fold()
    dinner = first_sum.tied(dinner)
    first_sum.send()
    dinner = dinner.reshape(micro, slots, width)
    dqkv, rate_late, state = ttt_backward(projected, dinner, rate_lanes, saved, None, gain_lanes, 4, slots // MINI, None)
    dqkv, state = first_sum.tied(dqkv, state)
    first_sum.fold()
    dqkv, state = first_sum.tied(dqkv, state)
    first_sum.send()
    dqkv, rate_early, state = ttt_backward(projected, dinner, rate_lanes, saved, state, gain_lanes, 0, 4, dqkv)
    dqkv = dqkv.reshape(rows, 3 * width)
    rate_back = jnp.concatenate([rate_early, rate_late], axis=0)
    early = weight_grads(table, normed, dqkv, devices)
    dqkv, early = first_sum.tied(dqkv, list(early))
    first_sum.fold()
    dqkv, early = first_sum.tied(dqkv, early)
    first_sum.send()
    early = links.exchange_cores(in_order(table, tuple(early), device_rows))
    *late, dlog = last_grads(shared, normed, dqkv, sums, state, rate_back, rest_lanes, devices)
    late, dlog, early = first_sum.tied(list(late), dlog, early)
    late = links.exchange_cores(in_order(shared, tuple(late), device_rows))
    first_sum.fold()
    late = first_sum.tied(late)
    first_sum.send()
    second_sum = Scatter(
        links, [[(list(early), 0, 2 * width)], [(list(late), 0, width + 2 * PAIR)]], whole_rows, 1, PAIR
    )
    second_sum.fold()
    dlog = second_sum.tied(dlog)
    second_sum.send()
    grad_tokens = None
    for half in range(2):
        grad_tokens = finish(inputs, dfirst, dqkv, dgate, dlog, whole, vec_rows, half, grad_tokens)
        grad_tokens = second_sum.tied(grad_tokens)
        second_sum.fold()
        second_sum.send()
    early, late = second_sum.result()
    large, down = first_sum.result()
    part = hidden // dp
    large = large.reshape(device_rows, 2, -1)
    both = large[:, :, :hidden].reshape(device_rows, dp, 2, part).transpose(0, 2, 1, 3).reshape(device_rows, 2 * hidden)
    middle = large[:, :, hidden:].reshape(device_rows, 2 * width)
    out_small = late[:, width : width + PAIR] + late[:, width + PAIR :]
    out_out, out_gate_in = middle[:, :width], middle[:, width:]
    out_mixer = jnp.concatenate([early, late[:, :width], out_gate_in], axis=1)
    out_eta = out_small[:, ETA : ETA + heads]
    out_norm_one = jnp.sum(mixer_in.astype(full) * out_mixer, axis=1) + jnp.sum(w_eta.astype(full) * out_eta, axis=1)
    out_norm_one = out_norm_one / norm_one.astype(full)
    out_inner_b, out_gain, out_shift, _, out_post_gain, out_post_shift, out_norm_two = (
        out_small[:, VECTORS + place] for place in range(7)
    )
    return (
        block_out.reshape(tokens.shape),
        grad_tokens.reshape(tokens.shape),
        out_mixer,
        out_eta,
        out_small[0, BIAS : BIAS + heads],
        out_out,
        out_small[:, :head],
        out_inner_b,
        out_gain,
        out_shift,
        out_norm_one,
        out_post_gain,
        out_post_shift,
        both,
        down.reshape(3, unit, -1, width // 3).transpose(2, 1, 0, 3).reshape(down_rows, width),
        out_norm_two,
    )


def drain(phases, arrays):
    try:
        while True:
            arrays = phases.send(arrays)
    except StopIteration:
        return arrays


def solution(mesh):
    split = ("dp", "fsdp")
    row, vector, token = P(split, None), P(split), P(None, split, None)
    dp, fsdp = mesh.shape["dp"], mesh.shape["fsdp"]
    return jax.shard_map(
        lambda *arrays: body(dp, fsdp, *arrays),
        mesh=mesh,
        in_specs=(token, P(None, split), token, row, row, P(), row, row) + (vector,) * 6 + (row, row, vector),
        out_specs=(token, token, row, row, P(), row, row) + (vector,) * 6 + (row, row, vector),
        check_vma=False,
    )
```
